32 devices in a mesh: groups: 2 (over y), tp: 4 (over z), pd: 4 (over x, core).
Axes of the slice: x: 2, y: 2, z: 4, core: 2. Of those that a mesh axis runs over, the one named last changes fastest.
Arguments:
- prefill_hidden: bfloat16 [49152, 7168], P(('groups', 'pd'), 'tp'), parts along dimension 0, may hold values from -6 to 6
- draft_hidden: bfloat16 [64, 7168], P(('groups', 'pd'), 'tp'), parts along dimension 0, may hold values from -6 to 6
- kv_down: bfloat16 [7168, 576], P('tp'), may hold values from -0.0625 to 0.0625
- kv_gain: float32 [512], replicated, may hold values from 0.1 to 1.9
- query_latent: bfloat16 [32, 2, 1536], P('groups'), parts along dimension 0, may hold values from -110 to 110, as said below
- q_up: bfloat16 [1536, 24576], P(None, 'tp'), may hold values from -0.15625 to 0.15625
- kv_up: bfloat16 [512, 32768], P(None, 'tp'), may hold values from -0.25 to 0.25
- owners: int32 [32], P('groups'), parts along dimension 0, may hold values from 0 to 3, as said below
- segment_ids: int32 [32, 1536], P('groups'), parts along dimension 0, may hold values from 0 to 3, never falling along the last dimension, each value on 1 to 768 neighbouring positions
- accepted: int32 [32], P('groups'), parts along dimension 0, may hold values from 0 to 1
Outputs:
- owner_decoded: bfloat16 [64, 16384], P(('groups', 'pd'), 'tp'), parts along dimension 0
- owner_cache: bfloat16 [32, 1536, 576], P(('groups', 'pd'), 'tp'), parts along dimension 0
The draws below stay inside these ranges and needn't reach their ends.
There are 2 independent parts, one for each index of `groups`. The reference program is written for one: setup_inputs(seed, part) draws one part's arguments, and reference() takes and returns one part's arrays. A program takes and returns all parts, laid end to end along the dimension named above; an argument that names none is the same for every part. Nothing has to cross between parts.
Inputs may be any that keep to these rules, and one draw needn't show every extreme that they name: Owners are pd indices. Requests p * 4 to p * 4 + 3 belong to prefill rank p, and those 4 requests have 4 different owners; one owner holds a request of every prefill rank. `query_latent`: A few new tokens may have large query latents.
All inputs are finite; a program needn't handle non-finite values.
Results may differ from the reference program's by a relative error of at most 0.0117.
The reference program's roundings to bfloat16 on the way count: a program that leaves them out, or rounds other values in their place, can miss the bound.
Values may be sent and summed in bfloat16 or wider, within the bound.
No kernel may reach another device: no remote copies, remote signals or barrier semaphores. Data moves between devices by JAX's collectives and lax.ppermute only.
A program may use at most 192 MiB of HBM per device.

```python
import math
import jax
import jax.numpy as jnp
import numpy as np
from jax import lax

D = 7168
H = 128
DN = 128
DR = 64
DV = 128
KVL = 512
QL = 1536
PRE_TOK = 1536
RP = 4
R = 16
N_PD = 4


def draw_query_latent(key, part):
    key = jax.random.fold_in(key, 7)
    base = jax.random.truncated_normal(key, -4.0, 4.0, (R, 2, QL), jnp.float32)
    return base.astype(jnp.bfloat16)


def draw_owners(key, part):
    key = jax.random.fold_in(key, 11)
    busiest_key, rest_key = jax.random.split(key)
    busiest = jax.random.randint(busiest_key, (), 0, N_PD, jnp.int32)

    def one_rank(rank_key):
        pick_key, order_key = jax.random.split(rank_key)
        others = jax.random.permutation(pick_key, N_PD - 1).astype(jnp.int32)
        others = others + (others >= busiest).astype(jnp.int32)
        chosen = jnp.concatenate([busiest[None], others[:RP - 1]])
        return jax.random.permutation(order_key, chosen)
    return jax.vmap(one_rank)(jax.random.split(rest_key, N_PD)).reshape(-1).astype(jnp.int32)


def touch_ends(drawn, stream_key, smallest, high):
    longest = drawn.shape.index(max(drawn.shape))
    spots = []
    for shift in (0, 1):
        where = [jax.random.randint(jax.random.fold_in(stream_key, axis), (), 0, length) for axis, length in enumerate(drawn.shape)]
        where[longest] = (where[longest] + shift) % drawn.shape[longest]
        spots.append(tuple(where))
    return drawn.at[spots[0]].set(smallest).at[spots[1]].set(high)


def block_levels(own_key, shape, pieces, smallest, top_value):
    factor_of = 1.0
    for dim, blocks in pieces:
        steps = jax.random.uniform(jax.random.fold_in(jax.random.fold_in(own_key, 6), dim), (blocks,), jnp.float32, smallest / len(pieces), top_value / len(pieces))
        factor_of = factor_of * jnp.repeat(jnp.exp(steps), shape[dim] // blocks).reshape((-1,) + (1,) * (len(shape) - 1 - dim))
    return factor_of


def length_profile(count, total, bound, skew):
    weights = [(1 << 20) // math.isqrt(standing ** skew) + 1 for standing in range(2, count + 1)]
    surplus, holding = total - bound - (count - 1), [1] * (count - 1)
    while surplus > 0:
        candidates = [i for i in range(count - 1) if holding[i] < bound]
        pool, budget = sum([weights[i] for i in candidates]), surplus
        for i in candidates:
            extra = min(bound - holding[i], max(1, budget * weights[i] // pool), surplus)
            holding[i] = holding[i] + extra
            surplus = surplus - extra
    return np.array([bound] + holding)


def uneven_parts(key, amount, total, most, skew):
    if amount == 2:
        one = jax.random.randint(key, (), max(1, total - most), min(most, total - 1) + 1)
        return jnp.stack([one, total - one])
    sizes = jnp.asarray(length_profile(amount, total, most, skew), jnp.int32)
    pairs = (amount - 1) // 2
    source_of, receiver = sizes[1:1 + 2 * pairs:2], sizes[2:2 + 2 * pairs:2]
    slack = jnp.minimum(source_of - 1, most - receiver)
    passed = jax.random.randint(jax.random.fold_in(key, 1), (pairs,), 0, 1 << 20) % (slack + 1)
    sizes = sizes.at[1:1 + 2 * pairs:2].set(source_of - passed).at[2:2 + 2 * pairs:2].set(receiver + passed)
    return sizes[jax.random.permutation(jax.random.fold_in(key, 2), amount)]


def gaussian(own_key, dims, deviation, reach, pieces=(), held_as=jnp.bfloat16):
    array = deviation * jax.random.normal(own_key, dims, jnp.float32)
    if pieces:
        array = array * block_levels(own_key, dims, pieces, -0.22, 0.18)
    return jnp.clip(array, -reach, reach).astype(held_as)


def setup_inputs(seed: int = 0, part: int = 0) -> dict:
    arg_keys = jax.random.split(jax.random.key(seed), 11)
    part_keys = jax.random.split(jax.random.fold_in(arg_keys[10], part), 11)
    return {
        "prefill_hidden": gaussian(part_keys[0], (R * PRE_TOK, D), 1.0, 6.0, ((0, 4), (1, 4))),
        "draft_hidden": gaussian(part_keys[1], (R * 2, D), 1.0, 6.0, ((0, 4), (1, 4))),
        "kv_down": gaussian(arg_keys[2], (D, KVL + DR), D ** -0.5, 0.0625, ((0, 4),)),
        "kv_gain": jnp.clip(1.0 + 0.18 * jax.random.normal(arg_keys[3], (KVL,), jnp.float32), 0.1, 1.9),
        "query_latent": draw_query_latent(jax.random.fold_in(jax.random.fold_in(arg_keys[10], part), 71), part),
        "q_up": gaussian(arg_keys[5], (QL, H * (DN + DR)), QL ** -0.5, 0.15625, ((1, 4),)),
        "kv_up": gaussian(arg_keys[6], (KVL, H * (DN + DV)), KVL ** -0.5, 0.25, ((1, 4),)),
        "owners": draw_owners(jax.random.fold_in(jax.random.fold_in(arg_keys[10], part), 71), part),
        "segment_ids": jax.vmap(lambda own: jnp.searchsorted(jnp.cumsum(uneven_parts(own, 4, PRE_TOK, PRE_TOK // 2, 1)), jnp.arange(PRE_TOK), side="right"))(jax.random.split(part_keys[8], R)).reshape((R, PRE_TOK)).astype(jnp.int32),
        "accepted": touch_ends(jax.random.randint(part_keys[9], (R,), 0, 2), jax.random.fold_in(part_keys[9], 1), 0, 1).astype(jnp.int32),
    }


def rms_latent(comp, gain):
    lat = comp[:, :KVL]
    scale = lax.rsqrt(lax.optimization_barrier(jnp.mean(lat * lat, axis=-1, keepdims=True)) + 1e-06)
    return (lat * scale * gain).astype(jnp.bfloat16)

def rotate(values, position):
    half = values.shape[-1] // 2
    freq = jnp.exp(-jnp.log(10000.0) * jnp.arange(half, dtype=jnp.float32) / half)
    angle = position.astype(jnp.float32)[..., None] * freq
    cosine = jnp.cos(angle)
    sine = jnp.sin(angle)
    first = values[..., :half]
    second = values[..., half:]
    return jnp.concatenate([first * cosine - second * sine, first * sine + second * cosine], -1)

def narrow(values):
    return lax.optimization_barrier(values.astype(jnp.bfloat16)).astype(jnp.float32)

def reference(prefill_hidden, draft_hidden, kv_down, kv_gain, query_latent, q_up, kv_up, owners, segment_ids, accepted):
    comp = jnp.dot(prefill_hidden, kv_down, preferred_element_type=jnp.float32)
    where_pos = jnp.tile(jnp.arange(PRE_TOK, dtype=jnp.int32), R)
    keys = jnp.concatenate([rms_latent(comp, kv_gain), rotate(comp[:, KVL:], where_pos).astype(jnp.bfloat16)], 1)
    keys = keys.reshape(R, PRE_TOK, KVL + DR)
    draft_comp = jnp.dot(draft_hidden, kv_down, preferred_element_type=jnp.float32)
    new_pos = jnp.broadcast_to(PRE_TOK + jnp.arange(2, dtype=jnp.int32)[None, :], (R, 2))
    draft_keys = jnp.concatenate([rms_latent(draft_comp, kv_gain), rotate(draft_comp[:, KVL:], new_pos.reshape(-1)).astype(jnp.bfloat16)], 1)
    draft_keys = draft_keys.reshape(R, 2, KVL + DR)
    query_full = jnp.dot(query_latent.reshape(R * 2, QL), q_up, preferred_element_type=jnp.float32).reshape(R, 2, H, DN + DR)
    q_nope = query_full[..., :DN].astype(jnp.bfloat16)
    q_rot = rotate(query_full[..., DN:], new_pos[:, :, None]).astype(jnp.bfloat16)
    up_heads = kv_up.reshape(KVL, H, DN + DV).astype(jnp.float32)
    q_abs = jnp.einsum('rjhd,khd->rjhk', q_nope.astype(jnp.float32), up_heads[:, :, :DN]).astype(jnp.bfloat16)
    scale = (DN + DR) ** (-0.5)
    draft_valid = (jnp.arange(2)[None, :] <= jnp.arange(2)[:, None])[:, None, :]
    results = []
    for request in range(R):
        every_key = jnp.concatenate([keys[request], draft_keys[request]], 0).astype(jnp.float32)
        current = segment_ids[request, PRE_TOK - 1]
        prompt_valid = jnp.broadcast_to((segment_ids[request] == current)[None, None, :], (2, 1, PRE_TOK))
        valid = jnp.concatenate([prompt_valid, draft_valid], 2)
        scores = jnp.einsum('jhk,tk->jht', q_abs[request].astype(jnp.float32), every_key[:, :KVL])
        scores = (scores + jnp.einsum('jhk,tk->jht', q_rot[request].astype(jnp.float32), every_key[:, KVL:])) * scale
        scores = jnp.where(valid, scores, -1e+30)
        top = lax.optimization_barrier(jnp.max(scores, axis=-1, keepdims=True))
        weights = jnp.where(valid, jnp.exp(scores - top), 0.0)
        total = lax.optimization_barrier(jnp.sum(weights, axis=-1))
        numer = jnp.einsum('jht,tk->jhk', narrow(weights), every_key[:, :KVL])
        attended = narrow(numer / total[..., None])
        head_out = jnp.einsum('jhk,khd->jhd', attended, up_heads[:, :, DN:])
        keep = (jnp.arange(2) <= accepted[request]).astype(jnp.float32)[:, None, None]
        results.append((head_out * keep).astype(jnp.bfloat16).reshape(2, H * DV))
    stacked = jnp.stack(results, 0)
    slots = (owners * N_PD + jnp.arange(R, dtype=jnp.int32) // RP).astype(jnp.int32)
    placed = jnp.zeros((N_PD * N_PD, 2, H * DV), jnp.bfloat16).at[slots].set(stacked)
    cache = jnp.zeros((N_PD * N_PD, PRE_TOK, KVL + DR), jnp.bfloat16).at[slots].set(keys)
    return (placed.reshape(N_PD * N_PD * 2, H * DV), cache)
```

```python
import jax
import jax.numpy as jnp
from jax import lax
from jax.experimental import pallas as pl
from jax.experimental.pallas import tpu as pltpu
from jax.sharding import PartitionSpec as P

DN = 128
DR = 64
DV = 128
KVL = 512
QL = 1536
PRE_TOK = 1536
RP = 4
WIDTH = KVL + DR
HALF = DR // 2
CODED = WIDTH + 16
UNIT = 128
LANES = RP * UNIT
STEPS = 256.0
TOP = 32767.0
BF = jnp.bfloat16
F32 = jnp.float32
NT = (((1,), (1,)), ((), ()))


def rms_latent(comp, gain):
    lat = comp[:, :KVL]
    scale = lax.rsqrt(jnp.mean(lat * lat, axis=-1, keepdims=True) + 1e-06)
    return (lat * scale * gain).astype(jnp.bfloat16)


def rotate(values, position):
    half = values.shape[-1] // 2
    freq = jnp.exp(-jnp.log(10000.0) * jnp.arange(half, dtype=jnp.float32) / half)
    angle = position.astype(jnp.float32)[..., None] * freq
    cosine = jnp.cos(angle)
    sine = jnp.sin(angle)
    first = values[..., :half]
    second = values[..., half:]
    return jnp.concatenate([first * cosine - second * sine, first * sine + second * cosine], -1)


def block_stats(keys, q_lat, q_pos, valid):
    scale = (DN + DR) ** (-0.5)
    scores = jnp.einsum("jhk,tk->jht", q_lat, keys[:, :KVL], preferred_element_type=jnp.float32)
    scores = (
        scores + jnp.einsum("jhk,tk->jht", q_pos, keys[:, KVL:], preferred_element_type=jnp.float32)
    ) * scale
    scores = jnp.where(valid, scores, -1e30)
    top = jnp.max(scores, axis=-1)
    weights = jnp.where(valid, jnp.exp(scores - top[..., None]), 0.0)
    total = jnp.sum(weights, axis=-1)
    numer = jnp.einsum(
        "jht,tk->jhk",
        weights.astype(jnp.bfloat16),
        keys[:, :KVL],
        preferred_element_type=jnp.float32,
    )
    return (top, total, numer)


def combine(left, right):
    top = jnp.maximum(left[0], right[0])
    left_scale = jnp.exp(left[0] - top)
    right_scale = jnp.exp(right[0] - top)
    total = left[1] * left_scale + right[1] * right_scale
    numer = left[2] * left_scale[..., None] + right[2] * right_scale[..., None]
    return (top, total, numer)


def local_general(
    prefill_hidden,
    draft_hidden,
    kv_down,
    kv_gain,
    query_latent,
    q_up,
    kv_up,
    owners,
    segment_ids,
    accepted,
):
    tp_count = lax.axis_size("tp")
    pd_count = lax.axis_size("pd")
    tp_rank = lax.axis_index("tp")
    mine_rank = lax.axis_index("pd")
    requests = owners.shape[0]
    share = PRE_TOK // tp_count
    width = KVL + DR
    local_hidden = prefill_hidden.reshape(RP, PRE_TOK, prefill_hidden.shape[1])
    summed = lax.psum_scatter(
        jnp.einsum(
            "rtd,dw->trw", local_hidden, kv_down, preferred_element_type=jnp.float32
        ).reshape(lax.axis_size("tp") * share, RP * width),
        "tp",
        scatter_dimension=0,
        tiled=True,
    ).reshape(share * RP, width)
    draft_sum = lax.psum(jnp.dot(draft_hidden, kv_down, preferred_element_type=jnp.float32), "tp")
    first_req = mine_rank * RP
    row_pos = jnp.broadcast_to(
        tp_rank * share + jnp.arange(share, dtype=jnp.int32)[:, None], (share, RP)
    )
    page_rows = jnp.concatenate(
        [
            rms_latent(summed, kv_gain),
            rotate(summed[:, KVL:], row_pos.reshape(-1)).astype(jnp.bfloat16),
        ],
        1,
    )
    page_rows = page_rows.reshape(share, RP, width)
    draft_pos = jnp.tile(PRE_TOK + jnp.arange(2, dtype=jnp.int32), RP)
    draft_rows = jnp.concatenate(
        [
            rms_latent(draft_sum, kv_gain),
            rotate(draft_sum[:, KVL:], draft_pos).astype(jnp.bfloat16),
        ],
        1,
    )
    draft_rows = draft_rows.reshape(RP, 2, width)
    my_owners = lax.dynamic_slice_in_dim(owners, first_req, RP, 0)
    routing = (my_owners[None, :] == jnp.arange(pd_count, dtype=jnp.int32)[:, None]).astype(
        jnp.bfloat16
    )
    send_pages = jnp.einsum(
        "dk,tkw->dtw", routing, page_rows, preferred_element_type=jnp.float32
    ).astype(jnp.bfloat16)
    send_drafts = jnp.einsum(
        "dk,kjw->djw", routing, draft_rows, preferred_element_type=jnp.float32
    ).astype(jnp.bfloat16)
    pages, drafts = (
        lax.all_to_all(send_pages, "pd", split_axis=0, concat_axis=0, tiled=True),
        lax.all_to_all(send_drafts, "pd", split_axis=0, concat_axis=0, tiled=True),
    )
    heads_local = q_up.shape[1] // (DN + DR)
    query_full = jnp.dot(
        query_latent.reshape(requests * 2, QL), q_up, preferred_element_type=jnp.float32
    )
    query_full = query_full.reshape(requests, 2, heads_local, DN + DR)
    new_pos = jnp.broadcast_to(PRE_TOK + jnp.arange(2, dtype=jnp.int32)[None, :], (requests, 2))
    q_nope = query_full[..., :DN].astype(jnp.bfloat16)
    q_rot = rotate(query_full[..., DN:], new_pos[:, :, None]).astype(jnp.bfloat16)
    up_heads = kv_up.reshape(KVL, heads_local, DN + DV)
    w_value = up_heads[:, :, DN:]
    q_abs = jnp.einsum(
        "rjhd,khd->rjhk", q_nope, up_heads[:, :, :DN], preferred_element_type=jnp.float32
    ).astype(jnp.bfloat16)
    owner_table = owners.reshape(pd_count, RP) == mine_rank
    holding = jnp.sum(owner_table.astype(jnp.int32), axis=1)
    slot_of = jnp.sum(
        owner_table.astype(jnp.int32) * jnp.arange(RP, dtype=jnp.int32)[None, :], axis=1
    )
    owned_count = jnp.sum(holding)
    order = jnp.argsort((1 - holding) * pd_count + jnp.arange(pd_count, dtype=jnp.int32))
    draft_valid = (jnp.arange(2)[None, :] <= jnp.arange(2)[:, None])[:, None, :]
    empty = jnp.zeros((pd_count, 2, heads_local * DV), jnp.bfloat16)

    def finish(stats, source, request, q_lat, q_pos, result):
        stats = combine(stats, block_stats(drafts[source], q_lat, q_pos, draft_valid))
        attended = (stats[2] / stats[1][..., None]).astype(jnp.bfloat16)
        head_out = jnp.einsum("jhk,khd->jhd", attended, w_value, preferred_element_type=jnp.float32)
        keep = (jnp.arange(2) <= accepted[request]).astype(jnp.float32)[:, None, None]
        answer = (head_out * keep).astype(jnp.bfloat16).reshape(1, 2, heads_local * DV)
        return lax.dynamic_update_slice(result, answer, (source, 0, 0))

    def attend(turn, result):
        source = order[turn]
        request = source * RP + slot_of[source]
        q_lat = q_abs[request]
        q_pos = q_rot[request]
        seg_row = segment_ids[request]
        current = seg_row[PRE_TOK - 1]
        init = (
            jnp.full((2, heads_local), -1e30, jnp.float32),
            jnp.zeros((2, heads_local), jnp.float32),
            jnp.zeros((2, heads_local, KVL), jnp.float32),
        )
        valid = (seg_row == current)[None, None, :]
        stats = combine(
            init,
            block_stats(
                lax.all_gather(pages[source], "tp", axis=0, tiled=True), q_lat, q_pos, valid
            ),
        )
        return finish(stats, source, request, q_lat, q_pos, result)

    result = lax.fori_loop(0, owned_count, attend, empty)
    return (result.reshape(pd_count * 2, heads_local * DV), pages)


def encode(values, out_ref):
    levels = []
    for first, last in ((0, KVL), (KVL, WIDTH)):
        block = values[first:last]
        top = jnp.maximum(jnp.max(jnp.abs(block), axis=0, keepdims=True), 1e-30)
        level = jnp.ceil(jnp.log2(top) * STEPS)
        codes = jnp.round(block * (jnp.exp2(level * (-1.0 / STEPS)) * TOP))
        codes = jnp.clip(codes, -TOP, TOP).astype(jnp.int32)
        out_ref[first:last, :] = codes.astype(jnp.int16)
        levels.append(level.astype(jnp.int32))
    row = lax.broadcasted_iota(jnp.int32, (16, values.shape[1]), 0)
    extra = jnp.where(row == 0, levels[0], jnp.where(row == 1, levels[1], 0))
    out_ref[WIDTH:CODED, :] = extra.astype(jnp.int16)


def decode(ref):
    level = ref[WIDTH:CODED, :].astype(jnp.int32).astype(F32)
    step = jnp.exp2(level * (1.0 / STEPS)) * (1.0 / TOP)
    lat = ref[0:KVL, :].astype(jnp.int32).astype(F32) * step[0:1]
    rot = ref[KVL:WIDTH, :].astype(jnp.int32).astype(F32) * step[1:2]
    return jnp.concatenate([lat, rot], 0)


def key_rows(comp, gain, cosine, sine):
    lat = comp[:KVL]
    scale = lax.rsqrt(jnp.mean(lat * lat, axis=0, keepdims=True) + 1e-06)
    first = comp[KVL : KVL + HALF]
    second = comp[KVL + HALF :]
    return jnp.concatenate(
        [
            lat * scale * gain,
            first * cosine - second * sine,
            first * sine + second * cosine,
        ],
        0,
    )


def project_kernel(order, hid_ref, down_ref, sum_ref, qa_ref, qb_ref, qc_ref):
    step = pl.program_id(0)
    rows = hid_ref[...].reshape(LANES, hid_ref.shape[-1])
    total = lax.dot_general(down_ref[...], rows, NT, preferred_element_type=F32)
    sum_ref[0] = total
    for which, ref in enumerate((qa_ref, qb_ref, qc_ref)):

        @pl.when(step == which)
        def _(ref=ref):
            encode(total, ref)


def project(order, hidden, down_t, unit, units):
    depth = hidden.shape[-1]
    coded = jax.ShapeDtypeStruct((CODED, LANES), jnp.int16)
    whole = pl.BlockSpec((CODED, LANES), lambda i, order: (0, 0))
    return pl.pallas_call(
        project_kernel,
        grid_spec=pltpu.PrefetchScalarGridSpec(
            num_scalar_prefetch=1,
            grid=(4,),
            in_specs=[
                pl.BlockSpec(
                    (RP, UNIT, depth), lambda i, order: (0, order[i] * units + unit, 0)
                ),
                pl.BlockSpec((WIDTH, depth), lambda i, order: (0, 0)),
            ],
            out_specs=[
                pl.BlockSpec((1, WIDTH, LANES), lambda i, order: (order[i], 0, 0)),
                whole,
                whole,
                whole,
            ],
        ),
        out_shape=[jax.ShapeDtypeStruct((4, WIDTH, LANES), F32), coded, coded, coded],
        compiler_params=pltpu.CompilerParams(vmem_limit_bytes=40 << 20),
        cost_estimate=pl.CostEstimate(
            flops=2 * 4 * LANES * depth * WIDTH,
            bytes_accessed=4 * LANES * (depth * 2 + WIDTH * 6),
            transcendentals=0,
        ),
        name="project",
    )(order, hidden, down_t)


def add_kernel(where, own_ref, got_ref, pass_ref, out_ref, held_ref):
    encode(own_ref[0] + decode(got_ref), out_ref)


def add_on(where, sums, got, passed):
    coded = jax.ShapeDtypeStruct((CODED, LANES), jnp.int16)
    return pl.pallas_call(
        add_kernel,
        grid_spec=pltpu.PrefetchScalarGridSpec(
            num_scalar_prefetch=1,
            grid=(RP,),
            in_specs=[
                pl.BlockSpec((1, WIDTH, UNIT), lambda i, where: (where[0], 0, i)),
                pl.BlockSpec((CODED, UNIT), lambda i, where: (0, i)),
                pl.BlockSpec(memory_space=pl.ANY),
            ],
            out_specs=[
                pl.BlockSpec((CODED, UNIT), lambda i, where: (0, i)),
                pl.BlockSpec(memory_space=pl.ANY),
            ],
        ),
        out_shape=[coded, jax.ShapeDtypeStruct(passed.shape, passed.dtype)],
        input_output_aliases={3: 1},
        compiler_params=pltpu.CompilerParams(vmem_limit_bytes=32 << 20),
        cost_estimate=pl.CostEstimate(
            flops=8 * LANES * WIDTH, bytes_accessed=8 * LANES * WIDTH, transcendentals=0
        ),
        name="add_on",
    )(where, sums, got, passed)


def finish_kernel(where, own_ref, one_ref, two_ref, three_ref, gain_ref, cos_ref, sin_ref, out_ref):
    comp = own_ref[0] + decode(one_ref) + decode(two_ref) + decode(three_ref)
    out_ref[...] = key_rows(comp, gain_ref[...], cos_ref[...], sin_ref[...]).astype(BF)


def finish(where, sums, blocks, gain, cosine, sine):
    part = pl.BlockSpec((CODED, UNIT), lambda i, where: (0, i))
    table = pl.BlockSpec((HALF, UNIT), lambda i, where: (0, 0))
    return pl.pallas_call(
        finish_kernel,
        grid_spec=pltpu.PrefetchScalarGridSpec(
            num_scalar_prefetch=1,
            grid=(RP,),
            in_specs=[
                pl.BlockSpec((1, WIDTH, UNIT), lambda i, where: (where[0], 0, i)),
                part,
                part,
                part,
                pl.BlockSpec((KVL, UNIT), lambda i, where: (0, 0)),
                table,
                table,
            ],
            out_specs=pl.BlockSpec((WIDTH, UNIT), lambda i, where: (0, i)),
        ),
        out_shape=jax.ShapeDtypeStruct((WIDTH, LANES), BF),
        compiler_params=pltpu.CompilerParams(vmem_limit_bytes=32 << 20),
        cost_estimate=pl.CostEstimate(
            flops=16 * LANES * WIDTH, bytes_accessed=12 * LANES * WIDTH, transcendentals=0
        ),
        name="finish",
    )(where, sums, *blocks, gain, cosine, sine)


def page_kernel(where, slots, has, own_ref, one_ref, two_ref, keys_ref, gain_ref, cos_ref, sin_ref, out_ref):
    slot = pl.program_id(0)
    out_ref[...] = jnp.zeros_like(out_ref)

    @pl.when((has[slot] > 0) & (where[0] == 1))
    def _():
        comp = own_ref[0] + decode(one_ref) + decode(two_ref)
        rows = key_rows(comp, gain_ref[...], cos_ref[...], sin_ref[...])
        out_ref[0] = rows.T.astype(BF)

    @pl.when((has[slot] > 0) & (where[0] != 1))
    def _():
        out_ref[0] = keys_ref[...].astype(F32).T.astype(BF)


def pages_of(where, slots, has, sums, blocks, keys, gain, cosine, sine):
    count = slots.shape[0]

    def lane(i, where, slots, has):
        return (0, slots[i])

    part = pl.BlockSpec((CODED, UNIT), lane)
    table = pl.BlockSpec((HALF, UNIT), lambda i, *_: (0, 0))
    return pl.pallas_call(
        page_kernel,
        grid_spec=pltpu.PrefetchScalarGridSpec(
            num_scalar_prefetch=3,
            grid=(count,),
            in_specs=[
                pl.BlockSpec(
                    (1, WIDTH, UNIT), lambda i, where, slots, has: (where[0], 0, slots[i])
                ),
                part,
                part,
                pl.BlockSpec((WIDTH, UNIT), lane),
                pl.BlockSpec((KVL, UNIT), lambda i, *_: (0, 0)),
                table,
                table,
            ],
            out_specs=pl.BlockSpec((1, UNIT, WIDTH), lambda i, *_: (i, 0, 0)),
        ),
        out_shape=jax.ShapeDtypeStruct((count, UNIT, WIDTH), BF),
        compiler_params=pltpu.CompilerParams(vmem_limit_bytes=32 << 20),
        cost_estimate=pl.CostEstimate(
            flops=16 * LANES * WIDTH, bytes_accessed=14 * LANES * WIDTH, transcendentals=0
        ),
        name="pages",
    )(where, slots, has, sums, *blocks, keys, gain, cosine, sine)


def query_kernel(lat_ref, up_ref, *refs):
    *key_refs, cos_ref, sin_ref, out_ref = refs
    full = jnp.dot(lat_ref[...], up_ref[...], preferred_element_type=F32)
    for h, key_ref in enumerate(key_refs):
        base = h * (DN + DR)
        nope = full[:, base : base + DN].astype(BF)
        first = full[:, base + DN : base + DN + HALF]
        second = full[:, base + DN + HALF : base + DN + DR]
        absorbed = lax.dot_general(nope, key_ref[...], NT, preferred_element_type=F32)
        cosine, sine = cos_ref[...], sin_ref[...]
        out_ref[h] = jnp.concatenate(
            [absorbed, first * cosine - second * sine, first * sine + second * cosine], 1
        )


def queries(latents, q_up, kv_up, cosine, sine):
    rows = latents.shape[0]
    heads = q_up.shape[1] // (DN + DR)
    step = 4
    key_spec = [
        pl.BlockSpec((KVL, DN), lambda i, h=h: (0, 2 * (step * i + h))) for h in range(step)
    ]
    table = pl.BlockSpec((rows, HALF), lambda i: (0, 0))
    return pl.pallas_call(
        query_kernel,
        grid=(heads // step,),
        in_specs=[
            pl.BlockSpec((rows, QL), lambda i: (0, 0)),
            pl.BlockSpec((QL, step * (DN + DR)), lambda i: (0, i)),
            *key_spec,
            table,
            table,
        ],
        out_specs=pl.BlockSpec((step, rows, WIDTH), lambda i: (i, 0, 0)),
        out_shape=jax.ShapeDtypeStruct((heads, rows, WIDTH), F32),
        compiler_params=pltpu.CompilerParams(vmem_limit_bytes=32 << 20),
        cost_estimate=pl.CostEstimate(
            flops=2 * rows * QL * q_up.shape[1],
            bytes_accessed=2 * QL * q_up.shape[1] + KVL * kv_up.shape[1],
            transcendentals=0,
        ),
        name="queries",
    )(latents, q_up, *([kv_up] * step), cosine, sine)


def attend_kernel(where, q_ref, *refs):
    key_refs, (valid_ref, draft_ref), out_refs = refs[:6], refs[6:8], refs[8:]
    request = pl.program_id(0)

    @pl.when(where[0] == 3)
    def _():
        scale = (DN + DR) ** (-0.5)
        local_rows = q_ref.shape[2]
        query = q_ref[...].reshape(4 * local_rows, WIDTH)
        keys = jnp.concatenate([ref[...] for ref in key_refs], 1)
        drafts = draft_ref[...]
        scores = jnp.dot(query, keys, preferred_element_type=F32) * scale
        scores = jnp.where(valid_ref[0] > 0.0, scores, -1e30)
        fresh = lax.dot_general(query, drafts, NT, preferred_element_type=F32) * scale
        row = lax.broadcasted_iota(jnp.int32, fresh.shape, 0)
        late = (row % local_rows) // (local_rows // 2)
        offset = lax.broadcasted_iota(jnp.int32, fresh.shape, 1) - 2 * request
        fresh = jnp.where((offset >= 0) & (offset <= late), fresh, -1e30)
        top = jnp.maximum(
            jnp.max(scores, axis=1, keepdims=True), jnp.max(fresh, axis=1, keepdims=True)
        )
        weights = jnp.exp(scores - top)
        fresh = jnp.exp(fresh - top)
        total = jnp.sum(weights, axis=1, keepdims=True) + jnp.sum(fresh, axis=1, keepdims=True)
        numer = lax.dot_general(weights.astype(BF), keys[:KVL], NT, preferred_element_type=F32)
        numer = numer + jnp.dot(fresh.astype(BF), drafts[:, :KVL], preferred_element_type=F32)
        result = (numer / total).astype(BF)
        for t, ref in enumerate(out_refs):
            ref[0] = result[t * local_rows : (t + 1) * local_rows]


def attend(where, query, keys, valid, drafts):
    local_rows = query.shape[2]
    key_spec = pl.BlockSpec((WIDTH, UNIT), lambda i, where: (0, i))
    out = jax.ShapeDtypeStruct((RP, local_rows, KVL), BF)
    return pl.pallas_call(
        attend_kernel,
        grid_spec=pltpu.PrefetchScalarGridSpec(
            num_scalar_prefetch=1,
            grid=(RP,),
            in_specs=[
                pl.BlockSpec((4, 1, local_rows, WIDTH), lambda i, where: (0, i, 0, 0)),
                *([key_spec] * len(keys)),
                pl.BlockSpec((1, 1, valid.shape[2]), lambda i, where: (i, 0, 0)),
                pl.BlockSpec(drafts.shape, lambda i, where: (0, 0)),
            ],
            out_specs=[pl.BlockSpec((1, local_rows, KVL), lambda i, where: (i, 0, 0))] * 4,
        ),
        out_shape=[out] * 4,
        compiler_params=pltpu.CompilerParams(vmem_limit_bytes=40 << 20),
        cost_estimate=pl.CostEstimate(
            flops=2 * RP * 4 * local_rows * 768 * (WIDTH + KVL),
            bytes_accessed=8 << 20,
            transcendentals=RP * 4 * local_rows * 768,
        ),
        name="attend",
    )(where, query, *keys, valid, drafts)


def heads_kernel(o_ref, keep_ref, *refs):
    *value_refs, out_ref = refs
    for h, value_ref in enumerate(value_refs):
        row = jnp.dot(o_ref[h].astype(BF), value_ref[...], preferred_element_type=F32)
        out_ref[:, h * DV : (h + 1) * DV] = row * keep_ref[...]


def heads_out(attended, keep, kv_up):
    heads, rows, _ = attended.shape
    step = 8
    value_spec = [
        pl.BlockSpec((KVL, DV), lambda i, h=h: (0, 2 * (step * i + h) + 1)) for h in range(step)
    ]
    return pl.pallas_call(
        heads_kernel,
        grid=(heads // step,),
        in_specs=[
            pl.BlockSpec((step, rows, KVL), lambda i: (i, 0, 0)),
            pl.BlockSpec((rows, DV), lambda i: (0, 0)),
            *value_spec,
        ],
        out_specs=pl.BlockSpec((rows, step * DV), lambda i: (0, i)),
        out_shape=jax.ShapeDtypeStruct((rows, heads * DV), F32),
        compiler_params=pltpu.CompilerParams(vmem_limit_bytes=32 << 20),
        cost_estimate=pl.CostEstimate(
            flops=2 * rows * KVL * heads * DV, bytes_accessed=KVL * heads * DV * 2, transcendentals=0
        ),
        name="heads_out",
    )(attended, keep, *([kv_up] * step))


def rope_tables(position):
    freq = jnp.exp(-jnp.log(10000.0) * jnp.arange(HALF, dtype=F32) / HALF)
    angle = position.astype(F32)[..., None] * freq
    return jnp.cos(angle), jnp.sin(angle)


def local_line(
    prefill_hidden,
    draft_hidden,
    kv_down,
    kv_gain,
    query_latent,
    q_up,
    kv_up,
    owners,
    segment_ids,
    accepted,
):
    pd_count = lax.axis_size("pd")
    z = lax.axis_index("tp")
    p = lax.axis_index("pd")
    share = PRE_TOK // 4
    units = share // UNIT
    first_req = p * RP
    where = z.astype(jnp.int32).reshape(1)

    def pick(*choices):
        return jnp.asarray(choices, jnp.int32)[z].reshape(1)

    order = jnp.asarray([[3, 2, 1, 0], [3, 2, 0, 1], [3, 2, 0, 1], [0, 2, 1, 3]], jnp.int32)[z]
    hidden = prefill_hidden.reshape(RP, PRE_TOK, prefill_hidden.shape[1])
    down_t = kv_down.T
    work = [project(order, hidden, down_t, u, units) for u in range(units)]
    sums = [w[0] for w in work]
    coded = [list(w[1:]) for w in work]

    latents = lax.dynamic_slice_in_dim(query_latent, first_req, RP, 0).reshape(RP * 2, QL)
    new_pos = jnp.tile(PRE_TOK + jnp.arange(2, dtype=jnp.int32), RP)
    new_cos, new_sin = rope_tables(new_pos)
    query = queries(latents, q_up, kv_up, new_cos, new_sin)
    heads = query.shape[0]
    query = (
        query.reshape(heads, RP, 2, WIDTH).transpose(1, 2, 0, 3).reshape(RP, 2 * heads, WIDTH)
    ).astype(BF)
    query = lax.all_gather(query, "tp", axis=0)
    draft = jnp.dot(draft_hidden, kv_down, preferred_element_type=F32)
    draft = jnp.sum(lax.all_gather(draft, "tp", axis=0), axis=0)
    draft_keys = jnp.concatenate(
        [rms_latent(draft, kv_gain), rotate(draft[:, KVL:], new_pos).astype(BF)], 1
    )
    draft_keys = jnp.pad(draft_keys, ((0, UNIT - RP * 2), (0, 0)))
    my_segments = lax.dynamic_slice_in_dim(segment_ids, first_req, RP, 0)
    valid = (my_segments == my_segments[:, -1:])[:, PRE_TOK // 2 :].astype(F32)
    valid = valid.reshape(RP, 1, PRE_TOK // 2)

    gain = jnp.broadcast_to(kv_gain[:, None], (KVL, UNIT))
    position = z * share + jnp.arange(share, dtype=jnp.int32).reshape(units, UNIT)
    cosine, sine = rope_tables(position)
    cosine, sine = jnp.swapaxes(cosine, 1, 2), jnp.swapaxes(sine, 1, 2)

    inward = [(0, 1), (3, 2)]
    sends = [(u, k) for u in range(units) for k in (0, 1)] + [(u, 2) for u in range(units)]
    own_of_add = {0: pick(0, 3, 0, 0), 1: pick(0, 2, 0, 0), 2: pick(0, 0, 1, 0)}
    got = {}
    added = {}
    nothing = jnp.zeros((8, 128), jnp.int16)
    for at, (u, k) in enumerate(sends):
        got[u, k] = lax.ppermute(coded[u][k], "tp", inward)
        ahead = sends[at + 2] if at + 2 < len(sends) else None
        passed = nothing if ahead is None else coded[ahead[0]][ahead[1]]
        added[u, k], passed = add_on(own_of_add[k], sums[u], got[u, k], passed)
        if ahead is not None:
            coded[ahead[0]][ahead[1]] = passed

    early = []
    moved = []
    own_mid = pick(0, 0, 3, 0)
    for u in range(units):
        outer = lax.ppermute(added[u, 0], "tp", [(1, 2), (2, 1)])
        outer, _ = add_on(own_mid, sums[u], outer, nothing)
        outer = lax.ppermute(outer, "tp", [(2, 3), (1, 0)])
        middle = lax.ppermute(added[u, 1], "tp", [(1, 2)])
        keys = finish(where, sums[u], (outer, got[u, 1], middle), gain, cosine[u], sine[u])
        early.append(keys)
        moved.append(lax.ppermute(keys, "tp", [(2, 3)]))

    result = attend(where, query, moved + early, valid, draft_keys)
    back = [lax.ppermute(result[t], "tp", [(3, t)]) for t in range(3)]
    attended = jnp.where(z == 3, result[3], back[0] + back[1] + back[2])
    attended = attended.reshape(RP, 2, heads, KVL).transpose(2, 0, 1, 3)
    attended = attended.reshape(heads, RP * 2, KVL).astype(F32)
    my_accepted = lax.dynamic_slice_in_dim(accepted, first_req, RP, 0)
    keep = (jnp.arange(2)[None, :] <= my_accepted[:, None]).astype(F32).reshape(RP * 2, 1)
    answer = heads_out(attended, jnp.broadcast_to(keep, (RP * 2, DV)), kv_up)
    answer = answer.reshape(RP, 2, heads * DV)

    my_owners = lax.dynamic_slice_in_dim(owners, first_req, RP, 0)
    routing = my_owners[None, :] == jnp.arange(pd_count, dtype=jnp.int32)[:, None]
    has = jnp.any(routing, axis=1)
    slots = jnp.sum(routing.astype(jnp.int32) * jnp.arange(RP, dtype=jnp.int32)[None, :], axis=1)
    placed = jnp.where(has[:, None, None], answer[slots], 0.0).astype(BF)
    placed = lax.all_to_all(placed, "pd", split_axis=0, concat_axis=0, tiled=True)

    pages = []
    for u in range(units):
        last = lax.ppermute(added[u, 2], "tp", [(2, 1)])
        page = pages_of(
            where,
            slots,
            has.astype(jnp.int32),
            sums[u],
            (got[u, 2], last),
            early[u],
            gain,
            cosine[u],
            sine[u],
        )
        pages.append(lax.all_to_all(page, "pd", split_axis=0, concat_axis=0, tiled=True))
    return (placed.reshape(pd_count * 2, heads * DV), jnp.concatenate(pages, 1))


def solution(mesh):
    placed = (
        P(("groups", "pd"), "tp"),
        P(("groups", "pd"), "tp"),
        P("tp", None),
        P(),
        P("groups", None, None),
        P(None, "tp"),
        P(None, "tp"),
        P("groups"),
        P("groups", None),
        P("groups"),
    )
    return jax.shard_map(
        local_line if mesh.shape["tp"] == 4 else local_general,
        mesh=mesh,
        in_specs=placed,
        out_specs=(P(("groups", "pd"), "tp"), P(("groups", "pd"), "tp", None)),
        check_vma=False,
    )
```

```python
import functools

import jax
import jax.numpy as jnp
from jax import lax
from jax.experimental import pallas as pl
from jax.experimental.pallas import tpu as pltpu
from jax.sharding import PartitionSpec as P

DN = 128
DR = 64
DV = 128
KVL = 512
QL = 1536
PRE_TOK = 1536
RP = 4
WIDTH = KVL + DR
HALF = DR // 2
CODED = WIDTH + 16
SHARE = PRE_TOK // 4
UNIT = 128
UNITS = SHARE // UNIT
LANES = RP * UNIT
STEPS = 256.0
TOP = 32767.0
BF = jnp.bfloat16
F32 = jnp.float32
I16 = jnp.int16
NT = (((1,), (1,)), ((), ()))
ROOM = pltpu.CompilerParams(vmem_limit_bytes=20 << 20)
ANY = pl.BlockSpec(memory_space=pl.ANY)
VMEM = pl.BlockSpec(memory_space=pltpu.VMEM)
SMEM = pl.BlockSpec(memory_space=pltpu.SMEM)
HBM = pl.BlockSpec(memory_space=pltpu.HBM)
WIDE = pltpu.CompilerParams(vmem_limit_bytes=44 << 20)


COST = pl.CostEstimate(flops=1024, bytes_accessed=1024, transcendentals=0)


def rms_latent(comp, gain):
    lat = comp[:, :KVL]
    scale = lax.rsqrt(jnp.mean(lat * lat, axis=-1, keepdims=True) + 1e-06)
    return (lat * scale * gain).astype(jnp.bfloat16)


def rotate(values, position):
    half = values.shape[-1] // 2
    freq = jnp.exp(-jnp.log(10000.0) * jnp.arange(half, dtype=jnp.float32) / half)
    angle = position.astype(jnp.float32)[..., None] * freq
    cosine = jnp.cos(angle)
    sine = jnp.sin(angle)
    first = values[..., :half]
    second = values[..., half:]
    return jnp.concatenate([first * cosine - second * sine, first * sine + second * cosine], -1)


def block_stats(keys, q_lat, q_pos, valid):
    scale = (DN + DR) ** (-0.5)
    scores = jnp.einsum("jhk,tk->jht", q_lat, keys[:, :KVL], preferred_element_type=jnp.float32)
    scores = (
        scores + jnp.einsum("jhk,tk->jht", q_pos, keys[:, KVL:], preferred_element_type=jnp.float32)
    ) * scale
    scores = jnp.where(valid, scores, -1e30)
    top = jnp.max(scores, axis=-1)
    weights = jnp.where(valid, jnp.exp(scores - top[..., None]), 0.0)
    total = jnp.sum(weights, axis=-1)
    numer = jnp.einsum(
        "jht,tk->jhk",
        weights.astype(jnp.bfloat16),
        keys[:, :KVL],
        preferred_element_type=jnp.float32,
    )
    return (top, total, numer)


def combine(left, right):
    top = jnp.maximum(left[0], right[0])
    left_scale = jnp.exp(left[0] - top)
    right_scale = jnp.exp(right[0] - top)
    total = left[1] * left_scale + right[1] * right_scale
    numer = left[2] * left_scale[..., None] + right[2] * right_scale[..., None]
    return (top, total, numer)


def local_general(
    prefill_hidden,
    draft_hidden,
    kv_down,
    kv_gain,
    query_latent,
    q_up,
    kv_up,
    owners,
    segment_ids,
    accepted,
):
    tp_count = lax.axis_size("tp")
    pd_count = lax.axis_size("pd")
    tp_rank = lax.axis_index("tp")
    mine_rank = lax.axis_index("pd")
    requests = owners.shape[0]
    share = PRE_TOK // tp_count
    width = KVL + DR
    local_hidden = prefill_hidden.reshape(RP, PRE_TOK, prefill_hidden.shape[1])
    summed = lax.psum_scatter(
        jnp.einsum(
            "rtd,dw->trw", local_hidden, kv_down, preferred_element_type=jnp.float32
        ).reshape(lax.axis_size("tp") * share, RP * width),
        "tp",
        scatter_dimension=0,
        tiled=True,
    ).reshape(share * RP, width)
    draft_sum = lax.psum(jnp.dot(draft_hidden, kv_down, preferred_element_type=jnp.float32), "tp")
    first_req = mine_rank * RP
    row_pos = jnp.broadcast_to(
        tp_rank * share + jnp.arange(share, dtype=jnp.int32)[:, None], (share, RP)
    )
    page_rows = jnp.concatenate(
        [
            rms_latent(summed, kv_gain),
            rotate(summed[:, KVL:], row_pos.reshape(-1)).astype(jnp.bfloat16),
        ],
        1,
    )
    page_rows = page_rows.reshape(share, RP, width)
    draft_pos = jnp.tile(PRE_TOK + jnp.arange(2, dtype=jnp.int32), RP)
    draft_rows = jnp.concatenate(
        [
            rms_latent(draft_sum, kv_gain),
            rotate(draft_sum[:, KVL:], draft_pos).astype(jnp.bfloat16),
        ],
        1,
    )
    draft_rows = draft_rows.reshape(RP, 2, width)
    my_owners = lax.dynamic_slice_in_dim(owners, first_req, RP, 0)
    routing = (my_owners[None, :] == jnp.arange(pd_count, dtype=jnp.int32)[:, None]).astype(
        jnp.bfloat16
    )
    send_pages = jnp.einsum(
        "dk,tkw->dtw", routing, page_rows, preferred_element_type=jnp.float32
    ).astype(jnp.bfloat16)
    send_drafts = jnp.einsum(
        "dk,kjw->djw", routing, draft_rows, preferred_element_type=jnp.float32
    ).astype(jnp.bfloat16)
    pages, drafts = (
        lax.all_to_all(send_pages, "pd", split_axis=0, concat_axis=0, tiled=True),
        lax.all_to_all(send_drafts, "pd", split_axis=0, concat_axis=0, tiled=True),
    )
    heads_local = q_up.shape[1] // (DN + DR)
    query_full = jnp.dot(
        query_latent.reshape(requests * 2, QL), q_up, preferred_element_type=jnp.float32
    )
    query_full = query_full.reshape(requests, 2, heads_local, DN + DR)
    new_pos = jnp.broadcast_to(PRE_TOK + jnp.arange(2, dtype=jnp.int32)[None, :], (requests, 2))
    q_nope = query_full[..., :DN].astype(jnp.bfloat16)
    q_rot = rotate(query_full[..., DN:], new_pos[:, :, None]).astype(jnp.bfloat16)
    up_heads = kv_up.reshape(KVL, heads_local, DN + DV)
    w_value = up_heads[:, :, DN:]
    q_abs = jnp.einsum(
        "rjhd,khd->rjhk", q_nope, up_heads[:, :, :DN], preferred_element_type=jnp.float32
    ).astype(jnp.bfloat16)
    owner_table = owners.reshape(pd_count, RP) == mine_rank
    holding = jnp.sum(owner_table.astype(jnp.int32), axis=1)
    slot_of = jnp.sum(
        owner_table.astype(jnp.int32) * jnp.arange(RP, dtype=jnp.int32)[None, :], axis=1
    )
    owned_count = jnp.sum(holding)
    order = jnp.argsort((1 - holding) * pd_count + jnp.arange(pd_count, dtype=jnp.int32))
    draft_valid = (jnp.arange(2)[None, :] <= jnp.arange(2)[:, None])[:, None, :]
    empty = jnp.zeros((pd_count, 2, heads_local * DV), jnp.bfloat16)

    def finish(stats, source, request, q_lat, q_pos, result):
        stats = combine(stats, block_stats(drafts[source], q_lat, q_pos, draft_valid))
        attended = (stats[2] / stats[1][..., None]).astype(jnp.bfloat16)
        head_out = jnp.einsum("jhk,khd->jhd", attended, w_value, preferred_element_type=jnp.float32)
        keep = (jnp.arange(2) <= accepted[request]).astype(jnp.float32)[:, None, None]
        answer = (head_out * keep).astype(jnp.bfloat16).reshape(1, 2, heads_local * DV)
        return lax.dynamic_update_slice(result, answer, (source, 0, 0))

    def attend(turn, result):
        source = order[turn]
        request = source * RP + slot_of[source]
        q_lat = q_abs[request]
        q_pos = q_rot[request]
        seg_row = segment_ids[request]
        current = seg_row[PRE_TOK - 1]
        init = (
            jnp.full((2, heads_local), -1e30, jnp.float32),
            jnp.zeros((2, heads_local), jnp.float32),
            jnp.zeros((2, heads_local, KVL), jnp.float32),
        )
        valid = (seg_row == current)[None, None, :]
        stats = combine(
            init,
            block_stats(
                lax.all_gather(pages[source], "tp", axis=0, tiled=True), q_lat, q_pos, valid
            ),
        )
        return finish(stats, source, request, q_lat, q_pos, result)

    result = lax.fori_loop(0, owned_count, attend, empty)
    return (result.reshape(pd_count * 2, heads_local * DV), pages)


def encode(values):
    levels = []
    parts = []
    for first, last in ((0, KVL), (KVL, WIDTH)):
        block = values[first:last]
        top = jnp.maximum(jnp.max(jnp.abs(block), axis=0, keepdims=True), 1e-30)
        level = jnp.ceil(jnp.log2(top) * STEPS)
        codes = jnp.round(block * (jnp.exp2(level * (-1.0 / STEPS)) * TOP))
        parts.append(jnp.clip(codes, -TOP, TOP).astype(jnp.int32).astype(I16))
        levels.append(level.astype(jnp.int32))
    row = lax.broadcasted_iota(jnp.int32, (16, values.shape[1]), 0)
    extra = jnp.where(row == 0, levels[0], jnp.where(row == 1, levels[1], 0))
    return jnp.concatenate([*parts, extra.astype(I16)], 0)


def decode(codes):
    level = codes[WIDTH:CODED].astype(jnp.int32).astype(F32)
    step = jnp.exp2(level * (1.0 / STEPS)) * (1.0 / TOP)
    lat = codes[0:KVL].astype(jnp.int32).astype(F32) * step[0:1]
    rot = codes[KVL:WIDTH].astype(jnp.int32).astype(F32) * step[1:2]
    return jnp.concatenate([lat, rot], 0)


def key_rows(comp, gain, cosine, sine):
    lat = comp[:KVL]
    scale = lax.rsqrt(jnp.mean(lat * lat, axis=0, keepdims=True) + 1e-06)
    first = comp[KVL : KVL + HALF]
    second = comp[KVL + HALF :]
    return jnp.concatenate(
        [
            lat * scale * gain,
            first * cosine - second * sine,
            first * sine + second * cosine,
        ],
        0,
    )


def project_kernel(request, table, hid_ref, down_ref, after_ref, sum_ref, code_ref, rows, arrived):
    copies = []
    for i in range(3):
        place = pl.ds(pl.multiple_of(table[i] * SHARE, SHARE), SHARE)
        copies.append(
            pltpu.make_async_copy(hid_ref.at[request, place], rows.at[i], arrived.at[i])
        )
        copies[i].start()
    for i in range(3):
        copies[i].wait()
        total = lax.dot_general(down_ref[...], rows[i], NT, preferred_element_type=F32)
        sum_ref[table[3 + i]] = total
        if i < 2:
            for first in range(0, SHARE, UNIT):
                lanes = slice(first, first + UNIT)
                code_ref[i, :, lanes] = encode(total[:, lanes])


def project(table, hidden, down_t, request, after):
    depth = hidden.shape[-1]
    return pl.pallas_call(
        functools.partial(project_kernel, request),
        in_specs=[SMEM, HBM, VMEM, ANY],
        out_specs=[VMEM, VMEM],
        out_shape=[
            jax.ShapeDtypeStruct((3, WIDTH, SHARE), F32),
            jax.ShapeDtypeStruct((2, CODED, SHARE), I16),
        ],
        scratch_shapes=[
            pltpu.VMEM((3, SHARE, depth), BF),
            pltpu.SemaphoreType.DMA((3,)),
        ],
        compiler_params=WIDE,
        cost_estimate=COST,
        name="project",
    )(table, hidden, down_t, after)


def project_last_kernel(table, hid_ref, down_ref, sum_ref, *refs):
    *code_refs, rows, arrived = refs
    copies = []
    for u in range(UNITS):
        place = pl.ds(SHARE + u * UNIT, UNIT)
        copies.append(
            pltpu.make_async_copy(hid_ref.at[:, place], rows.at[u], arrived.at[u])
        )
        copies[u].start()
    for u in range(UNITS):
        copies[u].wait()
        block = rows[u].reshape(LANES, rows.shape[-1])
        total = lax.dot_general(down_ref[...], block, NT, preferred_element_type=F32)
        sum_ref[u] = total
        for first in range(0, LANES, UNIT):
            lanes = slice(first, first + UNIT)
            code_refs[u][:, lanes] = encode(total[:, lanes])


def project_last(table, hidden, down_t):
    depth = hidden.shape[-1]
    return pl.pallas_call(
        project_last_kernel,
        in_specs=[SMEM, HBM, VMEM],
        out_specs=[VMEM] * (1 + UNITS),
        out_shape=[
            jax.ShapeDtypeStruct((UNITS, WIDTH, LANES), F32),
            *([jax.ShapeDtypeStruct((CODED, LANES), I16)] * UNITS),
        ],
        scratch_shapes=[
            pltpu.VMEM((UNITS, RP, UNIT, depth), BF),
            pltpu.SemaphoreType.DMA((UNITS,)),
        ],
        compiler_params=WIDE,
        cost_estimate=COST,
        name="project_last",
    )(table, hidden, down_t)


def add_kernel(table, own_ref, got_ref, after_ref, out_ref):
    for i in range(2):

        @pl.when(i < table[2])
        def _(i=i):
            for first in range(0, SHARE, UNIT):
                lanes = slice(first, first + UNIT)
                out_ref[i, :, lanes] = encode(
                    own_ref[table[i], :, lanes] + decode(got_ref[i, :, lanes])
                )


def add_on(table, sums, got, after):
    return pl.pallas_call(
        add_kernel,
        in_specs=[SMEM, VMEM, VMEM, ANY],
        out_specs=VMEM,
        out_shape=jax.ShapeDtypeStruct((2, CODED, SHARE), I16),
        compiler_params=ROOM,
        cost_estimate=COST,
        name="add_on",
    )(table, sums, got, after)


def add_two_kernel(table, own_ref, got_ref, side_ref, *refs):
    out_ref = refs[-1]

    @pl.when(table[2] > 0)
    def _():
        for first in range(0, SHARE, UNIT):
            lanes = slice(first, first + UNIT)
            out_ref[0, :, lanes] = encode(
                own_ref[table[0], :, lanes] + decode(got_ref[0, :, lanes])
            )

    @pl.when(table[2] > 1)
    def _():
        for first in range(0, SHARE, UNIT):
            lanes = slice(first, first + UNIT)
            total = own_ref[table[1], :, lanes] + decode(got_ref[1, :, lanes])
            out_ref[1, :, lanes] = encode(total + decode(side_ref[1, :, lanes]))


def add_two(table, sums, got, side, after):
    return pl.pallas_call(
        add_two_kernel,
        in_specs=[SMEM, VMEM, VMEM, VMEM, *([ANY] * len(after))],
        out_specs=VMEM,
        out_shape=jax.ShapeDtypeStruct((2, CODED, SHARE), I16),
        compiler_params=ROOM,
        cost_estimate=COST,
        name="add_two",
    )(table, sums, got, side, *after)


def add_last_kernel(unit, table, own_ref, got_ref, out_ref):
    @pl.when(table[7] == 2)
    def _():
        for first in range(0, LANES, UNIT):
            lanes = slice(first, first + UNIT)
            out_ref[:, lanes] = encode(own_ref[unit, :, lanes] + decode(got_ref[:, lanes]))


def add_last(table, sums, got, unit):
    return pl.pallas_call(
        functools.partial(add_last_kernel, unit),
        in_specs=[SMEM, VMEM, VMEM],
        out_specs=VMEM,
        out_shape=jax.ShapeDtypeStruct((CODED, LANES), I16),
        compiler_params=ROOM,
        cost_estimate=COST,
        name="add_last",
    )(table, sums, got)


def finish_kernel(table, own_ref, got_ref, mid_ref, gain_ref, cos_ref, sin_ref, *refs):
    midcos_ref, midsin_ref, out_ref = refs
    z = table[7]

    def write(place, lanes, comp, cosine, sine):
        rows = key_rows(comp, gain_ref[...], cosine[:, lanes], sine[:, lanes])
        out_ref[place, :, lanes] = rows.astype(BF)

    for first in range(0, SHARE, UNIT):
        lanes = slice(first, first + UNIT)

        @pl.when((z == 0) | (z == 3))
        def _(lanes=lanes):
            comp = own_ref[table[8], :, lanes] + decode(got_ref[0, :, lanes])
            write(0, lanes, comp, cos_ref, sin_ref)

        @pl.when(z == 3)
        def _(lanes=lanes):
            write(1, lanes, decode(got_ref[1, :, lanes]), midcos_ref, midsin_ref)

        @pl.when(z == 2)
        def _(lanes=lanes):
            write(0, lanes, decode(mid_ref[1, :, lanes]), midcos_ref, midsin_ref)


def finish(table, sums, got, sent, gain, tables):
    return pl.pallas_call(
        finish_kernel,
        in_specs=[SMEM, *([VMEM] * 8)],
        out_specs=VMEM,
        out_shape=jax.ShapeDtypeStruct((2, WIDTH, SHARE), BF),
        compiler_params=ROOM,
        cost_estimate=COST,
        name="finish",
    )(table, sums, got, sent, gain, *tables)


def page_kernel(unit, table, slots, has, own_ref, one_ref, two_ref, *refs):
    keys_refs, (gain_ref, cos_ref, sin_ref, out_ref) = refs[:RP], refs[RP:]
    place = slice(unit * UNIT, (unit + 1) * UNIT)

    def one_slot(slot, carry):
        @pl.when(has[slot] == 0)
        def _():
            out_ref[slot] = jnp.zeros((WIDTH, UNIT), BF)

        for r in range(RP):
            mine = (has[slot] > 0) & (slots[slot] == r)
            lanes = slice(r * UNIT, (r + 1) * UNIT)

            @pl.when(mine & (table[7] == 1))
            def _(lanes=lanes):
                comp = own_ref[unit, :, lanes] + decode(one_ref[:, lanes])
                comp = comp + decode(two_ref[:, lanes])
                rows = key_rows(comp, gain_ref[...], cos_ref[:, place], sin_ref[:, place])
                out_ref[slot] = rows.astype(BF)

            @pl.when(mine & (table[7] != 1))
            def _(r=r):
                out_ref[slot] = keys_refs[r][0, :, place]

        return carry

    lax.fori_loop(0, out_ref.shape[0], one_slot, 0)


def pages_of(table, slots, has, sums, one, two, keys, gain, cosine, sine, unit):
    count = slots.shape[0]
    return pl.pallas_call(
        functools.partial(page_kernel, unit),
        in_specs=[SMEM, SMEM, SMEM, *([VMEM] * (6 + RP))],
        out_specs=VMEM,
        out_shape=jax.ShapeDtypeStruct((count, WIDTH, UNIT), BF),
        compiler_params=ROOM,
        cost_estimate=COST,
        name="pages",
    )(table, slots, has, sums, one, two, *keys, gain, cosine, sine)


def query_kernel(lat_ref, up_ref, draft_ref, down_ref, *refs):
    *key_refs, cos_ref, sin_ref, out_ref, split_ref = refs

    @pl.when(pl.program_id(0) == 0)
    def _():
        rest = lax.dot_general(draft_ref[...], down_ref[...], NT, preferred_element_type=F32)
        for n in range(3):
            term = rest.astype(BF).astype(F32)
            split_ref[n] = term
            rest = rest - term
        split_ref[3] = jnp.zeros_like(rest)

    full = jnp.dot(lat_ref[...], up_ref[...], preferred_element_type=F32)
    for h, key_ref in enumerate(key_refs):
        base = h * (DN + DR)
        nope = full[:, base : base + DN].astype(BF)
        first = full[:, base + DN : base + DN + HALF]
        second = full[:, base + DN + HALF : base + DN + DR]
        absorbed = lax.dot_general(nope, key_ref[...], NT, preferred_element_type=F32)
        cosine, sine = cos_ref[...], sin_ref[...]
        out_ref[h] = jnp.concatenate(
            [absorbed, first * cosine - second * sine, first * sine + second * cosine], 1
        )


def queries(latents, q_up, kv_up, draft, down_t, cosine, sine, after):
    rows = latents.shape[0]
    heads = q_up.shape[1] // (DN + DR)
    step = 4
    key_spec = [
        pl.BlockSpec((KVL, DN), lambda i, h=h: (0, 2 * (step * i + h))) for h in range(step)
    ]
    whole = lambda i: (0, 0)
    table = pl.BlockSpec((rows, HALF), whole)
    body = lambda *refs: query_kernel(*refs[:-3], *refs[-2:])
    return pl.pallas_call(
        body,
        grid=(heads // step,),
        in_specs=[
            pl.BlockSpec((rows, QL), whole),
            pl.BlockSpec((QL, step * (DN + DR)), lambda i: (0, i)),
            pl.BlockSpec(draft.shape, whole),
            pl.BlockSpec(down_t.shape, whole),
            *key_spec,
            table,
            table,
            ANY,
        ],
        out_specs=[
            pl.BlockSpec((step, rows, WIDTH), lambda i: (i, 0, 0)),
            pl.BlockSpec((4, rows, WIDTH), lambda i: (0, 0, 0)),
        ],
        out_shape=[
            jax.ShapeDtypeStruct((heads, rows, WIDTH), F32),
            jax.ShapeDtypeStruct((4, rows, WIDTH), F32),
        ],
        compiler_params=WIDE,
        cost_estimate=COST,
        name="queries",
    )(latents, q_up, draft, down_t, *([kv_up] * step), cosine, sine, after)


def attend_kernel(table, *refs):
    q_ref, keys_refs, refs = refs[0], refs[1 : 1 + RP], refs[1 + RP :]
    valid_ref, gain_ref, cos_ref, sin_ref, *out_refs = refs

    @pl.when(table[7] == 3)
    def _():
        scale = (DN + DR) ** (-0.5)
        local_rows = out_refs[0].shape[1]
        new = 2 * RP
        base = RP * local_rows
        comp = 0.0
        for t in range(4):
            terms = q_ref[t, base : base + 4 * new, :].astype(F32)
            comp = comp + (terms[0:new] + terms[new : 2 * new] + terms[2 * new : 3 * new])
        lat = comp[:, :KVL]
        norm = lax.rsqrt(jnp.mean(lat * lat, axis=-1, keepdims=True) + 1e-06)
        first = comp[:, KVL : KVL + HALF]
        second = comp[:, KVL + HALF :]
        cosine, sine = cos_ref[...], sin_ref[...]
        drafts = jnp.concatenate(
            [
                lat * norm * gain_ref[...],
                first * cosine - second * sine,
                first * sine + second * cosine,
            ],
            1,
        )
        drafts = jnp.concatenate([drafts, jnp.zeros((UNIT - new, WIDTH), F32)], 0).astype(BF)
        for request in range(RP):
            mine = slice(request * local_rows, (request + 1) * local_rows)
            query = jnp.concatenate([q_ref[t, mine, :] for t in range(4)], 0)
            keys = jnp.concatenate([keys_refs[request][1], keys_refs[request][0]], 1)
            scores = jnp.dot(query, keys, preferred_element_type=F32) * scale
            scores = jnp.where(valid_ref[request] > 0.0, scores, -1e30)
            fresh = lax.dot_general(query, drafts, NT, preferred_element_type=F32) * scale
            row = lax.broadcasted_iota(jnp.int32, fresh.shape, 0)
            late = (row % local_rows) // (local_rows // 2)
            offset = lax.broadcasted_iota(jnp.int32, fresh.shape, 1) - 2 * request
            fresh = jnp.where((offset >= 0) & (offset <= late), fresh, -1e30)
            top = jnp.maximum(
                jnp.max(scores, axis=1, keepdims=True), jnp.max(fresh, axis=1, keepdims=True)
            )
            weights = jnp.exp(scores - top)
            fresh = jnp.exp(fresh - top)
            total = jnp.sum(weights, axis=1, keepdims=True)
            total = total + jnp.sum(fresh, axis=1, keepdims=True)
            numer = lax.dot_general(
                weights.astype(BF), keys[:KVL], NT, preferred_element_type=F32
            )
            numer = numer + jnp.dot(
                fresh.astype(BF), drafts[:, :KVL], preferred_element_type=F32
            )
            result = (numer / total).astype(BF)
            for t, ref in enumerate(out_refs):
                ref[request] = result[t * local_rows : (t + 1) * local_rows]


def attend(table, messages, keys, valid, gain, cosine, sine):
    local_rows = (messages.shape[1] - 4 * 2 * RP) // RP
    out = jax.ShapeDtypeStruct((RP, local_rows, KVL), BF)
    return pl.pallas_call(
        attend_kernel,
        in_specs=[SMEM, *([VMEM] * (1 + RP + 4))],
        out_specs=[VMEM] * 4,
        out_shape=[out] * 4,
        compiler_params=ROOM,
        cost_estimate=COST,
        name="attend",
    )(table, messages, *keys, valid, gain, cosine, sine)


def heads_kernel(o_ref, keep_ref, *refs):
    *value_refs, out_ref = refs
    for h, value_ref in enumerate(value_refs):
        row = jnp.dot(o_ref[h].astype(BF), value_ref[...], preferred_element_type=F32)
        out_ref[:, h * DV : (h + 1) * DV] = row * keep_ref[...]


def heads_out(attended, keep, kv_up):
    heads, rows, _ = attended.shape
    step = 8
    value_spec = [
        pl.BlockSpec((KVL, DV), lambda i, h=h: (0, 2 * (step * i + h) + 1)) for h in range(step)
    ]
    return pl.pallas_call(
        heads_kernel,
        grid=(heads // step,),
        in_specs=[
            pl.BlockSpec((step, rows, KVL), lambda i: (i, 0, 0)),
            pl.BlockSpec((rows, DV), lambda i: (0, 0)),
            *value_spec,
        ],
        out_specs=pl.BlockSpec((rows, step * DV), lambda i: (0, i)),
        out_shape=jax.ShapeDtypeStruct((rows, heads * DV), F32),
        compiler_params=WIDE,
        cost_estimate=COST,
        name="heads_out",
    )(attended, keep, *([kv_up] * step))


def rope_tables(position):
    freq = jnp.exp(-jnp.log(10000.0) * jnp.arange(HALF, dtype=F32) / HALF)
    angle = position.astype(F32)[..., None] * freq
    return jnp.cos(angle), jnp.sin(angle)


def local_line(
    prefill_hidden,
    draft_hidden,
    kv_down,
    kv_gain,
    query_latent,
    q_up,
    kv_up,
    owners,
    segment_ids,
    accepted,
):
    pd_count = lax.axis_size("pd")
    z = lax.axis_index("tp")
    p = lax.axis_index("pd")
    first_req = p * RP

    table = jnp.asarray(
        [
            [3, 2, 0, 2, 1, 0, 1, 0, 0],
            [3, 2, 0, 2, 1, 0, 0, 1, 0],
            [3, 2, 0, 2, 1, 0, 0, 2, 1],
            [0, 2, 3, 0, 1, 2, 1, 3, 2],
        ],
        jnp.int32,
    )[z]
    adds = jnp.asarray([[0, 0, 0], [2, 1, 2], [0, 0, 1], [0, 0, 0]], jnp.int32)[z]
    more = jnp.asarray([[0, 0, 0], [0, 0, 1], [2, 1, 2], [0, 0, 0]], jnp.int32)[z]

    hidden = prefill_hidden.reshape(RP, PRE_TOK, prefill_hidden.shape[1])
    down_t = kv_down.T
    inward = [(0, 1), (3, 2)]
    sums = [None] * RP
    inner = [None] * RP
    sums[0], coded = project(table, hidden, down_t, 0, down_t)
    inner[0] = lax.ppermute(coded, "tp", inward)

    latents = lax.dynamic_slice_in_dim(query_latent, first_req, RP, 0).reshape(RP * 2, QL)
    new_pos = jnp.tile(PRE_TOK + jnp.arange(2, dtype=jnp.int32), RP)
    new_cos, new_sin = rope_tables(new_pos)
    query, terms = queries(
        latents, q_up, kv_up, draft_hidden, down_t, new_cos, new_sin, sums[0]
    )
    heads = query.shape[0]
    query = query.reshape(heads, RP, 2, WIDTH).transpose(1, 2, 0, 3)
    message = jnp.concatenate(
        [query.reshape(RP * 2 * heads, WIDTH), terms.reshape(8 * RP, WIDTH)], 0
    ).astype(BF)
    messages = lax.all_gather(message, "tp", axis=0)

    for r in range(1, RP):
        sums[r], coded = project(table, hidden, down_t, r, message)
        inner[r] = lax.ppermute(coded, "tp", inward)
    sums_last, *coded = project_last(table, hidden, down_t)
    inner_last = [lax.ppermute(c, "tp", inward) for c in coded]

    my_segments = lax.dynamic_slice_in_dim(segment_ids, first_req, RP, 0)
    valid = (my_segments == my_segments[:, -1:])[:, PRE_TOK // 2 :].astype(F32)
    valid = valid.reshape(RP, 1, PRE_TOK // 2)
    gain = jnp.broadcast_to(kv_gain[:, None], (KVL, UNIT))
    steps = jnp.arange(SHARE, dtype=jnp.int32)
    tables = [t.T for t in (*rope_tables(z * SHARE + steps), *rope_tables(2 * SHARE + steps))]

    keys = []
    sent = [None] * RP
    across = [None] * RP

    def first_hop(r, after):
        block = add_on(adds, sums[r], inner[r], after)
        across[r] = lax.ppermute(block, "tp", [(1, 2), (2, 1)])

    def second_hop(r, after):
        sent[r] = add_two(more, sums[r], across[r], inner[r], after)
        outer = lax.ppermute(sent[r], "tp", [(2, 3), (1, 0)])
        keys.append(finish(table, sums[r], outer, sent[r], gain, tables))

    first_hop(0, sums[3])
    first_hop(1, coded[0])
    second_hop(0, [])
    first_hop(2, sent[0])
    second_hop(1, [])
    first_hop(3, sent[1])
    second_hop(2, [])
    second_hop(3, [])

    result = attend(table, messages, keys, valid, kv_gain.reshape(1, KVL), new_cos, new_sin)
    back = [lax.ppermute(result[t], "tp", [(3, t)]) for t in range(3)]
    attended = jnp.where(z == 3, result[3], back[0] + back[1] + back[2])
    attended = attended.reshape(RP, 2, heads, KVL).transpose(2, 0, 1, 3)
    attended = attended.reshape(heads, RP * 2, KVL).astype(F32)
    my_accepted = lax.dynamic_slice_in_dim(accepted, first_req, RP, 0)
    keep = (jnp.arange(2)[None, :] <= my_accepted[:, None]).astype(F32).reshape(RP * 2, 1)
    answer = heads_out(attended, jnp.broadcast_to(keep, (RP * 2, DV)), kv_up)
    answer = answer.reshape(RP, 2, heads * DV)

    my_owners = lax.dynamic_slice_in_dim(owners, first_req, RP, 0)
    routing = my_owners[None, :] == jnp.arange(pd_count, dtype=jnp.int32)[:, None]
    has = jnp.any(routing, axis=1)
    slots = jnp.sum(routing.astype(jnp.int32) * jnp.arange(RP, dtype=jnp.int32)[None, :], axis=1)
    placed = jnp.where(has[:, None, None], answer[slots], 0.0).astype(BF)
    placed = lax.all_to_all(placed, "pd", split_axis=0, concat_axis=0, tiled=True)

    cache = []
    for u in range(UNITS):
        last = add_last(table, sums_last, inner_last[u], u)
        last = lax.ppermute(last, "tp", [(2, 1)])
        page = pages_of(
            table,
            slots,
            has.astype(jnp.int32),
            sums_last,
            inner_last[u],
            last,
            keys,
            gain,
            tables[0],
            tables[1],
            u,
        )
        page = lax.all_to_all(page, "pd", split_axis=0, concat_axis=0, tiled=True)
        cache.append(page)
    cache = jnp.swapaxes(jnp.concatenate(cache, 2), 1, 2)
    return (placed.reshape(pd_count * 2, heads * DV), cache)


def solution(mesh):
    placed = (
        P(("groups", "pd"), "tp"),
        P(("groups", "pd"), "tp"),
        P("tp", None),
        P(),
        P("groups", None, None),
        P(None, "tp"),
        P(None, "tp"),
        P("groups"),
        P("groups", None),
        P("groups"),
    )
    return jax.shard_map(
        local_line if mesh.shape["tp"] == 4 else local_general,
        mesh=mesh,
        in_specs=placed,
        out_specs=(P(("groups", "pd"), "tp"), P(("groups", "pd"), "tp", None)),
        check_vma=False,
    )
```

```python
import functools

import jax
import jax.numpy as jnp
from jax import lax
from jax.experimental import pallas as pl
from jax.experimental.pallas import tpu as pltpu
from jax.sharding import PartitionSpec as P

DN = 128
DR = 64
DV = 128
KVL = 512
QL = 1536
PRE_TOK = 1536
RP = 4
WIDTH = KVL + DR
HALF = DR // 2
CODED = WIDTH + 16
SHARE = PRE_TOK // 4
UNIT = 128
UNITS = SHARE // UNIT
LANES = RP * UNIT
STEPS = 256.0
TOP = 32767.0
BF = jnp.bfloat16
F32 = jnp.float32
I16 = jnp.int16
NT = (((1,), (1,)), ((), ()))
ROOM = pltpu.CompilerParams(vmem_limit_bytes=60 << 20)
ANY = pl.BlockSpec(memory_space=pl.ANY)
VMEM = pl.BlockSpec(memory_space=pltpu.VMEM)
SMEM = pl.BlockSpec(memory_space=pltpu.SMEM)


COST = pl.CostEstimate(flops=1024, bytes_accessed=1024, transcendentals=0)


def rms_latent(comp, gain):
    lat = comp[:, :KVL]
    scale = lax.rsqrt(jnp.mean(lat * lat, axis=-1, keepdims=True) + 1e-06)
    return (lat * scale * gain).astype(jnp.bfloat16)


def rotate(values, position):
    half = values.shape[-1] // 2
    freq = jnp.exp(-jnp.log(10000.0) * jnp.arange(half, dtype=jnp.float32) / half)
    angle = position.astype(jnp.float32)[..., None] * freq
    cosine = jnp.cos(angle)
    sine = jnp.sin(angle)
    first = values[..., :half]
    second = values[..., half:]
    return jnp.concatenate([first * cosine - second * sine, first * sine + second * cosine], -1)


def block_stats(keys, q_lat, q_pos, valid):
    scale = (DN + DR) ** (-0.5)
    scores = jnp.einsum("jhk,tk->jht", q_lat, keys[:, :KVL], preferred_element_type=jnp.float32)
    scores = (
        scores + jnp.einsum("jhk,tk->jht", q_pos, keys[:, KVL:], preferred_element_type=jnp.float32)
    ) * scale
    scores = jnp.where(valid, scores, -1e30)
    top = jnp.max(scores, axis=-1)
    weights = jnp.where(valid, jnp.exp(scores - top[..., None]), 0.0)
    total = jnp.sum(weights, axis=-1)
    numer = jnp.einsum(
        "jht,tk->jhk",
        weights.astype(jnp.bfloat16),
        keys[:, :KVL],
        preferred_element_type=jnp.float32,
    )
    return (top, total, numer)


def combine(left, right):
    top = jnp.maximum(left[0], right[0])
    left_scale = jnp.exp(left[0] - top)
    right_scale = jnp.exp(right[0] - top)
    total = left[1] * left_scale + right[1] * right_scale
    numer = left[2] * left_scale[..., None] + right[2] * right_scale[..., None]
    return (top, total, numer)


def local_general(
    prefill_hidden,
    draft_hidden,
    kv_down,
    kv_gain,
    query_latent,
    q_up,
    kv_up,
    owners,
    segment_ids,
    accepted,
):
    tp_count = lax.axis_size("tp")
    pd_count = lax.axis_size("pd")
    tp_rank = lax.axis_index("tp")
    mine_rank = lax.axis_index("pd")
    requests = owners.shape[0]
    share = PRE_TOK // tp_count
    width = KVL + DR
    local_hidden = prefill_hidden.reshape(RP, PRE_TOK, prefill_hidden.shape[1])
    summed = lax.psum_scatter(
        jnp.einsum(
            "rtd,dw->trw", local_hidden, kv_down, preferred_element_type=jnp.float32
        ).reshape(lax.axis_size("tp") * share, RP * width),
        "tp",
        scatter_dimension=0,
        tiled=True,
    ).reshape(share * RP, width)
    draft_sum = lax.psum(jnp.dot(draft_hidden, kv_down, preferred_element_type=jnp.float32), "tp")
    first_req = mine_rank * RP
    row_pos = jnp.broadcast_to(
        tp_rank * share + jnp.arange(share, dtype=jnp.int32)[:, None], (share, RP)
    )
    page_rows = jnp.concatenate(
        [
            rms_latent(summed, kv_gain),
            rotate(summed[:, KVL:], row_pos.reshape(-1)).astype(jnp.bfloat16),
        ],
        1,
    )
    page_rows = page_rows.reshape(share, RP, width)
    draft_pos = jnp.tile(PRE_TOK + jnp.arange(2, dtype=jnp.int32), RP)
    draft_rows = jnp.concatenate(
        [
            rms_latent(draft_sum, kv_gain),
            rotate(draft_sum[:, KVL:], draft_pos).astype(jnp.bfloat16),
        ],
        1,
    )
    draft_rows = draft_rows.reshape(RP, 2, width)
    my_owners = lax.dynamic_slice_in_dim(owners, first_req, RP, 0)
    routing = (my_owners[None, :] == jnp.arange(pd_count, dtype=jnp.int32)[:, None]).astype(
        jnp.bfloat16
    )
    send_pages = jnp.einsum(
        "dk,tkw->dtw", routing, page_rows, preferred_element_type=jnp.float32
    ).astype(jnp.bfloat16)
    send_drafts = jnp.einsum(
        "dk,kjw->djw", routing, draft_rows, preferred_element_type=jnp.float32
    ).astype(jnp.bfloat16)
    pages, drafts = (
        lax.all_to_all(send_pages, "pd", split_axis=0, concat_axis=0, tiled=True),
        lax.all_to_all(send_drafts, "pd", split_axis=0, concat_axis=0, tiled=True),
    )
    heads_local = q_up.shape[1] // (DN + DR)
    query_full = jnp.dot(
        query_latent.reshape(requests * 2, QL), q_up, preferred_element_type=jnp.float32
    )
    query_full = query_full.reshape(requests, 2, heads_local, DN + DR)
    new_pos = jnp.broadcast_to(PRE_TOK + jnp.arange(2, dtype=jnp.int32)[None, :], (requests, 2))
    q_nope = query_full[..., :DN].astype(jnp.bfloat16)
    q_rot = rotate(query_full[..., DN:], new_pos[:, :, None]).astype(jnp.bfloat16)
    up_heads = kv_up.reshape(KVL, heads_local, DN + DV)
    w_value = up_heads[:, :, DN:]
    q_abs = jnp.einsum(
        "rjhd,khd->rjhk", q_nope, up_heads[:, :, :DN], preferred_element_type=jnp.float32
    ).astype(jnp.bfloat16)
    owner_table = owners.reshape(pd_count, RP) == mine_rank
    holding = jnp.sum(owner_table.astype(jnp.int32), axis=1)
    slot_of = jnp.sum(
        owner_table.astype(jnp.int32) * jnp.arange(RP, dtype=jnp.int32)[None, :], axis=1
    )
    owned_count = jnp.sum(holding)
    order = jnp.argsort((1 - holding) * pd_count + jnp.arange(pd_count, dtype=jnp.int32))
    draft_valid = (jnp.arange(2)[None, :] <= jnp.arange(2)[:, None])[:, None, :]
    empty = jnp.zeros((pd_count, 2, heads_local * DV), jnp.bfloat16)

    def finish(stats, source, request, q_lat, q_pos, result):
        stats = combine(stats, block_stats(drafts[source], q_lat, q_pos, draft_valid))
        attended = (stats[2] / stats[1][..., None]).astype(jnp.bfloat16)
        head_out = jnp.einsum("jhk,khd->jhd", attended, w_value, preferred_element_type=jnp.float32)
        keep = (jnp.arange(2) <= accepted[request]).astype(jnp.float32)[:, None, None]
        answer = (head_out * keep).astype(jnp.bfloat16).reshape(1, 2, heads_local * DV)
        return lax.dynamic_update_slice(result, answer, (source, 0, 0))

    def attend(turn, result):
        source = order[turn]
        request = source * RP + slot_of[source]
        q_lat = q_abs[request]
        q_pos = q_rot[request]
        seg_row = segment_ids[request]
        current = seg_row[PRE_TOK - 1]
        init = (
            jnp.full((2, heads_local), -1e30, jnp.float32),
            jnp.zeros((2, heads_local), jnp.float32),
            jnp.zeros((2, heads_local, KVL), jnp.float32),
        )
        valid = (seg_row == current)[None, None, :]
        stats = combine(
            init,
            block_stats(
                lax.all_gather(pages[source], "tp", axis=0, tiled=True), q_lat, q_pos, valid
            ),
        )
        return finish(stats, source, request, q_lat, q_pos, result)

    result = lax.fori_loop(0, owned_count, attend, empty)
    return (result.reshape(pd_count * 2, heads_local * DV), pages)


def encode(values):
    levels = []
    parts = []
    for first, last in ((0, KVL), (KVL, WIDTH)):
        block = values[first:last]
        top = jnp.maximum(jnp.max(jnp.abs(block), axis=0, keepdims=True), 1e-30)
        level = jnp.ceil(jnp.log2(top) * STEPS)
        codes = jnp.round(block * (jnp.exp2(level * (-1.0 / STEPS)) * TOP))
        parts.append(jnp.clip(codes, -TOP, TOP).astype(jnp.int32).astype(I16))
        levels.append(level.astype(jnp.int32))
    row = lax.broadcasted_iota(jnp.int32, (16, values.shape[1]), 0)
    extra = jnp.where(row == 0, levels[0], jnp.where(row == 1, levels[1], 0))
    return jnp.concatenate([*parts, extra.astype(I16)], 0)


def decode(codes):
    level = codes[WIDTH:CODED].astype(jnp.int32).astype(F32)
    step = jnp.exp2(level * (1.0 / STEPS)) * (1.0 / TOP)
    lat = codes[0:KVL].astype(jnp.int32).astype(F32) * step[0:1]
    rot = codes[KVL:WIDTH].astype(jnp.int32).astype(F32) * step[1:2]
    return jnp.concatenate([lat, rot], 0)


def key_rows(comp, gain, cosine, sine):
    lat = comp[:KVL]
    scale = lax.rsqrt(jnp.mean(lat * lat, axis=0, keepdims=True) + 1e-06)
    first = comp[KVL : KVL + HALF]
    second = comp[KVL + HALF :]
    return jnp.concatenate(
        [
            lat * scale * gain,
            first * cosine - second * sine,
            first * sine + second * cosine,
        ],
        0,
    )


def project_kernel(table, hid_ref, down_ref, *refs):
    *_, sum_ref, one_ref, two_ref = refs
    step = pl.program_id(0)
    total = lax.dot_general(down_ref[...], hid_ref[0], NT, preferred_element_type=F32)
    sum_ref[0] = total
    for i, ref in enumerate((one_ref, two_ref)):

        @pl.when((step == i) & (table[6] == 1))
        def _(ref=ref):
            for first in range(0, SHARE, UNIT):
                lanes = slice(first, first + UNIT)
                ref[0, :, lanes] = encode(total[:, lanes])


def project_pair_kernel(table, hid_ref, down_ref, *refs):
    *_, sum_ref, code_ref = refs
    step = pl.program_id(0)
    total = lax.dot_general(down_ref[...], hid_ref[0], NT, preferred_element_type=F32)
    sum_ref[0] = total

    @pl.when((step < 2) & (table[6] == 1))
    def _():
        for first in range(0, SHARE, UNIT):
            lanes = slice(first, first + UNIT)
            code_ref[0, :, lanes] = encode(total[:, lanes])


def project(table, hidden, down_t, request, pair, after):
    depth = hidden.shape[-1]
    if pair:
        codes = [(2, lambda i, table: (jnp.minimum(i, 1), 0, 0))]
    else:
        codes = [(1, lambda i, table: (0, 0, 0))] * 2
    return pl.pallas_call(
        project_pair_kernel if pair else project_kernel,
        grid_spec=pltpu.PrefetchScalarGridSpec(
            num_scalar_prefetch=1,
            grid=(3,),
            in_specs=[
                pl.BlockSpec((1, SHARE, depth), lambda i, table: (request, table[i], 0)),
                pl.BlockSpec((WIDTH, depth), lambda i, table: (0, 0)),
                *([ANY] * len(after)),
            ],
            out_specs=[
                pl.BlockSpec((1, WIDTH, SHARE), lambda i, table: (table[3 + i], 0, 0)),
                *[pl.BlockSpec((1, CODED, SHARE), place) for _, place in codes],
            ],
        ),
        out_shape=[
            jax.ShapeDtypeStruct((3, WIDTH, SHARE), F32),
            *[jax.ShapeDtypeStruct((count, CODED, SHARE), I16) for count, _ in codes],
        ],
        compiler_params=ROOM,
        cost_estimate=COST,
        name="project",
    )(table, hidden, down_t, *after)


def project_last_kernel(table, hid_ref, down_ref, *refs):
    sum_ref, *code_refs = refs[-1 - UNITS :]
    step = pl.program_id(0)
    rows = hid_ref[...].reshape(LANES, hid_ref.shape[-1])
    total = lax.dot_general(down_ref[...], rows, NT, preferred_element_type=F32)
    sum_ref[0] = total
    for u, ref in enumerate(code_refs):

        @pl.when((step == u) & (table[6] == 1))
        def _(ref=ref):
            for first in range(0, LANES, UNIT):
                lanes = slice(first, first + UNIT)
                ref[:, lanes] = encode(total[:, lanes])


def project_last(table, hidden, down_t, after):
    depth = hidden.shape[-1]
    return pl.pallas_call(
        project_last_kernel,
        grid_spec=pltpu.PrefetchScalarGridSpec(
            num_scalar_prefetch=1,
            grid=(UNITS,),
            in_specs=[
                pl.BlockSpec((RP, UNIT, depth), lambda i, table: (0, UNITS + i, 0)),
                pl.BlockSpec((WIDTH, depth), lambda i, table: (0, 0)),
                *([ANY] * len(after)),
            ],
            out_specs=[
                pl.BlockSpec((1, WIDTH, LANES), lambda i, table: (i, 0, 0)),
                *([pl.BlockSpec((CODED, LANES), lambda i, table: (0, 0))] * UNITS),
            ],
        ),
        out_shape=[
            jax.ShapeDtypeStruct((UNITS, WIDTH, LANES), F32),
            *([jax.ShapeDtypeStruct((CODED, LANES), I16)] * UNITS),
        ],
        compiler_params=ROOM,
        cost_estimate=COST,
        name="project_last",
    )(table, hidden, down_t, *after)


def add_kernel(side_at, table, own_ref, got_ref, *refs):
    out_ref = refs[-1]
    step = pl.program_id(0)
    for i in range(2):

        @pl.when((step == i) & (table[2] > i))
        def _(i=i):
            total = own_ref[0] + decode(got_ref[0])
            if i == side_at:
                total = total + decode(refs[0][0])
            out_ref[0] = encode(total)


def add_on(table, sums, got, side=None, side_at=None, after=()):
    count = got.shape[0]
    block = lambda i, j, table: (i, 0, j)
    extra = []
    if side is not None:
        last = side.shape[0] - 1
        extra = [pl.BlockSpec((1, CODED, UNIT), lambda i, j, table: (last, 0, j))]
    return pl.pallas_call(
        functools.partial(add_kernel, side_at),
        grid_spec=pltpu.PrefetchScalarGridSpec(
            num_scalar_prefetch=1,
            grid=(count, UNITS),
            in_specs=[
                pl.BlockSpec((1, WIDTH, UNIT), lambda i, j, table: (table[i], 0, j)),
                pl.BlockSpec((1, CODED, UNIT), block),
                *extra,
                *([ANY] * len(after)),
            ],
            out_specs=pl.BlockSpec((1, CODED, UNIT), block),
        ),
        out_shape=jax.ShapeDtypeStruct((count, CODED, SHARE), I16),
        compiler_params=ROOM,
        cost_estimate=COST,
        name="add_on",
    )(table, sums, got, *([] if side is None else [side]), *after)


def add_last_kernel(table, own_ref, got_ref, out_ref):
    @pl.when(table[7] == 2)
    def _():
        out_ref[...] = encode(own_ref[0] + decode(got_ref[...]))


def add_last(table, sums, got, unit):
    return pl.pallas_call(
        add_last_kernel,
        grid_spec=pltpu.PrefetchScalarGridSpec(
            num_scalar_prefetch=1,
            grid=(RP,),
            in_specs=[
                pl.BlockSpec((1, WIDTH, UNIT), lambda i, table: (unit, 0, i)),
                pl.BlockSpec((CODED, UNIT), lambda i, table: (0, i)),
            ],
            out_specs=pl.BlockSpec((CODED, UNIT), lambda i, table: (0, i)),
        ),
        out_shape=jax.ShapeDtypeStruct((CODED, LANES), I16),
        compiler_params=ROOM,
        cost_estimate=COST,
        name="add_last",
    )(table, sums, got)


def finish_kernel(table, own_ref, got_ref, mid_ref, sent_ref, gain_ref, cos_ref, sin_ref, *refs):
    midcos_ref, midsin_ref, *_, out_ref = refs
    z = table[7]

    def write(place, comp, cosine, sine):
        rows = key_rows(comp, gain_ref[...], cosine[...], sine[...])
        out_ref[0, place] = rows.astype(BF)

    @pl.when((z == 0) | (z == 3))
    def _():
        write(0, own_ref[0] + decode(got_ref[0]), cos_ref, sin_ref)

    @pl.when(z == 3)
    def _():
        write(1, decode(mid_ref[0]), midcos_ref, midsin_ref)

    @pl.when(z == 2)
    def _():
        write(0, decode(sent_ref[0]), midcos_ref, midsin_ref)


def finish(table, sums, got, mid, sent, gain, tables, held, request, after=()):
    lane = pl.BlockSpec((HALF, UNIT), lambda j, table: (0, j))
    first = pl.BlockSpec((1, CODED, UNIT), lambda j, table: (0, 0, j))
    last = mid.shape[0] - 1
    second = pl.BlockSpec((1, CODED, UNIT), lambda j, table: (last, 0, j))
    return pl.pallas_call(
        finish_kernel,
        grid_spec=pltpu.PrefetchScalarGridSpec(
            num_scalar_prefetch=1,
            grid=(UNITS,),
            in_specs=[
                pl.BlockSpec((1, WIDTH, UNIT), lambda j, table: (table[8], 0, j)),
                first,
                second,
                second,
                pl.BlockSpec((KVL, UNIT), lambda j, table: (0, 0)),
                lane,
                lane,
                lane,
                lane,
                ANY,
                *([ANY] * len(after)),
            ],
            out_specs=pl.BlockSpec((1, 2, WIDTH, UNIT), lambda j, table: (request, 0, 0, j)),
        ),
        out_shape=jax.ShapeDtypeStruct(held.shape, BF),
        input_output_aliases={10: 0},
        compiler_params=ROOM,
        cost_estimate=COST,
        name="finish",
    )(table, sums, got, mid, sent, gain, *tables, held, *after)


def page_kernel(table, slots, has, own_ref, one_ref, two_ref, keys_ref, gain_ref, cos_ref, sin_ref, out_ref):
    slot = pl.program_id(0)

    @pl.when(has[slot] == 0)
    def _():
        out_ref[...] = jnp.zeros_like(out_ref)

    @pl.when((has[slot] > 0) & (table[7] == 1))
    def _():
        comp = own_ref[0] + decode(one_ref[...]) + decode(two_ref[...])
        rows = key_rows(comp, gain_ref[...], cos_ref[...], sin_ref[...])
        out_ref[0] = rows.astype(BF)

    @pl.when((has[slot] > 0) & (table[7] != 1))
    def _():
        out_ref[0] = keys_ref[0, 0]


def pages_of(table, slots, has, sums, one, two, keys, gain, cosine, sine, unit):
    count = slots.shape[0]
    part = pl.BlockSpec((CODED, UNIT), lambda i, table, slots, has: (0, slots[i]))
    lane = pl.BlockSpec((HALF, UNIT), lambda i, *_: (0, unit))
    return pl.pallas_call(
        page_kernel,
        grid_spec=pltpu.PrefetchScalarGridSpec(
            num_scalar_prefetch=3,
            grid=(count,),
            in_specs=[
                pl.BlockSpec((1, WIDTH, UNIT), lambda i, table, slots, has: (unit, 0, slots[i])),
                part,
                part,
                pl.BlockSpec(
                    (1, 1, WIDTH, UNIT), lambda i, table, slots, has: (slots[i], 0, 0, unit)
                ),
                pl.BlockSpec((KVL, UNIT), lambda i, *_: (0, 0)),
                lane,
                lane,
            ],
            out_specs=pl.BlockSpec((1, WIDTH, UNIT), lambda i, *_: (i, 0, 0)),
        ),
        out_shape=jax.ShapeDtypeStruct((count, WIDTH, UNIT), BF),
        compiler_params=ROOM,
        cost_estimate=COST,
        name="pages",
    )(table, slots, has, sums, one, two, keys, gain, cosine, sine)


def query_kernel(lat_ref, up_ref, draft_ref, down_ref, *refs):
    *key_refs, cos_ref, sin_ref, out_ref, split_ref = refs

    @pl.when(pl.program_id(0) == 0)
    def _():
        rest = lax.dot_general(draft_ref[...], down_ref[...], NT, preferred_element_type=F32)
        for n in range(3):
            term = rest.astype(BF).astype(F32)
            split_ref[n] = term
            rest = rest - term
        split_ref[3] = jnp.zeros_like(rest)

    full = jnp.dot(lat_ref[...], up_ref[...], preferred_element_type=F32)
    for h, key_ref in enumerate(key_refs):
        base = h * (DN + DR)
        nope = full[:, base : base + DN].astype(BF)
        first = full[:, base + DN : base + DN + HALF]
        second = full[:, base + DN + HALF : base + DN + DR]
        absorbed = lax.dot_general(nope, key_ref[...], NT, preferred_element_type=F32)
        cosine, sine = cos_ref[...], sin_ref[...]
        out_ref[h] = jnp.concatenate(
            [absorbed, first * cosine - second * sine, first * sine + second * cosine], 1
        )


def queries(latents, q_up, kv_up, draft, down_t, cosine, sine, after):
    rows = latents.shape[0]
    heads = q_up.shape[1] // (DN + DR)
    step = 4
    key_spec = [
        pl.BlockSpec((KVL, DN), lambda i, h=h: (0, 2 * (step * i + h))) for h in range(step)
    ]
    whole = lambda i: (0, 0)
    table = pl.BlockSpec((rows, HALF), whole)
    body = lambda *refs: query_kernel(*refs[:-3], *refs[-2:])
    return pl.pallas_call(
        body,
        grid=(heads // step,),
        in_specs=[
            pl.BlockSpec((rows, QL), whole),
            pl.BlockSpec((QL, step * (DN + DR)), lambda i: (0, i)),
            pl.BlockSpec(draft.shape, whole),
            pl.BlockSpec(down_t.shape, whole),
            *key_spec,
            table,
            table,
            ANY,
        ],
        out_specs=[
            pl.BlockSpec((step, rows, WIDTH), lambda i: (i, 0, 0)),
            pl.BlockSpec((4, rows, WIDTH), lambda i: (0, 0, 0)),
        ],
        out_shape=[
            jax.ShapeDtypeStruct((heads, rows, WIDTH), F32),
            jax.ShapeDtypeStruct((4, rows, WIDTH), F32),
        ],
        compiler_params=ROOM,
        cost_estimate=COST,
        name="queries",
    )(latents, q_up, draft, down_t, *([kv_up] * step), cosine, sine, after)


def attend_kernel(table, q_ref, draft_ref, keys_ref, valid_ref, gain_ref, cos_ref, sin_ref, *out_refs):
    request = pl.program_id(0)

    @pl.when(table[7] == 3)
    def _():
        scale = (DN + DR) ** (-0.5)
        local_rows = out_refs[0].shape[1]
        new = 2 * RP
        comp = 0.0
        for t in range(4):
            terms = draft_ref[t].astype(F32)
            comp = comp + (terms[0:new] + terms[new : 2 * new] + terms[2 * new : 3 * new])
        lat = comp[:, :KVL]
        norm = lax.rsqrt(jnp.mean(lat * lat, axis=-1, keepdims=True) + 1e-06)
        first = comp[:, KVL : KVL + HALF]
        second = comp[:, KVL + HALF :]
        cosine, sine = cos_ref[...], sin_ref[...]
        drafts = jnp.concatenate(
            [
                lat * norm * gain_ref[...],
                first * cosine - second * sine,
                first * sine + second * cosine,
            ],
            1,
        )
        drafts = jnp.concatenate([drafts, jnp.zeros((UNIT - new, WIDTH), F32)], 0).astype(BF)
        query = jnp.concatenate([q_ref[t] for t in range(4)], 0)
        keys = jnp.concatenate([keys_ref[0, 1], keys_ref[0, 0]], 1)
        scores = jnp.dot(query, keys, preferred_element_type=F32) * scale
        scores = jnp.where(valid_ref[0] > 0.0, scores, -1e30)
        fresh = lax.dot_general(query, drafts, NT, preferred_element_type=F32) * scale
        row = lax.broadcasted_iota(jnp.int32, fresh.shape, 0)
        late = (row % local_rows) // (local_rows // 2)
        offset = lax.broadcasted_iota(jnp.int32, fresh.shape, 1) - 2 * request
        fresh = jnp.where((offset >= 0) & (offset <= late), fresh, -1e30)
        top = jnp.maximum(
            jnp.max(scores, axis=1, keepdims=True), jnp.max(fresh, axis=1, keepdims=True)
        )
        weights = jnp.exp(scores - top)
        fresh = jnp.exp(fresh - top)
        total = jnp.sum(weights, axis=1, keepdims=True) + jnp.sum(fresh, axis=1, keepdims=True)
        numer = lax.dot_general(weights.astype(BF), keys[:KVL], NT, preferred_element_type=F32)
        numer = numer + jnp.dot(fresh.astype(BF), drafts[:, :KVL], preferred_element_type=F32)
        result = (numer / total).astype(BF)
        for t, ref in enumerate(out_refs):
            ref[0] = result[t * local_rows : (t + 1) * local_rows]


def attend(table, messages, held, valid, gain, cosine, sine, after):
    new = 2 * RP
    local_rows = (messages.shape[1] - 4 * new) // RP
    last = RP * local_rows // (4 * new)
    out = jax.ShapeDtypeStruct((RP, local_rows, KVL), BF)
    whole = lambda i, table: (0, 0)
    body = lambda *refs: attend_kernel(*refs[:8], *refs[-4:])
    return pl.pallas_call(
        body,
        grid_spec=pltpu.PrefetchScalarGridSpec(
            num_scalar_prefetch=1,
            grid=(RP,),
            in_specs=[
                pl.BlockSpec((4, local_rows, WIDTH), lambda i, table: (0, i, 0)),
                pl.BlockSpec((4, 4 * new, WIDTH), lambda i, table: (0, last, 0)),
                pl.BlockSpec((1, 2, WIDTH, SHARE), lambda i, table: (i, 0, 0, 0)),
                pl.BlockSpec((1, 1, valid.shape[2]), lambda i, table: (i, 0, 0)),
                pl.BlockSpec((1, KVL), whole),
                pl.BlockSpec(cosine.shape, whole),
                pl.BlockSpec(sine.shape, whole),
                *([ANY] * len(after)),
            ],
            out_specs=[pl.BlockSpec((1, local_rows, KVL), lambda i, table: (i, 0, 0))] * 4,
        ),
        out_shape=[out] * 4,
        compiler_params=ROOM,
        cost_estimate=COST,
        name="attend",
    )(table, messages, messages, held, valid, gain, cosine, sine, *after)


def heads_kernel(o_ref, keep_ref, *refs):
    *value_refs, out_ref = refs
    for h, value_ref in enumerate(value_refs):
        row = jnp.dot(o_ref[h].astype(BF), value_ref[...], preferred_element_type=F32)
        out_ref[:, h * DV : (h + 1) * DV] = row * keep_ref[...]


def heads_out(attended, keep, kv_up):
    heads, rows, _ = attended.shape
    step = 8
    value_spec = [
        pl.BlockSpec((KVL, DV), lambda i, h=h: (0, 2 * (step * i + h) + 1)) for h in range(step)
    ]
    return pl.pallas_call(
        heads_kernel,
        grid=(heads // step,),
        in_specs=[
            pl.BlockSpec((step, rows, KVL), lambda i: (i, 0, 0)),
            pl.BlockSpec((rows, DV), lambda i: (0, 0)),
            *value_spec,
        ],
        out_specs=pl.BlockSpec((rows, step * DV), lambda i: (0, i)),
        out_shape=jax.ShapeDtypeStruct((rows, heads * DV), F32),
        compiler_params=ROOM,
        cost_estimate=COST,
        name="heads_out",
    )(attended, keep, *([kv_up] * step))


def rope_tables(position):
    freq = jnp.exp(-jnp.log(10000.0) * jnp.arange(HALF, dtype=F32) / HALF)
    angle = position.astype(F32)[..., None] * freq
    return jnp.cos(angle), jnp.sin(angle)


def local_line(
    prefill_hidden,
    draft_hidden,
    kv_down,
    kv_gain,
    query_latent,
    q_up,
    kv_up,
    owners,
    segment_ids,
    accepted,
):
    pd_count = lax.axis_size("pd")
    z = lax.axis_index("tp")
    p = lax.axis_index("pd")
    first_req = p * RP

    table = jnp.asarray(
        [
            [3, 2, 0, 2, 1, 0, 1, 0, 0],
            [3, 2, 0, 2, 1, 0, 0, 1, 0],
            [3, 2, 0, 2, 1, 0, 0, 2, 1],
            [0, 2, 3, 0, 1, 2, 1, 3, 2],
        ],
        jnp.int32,
    )[z]
    hops = jnp.asarray(
        [
            [[0, 0, 0], [2, 1, 2], [0, 0, 1], [0, 0, 0]],
            [[0, 0, 0], [0, 0, 1], [2, 1, 2], [0, 0, 0]],
            [[0, 0, 0], [2, 2, 1], [0, 0, 1], [0, 0, 0]],
            [[0, 0, 0], [1, 1, 1], [0, 0, 0], [0, 0, 0]],
            [[0, 0, 0], [0, 0, 1], [2, 2, 1], [0, 0, 0]],
            [[0, 0, 0], [0, 0, 0], [1, 1, 1], [0, 0, 0]],
        ],
        jnp.int32,
    )[:, z]

    hidden = prefill_hidden.reshape(RP, PRE_TOK, prefill_hidden.shape[1])
    down_t = kv_down.T
    inward = [(0, 1), (3, 2)]
    last = RP - 1
    sums = [None] * RP
    inner = [None] * RP
    for r in range(RP):
        sums[r], *coded = project(table, hidden, down_t, r, r < last, sums[max(r - 1, 0) : r])
        inner[r] = [lax.ppermute(c, "tp", inward) for c in coded]

    my_segments = lax.dynamic_slice_in_dim(segment_ids, first_req, RP, 0)
    valid = (my_segments == my_segments[:, -1:])[:, PRE_TOK // 2 :].astype(F32)
    valid = valid.reshape(RP, 1, PRE_TOK // 2)
    gain = jnp.broadcast_to(kv_gain[:, None], (KVL, UNIT))
    steps = jnp.arange(SHARE, dtype=jnp.int32)
    tables = [t.T for t in (*rope_tables(z * SHARE + steps), *rope_tables(2 * SHARE + steps))]

    held = jnp.zeros((RP, 2, WIDTH, SHARE), BF)
    across = [None] * RP
    sent = [None] * RP
    outer = [None] * RP

    def first_hop(r, after):
        block = add_on(hops[0], sums[r], inner[r][0], after=after)
        across[r] = lax.ppermute(block, "tp", [(1, 2), (2, 1)])
        return block

    def second_hop(r, after):
        block = add_on(hops[1], sums[r], across[r], inner[r][0], 1, after)
        sent[r] = block
        outer[r] = [lax.ppermute(block, "tp", [(2, 3), (1, 0)])] * 2

    block = first_hop(0, [sums[last]])

    latents = lax.dynamic_slice_in_dim(query_latent, first_req, RP, 0).reshape(RP * 2, QL)
    new_pos = jnp.tile(PRE_TOK + jnp.arange(2, dtype=jnp.int32), RP)
    new_cos, new_sin = rope_tables(new_pos)
    query, terms = queries(
        latents, q_up, kv_up, draft_hidden, down_t, new_cos, new_sin, block
    )
    heads = query.shape[0]
    query = query.reshape(heads, RP, 2, WIDTH).transpose(1, 2, 0, 3)
    message = jnp.concatenate(
        [query.reshape(RP * 2 * heads, WIDTH), terms.reshape(8 * RP, WIDTH)], 0
    ).astype(BF)
    messages = lax.all_gather(message, "tp", axis=0)

    first_hop(1, [query])
    second_hop(0, [])
    first_hop(2, [sent[0], message])
    second_hop(1, [])
    held = finish(table, sums[0], *outer[0], sent[0], gain, tables, held, 0, [sent[1]])

    one = add_on(hops[2], sums[last], inner[last][0], after=[sent[1]])
    sums_last, *coded = project_last(table, hidden, down_t, [one])
    inner_last = [lax.ppermute(c, "tp", inward) for c in coded]
    one = lax.ppermute(one, "tp", [(1, 2), (2, 1)])
    two = add_on(hops[3], sums[last], inner[last][1], after=[held, sums_last, messages])
    two = lax.ppermute(two, "tp", [(1, 2)])
    second_hop(2, [])
    held = finish(table, sums[1], *outer[1], sent[1], gain, tables, held, 1, [sent[2]])
    one = add_on(hops[4], sums[last], one, after=[held])
    one = lax.ppermute(one, "tp", [(2, 3), (1, 0)])
    lasts = [add_last(table, sums_last, inner_last[0], 0)]
    sent[last] = add_on(hops[5], sums[last], two, inner[last][1], 0, [lasts[0]])
    two = lax.ppermute(sent[last], "tp", [(2, 3)])
    lasts.append(add_last(table, sums_last, inner_last[1], 1))
    held = finish(table, sums[2], *outer[2], sent[2], gain, tables, held, 2, [lasts[1]])
    lasts.append(add_last(table, sums_last, inner_last[2], 2))
    held = finish(table, sums[last], one, two, sent[last], gain, tables, held, last, [])
    lasts = [lax.ppermute(block, "tp", [(2, 1)]) for block in lasts]

    result = attend(
        table, messages, held, valid, kv_gain.reshape(1, KVL), new_cos, new_sin, [lasts[0]]
    )
    back = [lax.ppermute(result[t], "tp", [(3, t)]) for t in range(3)]
    attended = jnp.where(z == 3, result[3], back[0] + back[1] + back[2])
    attended = attended.reshape(RP, 2, heads, KVL).transpose(2, 0, 1, 3)
    attended = attended.reshape(heads, RP * 2, KVL).astype(F32)
    my_accepted = lax.dynamic_slice_in_dim(accepted, first_req, RP, 0)
    keep = (jnp.arange(2)[None, :] <= my_accepted[:, None]).astype(F32).reshape(RP * 2, 1)
    answer = heads_out(attended, jnp.broadcast_to(keep, (RP * 2, DV)), kv_up)
    answer = answer.reshape(RP, 2, heads * DV)

    my_owners = lax.dynamic_slice_in_dim(owners, first_req, RP, 0)
    routing = my_owners[None, :] == jnp.arange(pd_count, dtype=jnp.int32)[:, None]
    has = jnp.any(routing, axis=1)
    slots = jnp.sum(routing.astype(jnp.int32) * jnp.arange(RP, dtype=jnp.int32)[None, :], axis=1)
    placed = jnp.where(has[:, None, None], answer[slots], 0.0).astype(BF)
    placed = lax.all_to_all(placed, "pd", split_axis=0, concat_axis=0, tiled=True)

    cache = []
    for u in range(UNITS):
        page = pages_of(
            table,
            slots,
            has.astype(jnp.int32),
            sums_last,
            inner_last[u],
            lasts[u],
            held,
            gain,
            tables[0],
            tables[1],
            u,
        )
        cache.append(lax.all_to_all(page, "pd", split_axis=0, concat_axis=0, tiled=True))
    cache = jnp.swapaxes(jnp.concatenate(cache, 2), 1, 2)
    return (placed.reshape(pd_count * 2, heads * DV), cache)


def solution(mesh):
    placed = (
        P(("groups", "pd"), "tp"),
        P(("groups", "pd"), "tp"),
        P("tp", None),
        P(),
        P("groups", None, None),
        P(None, "tp"),
        P(None, "tp"),
        P("groups"),
        P("groups", None),
        P("groups"),
    )
    return jax.shard_map(
        local_line if mesh.shape["tp"] == 4 else local_general,
        mesh=mesh,
        in_specs=placed,
        out_specs=(P(("groups", "pd"), "tp"), P(("groups", "pd"), "tp", None)),
        check_vma=False,
    )
```

```python
import functools

import jax
import jax.numpy as jnp
from jax import lax
from jax.experimental import pallas as pl
from jax.experimental.pallas import tpu as pltpu
from jax.sharding import PartitionSpec as P

DN = 128
DR = 64
DV = 128
KVL = 512
QL = 1536
PRE_TOK = 1536
RP = 4
WIDTH = KVL + DR
HALF = DR // 2
CODED = WIDTH + 16
SHARE = PRE_TOK // 4
UNIT = 128
UNITS = SHARE // UNIT
LANES = RP * UNIT
STEPS = 256.0
TOP = 32767.0
BF = jnp.bfloat16
F32 = jnp.float32
I16 = jnp.int16
NT = (((1,), (1,)), ((), ()))
ROOM = pltpu.CompilerParams(vmem_limit_bytes=60 << 20)
ANY = pl.BlockSpec(memory_space=pl.ANY)
VMEM = pl.BlockSpec(memory_space=pltpu.VMEM)
SMEM = pl.BlockSpec(memory_space=pltpu.SMEM)


COST = pl.CostEstimate(flops=1024, bytes_accessed=1024, transcendentals=0)


def rms_latent(comp, gain):
    lat = comp[:, :KVL]
    scale = lax.rsqrt(jnp.mean(lat * lat, axis=-1, keepdims=True) + 1e-06)
    return (lat * scale * gain).astype(jnp.bfloat16)


def rotate(values, position):
    half = values.shape[-1] // 2
    freq = jnp.exp(-jnp.log(10000.0) * jnp.arange(half, dtype=jnp.float32) / half)
    angle = position.astype(jnp.float32)[..., None] * freq
    cosine = jnp.cos(angle)
    sine = jnp.sin(angle)
    first = values[..., :half]
    second = values[..., half:]
    return jnp.concatenate([first * cosine - second * sine, first * sine + second * cosine], -1)


def block_stats(keys, q_lat, q_pos, valid):
    scale = (DN + DR) ** (-0.5)
    scores = jnp.einsum("jhk,tk->jht", q_lat, keys[:, :KVL], preferred_element_type=jnp.float32)
    scores = (
        scores + jnp.einsum("jhk,tk->jht", q_pos, keys[:, KVL:], preferred_element_type=jnp.float32)
    ) * scale
    scores = jnp.where(valid, scores, -1e30)
    top = jnp.max(scores, axis=-1)
    weights = jnp.where(valid, jnp.exp(scores - top[..., None]), 0.0)
    total = jnp.sum(weights, axis=-1)
    numer = jnp.einsum(
        "jht,tk->jhk",
        weights.astype(jnp.bfloat16),
        keys[:, :KVL],
        preferred_element_type=jnp.float32,
    )
    return (top, total, numer)


def combine(left, right):
    top = jnp.maximum(left[0], right[0])
    left_scale = jnp.exp(left[0] - top)
    right_scale = jnp.exp(right[0] - top)
    total = left[1] * left_scale + right[1] * right_scale
    numer = left[2] * left_scale[..., None] + right[2] * right_scale[..., None]
    return (top, total, numer)


def local_general(
    prefill_hidden,
    draft_hidden,
    kv_down,
    kv_gain,
    query_latent,
    q_up,
    kv_up,
    owners,
    segment_ids,
    accepted,
):
    tp_count = lax.axis_size("tp")
    pd_count = lax.axis_size("pd")
    tp_rank = lax.axis_index("tp")
    mine_rank = lax.axis_index("pd")
    requests = owners.shape[0]
    share = PRE_TOK // tp_count
    width = KVL + DR
    local_hidden = prefill_hidden.reshape(RP, PRE_TOK, prefill_hidden.shape[1])
    summed = lax.psum_scatter(
        jnp.einsum(
            "rtd,dw->trw", local_hidden, kv_down, preferred_element_type=jnp.float32
        ).reshape(lax.axis_size("tp") * share, RP * width),
        "tp",
        scatter_dimension=0,
        tiled=True,
    ).reshape(share * RP, width)
    draft_sum = lax.psum(jnp.dot(draft_hidden, kv_down, preferred_element_type=jnp.float32), "tp")
    first_req = mine_rank * RP
    row_pos = jnp.broadcast_to(
        tp_rank * share + jnp.arange(share, dtype=jnp.int32)[:, None], (share, RP)
    )
    page_rows = jnp.concatenate(
        [
            rms_latent(summed, kv_gain),
            rotate(summed[:, KVL:], row_pos.reshape(-1)).astype(jnp.bfloat16),
        ],
        1,
    )
    page_rows = page_rows.reshape(share, RP, width)
    draft_pos = jnp.tile(PRE_TOK + jnp.arange(2, dtype=jnp.int32), RP)
    draft_rows = jnp.concatenate(
        [
            rms_latent(draft_sum, kv_gain),
            rotate(draft_sum[:, KVL:], draft_pos).astype(jnp.bfloat16),
        ],
        1,
    )
    draft_rows = draft_rows.reshape(RP, 2, width)
    my_owners = lax.dynamic_slice_in_dim(owners, first_req, RP, 0)
    routing = (my_owners[None, :] == jnp.arange(pd_count, dtype=jnp.int32)[:, None]).astype(
        jnp.bfloat16
    )
    send_pages = jnp.einsum(
        "dk,tkw->dtw", routing, page_rows, preferred_element_type=jnp.float32
    ).astype(jnp.bfloat16)
    send_drafts = jnp.einsum(
        "dk,kjw->djw", routing, draft_rows, preferred_element_type=jnp.float32
    ).astype(jnp.bfloat16)
    pages, drafts = (
        lax.all_to_all(send_pages, "pd", split_axis=0, concat_axis=0, tiled=True),
        lax.all_to_all(send_drafts, "pd", split_axis=0, concat_axis=0, tiled=True),
    )
    heads_local = q_up.shape[1] // (DN + DR)
    query_full = jnp.dot(
        query_latent.reshape(requests * 2, QL), q_up, preferred_element_type=jnp.float32
    )
    query_full = query_full.reshape(requests, 2, heads_local, DN + DR)
    new_pos = jnp.broadcast_to(PRE_TOK + jnp.arange(2, dtype=jnp.int32)[None, :], (requests, 2))
    q_nope = query_full[..., :DN].astype(jnp.bfloat16)
    q_rot = rotate(query_full[..., DN:], new_pos[:, :, None]).astype(jnp.bfloat16)
    up_heads = kv_up.reshape(KVL, heads_local, DN + DV)
    w_value = up_heads[:, :, DN:]
    q_abs = jnp.einsum(
        "rjhd,khd->rjhk", q_nope, up_heads[:, :, :DN], preferred_element_type=jnp.float32
    ).astype(jnp.bfloat16)
    owner_table = owners.reshape(pd_count, RP) == mine_rank
    holding = jnp.sum(owner_table.astype(jnp.int32), axis=1)
    slot_of = jnp.sum(
        owner_table.astype(jnp.int32) * jnp.arange(RP, dtype=jnp.int32)[None, :], axis=1
    )
    owned_count = jnp.sum(holding)
    order = jnp.argsort((1 - holding) * pd_count + jnp.arange(pd_count, dtype=jnp.int32))
    draft_valid = (jnp.arange(2)[None, :] <= jnp.arange(2)[:, None])[:, None, :]
    empty = jnp.zeros((pd_count, 2, heads_local * DV), jnp.bfloat16)

    def finish(stats, source, request, q_lat, q_pos, result):
        stats = combine(stats, block_stats(drafts[source], q_lat, q_pos, draft_valid))
        attended = (stats[2] / stats[1][..., None]).astype(jnp.bfloat16)
        head_out = jnp.einsum("jhk,khd->jhd", attended, w_value, preferred_element_type=jnp.float32)
        keep = (jnp.arange(2) <= accepted[request]).astype(jnp.float32)[:, None, None]
        answer = (head_out * keep).astype(jnp.bfloat16).reshape(1, 2, heads_local * DV)
        return lax.dynamic_update_slice(result, answer, (source, 0, 0))

    def attend(turn, result):
        source = order[turn]
        request = source * RP + slot_of[source]
        q_lat = q_abs[request]
        q_pos = q_rot[request]
        seg_row = segment_ids[request]
        current = seg_row[PRE_TOK - 1]
        init = (
            jnp.full((2, heads_local), -1e30, jnp.float32),
            jnp.zeros((2, heads_local), jnp.float32),
            jnp.zeros((2, heads_local, KVL), jnp.float32),
        )
        valid = (seg_row == current)[None, None, :]
        stats = combine(
            init,
            block_stats(
                lax.all_gather(pages[source], "tp", axis=0, tiled=True), q_lat, q_pos, valid
            ),
        )
        return finish(stats, source, request, q_lat, q_pos, result)

    result = lax.fori_loop(0, owned_count, attend, empty)
    return (result.reshape(pd_count * 2, heads_local * DV), pages)


def encode(values):
    levels = []
    parts = []
    for first, last in ((0, KVL), (KVL, WIDTH)):
        block = values[first:last]
        top = jnp.maximum(jnp.max(jnp.abs(block), axis=0, keepdims=True), 1e-30)
        level = jnp.ceil(jnp.log2(top) * STEPS)
        codes = jnp.round(block * (jnp.exp2(level * (-1.0 / STEPS)) * TOP))
        parts.append(jnp.clip(codes, -TOP, TOP).astype(jnp.int32).astype(I16))
        levels.append(level.astype(jnp.int32))
    row = lax.broadcasted_iota(jnp.int32, (16, values.shape[1]), 0)
    extra = jnp.where(row == 0, levels[0], jnp.where(row == 1, levels[1], 0))
    return jnp.concatenate([*parts, extra.astype(I16)], 0)


def decode(codes):
    level = codes[WIDTH:CODED].astype(jnp.int32).astype(F32)
    step = jnp.exp2(level * (1.0 / STEPS)) * (1.0 / TOP)
    lat = codes[0:KVL].astype(jnp.int32).astype(F32) * step[0:1]
    rot = codes[KVL:WIDTH].astype(jnp.int32).astype(F32) * step[1:2]
    return jnp.concatenate([lat, rot], 0)


def key_rows(comp, gain, cosine, sine):
    lat = comp[:KVL]
    scale = lax.rsqrt(jnp.mean(lat * lat, axis=0, keepdims=True) + 1e-06)
    first = comp[KVL : KVL + HALF]
    second = comp[KVL + HALF :]
    return jnp.concatenate(
        [
            lat * scale * gain,
            first * cosine - second * sine,
            first * sine + second * cosine,
        ],
        0,
    )


def far(z, i):
    return jnp.where(z < 2, 3 - i, i)


def near(z, i):
    return jnp.where(z < 2, i, 3 - i)


def outer_rank(z):
    return (z == 0) | (z == 3)


def project_far_kernel(rank, hid_ref, down_ref, *refs):
    sum_ref, code_ref = refs[-2:]
    total = lax.dot_general(down_ref[...], hid_ref[0], NT, preferred_element_type=F32)
    for u in range(UNITS):
        sum_ref[0, u] = total[:, u * UNIT : (u + 1) * UNIT]

    @pl.when(outer_rank(rank[0]))
    def _():
        for u in range(UNITS):
            code_ref[0, u] = encode(total[:, u * UNIT : (u + 1) * UNIT])


def project_far(rank, hidden, down_t, request, after):
    depth = hidden.shape[-1]
    return pl.pallas_call(
        project_far_kernel,
        grid_spec=pltpu.PrefetchScalarGridSpec(
            num_scalar_prefetch=1,
            grid=(2,),
            in_specs=[
                pl.BlockSpec((1, SHARE, depth), lambda i, rank: (request, far(rank[0], i), 0)),
                pl.BlockSpec((WIDTH, depth), lambda i, rank: (0, 0)),
                *([ANY] * len(after)),
            ],
            out_specs=[
                pl.BlockSpec((1, UNITS, WIDTH, UNIT), lambda i, rank: (i, 0, 0, 0)),
                pl.BlockSpec((1, UNITS, CODED, UNIT), lambda i, rank: (i, 0, 0, 0)),
            ],
        ),
        out_shape=[
            jax.ShapeDtypeStruct((2, UNITS, WIDTH, UNIT), F32),
            jax.ShapeDtypeStruct((2, UNITS, CODED, UNIT), I16),
        ],
        compiler_params=ROOM,
        cost_estimate=COST,
        name="project_far",
    )(rank, hidden, down_t, *after)


def project_near_kernel(rank, hid_ref, down_ref, *refs):
    sum_ref, *code_refs = refs[-3:]
    unit = pl.program_id(0)
    rows = hid_ref[...].reshape(LANES, hid_ref.shape[-1])
    total = lax.dot_general(down_ref[...], rows, NT, preferred_element_type=F32)
    for r in range(RP):
        sum_ref[0, 0, r] = total[:, r * UNIT : (r + 1) * UNIT]
    coded = outer_rank(rank[0]) & (pl.program_id(1) == 1)
    for mine, ref in zip((unit == 0, unit > 0), code_refs):

        @pl.when(coded & mine)
        def _(ref=ref):
            for r in range(RP):
                ref[0, r] = encode(total[:, r * UNIT : (r + 1) * UNIT])


def project_near(rank, hidden, down_t, after):
    depth = hidden.shape[-1]
    return pl.pallas_call(
        project_near_kernel,
        grid_spec=pltpu.PrefetchScalarGridSpec(
            num_scalar_prefetch=1,
            grid=(UNITS, 2),
            in_specs=[
                pl.BlockSpec(
                    (RP, UNIT, depth), lambda u, i, rank: (0, near(rank[0], i) * UNITS + u, 0)
                ),
                pl.BlockSpec((WIDTH, depth), lambda u, i, rank: (0, 0)),
                *([ANY] * len(after)),
            ],
            out_specs=[
                pl.BlockSpec((1, 1, RP, WIDTH, UNIT), lambda u, i, rank: (u, i, 0, 0, 0)),
                pl.BlockSpec((1, RP, CODED, UNIT), lambda u, i, rank: (0, 0, 0, 0)),
                pl.BlockSpec(
                    (1, RP, CODED, UNIT), lambda u, i, rank: (jnp.maximum(u, 1) - 1, 0, 0, 0)
                ),
            ],
        ),
        out_shape=[
            jax.ShapeDtypeStruct((UNITS, 2, RP, WIDTH, UNIT), F32),
            jax.ShapeDtypeStruct((1, RP, CODED, UNIT), I16),
            jax.ShapeDtypeStruct((UNITS - 1, RP, CODED, UNIT), I16),
        ],
        compiler_params=ROOM,
        cost_estimate=COST,
        name="project_near",
    )(rank, hidden, down_t, *after)


def add_kernel(rank, own_ref, got_ref, *refs):
    @pl.when(~outer_rank(rank[0]))
    def _():
        for u in range(UNITS):
            refs[-1][0, u] = encode(own_ref[u] + decode(got_ref[0, u]))


def add_on(rank, own, got, request=None, after=()):
    chunk = lambda i, rank: (i, 0, 0, 0)
    if request is None:
        own_spec = pl.BlockSpec((None, UNITS, WIDTH, UNIT), chunk)
    else:
        own_spec = pl.BlockSpec(
            (UNITS, None, None, WIDTH, UNIT), lambda i, rank: (0, i, request, 0, 0)
        )
    return pl.pallas_call(
        add_kernel,
        grid_spec=pltpu.PrefetchScalarGridSpec(
            num_scalar_prefetch=1,
            grid=(2,),
            in_specs=[
                own_spec,
                pl.BlockSpec((1, UNITS, CODED, UNIT), chunk),
                *([ANY] * len(after)),
            ],
            out_specs=pl.BlockSpec((1, UNITS, CODED, UNIT), chunk),
        ),
        out_shape=jax.ShapeDtypeStruct((2, UNITS, CODED, UNIT), I16),
        compiler_params=ROOM,
        cost_estimate=COST,
        name="add_on",
    )(rank, own, got, *after)


def page_kernel(rank, slot, own_ref, *refs):
    got_refs, sent_refs, refs = refs[:RP], refs[RP : 2 * RP], refs[2 * RP :]
    side_ref, gain_ref, cos_ref, sin_ref = refs[:4]
    out_ref = refs[-1]
    request = pl.program_id(0)

    def write(comp):
        out_ref[0] = key_rows(comp, gain_ref[...], cos_ref[0], sin_ref[0]).astype(BF)

    for r in range(RP):

        @pl.when((request == r) & outer_rank(rank[0]))
        def _(r=r):
            write(own_ref[...] + decode(got_refs[r][0, 0]))

        @pl.when((request == r) & ~outer_rank(rank[0]))
        def _(r=r):
            write(decode(sent_refs[r][0, 0]) + decode(side_ref[...]))


def pages_of(rank, slot, own, got, sent, side, place, gain, cosine, sine, count, unit):
    first = pl.BlockSpec((1, 1, CODED, UNIT), lambda i, *_: (0, unit, 0, 0))
    second = pl.BlockSpec((1, 1, CODED, UNIT), lambda i, *_: (1, unit, 0, 0))
    table = pl.BlockSpec((1, HALF, UNIT), lambda i, *_: (unit, 0, 0))
    base = [jnp.zeros((count, WIDTH, UNIT), BF)] if count > RP else []
    return pl.pallas_call(
        page_kernel,
        grid_spec=pltpu.PrefetchScalarGridSpec(
            num_scalar_prefetch=2,
            grid=(RP,),
            in_specs=[
                pl.BlockSpec((None, None, None, WIDTH, UNIT), lambda i, *_: (unit, 0, i, 0, 0)),
                *([first] * RP),
                *([second] * RP),
                pl.BlockSpec((None, None, CODED, UNIT), lambda i, *_: (place, i, 0, 0)),
                pl.BlockSpec((KVL, UNIT), lambda i, *_: (0, 0)),
                table,
                table,
                *([ANY] * len(base)),
            ],
            out_specs=pl.BlockSpec((1, WIDTH, UNIT), lambda i, rank, slot: (slot[i], 0, 0)),
        ),
        out_shape=jax.ShapeDtypeStruct((count, WIDTH, UNIT), BF),
        input_output_aliases={7 + 2 * RP: 0} if base else {},
        compiler_params=ROOM,
        cost_estimate=COST,
        name="pages",
    )(rank, slot, own, *got, *sent, side, gain, cosine, sine, *base)


def query_kernel(lat_ref, up_ref, draft_ref, down_ref, *refs):
    *key_refs, cos_ref, sin_ref, out_ref, split_ref = refs

    @pl.when(pl.program_id(0) == 0)
    def _():
        rest = lax.dot_general(draft_ref[...], down_ref[...], NT, preferred_element_type=F32)
        for n in range(3):
            term = rest.astype(BF).astype(F32)
            split_ref[n] = term
            rest = rest - term
        split_ref[3] = jnp.zeros_like(rest)

    full = jnp.dot(lat_ref[...], up_ref[...], preferred_element_type=F32)
    for h, key_ref in enumerate(key_refs):
        base = h * (DN + DR)
        nope = full[:, base : base + DN].astype(BF)
        first = full[:, base + DN : base + DN + HALF]
        second = full[:, base + DN + HALF : base + DN + DR]
        absorbed = lax.dot_general(nope, key_ref[...], NT, preferred_element_type=F32)
        cosine, sine = cos_ref[...], sin_ref[...]
        out_ref[h] = jnp.concatenate(
            [absorbed, first * cosine - second * sine, first * sine + second * cosine], 1
        )


def queries(latents, q_up, kv_up, draft, down_t, cosine, sine, after):
    rows = latents.shape[0]
    heads = q_up.shape[1] // (DN + DR)
    step = 4
    key_spec = [
        pl.BlockSpec((KVL, DN), lambda i, h=h: (0, 2 * (step * i + h))) for h in range(step)
    ]
    whole = lambda i: (0, 0)
    table = pl.BlockSpec((rows, HALF), whole)
    body = lambda *refs: query_kernel(*refs[:-3], *refs[-2:])
    return pl.pallas_call(
        body,
        grid=(heads // step,),
        in_specs=[
            pl.BlockSpec((rows, QL), whole),
            pl.BlockSpec((QL, step * (DN + DR)), lambda i: (0, i)),
            pl.BlockSpec(draft.shape, whole),
            pl.BlockSpec(down_t.shape, whole),
            *key_spec,
            table,
            table,
            ANY,
        ],
        out_specs=[
            pl.BlockSpec((step, rows, WIDTH), lambda i: (i, 0, 0)),
            pl.BlockSpec((4, rows, WIDTH), lambda i: (0, 0, 0)),
        ],
        out_shape=[
            jax.ShapeDtypeStruct((heads, rows, WIDTH), F32),
            jax.ShapeDtypeStruct((4, rows, WIDTH), F32),
        ],
        compiler_params=ROOM,
        cost_estimate=COST,
        name="queries",
    )(latents, q_up, draft, down_t, *([kv_up] * step), cosine, sine, after)


def attend_kernel(rank, q_ref, draft_ref, *refs):
    own_ref, got_refs, refs = refs[0], refs[1 : 1 + RP], refs[1 + RP :]
    column_ref, cos_ref, sin_ref, midcos_ref, midsin_ref, refs = *refs[:5], refs[5:]
    valid_ref, gain_ref, newcos_ref, newsin_ref, refs = *refs[:4], refs[4:]
    out_refs, keys_ref = refs[-5:-1], refs[-1]
    request = pl.program_id(0)

    @pl.when(rank[0] == 3)
    def _():
        for r in range(RP):

            @pl.when(request == r)
            def _(r=r):
                for i, (cosine, sine) in enumerate(
                    ((cos_ref, sin_ref), (midcos_ref, midsin_ref))
                ):
                    for u in range(UNITS):
                        comp = own_ref[u, i] + decode(got_refs[r][i, u])
                        rows = key_rows(comp, column_ref[...], cosine[u], sine[u])
                        start = (1 - i) * SHARE + u * UNIT
                        keys_ref[:, start : start + UNIT] = rows.astype(BF)

        scale = (DN + DR) ** (-0.5)
        local_rows = out_refs[0].shape[1]
        new = 2 * RP
        comp = 0.0
        for t in range(4):
            terms = draft_ref[t].astype(F32)
            comp = comp + (terms[0:new] + terms[new : 2 * new] + terms[2 * new : 3 * new])
        lat = comp[:, :KVL]
        norm = lax.rsqrt(jnp.mean(lat * lat, axis=-1, keepdims=True) + 1e-06)
        first = comp[:, KVL : KVL + HALF]
        second = comp[:, KVL + HALF :]
        cosine, sine = newcos_ref[...], newsin_ref[...]
        drafts = jnp.concatenate(
            [
                lat * norm * gain_ref[...],
                first * cosine - second * sine,
                first * sine + second * cosine,
            ],
            1,
        )
        drafts = jnp.concatenate([drafts, jnp.zeros((UNIT - new, WIDTH), F32)], 0).astype(BF)
        query = jnp.concatenate([q_ref[t] for t in range(4)], 0)
        scores = jnp.dot(query, keys_ref[...], preferred_element_type=F32) * scale
        scores = jnp.where(valid_ref[0] > 0.0, scores, -1e30)
        fresh = lax.dot_general(query, drafts, NT, preferred_element_type=F32) * scale
        row = lax.broadcasted_iota(jnp.int32, fresh.shape, 0)
        late = (row % local_rows) // (local_rows // 2)
        offset = lax.broadcasted_iota(jnp.int32, fresh.shape, 1) - 2 * request
        fresh = jnp.where((offset >= 0) & (offset <= late), fresh, -1e30)
        top = jnp.maximum(
            jnp.max(scores, axis=1, keepdims=True), jnp.max(fresh, axis=1, keepdims=True)
        )
        weights = jnp.exp(scores - top)
        fresh = jnp.exp(fresh - top)
        total = jnp.sum(weights, axis=1, keepdims=True) + jnp.sum(fresh, axis=1, keepdims=True)
        numer = lax.dot_general(
            weights.astype(BF), keys_ref[0:KVL, :], NT, preferred_element_type=F32
        )
        numer = numer + jnp.dot(fresh.astype(BF), drafts[:, :KVL], preferred_element_type=F32)
        result = (numer / total).astype(BF)
        for t, ref in enumerate(out_refs):
            ref[0] = result[t * local_rows : (t + 1) * local_rows]


def attend(rank, messages, own, got, column, tables, valid, gain, cosine, sine, after):
    new = 2 * RP
    local_rows = (messages.shape[1] - 4 * new) // RP
    last = RP * local_rows // (4 * new)
    out = jax.ShapeDtypeStruct((RP, local_rows, KVL), BF)
    whole = lambda i, rank: (0, 0)
    whole3 = lambda i, rank: (0, 0, 0)
    return pl.pallas_call(
        attend_kernel,
        grid_spec=pltpu.PrefetchScalarGridSpec(
            num_scalar_prefetch=1,
            grid=(RP,),
            in_specs=[
                pl.BlockSpec((4, local_rows, WIDTH), lambda i, rank: (0, i, 0)),
                pl.BlockSpec((4, 4 * new, WIDTH), lambda i, rank: (0, last, 0)),
                pl.BlockSpec(
                    (UNITS, 2, None, WIDTH, UNIT), lambda i, rank: (0, 0, i, 0, 0)
                ),
                *([pl.BlockSpec((2, UNITS, CODED, UNIT), lambda i, rank: (0, 0, 0, 0))] * RP),
                pl.BlockSpec((KVL, UNIT), whole),
                *([pl.BlockSpec((UNITS, HALF, UNIT), whole3)] * 4),
                pl.BlockSpec((1, 1, valid.shape[2]), lambda i, rank: (i, 0, 0)),
                pl.BlockSpec((1, KVL), whole),
                pl.BlockSpec(cosine.shape, whole),
                pl.BlockSpec(sine.shape, whole),
                *([ANY] * len(after)),
            ],
            out_specs=[pl.BlockSpec((1, local_rows, KVL), lambda i, rank: (i, 0, 0))] * 4,
            scratch_shapes=[pltpu.VMEM((WIDTH, 2 * SHARE), BF)],
        ),
        out_shape=[out] * 4,
        compiler_params=ROOM,
        cost_estimate=COST,
        name="attend",
    )(rank, messages, messages, own, *got, column, *tables, valid, gain, cosine, sine, *after)


def heads_kernel(o_ref, keep_ref, *refs):
    *value_refs, out_ref = refs
    for h, value_ref in enumerate(value_refs):
        row = jnp.dot(o_ref[h].astype(BF), value_ref[...], preferred_element_type=F32)
        out_ref[:, h * DV : (h + 1) * DV] = row * keep_ref[...]


def heads_out(attended, keep, kv_up):
    heads, rows, _ = attended.shape
    step = 8
    value_spec = [
        pl.BlockSpec((KVL, DV), lambda i, h=h: (0, 2 * (step * i + h) + 1)) for h in range(step)
    ]
    return pl.pallas_call(
        heads_kernel,
        grid=(heads // step,),
        in_specs=[
            pl.BlockSpec((step, rows, KVL), lambda i: (i, 0, 0)),
            pl.BlockSpec((rows, DV), lambda i: (0, 0)),
            *value_spec,
        ],
        out_specs=pl.BlockSpec((rows, step * DV), lambda i: (0, i)),
        out_shape=jax.ShapeDtypeStruct((rows, heads * DV), F32),
        compiler_params=ROOM,
        cost_estimate=COST,
        name="heads_out",
    )(attended, keep, *([kv_up] * step))


def rope_tables(position):
    freq = jnp.exp(-jnp.log(10000.0) * jnp.arange(HALF, dtype=F32) / HALF)
    angle = position.astype(F32)[..., None] * freq
    return jnp.cos(angle), jnp.sin(angle)


def local_line(
    prefill_hidden,
    draft_hidden,
    kv_down,
    kv_gain,
    query_latent,
    q_up,
    kv_up,
    owners,
    segment_ids,
    accepted,
):
    pd_count = lax.axis_size("pd")
    z = lax.axis_index("tp")
    p = lax.axis_index("pd")
    first_req = p * RP

    rank = z.astype(jnp.int32).reshape(1)
    hidden = prefill_hidden.reshape(RP, PRE_TOK, prefill_hidden.shape[1])
    down_t = kv_down.T
    inward, across, outward = [(0, 1), (3, 2)], [(1, 2), (2, 1)], [(2, 3), (1, 0)]

    far_sums, inner = [], []
    for r in range(RP):
        total, codes = project_far(rank, hidden, down_t, r, far_sums[-1:])
        far_sums.append(total)
        inner.append(lax.ppermute(codes, "tp", inward))

    def first_hop(r, after):
        block = add_on(rank, far_sums[r], inner[r], after=after)
        crossed.append(lax.ppermute(block, "tp", across))
        return block

    def second_hop(r, after):
        block = add_on(rank, near_sums, crossed[r], r, after)
        sent.append(block)
        outer.append(lax.ppermute(block, "tp", outward))
        return block

    crossed, sent, outer = [], [], []
    block = first_hop(0, far_sums[-1:])
    near_sums, *side = project_near(rank, hidden, down_t, [block])
    first_hop(1, [near_sums])
    block = second_hop(0, [])

    latents = lax.dynamic_slice_in_dim(query_latent, first_req, RP, 0).reshape(RP * 2, QL)
    new_pos = jnp.tile(PRE_TOK + jnp.arange(2, dtype=jnp.int32), RP)
    new_cos, new_sin = rope_tables(new_pos)
    query, terms = queries(
        latents, q_up, kv_up, draft_hidden, down_t, new_cos, new_sin, block
    )
    heads = query.shape[0]
    query = query.reshape(heads, RP, 2, WIDTH).transpose(1, 2, 0, 3)
    message = jnp.concatenate(
        [query.reshape(RP * 2 * heads, WIDTH), terms.reshape(8 * RP, WIDTH)], 0
    ).astype(BF)
    messages = lax.all_gather(message, "tp", axis=0)

    my_segments = lax.dynamic_slice_in_dim(segment_ids, first_req, RP, 0)
    valid = (my_segments == my_segments[:, -1:])[:, PRE_TOK // 2 :].astype(F32)
    valid = valid.reshape(RP, 1, PRE_TOK // 2)
    column = jnp.broadcast_to(kv_gain[:, None], (KVL, UNIT))
    steps = jnp.arange(SHARE, dtype=jnp.int32).reshape(UNITS, UNIT)
    tables = [
        jnp.swapaxes(t, 1, 2)
        for t in (*rope_tables(z * SHARE + steps), *rope_tables(2 * SHARE + steps))
    ]

    block = first_hop(2, [message])
    second_hop(1, [block, outer[0]])
    block = first_hop(3, [sent[1]])
    side = [lax.ppermute(codes, "tp", inward) for codes in side]
    second_hop(2, [block, messages, outer[1]])
    second_hop(3, [side[0], outer[2]])

    result = attend(
        rank,
        messages,
        near_sums,
        outer,
        column,
        tables,
        valid,
        kv_gain.reshape(1, KVL),
        new_cos,
        new_sin,
        [],
    )
    back = [lax.ppermute(result[t], "tp", [(3, t)]) for t in range(3)]
    attended = jnp.where(z == 3, result[3], back[0] + back[1] + back[2])
    attended = attended.reshape(RP, 2, heads, KVL).transpose(2, 0, 1, 3)
    attended = attended.reshape(heads, RP * 2, KVL).astype(F32)
    my_accepted = lax.dynamic_slice_in_dim(accepted, first_req, RP, 0)
    keep = (jnp.arange(2)[None, :] <= my_accepted[:, None]).astype(F32).reshape(RP * 2, 1)
    answer = heads_out(attended, jnp.broadcast_to(keep, (RP * 2, DV)), kv_up)
    answer = answer.reshape(RP, 2, heads * DV)

    my_owners = lax.dynamic_slice_in_dim(owners, first_req, RP, 0)
    routing = my_owners[None, :] == jnp.arange(pd_count, dtype=jnp.int32)[:, None]
    has = jnp.any(routing, axis=1)
    slots = jnp.sum(routing.astype(jnp.int32) * jnp.arange(RP, dtype=jnp.int32)[None, :], axis=1)
    placed = jnp.where(has[:, None, None], answer[slots], 0.0).astype(BF)
    placed = lax.all_to_all(placed, "pd", split_axis=0, concat_axis=0, tiled=True)

    cache = []
    for u in range(UNITS):
        page = pages_of(
            rank,
            my_owners,
            near_sums,
            outer,
            sent,
            side[u > 0],
            max(u - 1, 0),
            column,
            tables[0],
            tables[1],
            pd_count,
            u,
        )
        cache.append(lax.all_to_all(page, "pd", split_axis=0, concat_axis=0, tiled=True))
    cache = jnp.swapaxes(jnp.concatenate(cache, 2), 1, 2)
    return (placed.reshape(pd_count * 2, heads * DV), cache)


def solution(mesh):
    placed = (
        P(("groups", "pd"), "tp"),
        P(("groups", "pd"), "tp"),
        P("tp", None),
        P(),
        P("groups", None, None),
        P(None, "tp"),
        P(None, "tp"),
        P("groups"),
        P("groups", None),
        P("groups"),
    )
    return jax.shard_map(
        local_line if mesh.shape["tp"] == 4 else local_general,
        mesh=mesh,
        in_specs=placed,
        out_specs=(P(("groups", "pd"), "tp"), P(("groups", "pd"), "tp", None)),
        check_vma=False,
    )
```

```python
import functools

import jax
import jax.numpy as jnp
from jax import lax
from jax.experimental import pallas as pl
from jax.experimental.pallas import tpu as pltpu
from jax.sharding import PartitionSpec as P

DN = 128
DR = 64
DV = 128
KVL = 512
QL = 1536
PRE_TOK = 1536
RP = 4
WIDTH = KVL + DR
HALF = DR // 2
CODED = WIDTH + 16
SHARE = PRE_TOK // 4
UNIT = 128
UNITS = SHARE // UNIT
LANES = RP * UNIT
STEPS = 256.0
TOP = 32767.0
BF = jnp.bfloat16
F32 = jnp.float32
I16 = jnp.int16
NT = (((1,), (1,)), ((), ()))
ROOM = pltpu.CompilerParams(vmem_limit_bytes=60 << 20)
ANY = pl.BlockSpec(memory_space=pl.ANY)
VMEM = pl.BlockSpec(memory_space=pltpu.VMEM)
SMEM = pl.BlockSpec(memory_space=pltpu.SMEM)


COST = pl.CostEstimate(flops=1024, bytes_accessed=1024, transcendentals=0)


def rms_latent(comp, gain):
    lat = comp[:, :KVL]
    scale = lax.rsqrt(jnp.mean(lat * lat, axis=-1, keepdims=True) + 1e-06)
    return (lat * scale * gain).astype(jnp.bfloat16)


def rotate(values, position):
    half = values.shape[-1] // 2
    freq = jnp.exp(-jnp.log(10000.0) * jnp.arange(half, dtype=jnp.float32) / half)
    angle = position.astype(jnp.float32)[..., None] * freq
    cosine = jnp.cos(angle)
    sine = jnp.sin(angle)
    first = values[..., :half]
    second = values[..., half:]
    return jnp.concatenate([first * cosine - second * sine, first * sine + second * cosine], -1)


def block_stats(keys, q_lat, q_pos, valid):
    scale = (DN + DR) ** (-0.5)
    scores = jnp.einsum("jhk,tk->jht", q_lat, keys[:, :KVL], preferred_element_type=jnp.float32)
    scores = (
        scores + jnp.einsum("jhk,tk->jht", q_pos, keys[:, KVL:], preferred_element_type=jnp.float32)
    ) * scale
    scores = jnp.where(valid, scores, -1e30)
    top = jnp.max(scores, axis=-1)
    weights = jnp.where(valid, jnp.exp(scores - top[..., None]), 0.0)
    total = jnp.sum(weights, axis=-1)
    numer = jnp.einsum(
        "jht,tk->jhk",
        weights.astype(jnp.bfloat16),
        keys[:, :KVL],
        preferred_element_type=jnp.float32,
    )
    return (top, total, numer)


def combine(left, right):
    top = jnp.maximum(left[0], right[0])
    left_scale = jnp.exp(left[0] - top)
    right_scale = jnp.exp(right[0] - top)
    total = left[1] * left_scale + right[1] * right_scale
    numer = left[2] * left_scale[..., None] + right[2] * right_scale[..., None]
    return (top, total, numer)


def local_general(
    prefill_hidden,
    draft_hidden,
    kv_down,
    kv_gain,
    query_latent,
    q_up,
    kv_up,
    owners,
    segment_ids,
    accepted,
):
    tp_count = lax.axis_size("tp")
    pd_count = lax.axis_size("pd")
    tp_rank = lax.axis_index("tp")
    mine_rank = lax.axis_index("pd")
    requests = owners.shape[0]
    share = PRE_TOK // tp_count
    width = KVL + DR
    local_hidden = prefill_hidden.reshape(RP, PRE_TOK, prefill_hidden.shape[1])
    summed = lax.psum_scatter(
        jnp.einsum(
            "rtd,dw->trw", local_hidden, kv_down, preferred_element_type=jnp.float32
        ).reshape(lax.axis_size("tp") * share, RP * width),
        "tp",
        scatter_dimension=0,
        tiled=True,
    ).reshape(share * RP, width)
    draft_sum = lax.psum(jnp.dot(draft_hidden, kv_down, preferred_element_type=jnp.float32), "tp")
    first_req = mine_rank * RP
    row_pos = jnp.broadcast_to(
        tp_rank * share + jnp.arange(share, dtype=jnp.int32)[:, None], (share, RP)
    )
    page_rows = jnp.concatenate(
        [
            rms_latent(summed, kv_gain),
            rotate(summed[:, KVL:], row_pos.reshape(-1)).astype(jnp.bfloat16),
        ],
        1,
    )
    page_rows = page_rows.reshape(share, RP, width)
    draft_pos = jnp.tile(PRE_TOK + jnp.arange(2, dtype=jnp.int32), RP)
    draft_rows = jnp.concatenate(
        [
            rms_latent(draft_sum, kv_gain),
            rotate(draft_sum[:, KVL:], draft_pos).astype(jnp.bfloat16),
        ],
        1,
    )
    draft_rows = draft_rows.reshape(RP, 2, width)
    my_owners = lax.dynamic_slice_in_dim(owners, first_req, RP, 0)
    routing = (my_owners[None, :] == jnp.arange(pd_count, dtype=jnp.int32)[:, None]).astype(
        jnp.bfloat16
    )
    send_pages = jnp.einsum(
        "dk,tkw->dtw", routing, page_rows, preferred_element_type=jnp.float32
    ).astype(jnp.bfloat16)
    send_drafts = jnp.einsum(
        "dk,kjw->djw", routing, draft_rows, preferred_element_type=jnp.float32
    ).astype(jnp.bfloat16)
    pages, drafts = (
        lax.all_to_all(send_pages, "pd", split_axis=0, concat_axis=0, tiled=True),
        lax.all_to_all(send_drafts, "pd", split_axis=0, concat_axis=0, tiled=True),
    )
    heads_local = q_up.shape[1] // (DN + DR)
    query_full = jnp.dot(
        query_latent.reshape(requests * 2, QL), q_up, preferred_element_type=jnp.float32
    )
    query_full = query_full.reshape(requests, 2, heads_local, DN + DR)
    new_pos = jnp.broadcast_to(PRE_TOK + jnp.arange(2, dtype=jnp.int32)[None, :], (requests, 2))
    q_nope = query_full[..., :DN].astype(jnp.bfloat16)
    q_rot = rotate(query_full[..., DN:], new_pos[:, :, None]).astype(jnp.bfloat16)
    up_heads = kv_up.reshape(KVL, heads_local, DN + DV)
    w_value = up_heads[:, :, DN:]
    q_abs = jnp.einsum(
        "rjhd,khd->rjhk", q_nope, up_heads[:, :, :DN], preferred_element_type=jnp.float32
    ).astype(jnp.bfloat16)
    owner_table = owners.reshape(pd_count, RP) == mine_rank
    holding = jnp.sum(owner_table.astype(jnp.int32), axis=1)
    slot_of = jnp.sum(
        owner_table.astype(jnp.int32) * jnp.arange(RP, dtype=jnp.int32)[None, :], axis=1
    )
    owned_count = jnp.sum(holding)
    order = jnp.argsort((1 - holding) * pd_count + jnp.arange(pd_count, dtype=jnp.int32))
    draft_valid = (jnp.arange(2)[None, :] <= jnp.arange(2)[:, None])[:, None, :]
    empty = jnp.zeros((pd_count, 2, heads_local * DV), jnp.bfloat16)

    def finish(stats, source, request, q_lat, q_pos, result):
        stats = combine(stats, block_stats(drafts[source], q_lat, q_pos, draft_valid))
        attended = (stats[2] / stats[1][..., None]).astype(jnp.bfloat16)
        head_out = jnp.einsum("jhk,khd->jhd", attended, w_value, preferred_element_type=jnp.float32)
        keep = (jnp.arange(2) <= accepted[request]).astype(jnp.float32)[:, None, None]
        answer = (head_out * keep).astype(jnp.bfloat16).reshape(1, 2, heads_local * DV)
        return lax.dynamic_update_slice(result, answer, (source, 0, 0))

    def attend(turn, result):
        source = order[turn]
        request = source * RP + slot_of[source]
        q_lat = q_abs[request]
        q_pos = q_rot[request]
        seg_row = segment_ids[request]
        current = seg_row[PRE_TOK - 1]
        init = (
            jnp.full((2, heads_local), -1e30, jnp.float32),
            jnp.zeros((2, heads_local), jnp.float32),
            jnp.zeros((2, heads_local, KVL), jnp.float32),
        )
        valid = (seg_row == current)[None, None, :]
        stats = combine(
            init,
            block_stats(
                lax.all_gather(pages[source], "tp", axis=0, tiled=True), q_lat, q_pos, valid
            ),
        )
        return finish(stats, source, request, q_lat, q_pos, result)

    result = lax.fori_loop(0, owned_count, attend, empty)
    return (result.reshape(pd_count * 2, heads_local * DV), pages)


def encode(values):
    levels = []
    parts = []
    for first, last in ((0, KVL), (KVL, WIDTH)):
        block = values[first:last]
        top = jnp.maximum(jnp.max(jnp.abs(block), axis=0, keepdims=True), 1e-30)
        level = jnp.ceil(jnp.log2(top) * STEPS)
        codes = jnp.round(block * (jnp.exp2(level * (-1.0 / STEPS)) * TOP))
        parts.append(jnp.clip(codes, -TOP, TOP).astype(jnp.int32).astype(I16))
        levels.append(level.astype(jnp.int32))
    row = lax.broadcasted_iota(jnp.int32, (16, values.shape[1]), 0)
    extra = jnp.where(row == 0, levels[0], jnp.where(row == 1, levels[1], 0))
    return jnp.concatenate([*parts, extra.astype(I16)], 0)


def decode(codes):
    level = codes[WIDTH:CODED].astype(jnp.int32).astype(F32)
    step = jnp.exp2(level * (1.0 / STEPS)) * (1.0 / TOP)
    lat = codes[0:KVL].astype(jnp.int32).astype(F32) * step[0:1]
    rot = codes[KVL:WIDTH].astype(jnp.int32).astype(F32) * step[1:2]
    return jnp.concatenate([lat, rot], 0)


def key_rows(comp, gain, cosine, sine):
    lat = comp[:KVL]
    scale = lax.rsqrt(jnp.mean(lat * lat, axis=0, keepdims=True) + 1e-06)
    first = comp[KVL : KVL + HALF]
    second = comp[KVL + HALF :]
    return jnp.concatenate(
        [
            lat * scale * gain,
            first * cosine - second * sine,
            first * sine + second * cosine,
        ],
        0,
    )


def far(z, i):
    return jnp.where(z < 2, 3 - i, i)


def near(z, i):
    return jnp.where(z < 2, i, 3 - i)


def outer_rank(z):
    return (z == 0) | (z == 3)


def project_far_kernel(rank, hid_ref, down_ref, *refs):
    sum_ref, code_ref = refs[-2:]
    total = lax.dot_general(down_ref[...], hid_ref[0], NT, preferred_element_type=F32)
    for u in range(UNITS):
        sum_ref[0, u] = total[:, u * UNIT : (u + 1) * UNIT]

    @pl.when(outer_rank(rank[0]))
    def _():
        for u in range(UNITS):
            code_ref[0, u] = encode(total[:, u * UNIT : (u + 1) * UNIT])


def project_far(rank, hidden, down_t, request, after):
    depth = hidden.shape[-1]
    return pl.pallas_call(
        project_far_kernel,
        grid_spec=pltpu.PrefetchScalarGridSpec(
            num_scalar_prefetch=1,
            grid=(2,),
            in_specs=[
                pl.BlockSpec((1, SHARE, depth), lambda i, rank: (request, far(rank[0], i), 0)),
                pl.BlockSpec((WIDTH, depth), lambda i, rank: (0, 0)),
                *([ANY] * len(after)),
            ],
            out_specs=[
                pl.BlockSpec((1, UNITS, WIDTH, UNIT), lambda i, rank: (i, 0, 0, 0)),
                pl.BlockSpec((1, UNITS, CODED, UNIT), lambda i, rank: (i, 0, 0, 0)),
            ],
        ),
        out_shape=[
            jax.ShapeDtypeStruct((2, UNITS, WIDTH, UNIT), F32),
            jax.ShapeDtypeStruct((2, UNITS, CODED, UNIT), I16),
        ],
        compiler_params=ROOM,
        cost_estimate=COST,
        name="project_far",
    )(rank, hidden, down_t, *after)


def project_near_kernel(rank, hid_ref, down_ref, *refs):
    sum_ref, *code_refs = refs[-3:]
    unit = pl.program_id(0)
    rows = hid_ref[...].reshape(LANES, hid_ref.shape[-1])
    total = lax.dot_general(down_ref[...], rows, NT, preferred_element_type=F32)
    for r in range(RP):
        sum_ref[0, 0, r] = total[:, r * UNIT : (r + 1) * UNIT]
    coded = outer_rank(rank[0]) & (pl.program_id(1) == 1)
    for mine, ref in zip((unit == 0, unit > 0), code_refs):

        @pl.when(coded & mine)
        def _(ref=ref):
            for r in range(RP):
                ref[0, r] = encode(total[:, r * UNIT : (r + 1) * UNIT])


def project_near(rank, hidden, down_t, after):
    depth = hidden.shape[-1]
    return pl.pallas_call(
        project_near_kernel,
        grid_spec=pltpu.PrefetchScalarGridSpec(
            num_scalar_prefetch=1,
            grid=(UNITS, 2),
            in_specs=[
                pl.BlockSpec(
                    (RP, UNIT, depth), lambda u, i, rank: (0, near(rank[0], i) * UNITS + u, 0)
                ),
                pl.BlockSpec((WIDTH, depth), lambda u, i, rank: (0, 0)),
                *([ANY] * len(after)),
            ],
            out_specs=[
                pl.BlockSpec((1, 1, RP, WIDTH, UNIT), lambda u, i, rank: (u, i, 0, 0, 0)),
                pl.BlockSpec((1, RP, CODED, UNIT), lambda u, i, rank: (0, 0, 0, 0)),
                pl.BlockSpec(
                    (1, RP, CODED, UNIT), lambda u, i, rank: (jnp.maximum(u, 1) - 1, 0, 0, 0)
                ),
            ],
        ),
        out_shape=[
            jax.ShapeDtypeStruct((UNITS, 2, RP, WIDTH, UNIT), F32),
            jax.ShapeDtypeStruct((1, RP, CODED, UNIT), I16),
            jax.ShapeDtypeStruct((UNITS - 1, RP, CODED, UNIT), I16),
        ],
        compiler_params=ROOM,
        cost_estimate=COST,
        name="project_near",
    )(rank, hidden, down_t, *after)


def add_kernel(rank, own_ref, got_ref, *refs):
    @pl.when(~outer_rank(rank[0]))
    def _():
        for u in range(UNITS):
            refs[-1][0, u] = encode(own_ref[u] + decode(got_ref[0, u]))


def add_on(rank, own, got, request=None, after=()):
    chunk = lambda i, rank: (i, 0, 0, 0)
    if request is None:
        own_spec = pl.BlockSpec((None, UNITS, WIDTH, UNIT), chunk)
    else:
        own_spec = pl.BlockSpec(
            (UNITS, None, None, WIDTH, UNIT), lambda i, rank: (0, i, request, 0, 0)
        )
    return pl.pallas_call(
        add_kernel,
        grid_spec=pltpu.PrefetchScalarGridSpec(
            num_scalar_prefetch=1,
            grid=(2,),
            in_specs=[
                own_spec,
                pl.BlockSpec((1, UNITS, CODED, UNIT), chunk),
                *([ANY] * len(after)),
            ],
            out_specs=pl.BlockSpec((1, UNITS, CODED, UNIT), chunk),
        ),
        out_shape=jax.ShapeDtypeStruct((2, UNITS, CODED, UNIT), I16),
        compiler_params=ROOM,
        cost_estimate=COST,
        name="add_on",
    )(rank, own, got, *after)


def page_kernel(rank, slot, own_ref, *refs):
    got_refs, sent_refs, refs = refs[:RP], refs[RP : 2 * RP], refs[2 * RP :]
    side_refs, (gain_ref, cos_ref, sin_ref), out_ref = refs[:2], refs[2:5], refs[-1]
    request = pl.program_id(0)

    def write(u, comp):
        rows = key_rows(comp, gain_ref[...], cos_ref[u], sin_ref[u])
        out_ref[0, :, u * UNIT : (u + 1) * UNIT] = rows.astype(BF)

    for r in range(RP):

        @pl.when((request == r) & outer_rank(rank[0]))
        def _(r=r):
            for u in range(UNITS):
                write(u, own_ref[u] + decode(got_refs[r][u]))

        @pl.when((request == r) & ~outer_rank(rank[0]))
        def _(r=r):
            for u in range(UNITS):
                side = side_refs[u > 0][max(u - 1, 0)]
                write(u, decode(sent_refs[r][u]) + decode(side))


def pages_of(rank, slot, own, got, sent, side, gain, cosine, sine, count):
    first = pl.BlockSpec((None, UNITS, CODED, UNIT), lambda i, *_: (0, 0, 0, 0))
    second = pl.BlockSpec((None, UNITS, CODED, UNIT), lambda i, *_: (1, 0, 0, 0))
    table = pl.BlockSpec((UNITS, HALF, UNIT), lambda i, *_: (0, 0, 0))
    base = [jnp.zeros((count, WIDTH, SHARE), BF)] if count > RP else []
    return pl.pallas_call(
        page_kernel,
        grid_spec=pltpu.PrefetchScalarGridSpec(
            num_scalar_prefetch=2,
            grid=(RP,),
            in_specs=[
                pl.BlockSpec((UNITS, None, None, WIDTH, UNIT), lambda i, *_: (0, 0, i, 0, 0)),
                *([first] * RP),
                *([second] * RP),
                pl.BlockSpec((1, None, CODED, UNIT), lambda i, *_: (0, i, 0, 0)),
                pl.BlockSpec((UNITS - 1, None, CODED, UNIT), lambda i, *_: (0, i, 0, 0)),
                pl.BlockSpec((KVL, UNIT), lambda i, *_: (0, 0)),
                table,
                table,
                *([ANY] * len(base)),
            ],
            out_specs=pl.BlockSpec((1, WIDTH, SHARE), lambda i, rank, slot: (slot[i], 0, 0)),
        ),
        out_shape=jax.ShapeDtypeStruct((count, WIDTH, SHARE), BF),
        input_output_aliases={8 + 2 * RP: 0} if base else {},
        compiler_params=ROOM,
        cost_estimate=COST,
        name="pages",
    )(rank, slot, own, *got, *sent, *side, gain, cosine, sine, *base)


def query_kernel(lat_ref, up_ref, draft_ref, down_ref, *refs):
    *key_refs, cos_ref, sin_ref, out_ref, split_ref = refs

    @pl.when(pl.program_id(0) == 0)
    def _():
        rest = lax.dot_general(draft_ref[...], down_ref[...], NT, preferred_element_type=F32)
        for n in range(3):
            term = rest.astype(BF).astype(F32)
            split_ref[n] = term
            rest = rest - term
        split_ref[3] = jnp.zeros_like(rest)

    full = jnp.dot(lat_ref[...], up_ref[...], preferred_element_type=F32)
    for h, key_ref in enumerate(key_refs):
        base = h * (DN + DR)
        nope = full[:, base : base + DN].astype(BF)
        first = full[:, base + DN : base + DN + HALF]
        second = full[:, base + DN + HALF : base + DN + DR]
        absorbed = lax.dot_general(nope, key_ref[...], NT, preferred_element_type=F32)
        cosine, sine = cos_ref[...], sin_ref[...]
        out_ref[h] = jnp.concatenate(
            [absorbed, first * cosine - second * sine, first * sine + second * cosine], 1
        )


def queries(latents, q_up, kv_up, draft, down_t, cosine, sine, after):
    rows = latents.shape[0]
    heads = q_up.shape[1] // (DN + DR)
    step = 4
    key_spec = [
        pl.BlockSpec((KVL, DN), lambda i, h=h: (0, 2 * (step * i + h))) for h in range(step)
    ]
    whole = lambda i: (0, 0)
    table = pl.BlockSpec((rows, HALF), whole)
    body = lambda *refs: query_kernel(*refs[:-3], *refs[-2:])
    return pl.pallas_call(
        body,
        grid=(heads // step,),
        in_specs=[
            pl.BlockSpec((rows, QL), whole),
            pl.BlockSpec((QL, step * (DN + DR)), lambda i: (0, i)),
            pl.BlockSpec(draft.shape, whole),
            pl.BlockSpec(down_t.shape, whole),
            *key_spec,
            table,
            table,
            ANY,
        ],
        out_specs=[
            pl.BlockSpec((step, rows, WIDTH), lambda i: (i, 0, 0)),
            pl.BlockSpec((4, rows, WIDTH), lambda i: (0, 0, 0)),
        ],
        out_shape=[
            jax.ShapeDtypeStruct((heads, rows, WIDTH), F32),
            jax.ShapeDtypeStruct((4, rows, WIDTH), F32),
        ],
        compiler_params=ROOM,
        cost_estimate=COST,
        name="queries",
    )(latents, q_up, draft, down_t, *([kv_up] * step), cosine, sine, after)


def attend_kernel(rank, q_ref, draft_ref, *refs):
    own_ref, got_refs, refs = refs[0], refs[1 : 1 + RP], refs[1 + RP :]
    column_ref, cos_ref, sin_ref, midcos_ref, midsin_ref, refs = *refs[:5], refs[5:]
    valid_ref, gain_ref, newcos_ref, newsin_ref, refs = *refs[:4], refs[4:]
    out_refs, keys_ref = refs[-5:-1], refs[-1]
    request = pl.program_id(0)

    @pl.when(rank[0] == 3)
    def _():
        for r in range(RP):

            @pl.when(request == r)
            def _(r=r):
                for i, (cosine, sine) in enumerate(
                    ((cos_ref, sin_ref), (midcos_ref, midsin_ref))
                ):
                    for u in range(UNITS):
                        comp = own_ref[u, i] + decode(got_refs[r][i, u])
                        rows = key_rows(comp, column_ref[...], cosine[u], sine[u])
                        start = (1 - i) * SHARE + u * UNIT
                        keys_ref[:, start : start + UNIT] = rows.astype(BF)

        scale = (DN + DR) ** (-0.5)
        local_rows = out_refs[0].shape[1]
        new = 2 * RP
        comp = 0.0
        for t in range(4):
            terms = draft_ref[t].astype(F32)
            comp = comp + (terms[0:new] + terms[new : 2 * new] + terms[2 * new : 3 * new])
        lat = comp[:, :KVL]
        norm = lax.rsqrt(jnp.mean(lat * lat, axis=-1, keepdims=True) + 1e-06)
        first = comp[:, KVL : KVL + HALF]
        second = comp[:, KVL + HALF :]
        cosine, sine = newcos_ref[...], newsin_ref[...]
        drafts = jnp.concatenate(
            [
                lat * norm * gain_ref[...],
                first * cosine - second * sine,
                first * sine + second * cosine,
            ],
            1,
        )
        drafts = jnp.concatenate([drafts, jnp.zeros((UNIT - new, WIDTH), F32)], 0).astype(BF)
        query = jnp.concatenate([q_ref[t] for t in range(4)], 0)
        scores = jnp.dot(query, keys_ref[...], preferred_element_type=F32) * scale
        scores = jnp.where(valid_ref[0] > 0.0, scores, -1e30)
        fresh = lax.dot_general(query, drafts, NT, preferred_element_type=F32) * scale
        row = lax.broadcasted_iota(jnp.int32, fresh.shape, 0)
        late = (row % local_rows) // (local_rows // 2)
        offset = lax.broadcasted_iota(jnp.int32, fresh.shape, 1) - 2 * request
        fresh = jnp.where((offset >= 0) & (offset <= late), fresh, -1e30)
        top = jnp.maximum(
            jnp.max(scores, axis=1, keepdims=True), jnp.max(fresh, axis=1, keepdims=True)
        )
        weights = jnp.exp(scores - top)
        fresh = jnp.exp(fresh - top)
        total = jnp.sum(weights, axis=1, keepdims=True) + jnp.sum(fresh, axis=1, keepdims=True)
        numer = lax.dot_general(
            weights.astype(BF), keys_ref[0:KVL, :], NT, preferred_element_type=F32
        )
        numer = numer + jnp.dot(fresh.astype(BF), drafts[:, :KVL], preferred_element_type=F32)
        result = (numer / total).astype(BF)
        for t, ref in enumerate(out_refs):
            ref[0] = result[t * local_rows : (t + 1) * local_rows]


def attend(rank, messages, own, got, column, tables, valid, gain, cosine, sine, after):
    new = 2 * RP
    local_rows = (messages.shape[1] - 4 * new) // RP
    last = RP * local_rows // (4 * new)
    out = jax.ShapeDtypeStruct((RP, local_rows, KVL), BF)
    whole = lambda i, rank: (0, 0)
    whole3 = lambda i, rank: (0, 0, 0)
    return pl.pallas_call(
        attend_kernel,
        grid_spec=pltpu.PrefetchScalarGridSpec(
            num_scalar_prefetch=1,
            grid=(RP,),
            in_specs=[
                pl.BlockSpec((4, local_rows, WIDTH), lambda i, rank: (0, i, 0)),
                pl.BlockSpec((4, 4 * new, WIDTH), lambda i, rank: (0, last, 0)),
                pl.BlockSpec(
                    (UNITS, 2, None, WIDTH, UNIT), lambda i, rank: (0, 0, i, 0, 0)
                ),
                *([pl.BlockSpec((2, UNITS, CODED, UNIT), lambda i, rank: (0, 0, 0, 0))] * RP),
                pl.BlockSpec((KVL, UNIT), whole),
                *([pl.BlockSpec((UNITS, HALF, UNIT), whole3)] * 4),
                pl.BlockSpec((1, 1, valid.shape[2]), lambda i, rank: (i, 0, 0)),
                pl.BlockSpec((1, KVL), whole),
                pl.BlockSpec(cosine.shape, whole),
                pl.BlockSpec(sine.shape, whole),
                *([ANY] * len(after)),
            ],
            out_specs=[pl.BlockSpec((1, local_rows, KVL), lambda i, rank: (i, 0, 0))] * 4,
            scratch_shapes=[pltpu.VMEM((WIDTH, 2 * SHARE), BF)],
        ),
        out_shape=[out] * 4,
        compiler_params=ROOM,
        cost_estimate=COST,
        name="attend",
    )(rank, messages, messages, own, *got, column, *tables, valid, gain, cosine, sine, *after)


def heads_kernel(step, o_ref, keep_ref, *refs):
    out_ref = refs[-1]
    for h, value_ref in enumerate(refs[:step]):
        row = jnp.dot(o_ref[h].astype(BF), value_ref[...], preferred_element_type=F32)
        out_ref[:, h * DV : (h + 1) * DV] = row * keep_ref[...]


def heads_out(attended, keep, kv_up, after):
    heads, rows, _ = attended.shape
    step = 8
    value_spec = [
        pl.BlockSpec((KVL, DV), lambda i, h=h: (0, 2 * (step * i + h) + 1)) for h in range(step)
    ]
    return pl.pallas_call(
        functools.partial(heads_kernel, step),
        grid=(heads // step,),
        in_specs=[
            pl.BlockSpec((step, rows, KVL), lambda i: (i, 0, 0)),
            pl.BlockSpec((rows, DV), lambda i: (0, 0)),
            *value_spec,
            *([ANY] * len(after)),
        ],
        out_specs=pl.BlockSpec((rows, step * DV), lambda i: (0, i)),
        out_shape=jax.ShapeDtypeStruct((rows, heads * DV), F32),
        compiler_params=ROOM,
        cost_estimate=COST,
        name="heads_out",
    )(attended, keep, *([kv_up] * step), *after)


def rope_tables(position):
    freq = jnp.exp(-jnp.log(10000.0) * jnp.arange(HALF, dtype=F32) / HALF)
    angle = position.astype(F32)[..., None] * freq
    return jnp.cos(angle), jnp.sin(angle)


def local_line(
    prefill_hidden,
    draft_hidden,
    kv_down,
    kv_gain,
    query_latent,
    q_up,
    kv_up,
    owners,
    segment_ids,
    accepted,
):
    pd_count = lax.axis_size("pd")
    z = lax.axis_index("tp")
    p = lax.axis_index("pd")
    first_req = p * RP

    rank = z.astype(jnp.int32).reshape(1)
    hidden = prefill_hidden.reshape(RP, PRE_TOK, prefill_hidden.shape[1])
    down_t = kv_down.T
    inward, across, outward = [(0, 1), (3, 2)], [(1, 2), (2, 1)], [(2, 3), (1, 0)]

    far_sums, inner = [], []
    for r in range(RP):
        total, codes = project_far(rank, hidden, down_t, r, far_sums[-1:])
        far_sums.append(total)
        inner.append(lax.ppermute(codes, "tp", inward))

    def first_hop(r, after):
        block = add_on(rank, far_sums[r], inner[r], after=after)
        crossed.append(lax.ppermute(block, "tp", across))
        return block

    def second_hop(r, after):
        block = add_on(rank, near_sums, crossed[r], r, after)
        sent.append(block)
        outer.append(lax.ppermute(block, "tp", outward))
        return block

    crossed, sent, outer = [], [], []
    block = first_hop(0, far_sums[-1:])
    near_sums, *side = project_near(rank, hidden, down_t, [block])
    first_hop(1, [near_sums])
    second_hop(0, [])
    first_hop(2, [sent[0]])
    block = second_hop(1, [outer[0]])

    latents = lax.dynamic_slice_in_dim(query_latent, first_req, RP, 0).reshape(RP * 2, QL)
    new_pos = jnp.tile(PRE_TOK + jnp.arange(2, dtype=jnp.int32), RP)
    new_cos, new_sin = rope_tables(new_pos)
    query, terms = queries(
        latents, q_up, kv_up, draft_hidden, down_t, new_cos, new_sin, block
    )
    heads = query.shape[0]
    query = query.reshape(heads, RP, 2, WIDTH).transpose(1, 2, 0, 3)
    message = jnp.concatenate(
        [query.reshape(RP * 2 * heads, WIDTH), terms.reshape(8 * RP, WIDTH)], 0
    ).astype(BF)
    messages = lax.all_gather(message, "tp", axis=0)

    my_segments = lax.dynamic_slice_in_dim(segment_ids, first_req, RP, 0)
    valid = (my_segments == my_segments[:, -1:])[:, PRE_TOK // 2 :].astype(F32)
    valid = valid.reshape(RP, 1, PRE_TOK // 2)
    column = jnp.broadcast_to(kv_gain[:, None], (KVL, UNIT))
    steps = jnp.arange(SHARE, dtype=jnp.int32).reshape(UNITS, UNIT)
    tables = [
        jnp.swapaxes(t, 1, 2)
        for t in (*rope_tables(z * SHARE + steps), *rope_tables(2 * SHARE + steps))
    ]

    block = first_hop(3, [message, column, valid, *tables])
    side = [lax.ppermute(codes, "tp", inward) for codes in side]
    second_hop(2, [block, outer[1]])
    second_hop(3, [side[0], outer[2]])

    result = attend(
        rank,
        messages,
        near_sums,
        outer,
        column,
        tables,
        valid,
        kv_gain.reshape(1, KVL),
        new_cos,
        new_sin,
        [],
    )
    back = [lax.ppermute(result[t], "tp", [(3, t)]) for t in range(3)]

    my_owners = lax.dynamic_slice_in_dim(owners, first_req, RP, 0)
    pages = pages_of(
        rank,
        my_owners,
        near_sums,
        outer,
        sent,
        side,
        column,
        tables[0],
        tables[1],
        pd_count,
    )
    cache = lax.all_to_all(pages, "pd", split_axis=0, concat_axis=0, tiled=True)
    cache = jnp.swapaxes(cache, 1, 2)

    attended = jnp.where(z == 3, result[3], back[0] + back[1] + back[2])
    attended = attended.reshape(RP, 2, heads, KVL).transpose(2, 0, 1, 3)
    attended = attended.reshape(heads, RP * 2, KVL).astype(F32)
    my_accepted = lax.dynamic_slice_in_dim(accepted, first_req, RP, 0)
    keep = (jnp.arange(2)[None, :] <= my_accepted[:, None]).astype(F32).reshape(RP * 2, 1)
    answer = heads_out(attended, jnp.broadcast_to(keep, (RP * 2, DV)), kv_up, [pages])
    answer = answer.reshape(RP, 2, heads * DV)
    routing = my_owners[None, :] == jnp.arange(pd_count, dtype=jnp.int32)[:, None]
    has = jnp.any(routing, axis=1)
    slots = jnp.sum(routing.astype(jnp.int32) * jnp.arange(RP, dtype=jnp.int32)[None, :], axis=1)
    placed = jnp.where(has[:, None, None], answer[slots], 0.0).astype(BF)
    placed = lax.all_to_all(placed, "pd", split_axis=0, concat_axis=0, tiled=True)
    return (placed.reshape(pd_count * 2, heads * DV), cache)


def solution(mesh):
    placed = (
        P(("groups", "pd"), "tp"),
        P(("groups", "pd"), "tp"),
        P("tp", None),
        P(),
        P("groups", None, None),
        P(None, "tp"),
        P(None, "tp"),
        P("groups"),
        P("groups", None),
        P("groups"),
    )
    return jax.shard_map(
        local_line if mesh.shape["tp"] == 4 else local_general,
        mesh=mesh,
        in_specs=placed,
        out_specs=(P(("groups", "pd"), "tp"), P(("groups", "pd"), "tp", None)),
        check_vma=False,
    )
```

```python
import functools

import jax
import jax.numpy as jnp
from jax import lax
from jax.experimental import pallas as pl
from jax.experimental.pallas import tpu as pltpu
from jax.sharding import PartitionSpec as P

DN = 128
DR = 64
DV = 128
KVL = 512
QL = 1536
PRE_TOK = 1536
RP = 4
WIDTH = KVL + DR
HALF = DR // 2
PART = WIDTH // 2
CODED = WIDTH + 16
SHARE = PRE_TOK // 4
UNIT = 128
UNITS = SHARE // UNIT
LANES = RP * UNIT
STEPS = 256.0
TOP = 32767.0
BF = jnp.bfloat16
F32 = jnp.float32
I16 = jnp.int16
NT = (((1,), (1,)), ((), ()))
ROOM = pltpu.CompilerParams(vmem_limit_bytes=60 << 20)
SOME = pltpu.CompilerParams(vmem_limit_bytes=60 << 20)
ANY = pl.BlockSpec(memory_space=pl.ANY)
VMEM = pl.BlockSpec(memory_space=pltpu.VMEM)
SMEM = pl.BlockSpec(memory_space=pltpu.SMEM)


COST = pl.CostEstimate(flops=1024, bytes_accessed=1024, transcendentals=0)


def rms_latent(comp, gain):
    lat = comp[:, :KVL]
    scale = lax.rsqrt(jnp.mean(lat * lat, axis=-1, keepdims=True) + 1e-06)
    return (lat * scale * gain).astype(jnp.bfloat16)


def rotate(values, position):
    half = values.shape[-1] // 2
    freq = jnp.exp(-jnp.log(10000.0) * jnp.arange(half, dtype=jnp.float32) / half)
    angle = position.astype(jnp.float32)[..., None] * freq
    cosine = jnp.cos(angle)
    sine = jnp.sin(angle)
    first = values[..., :half]
    second = values[..., half:]
    return jnp.concatenate([first * cosine - second * sine, first * sine + second * cosine], -1)


def block_stats(keys, q_lat, q_pos, valid):
    scale = (DN + DR) ** (-0.5)
    scores = jnp.einsum("jhk,tk->jht", q_lat, keys[:, :KVL], preferred_element_type=jnp.float32)
    scores = (
        scores + jnp.einsum("jhk,tk->jht", q_pos, keys[:, KVL:], preferred_element_type=jnp.float32)
    ) * scale
    scores = jnp.where(valid, scores, -1e30)
    top = jnp.max(scores, axis=-1)
    weights = jnp.where(valid, jnp.exp(scores - top[..., None]), 0.0)
    total = jnp.sum(weights, axis=-1)
    numer = jnp.einsum(
        "jht,tk->jhk",
        weights.astype(jnp.bfloat16),
        keys[:, :KVL],
        preferred_element_type=jnp.float32,
    )
    return (top, total, numer)


def combine(left, right):
    top = jnp.maximum(left[0], right[0])
    left_scale = jnp.exp(left[0] - top)
    right_scale = jnp.exp(right[0] - top)
    total = left[1] * left_scale + right[1] * right_scale
    numer = left[2] * left_scale[..., None] + right[2] * right_scale[..., None]
    return (top, total, numer)


def local_general(
    prefill_hidden,
    draft_hidden,
    kv_down,
    kv_gain,
    query_latent,
    q_up,
    kv_up,
    owners,
    segment_ids,
    accepted,
):
    tp_count = lax.axis_size("tp")
    pd_count = lax.axis_size("pd")
    tp_rank = lax.axis_index("tp")
    mine_rank = lax.axis_index("pd")
    requests = owners.shape[0]
    share = PRE_TOK // tp_count
    width = KVL + DR
    local_hidden = prefill_hidden.reshape(RP, PRE_TOK, prefill_hidden.shape[1])
    summed = lax.psum_scatter(
        jnp.einsum(
            "rtd,dw->trw", local_hidden, kv_down, preferred_element_type=jnp.float32
        ).reshape(lax.axis_size("tp") * share, RP * width),
        "tp",
        scatter_dimension=0,
        tiled=True,
    ).reshape(share * RP, width)
    draft_sum = lax.psum(jnp.dot(draft_hidden, kv_down, preferred_element_type=jnp.float32), "tp")
    first_req = mine_rank * RP
    row_pos = jnp.broadcast_to(
        tp_rank * share + jnp.arange(share, dtype=jnp.int32)[:, None], (share, RP)
    )
    page_rows = jnp.concatenate(
        [
            rms_latent(summed, kv_gain),
            rotate(summed[:, KVL:], row_pos.reshape(-1)).astype(jnp.bfloat16),
        ],
        1,
    )
    page_rows = page_rows.reshape(share, RP, width)
    draft_pos = jnp.tile(PRE_TOK + jnp.arange(2, dtype=jnp.int32), RP)
    draft_rows = jnp.concatenate(
        [
            rms_latent(draft_sum, kv_gain),
            rotate(draft_sum[:, KVL:], draft_pos).astype(jnp.bfloat16),
        ],
        1,
    )
    draft_rows = draft_rows.reshape(RP, 2, width)
    my_owners = lax.dynamic_slice_in_dim(owners, first_req, RP, 0)
    routing = (my_owners[None, :] == jnp.arange(pd_count, dtype=jnp.int32)[:, None]).astype(
        jnp.bfloat16
    )
    send_pages = jnp.einsum(
        "dk,tkw->dtw", routing, page_rows, preferred_element_type=jnp.float32
    ).astype(jnp.bfloat16)
    send_drafts = jnp.einsum(
        "dk,kjw->djw", routing, draft_rows, preferred_element_type=jnp.float32
    ).astype(jnp.bfloat16)
    pages, drafts = (
        lax.all_to_all(send_pages, "pd", split_axis=0, concat_axis=0, tiled=True),
        lax.all_to_all(send_drafts, "pd", split_axis=0, concat_axis=0, tiled=True),
    )
    heads_local = q_up.shape[1] // (DN + DR)
    query_full = jnp.dot(
        query_latent.reshape(requests * 2, QL), q_up, preferred_element_type=jnp.float32
    )
    query_full = query_full.reshape(requests, 2, heads_local, DN + DR)
    new_pos = jnp.broadcast_to(PRE_TOK + jnp.arange(2, dtype=jnp.int32)[None, :], (requests, 2))
    q_nope = query_full[..., :DN].astype(jnp.bfloat16)
    q_rot = rotate(query_full[..., DN:], new_pos[:, :, None]).astype(jnp.bfloat16)
    up_heads = kv_up.reshape(KVL, heads_local, DN + DV)
    w_value = up_heads[:, :, DN:]
    q_abs = jnp.einsum(
        "rjhd,khd->rjhk", q_nope, up_heads[:, :, :DN], preferred_element_type=jnp.float32
    ).astype(jnp.bfloat16)
    owner_table = owners.reshape(pd_count, RP) == mine_rank
    holding = jnp.sum(owner_table.astype(jnp.int32), axis=1)
    slot_of = jnp.sum(
        owner_table.astype(jnp.int32) * jnp.arange(RP, dtype=jnp.int32)[None, :], axis=1
    )
    owned_count = jnp.sum(holding)
    order = jnp.argsort((1 - holding) * pd_count + jnp.arange(pd_count, dtype=jnp.int32))
    draft_valid = (jnp.arange(2)[None, :] <= jnp.arange(2)[:, None])[:, None, :]
    empty = jnp.zeros((pd_count, 2, heads_local * DV), jnp.bfloat16)

    def finish(stats, source, request, q_lat, q_pos, result):
        stats = combine(stats, block_stats(drafts[source], q_lat, q_pos, draft_valid))
        attended = (stats[2] / stats[1][..., None]).astype(jnp.bfloat16)
        head_out = jnp.einsum("jhk,khd->jhd", attended, w_value, preferred_element_type=jnp.float32)
        keep = (jnp.arange(2) <= accepted[request]).astype(jnp.float32)[:, None, None]
        answer = (head_out * keep).astype(jnp.bfloat16).reshape(1, 2, heads_local * DV)
        return lax.dynamic_update_slice(result, answer, (source, 0, 0))

    def attend(turn, result):
        source = order[turn]
        request = source * RP + slot_of[source]
        q_lat = q_abs[request]
        q_pos = q_rot[request]
        seg_row = segment_ids[request]
        current = seg_row[PRE_TOK - 1]
        init = (
            jnp.full((2, heads_local), -1e30, jnp.float32),
            jnp.zeros((2, heads_local), jnp.float32),
            jnp.zeros((2, heads_local, KVL), jnp.float32),
        )
        valid = (seg_row == current)[None, None, :]
        stats = combine(
            init,
            block_stats(
                lax.all_gather(pages[source], "tp", axis=0, tiled=True), q_lat, q_pos, valid
            ),
        )
        return finish(stats, source, request, q_lat, q_pos, result)

    result = lax.fori_loop(0, owned_count, attend, empty)
    return (result.reshape(pd_count * 2, heads_local * DV), pages)


def encode(values):
    levels = []
    parts = []
    for first, last in ((0, KVL), (KVL, WIDTH)):
        block = values[first:last]
        top = jnp.maximum(jnp.max(jnp.abs(block), axis=0, keepdims=True), 1e-30)
        level = jnp.ceil(jnp.log2(top) * STEPS)
        codes = jnp.round(block * (jnp.exp2(level * (-1.0 / STEPS)) * TOP))
        parts.append(jnp.clip(codes, -TOP, TOP).astype(jnp.int32).astype(I16))
        levels.append(level.astype(jnp.int32))
    row = lax.broadcasted_iota(jnp.int32, (16, values.shape[1]), 0)
    extra = jnp.where(row == 0, levels[0], jnp.where(row == 1, levels[1], 0))
    return jnp.concatenate([*parts, extra.astype(I16)], 0)


def decode(codes):
    level = codes[WIDTH:CODED].astype(jnp.int32).astype(F32)
    step = jnp.exp2(level * (1.0 / STEPS)) * (1.0 / TOP)
    lat = codes[0:KVL].astype(jnp.int32).astype(F32) * step[0:1]
    rot = codes[KVL:WIDTH].astype(jnp.int32).astype(F32) * step[1:2]
    return jnp.concatenate([lat, rot], 0)


def key_rows(comp, gain, cosine, sine):
    lat = comp[:KVL]
    scale = lax.rsqrt(jnp.mean(lat * lat, axis=0, keepdims=True) + 1e-06)
    first = comp[KVL : KVL + HALF]
    second = comp[KVL + HALF :]
    return jnp.concatenate(
        [
            lat * scale * gain,
            first * cosine - second * sine,
            first * sine + second * cosine,
        ],
        0,
    )


def far(z, i):
    return jnp.where(z < 2, 3 - i, i)


def near(z, i):
    return jnp.where(z < 2, i, 3 - i)


def outer_rank(z):
    return (z == 0) | (z == 3)


def project_far_kernel(rank, hid_ref, down_ref, *refs):
    sum_ref, code_ref = refs[-2:]
    total = lax.dot_general(down_ref[...], hid_ref[0], NT, preferred_element_type=F32)
    for u in range(UNITS):
        sum_ref[0, u] = total[:, u * UNIT : (u + 1) * UNIT]

    @pl.when(outer_rank(rank[0]))
    def _():
        for u in range(UNITS):
            code_ref[0, u] = encode(total[:, u * UNIT : (u + 1) * UNIT])


def project_far(rank, hidden, down_t, request, after):
    depth = hidden.shape[-1]
    return pl.pallas_call(
        project_far_kernel,
        grid_spec=pltpu.PrefetchScalarGridSpec(
            num_scalar_prefetch=1,
            grid=(2,),
            in_specs=[
                pl.BlockSpec((1, SHARE, depth), lambda i, rank: (request, far(rank[0], i), 0)),
                pl.BlockSpec((WIDTH, depth), lambda i, rank: (0, 0)),
                *([ANY] * len(after)),
            ],
            out_specs=[
                pl.BlockSpec((1, UNITS, WIDTH, UNIT), lambda i, rank: (i, 0, 0, 0)),
                pl.BlockSpec((1, UNITS, CODED, UNIT), lambda i, rank: (i, 0, 0, 0)),
            ],
        ),
        out_shape=[
            jax.ShapeDtypeStruct((2, UNITS, WIDTH, UNIT), F32),
            jax.ShapeDtypeStruct((2, UNITS, CODED, UNIT), I16),
        ],
        compiler_params=ROOM,
        cost_estimate=COST,
        name="project_far",
    )(rank, hidden, down_t, *after)


def project_near_kernel(rank, hid_ref, down_ref, *refs):
    sum_ref, *code_refs = refs[-3:]
    unit = pl.program_id(0)
    rows = hid_ref[...].reshape(LANES, hid_ref.shape[-1])
    total = lax.dot_general(down_ref[...], rows, NT, preferred_element_type=F32)
    for r in range(RP):
        sum_ref[0, 0, r] = total[:, r * UNIT : (r + 1) * UNIT]
    coded = outer_rank(rank[0]) & (pl.program_id(1) == 1)
    for mine, ref in zip((unit == 0, unit > 0), code_refs):

        @pl.when(coded & mine)
        def _(ref=ref):
            for r in range(RP):
                ref[0, r] = encode(total[:, r * UNIT : (r + 1) * UNIT])


def project_near(rank, hidden, down_t, after):
    depth = hidden.shape[-1]
    return pl.pallas_call(
        project_near_kernel,
        grid_spec=pltpu.PrefetchScalarGridSpec(
            num_scalar_prefetch=1,
            grid=(UNITS, 2),
            in_specs=[
                pl.BlockSpec(
                    (RP, UNIT, depth), lambda u, i, rank: (0, near(rank[0], i) * UNITS + u, 0)
                ),
                pl.BlockSpec((WIDTH, depth), lambda u, i, rank: (0, 0)),
                *([ANY] * len(after)),
            ],
            out_specs=[
                pl.BlockSpec((1, 1, RP, WIDTH, UNIT), lambda u, i, rank: (u, i, 0, 0, 0)),
                pl.BlockSpec((1, RP, CODED, UNIT), lambda u, i, rank: (0, 0, 0, 0)),
                pl.BlockSpec(
                    (1, RP, CODED, UNIT), lambda u, i, rank: (jnp.maximum(u, 1) - 1, 0, 0, 0)
                ),
            ],
        ),
        out_shape=[
            jax.ShapeDtypeStruct((UNITS, 2, RP, WIDTH, UNIT), F32),
            jax.ShapeDtypeStruct((1, RP, CODED, UNIT), I16),
            jax.ShapeDtypeStruct((UNITS - 1, RP, CODED, UNIT), I16),
        ],
        compiler_params=ROOM,
        cost_estimate=COST,
        name="project_near",
    )(rank, hidden, down_t, *after)


def add_kernel(rank, own_ref, got_ref, *refs):
    @pl.when(~outer_rank(rank[0]))
    def _():
        for u in range(UNITS):
            refs[-1][0, u] = encode(own_ref[u] + decode(got_ref[0, u]))


def add_on(rank, own, got, request=None, after=()):
    chunk = lambda i, rank: (i, 0, 0, 0)
    if request is None:
        own_spec = pl.BlockSpec((None, UNITS, WIDTH, UNIT), chunk)
    else:
        own_spec = pl.BlockSpec(
            (UNITS, None, None, WIDTH, UNIT), lambda i, rank: (0, i, request, 0, 0)
        )
    return pl.pallas_call(
        add_kernel,
        grid_spec=pltpu.PrefetchScalarGridSpec(
            num_scalar_prefetch=1,
            grid=(2,),
            in_specs=[
                own_spec,
                pl.BlockSpec((1, UNITS, CODED, UNIT), chunk),
                *([ANY] * len(after)),
            ],
            out_specs=pl.BlockSpec((1, UNITS, CODED, UNIT), chunk),
        ),
        out_shape=jax.ShapeDtypeStruct((2, UNITS, CODED, UNIT), I16),
        compiler_params=SOME,
        cost_estimate=COST,
        name="add_on",
    )(rank, own, got, *after)


def page_kernel(requests, rank, slot, own_ref, *refs):
    count = len(requests)
    got_refs, sent_refs, refs = refs[:count], refs[count : 2 * count], refs[2 * count :]
    side_refs, (gain_ref, cos_ref, sin_ref), out_refs = refs[:2], refs[2:5], refs[-2:]
    step = pl.program_id(0)

    def write(u, comp):
        rows = key_rows(comp, gain_ref[...], cos_ref[u], sin_ref[u]).astype(BF)
        for n, ref in enumerate(out_refs):
            part = rows[n * PART : (n + 1) * PART]
            ref[0, :, u * UNIT : (u + 1) * UNIT] = part

    for k in range(count):

        @pl.when((step == k) & outer_rank(rank[0]))
        def _(k=k):
            for u in range(UNITS):
                write(u, own_ref[u] + decode(got_refs[k][u]))

        @pl.when((step == k) & ~outer_rank(rank[0]))
        def _(k=k):
            for u in range(UNITS):
                side = side_refs[u > 0][max(u - 1, 0)]
                write(u, decode(sent_refs[k][u]) + decode(side))


def pages_of(requests, rank, slot, own, got, sent, side, gain, cosine, sine, base, count, after):
    first = pl.BlockSpec((None, UNITS, CODED, UNIT), lambda i, *_: (0, 0, 0, 0))
    second = pl.BlockSpec((None, UNITS, CODED, UNIT), lambda i, *_: (1, 0, 0, 0))
    table = pl.BlockSpec((UNITS, HALF, UNIT), lambda i, *_: (0, 0, 0))
    start, total = requests[0], len(requests)
    got, sent = got[start : start + total], sent[start : start + total]
    return pl.pallas_call(
        functools.partial(page_kernel, requests),
        grid_spec=pltpu.PrefetchScalarGridSpec(
            num_scalar_prefetch=2,
            grid=(total,),
            in_specs=[
                pl.BlockSpec(
                    (UNITS, None, None, WIDTH, UNIT), lambda i, *_: (0, 0, i + start, 0, 0)
                ),
                *([first] * total),
                *([second] * total),
                pl.BlockSpec((1, None, CODED, UNIT), lambda i, *_: (0, i + start, 0, 0)),
                pl.BlockSpec((UNITS - 1, None, CODED, UNIT), lambda i, *_: (0, i + start, 0, 0)),
                pl.BlockSpec((KVL, UNIT), lambda i, *_: (0, 0)),
                table,
                table,
                *([ANY] * (len(base) + len(after))),
            ],
            out_specs=[
                pl.BlockSpec((1, PART, SHARE), lambda i, rank, slot: (slot[i + start], 0, 0))
            ]
            * 2,
        ),
        out_shape=[jax.ShapeDtypeStruct((count, PART, SHARE), BF)] * 2,
        input_output_aliases={8 + 2 * total + n: n for n in range(len(base))},
        compiler_params=ROOM,
        cost_estimate=COST,
        name="pages",
    )(rank, slot, own, *got, *sent, *side, gain, cosine, sine, *base, *after)


def query_kernel(lat_ref, up_ref, draft_ref, down_ref, *refs):
    *key_refs, cos_ref, sin_ref, out_ref, split_ref = refs

    @pl.when(pl.program_id(0) == 0)
    def _():
        rest = lax.dot_general(draft_ref[...], down_ref[...], NT, preferred_element_type=F32)
        for n in range(3):
            term = rest.astype(BF).astype(F32)
            split_ref[n] = term
            rest = rest - term
        split_ref[3] = jnp.zeros_like(rest)

    full = jnp.dot(lat_ref[...], up_ref[...], preferred_element_type=F32)
    for h, key_ref in enumerate(key_refs):
        base = h * (DN + DR)
        nope = full[:, base : base + DN].astype(BF)
        first = full[:, base + DN : base + DN + HALF]
        second = full[:, base + DN + HALF : base + DN + DR]
        absorbed = lax.dot_general(nope, key_ref[...], NT, preferred_element_type=F32)
        cosine, sine = cos_ref[...], sin_ref[...]
        out_ref[h] = jnp.concatenate(
            [absorbed, first * cosine - second * sine, first * sine + second * cosine], 1
        )


def queries(latents, q_up, kv_up, draft, down_t, cosine, sine, after):
    rows = latents.shape[0]
    heads = q_up.shape[1] // (DN + DR)
    step = 4
    key_spec = [
        pl.BlockSpec((KVL, DN), lambda i, h=h: (0, 2 * (step * i + h))) for h in range(step)
    ]
    whole = lambda i: (0, 0)
    table = pl.BlockSpec((rows, HALF), whole)
    body = lambda *refs: query_kernel(*refs[:-3], *refs[-2:])
    return pl.pallas_call(
        body,
        grid=(heads // step,),
        in_specs=[
            pl.BlockSpec((rows, QL), whole),
            pl.BlockSpec((QL, step * (DN + DR)), lambda i: (0, i)),
            pl.BlockSpec(draft.shape, whole),
            pl.BlockSpec(down_t.shape, whole),
            *key_spec,
            table,
            table,
            ANY,
        ],
        out_specs=[
            pl.BlockSpec((step, rows, WIDTH), lambda i: (i, 0, 0)),
            pl.BlockSpec((4, rows, WIDTH), lambda i: (0, 0, 0)),
        ],
        out_shape=[
            jax.ShapeDtypeStruct((heads, rows, WIDTH), F32),
            jax.ShapeDtypeStruct((4, rows, WIDTH), F32),
        ],
        compiler_params=ROOM,
        cost_estimate=COST,
        name="queries",
    )(latents, q_up, draft, down_t, *([kv_up] * step), cosine, sine, after)


def attend_kernel(requests, rank, q_ref, draft_ref, *refs):
    count = len(requests)
    own_ref, got_refs, refs = refs[0], refs[1 : 1 + count], refs[1 + count :]
    column_ref, cos_ref, sin_ref, midcos_ref, midsin_ref, refs = *refs[:5], refs[5:]
    valid_ref, gain_ref, newcos_ref, newsin_ref, refs = *refs[:4], refs[4:]
    out_refs, keys_ref = refs[-5:-1], refs[-1]
    step = pl.program_id(0)
    request = step + requests[0]

    @pl.when(rank[0] == 3)
    def _():
        for k in range(count):

            @pl.when(step == k)
            def _(k=k):
                for i, (cosine, sine) in enumerate(
                    ((cos_ref, sin_ref), (midcos_ref, midsin_ref))
                ):
                    for u in range(UNITS):
                        comp = own_ref[u, i] + decode(got_refs[k][i, u])
                        rows = key_rows(comp, column_ref[...], cosine[u], sine[u])
                        start = (1 - i) * SHARE + u * UNIT
                        keys_ref[:, start : start + UNIT] = rows.astype(BF)

        scale = (DN + DR) ** (-0.5)
        local_rows = out_refs[0].shape[1]
        new = 2 * RP
        comp = 0.0
        for t in range(4):
            terms = draft_ref[t].astype(F32)
            comp = comp + (terms[0:new] + terms[new : 2 * new] + terms[2 * new : 3 * new])
        lat = comp[:, :KVL]
        norm = lax.rsqrt(jnp.mean(lat * lat, axis=-1, keepdims=True) + 1e-06)
        first = comp[:, KVL : KVL + HALF]
        second = comp[:, KVL + HALF :]
        cosine, sine = newcos_ref[...], newsin_ref[...]
        drafts = jnp.concatenate(
            [
                lat * norm * gain_ref[...],
                first * cosine - second * sine,
                first * sine + second * cosine,
            ],
            1,
        )
        drafts = jnp.concatenate([drafts, jnp.zeros((UNIT - new, WIDTH), F32)], 0).astype(BF)
        query = jnp.concatenate([q_ref[t] for t in range(4)], 0)
        scores = jnp.dot(query, keys_ref[...], preferred_element_type=F32) * scale
        scores = jnp.where(valid_ref[0] > 0.0, scores, -1e30)
        fresh = lax.dot_general(query, drafts, NT, preferred_element_type=F32) * scale
        row = lax.broadcasted_iota(jnp.int32, fresh.shape, 0)
        late = (row % local_rows) // (local_rows // 2)
        offset = lax.broadcasted_iota(jnp.int32, fresh.shape, 1) - 2 * request
        fresh = jnp.where((offset >= 0) & (offset <= late), fresh, -1e30)
        top = jnp.maximum(
            jnp.max(scores, axis=1, keepdims=True), jnp.max(fresh, axis=1, keepdims=True)
        )
        weights = jnp.exp(scores - top)
        fresh = jnp.exp(fresh - top)
        total = jnp.sum(weights, axis=1, keepdims=True) + jnp.sum(fresh, axis=1, keepdims=True)
        numer = lax.dot_general(
            weights.astype(BF), keys_ref[0:KVL, :], NT, preferred_element_type=F32
        )
        numer = numer + jnp.dot(fresh.astype(BF), drafts[:, :KVL], preferred_element_type=F32)
        result = (numer / total).astype(BF)
        for t, ref in enumerate(out_refs):
            ref[0] = result[t * local_rows : (t + 1) * local_rows]


def attend(requests, rank, messages, own, got, column, tables, valid, gain, cosine, sine, after):
    new = 2 * RP
    local_rows = (messages.shape[1] - 4 * new) // RP
    last = RP * local_rows // (4 * new)
    start, count = requests[0], len(requests)
    got = got[start : start + count]
    out = jax.ShapeDtypeStruct((count, local_rows, KVL), BF)
    whole = lambda i, rank: (0, 0)
    whole3 = lambda i, rank: (0, 0, 0)
    return pl.pallas_call(
        functools.partial(attend_kernel, requests),
        grid_spec=pltpu.PrefetchScalarGridSpec(
            num_scalar_prefetch=1,
            grid=(count,),
            in_specs=[
                pl.BlockSpec((4, local_rows, WIDTH), lambda i, rank: (0, i + start, 0)),
                pl.BlockSpec((4, 4 * new, WIDTH), lambda i, rank: (0, last, 0)),
                pl.BlockSpec(
                    (UNITS, 2, None, WIDTH, UNIT), lambda i, rank: (0, 0, i + start, 0, 0)
                ),
                *([pl.BlockSpec((2, UNITS, CODED, UNIT), lambda i, rank: (0, 0, 0, 0))] * count),
                pl.BlockSpec((KVL, UNIT), whole),
                *([pl.BlockSpec((UNITS, HALF, UNIT), whole3)] * 4),
                pl.BlockSpec((1, 1, valid.shape[2]), lambda i, rank: (i + start, 0, 0)),
                pl.BlockSpec((1, KVL), whole),
                pl.BlockSpec(cosine.shape, whole),
                pl.BlockSpec(sine.shape, whole),
                *([ANY] * len(after)),
            ],
            out_specs=[pl.BlockSpec((1, local_rows, KVL), lambda i, rank: (i, 0, 0))] * 4,
            scratch_shapes=[pltpu.VMEM((WIDTH, 2 * SHARE), BF)],
        ),
        out_shape=[out] * 4,
        compiler_params=ROOM,
        cost_estimate=COST,
        name="attend",
    )(rank, messages, messages, own, *got, column, *tables, valid, gain, cosine, sine, *after)


def heads_kernel(step, o_ref, keep_ref, *refs):
    out_ref = refs[-1]
    for h, value_ref in enumerate(refs[:step]):
        row = jnp.dot(o_ref[h].astype(BF), value_ref[...], preferred_element_type=F32)
        out_ref[:, h * DV : (h + 1) * DV] = row * keep_ref[...]


def heads_out(attended, keep, kv_up, after):
    heads, rows, _ = attended.shape
    step = 8
    value_spec = [
        pl.BlockSpec((KVL, DV), lambda i, h=h: (0, 2 * (step * i + h) + 1)) for h in range(step)
    ]
    return pl.pallas_call(
        functools.partial(heads_kernel, step),
        grid=(heads // step,),
        in_specs=[
            pl.BlockSpec((step, rows, KVL), lambda i: (i, 0, 0)),
            pl.BlockSpec((rows, DV), lambda i: (0, 0)),
            *value_spec,
            *([ANY] * len(after)),
        ],
        out_specs=pl.BlockSpec((rows, step * DV), lambda i: (0, i)),
        out_shape=jax.ShapeDtypeStruct((rows, heads * DV), F32),
        compiler_params=ROOM,
        cost_estimate=COST,
        name="heads_out",
    )(attended, keep, *([kv_up] * step), *after)


def route_kernel(slot, answer_ref, *refs):
    out_ref = refs[-1]
    out_ref[...] = jnp.zeros_like(out_ref)
    for r in range(RP):
        out_ref[slot[r]] = answer_ref[2 * r : 2 * r + 2, :]


def route(slot, answer, count, after):
    width = answer.shape[1]
    return pl.pallas_call(
        route_kernel,
        in_specs=[SMEM, VMEM, *([ANY] * len(after))],
        out_specs=VMEM,
        out_shape=jax.ShapeDtypeStruct((count, 2, width), F32),
        compiler_params=SOME,
        cost_estimate=COST,
        name="route",
    )(slot, answer, *after)


def rope_tables(position):
    freq = jnp.exp(-jnp.log(10000.0) * jnp.arange(HALF, dtype=F32) / HALF)
    angle = position.astype(F32)[..., None] * freq
    return jnp.cos(angle), jnp.sin(angle)


def local_line(
    prefill_hidden,
    draft_hidden,
    kv_down,
    kv_gain,
    query_latent,
    q_up,
    kv_up,
    owners,
    segment_ids,
    accepted,
):
    pd_count = lax.axis_size("pd")
    z = lax.axis_index("tp")
    p = lax.axis_index("pd")
    first_req = p * RP

    rank = z.astype(jnp.int32).reshape(1)
    hidden = prefill_hidden.reshape(RP, PRE_TOK, prefill_hidden.shape[1])
    down_t = kv_down.T
    inward, across, outward = [(0, 1), (3, 2)], [(1, 2), (2, 1)], [(2, 3), (1, 0)]

    far_sums, inner, crossed, sent, outer = [], [], [], [], []

    def send_far(r, after):
        total, codes = project_far(rank, hidden, down_t, r, after)
        far_sums.append(total)
        inner.append(lax.ppermute(codes, "tp", inward))

    def first_hop(r, after):
        block = add_on(rank, far_sums[r], inner[r], after=after)
        crossed.append(lax.ppermute(block, "tp", across))
        return block

    def second_hop(r, after):
        block = add_on(rank, near_sums, crossed[r], r, after)
        sent.append(block)
        outer.append(lax.ppermute(block, "tp", outward))
        return block

    send_far(0, [])
    send_far(1, far_sums[:1])

    latents = lax.dynamic_slice_in_dim(query_latent, first_req, RP, 0).reshape(RP * 2, QL)
    new_pos = jnp.tile(PRE_TOK + jnp.arange(2, dtype=jnp.int32), RP)
    new_cos, new_sin = rope_tables(new_pos)
    query, terms = queries(
        latents, q_up, kv_up, draft_hidden, down_t, new_cos, new_sin, far_sums[1]
    )
    heads = query.shape[0]
    query = query.reshape(heads, RP, 2, WIDTH).transpose(1, 2, 0, 3)
    message = jnp.concatenate(
        [query.reshape(RP * 2 * heads, WIDTH), terms.reshape(8 * RP, WIDTH)], 0
    ).astype(BF)
    messages = lax.all_gather(message, "tp", axis=0)

    block = first_hop(0, [message])
    send_far(2, [block])
    near_sums, *side = project_near(rank, hidden, down_t, far_sums[2:])
    block = first_hop(1, [near_sums])
    block = second_hop(0, [block])
    send_far(3, [block])
    block = first_hop(2, far_sums[3:])
    block = second_hop(1, [block, messages, outer[0]])

    my_segments = lax.dynamic_slice_in_dim(segment_ids, first_req, RP, 0)
    valid = (my_segments == my_segments[:, -1:])[:, PRE_TOK // 2 :].astype(F32)
    valid = valid.reshape(RP, 1, PRE_TOK // 2)
    column = jnp.broadcast_to(kv_gain[:, None], (KVL, UNIT))
    steps = jnp.arange(SHARE, dtype=jnp.int32).reshape(UNITS, UNIT)
    tables = [
        jnp.swapaxes(t, 1, 2)
        for t in (*rope_tables(z * SHARE + steps), *rope_tables(2 * SHARE + steps))
    ]

    block = first_hop(3, [block, column, valid, *tables])
    side = [lax.ppermute(codes, "tp", inward) for codes in side]
    second_hop(2, [block, outer[1]])
    block = second_hop(3, [side[0], outer[2]])

    def attend_to(requests, after):
        result = attend(
            requests,
            rank,
            messages,
            near_sums,
            outer,
            column,
            tables,
            valid,
            kv_gain.reshape(1, KVL),
            new_cos,
            new_sin,
            after,
        )
        return result, [lax.ppermute(result[t], "tp", [(3, t)]) for t in range(3)]

    my_owners = lax.dynamic_slice_in_dim(owners, first_req, RP, 0)
    early, late = tuple(range(RP - 1)), (RP - 1,)

    def pages_to(requests, base, after):
        return pages_of(
            requests,
            rank,
            my_owners,
            near_sums,
            outer,
            sent,
            side,
            column,
            tables[0],
            tables[1],
            base,
            pd_count,
            after,
        )

    results, backs = [None] * 2, [None] * 2
    results[0], backs[0] = attend_to(early, [block])
    base = [jnp.zeros((pd_count, PART, SHARE), BF)] * 2 if pd_count > RP else []
    pages = pages_to(early, base, results[0][:1])
    results[1], backs[1] = attend_to(late, pages[:1])
    pages = pages_to(late, pages, [*results[1][:1], *backs[0]])
    cache = [lax.all_to_all(page, "pd", split_axis=0, concat_axis=0, tiled=True) for page in pages]

    attended = [
        jnp.where(z == 3, result[3], back[0] + back[1] + back[2])
        for result, back in zip(results, backs)
    ]
    attended = jnp.concatenate(attended, 0).reshape(RP, 2, heads, KVL).transpose(2, 0, 1, 3)
    attended = attended.reshape(heads, RP * 2, KVL).astype(F32)
    my_accepted = lax.dynamic_slice_in_dim(accepted, first_req, RP, 0)
    keep = (jnp.arange(2)[None, :] <= my_accepted[:, None]).astype(F32).reshape(RP * 2, 1)
    answer = heads_out(attended, jnp.broadcast_to(keep, (RP * 2, DV)), kv_up, pages[:1])
    placed = route(my_owners, answer, pd_count, cache[:1]).astype(BF)
    placed = lax.all_to_all(placed, "pd", split_axis=0, concat_axis=0, tiled=True)
    cache = jnp.swapaxes(jnp.concatenate(cache, 1), 1, 2)
    return (placed.reshape(pd_count * 2, heads * DV), cache)


def solution(mesh):
    placed = (
        P(("groups", "pd"), "tp"),
        P(("groups", "pd"), "tp"),
        P("tp", None),
        P(),
        P("groups", None, None),
        P(None, "tp"),
        P(None, "tp"),
        P("groups"),
        P("groups", None),
        P("groups"),
    )
    return jax.shard_map(
        local_line if mesh.shape["tp"] == 4 else local_general,
        mesh=mesh,
        in_specs=placed,
        out_specs=(P(("groups", "pd"), "tp"), P(("groups", "pd"), "tp", None)),
        check_vma=False,
    )
```

```python
import functools

import jax
import jax.numpy as jnp
from jax import lax
from jax.experimental import pallas as pl
from jax.experimental.pallas import tpu as pltpu
from jax.sharding import PartitionSpec as P

DN = 128
DR = 64
DV = 128
KVL = 512
QL = 1536
PRE_TOK = 1536
RP = 4
WIDTH = KVL + DR
HALF = DR // 2
PART = WIDTH // 2
CODED = WIDTH + 16
SHARE = PRE_TOK // 4
UNIT = 128
UNITS = SHARE // UNIT
LANES = RP * UNIT
STEPS = 256.0
TOP = 32767.0
BF = jnp.bfloat16
F32 = jnp.float32
I16 = jnp.int16
NT = (((1,), (1,)), ((), ()))
ROOM = pltpu.CompilerParams(vmem_limit_bytes=60 << 20)
SOME = pltpu.CompilerParams(vmem_limit_bytes=60 << 20)
ANY = pl.BlockSpec(memory_space=pl.ANY)
VMEM = pl.BlockSpec(memory_space=pltpu.VMEM)
SMEM = pl.BlockSpec(memory_space=pltpu.SMEM)


COST = pl.CostEstimate(flops=1024, bytes_accessed=1024, transcendentals=0)


def rms_latent(comp, gain):
    lat = comp[:, :KVL]
    scale = lax.rsqrt(jnp.mean(lat * lat, axis=-1, keepdims=True) + 1e-06)
    return (lat * scale * gain).astype(jnp.bfloat16)


def rotate(values, position):
    half = values.shape[-1] // 2
    freq = jnp.exp(-jnp.log(10000.0) * jnp.arange(half, dtype=jnp.float32) / half)
    angle = position.astype(jnp.float32)[..., None] * freq
    cosine = jnp.cos(angle)
    sine = jnp.sin(angle)
    first = values[..., :half]
    second = values[..., half:]
    return jnp.concatenate([first * cosine - second * sine, first * sine + second * cosine], -1)


def block_stats(keys, q_lat, q_pos, valid):
    scale = (DN + DR) ** (-0.5)
    scores = jnp.einsum("jhk,tk->jht", q_lat, keys[:, :KVL], preferred_element_type=jnp.float32)
    scores = (
        scores + jnp.einsum("jhk,tk->jht", q_pos, keys[:, KVL:], preferred_element_type=jnp.float32)
    ) * scale
    scores = jnp.where(valid, scores, -1e30)
    top = jnp.max(scores, axis=-1)
    weights = jnp.where(valid, jnp.exp(scores - top[..., None]), 0.0)
    total = jnp.sum(weights, axis=-1)
    numer = jnp.einsum(
        "jht,tk->jhk",
        weights.astype(jnp.bfloat16),
        keys[:, :KVL],
        preferred_element_type=jnp.float32,
    )
    return (top, total, numer)


def combine(left, right):
    top = jnp.maximum(left[0], right[0])
    left_scale = jnp.exp(left[0] - top)
    right_scale = jnp.exp(right[0] - top)
    total = left[1] * left_scale + right[1] * right_scale
    numer = left[2] * left_scale[..., None] + right[2] * right_scale[..., None]
    return (top, total, numer)


def local_general(
    prefill_hidden,
    draft_hidden,
    kv_down,
    kv_gain,
    query_latent,
    q_up,
    kv_up,
    owners,
    segment_ids,
    accepted,
):
    tp_count = lax.axis_size("tp")
    pd_count = lax.axis_size("pd")
    tp_rank = lax.axis_index("tp")
    mine_rank = lax.axis_index("pd")
    requests = owners.shape[0]
    share = PRE_TOK // tp_count
    width = KVL + DR
    local_hidden = prefill_hidden.reshape(RP, PRE_TOK, prefill_hidden.shape[1])
    summed = lax.psum_scatter(
        jnp.einsum(
            "rtd,dw->trw", local_hidden, kv_down, preferred_element_type=jnp.float32
        ).reshape(lax.axis_size("tp") * share, RP * width),
        "tp",
        scatter_dimension=0,
        tiled=True,
    ).reshape(share * RP, width)
    draft_sum = lax.psum(jnp.dot(draft_hidden, kv_down, preferred_element_type=jnp.float32), "tp")
    first_req = mine_rank * RP
    row_pos = jnp.broadcast_to(
        tp_rank * share + jnp.arange(share, dtype=jnp.int32)[:, None], (share, RP)
    )
    page_rows = jnp.concatenate(
        [
            rms_latent(summed, kv_gain),
            rotate(summed[:, KVL:], row_pos.reshape(-1)).astype(jnp.bfloat16),
        ],
        1,
    )
    page_rows = page_rows.reshape(share, RP, width)
    draft_pos = jnp.tile(PRE_TOK + jnp.arange(2, dtype=jnp.int32), RP)
    draft_rows = jnp.concatenate(
        [
            rms_latent(draft_sum, kv_gain),
            rotate(draft_sum[:, KVL:], draft_pos).astype(jnp.bfloat16),
        ],
        1,
    )
    draft_rows = draft_rows.reshape(RP, 2, width)
    my_owners = lax.dynamic_slice_in_dim(owners, first_req, RP, 0)
    routing = (my_owners[None, :] == jnp.arange(pd_count, dtype=jnp.int32)[:, None]).astype(
        jnp.bfloat16
    )
    send_pages = jnp.einsum(
        "dk,tkw->dtw", routing, page_rows, preferred_element_type=jnp.float32
    ).astype(jnp.bfloat16)
    send_drafts = jnp.einsum(
        "dk,kjw->djw", routing, draft_rows, preferred_element_type=jnp.float32
    ).astype(jnp.bfloat16)
    pages, drafts = (
        lax.all_to_all(send_pages, "pd", split_axis=0, concat_axis=0, tiled=True),
        lax.all_to_all(send_drafts, "pd", split_axis=0, concat_axis=0, tiled=True),
    )
    heads_local = q_up.shape[1] // (DN + DR)
    query_full = jnp.dot(
        query_latent.reshape(requests * 2, QL), q_up, preferred_element_type=jnp.float32
    )
    query_full = query_full.reshape(requests, 2, heads_local, DN + DR)
    new_pos = jnp.broadcast_to(PRE_TOK + jnp.arange(2, dtype=jnp.int32)[None, :], (requests, 2))
    q_nope = query_full[..., :DN].astype(jnp.bfloat16)
    q_rot = rotate(query_full[..., DN:], new_pos[:, :, None]).astype(jnp.bfloat16)
    up_heads = kv_up.reshape(KVL, heads_local, DN + DV)
    w_value = up_heads[:, :, DN:]
    q_abs = jnp.einsum(
        "rjhd,khd->rjhk", q_nope, up_heads[:, :, :DN], preferred_element_type=jnp.float32
    ).astype(jnp.bfloat16)
    owner_table = owners.reshape(pd_count, RP) == mine_rank
    holding = jnp.sum(owner_table.astype(jnp.int32), axis=1)
    slot_of = jnp.sum(
        owner_table.astype(jnp.int32) * jnp.arange(RP, dtype=jnp.int32)[None, :], axis=1
    )
    owned_count = jnp.sum(holding)
    order = jnp.argsort((1 - holding) * pd_count + jnp.arange(pd_count, dtype=jnp.int32))
    draft_valid = (jnp.arange(2)[None, :] <= jnp.arange(2)[:, None])[:, None, :]
    empty = jnp.zeros((pd_count, 2, heads_local * DV), jnp.bfloat16)

    def finish(stats, source, request, q_lat, q_pos, result):
        stats = combine(stats, block_stats(drafts[source], q_lat, q_pos, draft_valid))
        attended = (stats[2] / stats[1][..., None]).astype(jnp.bfloat16)
        head_out = jnp.einsum("jhk,khd->jhd", attended, w_value, preferred_element_type=jnp.float32)
        keep = (jnp.arange(2) <= accepted[request]).astype(jnp.float32)[:, None, None]
        answer = (head_out * keep).astype(jnp.bfloat16).reshape(1, 2, heads_local * DV)
        return lax.dynamic_update_slice(result, answer, (source, 0, 0))

    def attend(turn, result):
        source = order[turn]
        request = source * RP + slot_of[source]
        q_lat = q_abs[request]
        q_pos = q_rot[request]
        seg_row = segment_ids[request]
        current = seg_row[PRE_TOK - 1]
        init = (
            jnp.full((2, heads_local), -1e30, jnp.float32),
            jnp.zeros((2, heads_local), jnp.float32),
            jnp.zeros((2, heads_local, KVL), jnp.float32),
        )
        valid = (seg_row == current)[None, None, :]
        stats = combine(
            init,
            block_stats(
                lax.all_gather(pages[source], "tp", axis=0, tiled=True), q_lat, q_pos, valid
            ),
        )
        return finish(stats, source, request, q_lat, q_pos, result)

    result = lax.fori_loop(0, owned_count, attend, empty)
    return (result.reshape(pd_count * 2, heads_local * DV), pages)


def encode(values):
    levels = []
    parts = []
    for first, last in ((0, KVL), (KVL, WIDTH)):
        block = values[first:last]
        top = jnp.maximum(jnp.max(jnp.abs(block), axis=0, keepdims=True), 1e-30)
        level = jnp.ceil(jnp.log2(top) * STEPS)
        codes = jnp.round(block * (jnp.exp2(level * (-1.0 / STEPS)) * TOP))
        parts.append(jnp.clip(codes, -TOP, TOP).astype(jnp.int32).astype(I16))
        levels.append(level.astype(jnp.int32))
    row = lax.broadcasted_iota(jnp.int32, (16, values.shape[1]), 0)
    extra = jnp.where(row == 0, levels[0], jnp.where(row == 1, levels[1], 0))
    return jnp.concatenate([*parts, extra.astype(I16)], 0)


def decode(codes):
    level = codes[WIDTH:CODED].astype(jnp.int32).astype(F32)
    step = jnp.exp2(level * (1.0 / STEPS)) * (1.0 / TOP)
    lat = codes[0:KVL].astype(jnp.int32).astype(F32) * step[0:1]
    rot = codes[KVL:WIDTH].astype(jnp.int32).astype(F32) * step[1:2]
    return jnp.concatenate([lat, rot], 0)


def key_rows(comp, gain, cosine, sine):
    lat = comp[:KVL]
    scale = lax.rsqrt(jnp.mean(lat * lat, axis=0, keepdims=True) + 1e-06)
    first = comp[KVL : KVL + HALF]
    second = comp[KVL + HALF :]
    return jnp.concatenate(
        [
            lat * scale * gain,
            first * cosine - second * sine,
            first * sine + second * cosine,
        ],
        0,
    )


def far(z, i):
    return jnp.where(z < 2, 3 - i, i)


def near(z, i):
    return jnp.where(z < 2, i, 3 - i)


def outer_rank(z):
    return (z == 0) | (z == 3)


def project_far_kernel(rank, hid_ref, down_ref, *refs):
    sum_ref, code_ref = refs[-2:]
    total = lax.dot_general(down_ref[...], hid_ref[0], NT, preferred_element_type=F32)
    for u in range(UNITS):
        sum_ref[0, u] = total[:, u * UNIT : (u + 1) * UNIT]

    @pl.when(outer_rank(rank[0]))
    def _():
        for u in range(UNITS):
            code_ref[0, u] = encode(total[:, u * UNIT : (u + 1) * UNIT])


def project_far(rank, hidden, down_t, request, after):
    depth = hidden.shape[-1]
    return pl.pallas_call(
        project_far_kernel,
        grid_spec=pltpu.PrefetchScalarGridSpec(
            num_scalar_prefetch=1,
            grid=(2,),
            in_specs=[
                pl.BlockSpec((1, SHARE, depth), lambda i, rank: (request, far(rank[0], i), 0)),
                VMEM,
                *([ANY] * len(after)),
            ],
            out_specs=[
                pl.BlockSpec((1, UNITS, WIDTH, UNIT), lambda i, rank: (i, 0, 0, 0)),
                pl.BlockSpec((1, UNITS, CODED, UNIT), lambda i, rank: (i, 0, 0, 0)),
            ],
        ),
        out_shape=[
            jax.ShapeDtypeStruct((2, UNITS, WIDTH, UNIT), F32),
            jax.ShapeDtypeStruct((2, UNITS, CODED, UNIT), I16),
        ],
        compiler_params=ROOM,
        cost_estimate=COST,
        name="project_far",
    )(rank, hidden, down_t, *after)


def project_near_kernel(rank, hid_ref, down_ref, *refs):
    sum_ref, *code_refs = refs[-3:]
    unit = pl.program_id(0)
    rows = hid_ref[...].reshape(LANES, hid_ref.shape[-1])
    total = lax.dot_general(down_ref[...], rows, NT, preferred_element_type=F32)
    for r in range(RP):
        sum_ref[0, 0, r] = total[:, r * UNIT : (r + 1) * UNIT]
    coded = outer_rank(rank[0]) & (pl.program_id(1) == 1)
    for mine, ref in zip((unit == 0, unit > 0), code_refs):

        @pl.when(coded & mine)
        def _(ref=ref):
            for r in range(RP):
                ref[0, r] = encode(total[:, r * UNIT : (r + 1) * UNIT])


def project_near(rank, hidden, down_t, after):
    depth = hidden.shape[-1]
    return pl.pallas_call(
        project_near_kernel,
        grid_spec=pltpu.PrefetchScalarGridSpec(
            num_scalar_prefetch=1,
            grid=(UNITS, 2),
            in_specs=[
                pl.BlockSpec(
                    (RP, UNIT, depth), lambda u, i, rank: (0, near(rank[0], i) * UNITS + u, 0)
                ),
                VMEM,
                *([ANY] * len(after)),
            ],
            out_specs=[
                pl.BlockSpec((1, 1, RP, WIDTH, UNIT), lambda u, i, rank: (u, i, 0, 0, 0)),
                pl.BlockSpec((1, RP, CODED, UNIT), lambda u, i, rank: (0, 0, 0, 0)),
                pl.BlockSpec(
                    (1, RP, CODED, UNIT), lambda u, i, rank: (jnp.maximum(u, 1) - 1, 0, 0, 0)
                ),
            ],
        ),
        out_shape=[
            jax.ShapeDtypeStruct((UNITS, 2, RP, WIDTH, UNIT), F32),
            jax.ShapeDtypeStruct((1, RP, CODED, UNIT), I16),
            jax.ShapeDtypeStruct((UNITS - 1, RP, CODED, UNIT), I16),
        ],
        compiler_params=ROOM,
        cost_estimate=COST,
        name="project_near",
    )(rank, hidden, down_t, *after)


def add_kernel(rank, own_ref, got_ref, *refs):
    @pl.when(~outer_rank(rank[0]))
    def _():
        for u in range(UNITS):
            refs[-1][0, u] = encode(own_ref[u] + decode(got_ref[0, u]))


def add_on(rank, own, got, request=None, after=()):
    chunk = lambda i, rank: (i, 0, 0, 0)
    if request is None:
        own_spec = pl.BlockSpec((None, UNITS, WIDTH, UNIT), chunk)
    else:
        own_spec = pl.BlockSpec(
            (UNITS, None, None, WIDTH, UNIT), lambda i, rank: (0, i, request, 0, 0)
        )
    return pl.pallas_call(
        add_kernel,
        grid_spec=pltpu.PrefetchScalarGridSpec(
            num_scalar_prefetch=1,
            grid=(2,),
            in_specs=[
                own_spec,
                pl.BlockSpec((1, UNITS, CODED, UNIT), chunk),
                *([ANY] * len(after)),
            ],
            out_specs=pl.BlockSpec((1, UNITS, CODED, UNIT), chunk),
        ),
        out_shape=jax.ShapeDtypeStruct((2, UNITS, CODED, UNIT), I16),
        compiler_params=SOME,
        cost_estimate=COST,
        name="add_on",
    )(rank, own, got, *after)


def page_kernel(requests, halves, rank, slot, own_ref, *refs):
    count = len(requests)
    got_refs, sent_refs, refs = refs[:count], refs[count : 2 * count], refs[2 * count :]
    side_refs, (gain_ref, cos_ref, sin_ref) = refs[:2], refs[2:5]
    out_refs = refs[-len(halves) :]
    step = pl.program_id(0)

    def write(u, comp):
        rows = key_rows(comp, gain_ref[...], cos_ref[u], sin_ref[u]).astype(BF)
        for n, ref in zip(halves, out_refs):
            part = rows[n * PART : (n + 1) * PART]
            ref[0, :, u * UNIT : (u + 1) * UNIT] = part

    for k in range(count):

        @pl.when((step == k) & outer_rank(rank[0]))
        def _(k=k):
            for u in range(UNITS):
                write(u, own_ref[u] + decode(got_refs[k][u]))

        @pl.when((step == k) & ~outer_rank(rank[0]))
        def _(k=k):
            for u in range(UNITS):
                side = side_refs[u > 0][max(u - 1, 0)]
                write(u, decode(sent_refs[k][u]) + decode(side))


def pages_of(requests, halves, rank, slot, own, got, sent, side, gain, cosine, sine, base, count, after):
    first = pl.BlockSpec((None, UNITS, CODED, UNIT), lambda i, *_: (0, 0, 0, 0))
    second = pl.BlockSpec((None, UNITS, CODED, UNIT), lambda i, *_: (1, 0, 0, 0))
    table = pl.BlockSpec((UNITS, HALF, UNIT), lambda i, *_: (0, 0, 0))
    start, total = requests[0], len(requests)
    got, sent = got[start : start + total], sent[start : start + total]
    return pl.pallas_call(
        functools.partial(page_kernel, requests, halves),
        grid_spec=pltpu.PrefetchScalarGridSpec(
            num_scalar_prefetch=2,
            grid=(total,),
            in_specs=[
                pl.BlockSpec(
                    (UNITS, None, None, WIDTH, UNIT), lambda i, *_: (0, 0, i + start, 0, 0)
                ),
                *([first] * total),
                *([second] * total),
                pl.BlockSpec((1, None, CODED, UNIT), lambda i, *_: (0, i + start, 0, 0)),
                pl.BlockSpec((UNITS - 1, None, CODED, UNIT), lambda i, *_: (0, i + start, 0, 0)),
                pl.BlockSpec((KVL, UNIT), lambda i, *_: (0, 0)),
                table,
                table,
                *([ANY] * (len(base) + len(after))),
            ],
            out_specs=[
                pl.BlockSpec((1, PART, SHARE), lambda i, rank, slot: (slot[i + start], 0, 0))
            ]
            * len(halves),
        ),
        out_shape=[jax.ShapeDtypeStruct((count, PART, SHARE), BF)] * len(halves),
        input_output_aliases={8 + 2 * total + n: n for n in range(len(base))},
        compiler_params=ROOM,
        cost_estimate=COST,
        name="pages",
    )(rank, slot, own, *got, *sent, *side, gain, cosine, sine, *base, *after)


def query_kernel(lat_ref, up_ref, draft_ref, down_ref, *refs):
    *key_refs, cos_ref, sin_ref, out_ref, split_ref = refs

    @pl.when(pl.program_id(0) == 0)
    def _():
        rest = lax.dot_general(draft_ref[...], down_ref[...], NT, preferred_element_type=F32)
        for n in range(3):
            term = rest.astype(BF).astype(F32)
            split_ref[n] = term
            rest = rest - term
        split_ref[3] = jnp.zeros_like(rest)

    full = jnp.dot(lat_ref[...], up_ref[...], preferred_element_type=F32)
    for h, key_ref in enumerate(key_refs):
        base = h * (DN + DR)
        nope = full[:, base : base + DN].astype(BF)
        first = full[:, base + DN : base + DN + HALF]
        second = full[:, base + DN + HALF : base + DN + DR]
        absorbed = lax.dot_general(nope, key_ref[...], NT, preferred_element_type=F32)
        cosine, sine = cos_ref[...], sin_ref[...]
        out_ref[h] = jnp.concatenate(
            [absorbed, first * cosine - second * sine, first * sine + second * cosine], 1
        )


def queries(latents, q_up, kv_up, draft, down_t, cosine, sine, after):
    rows = latents.shape[0]
    heads = q_up.shape[1] // (DN + DR)
    step = 4
    key_spec = [
        pl.BlockSpec((KVL, DN), lambda i, h=h: (0, 2 * (step * i + h))) for h in range(step)
    ]
    whole = lambda i: (0, 0)
    table = pl.BlockSpec((rows, HALF), whole)
    body = lambda *refs: query_kernel(*refs[:-3], *refs[-2:])
    return pl.pallas_call(
        body,
        grid=(heads // step,),
        in_specs=[
            pl.BlockSpec((rows, QL), whole),
            pl.BlockSpec((QL, step * (DN + DR)), lambda i: (0, i)),
            pl.BlockSpec(draft.shape, whole),
            pl.BlockSpec(down_t.shape, whole),
            *key_spec,
            table,
            table,
            ANY,
        ],
        out_specs=[
            pl.BlockSpec((step, rows, WIDTH), lambda i: (i, 0, 0)),
            pl.BlockSpec((4, rows, WIDTH), lambda i: (0, 0, 0)),
        ],
        out_shape=[
            jax.ShapeDtypeStruct((heads, rows, WIDTH), F32),
            jax.ShapeDtypeStruct((4, rows, WIDTH), F32),
        ],
        compiler_params=ROOM,
        cost_estimate=COST,
        name="queries",
    )(latents, q_up, draft, down_t, *([kv_up] * step), cosine, sine, after)


def attend_kernel(requests, rank, *refs):
    count = len(requests)
    q_refs, draft_refs, refs = refs[:4], refs[4:8], refs[8:]
    own_ref, got_refs, refs = refs[0], refs[1 : 1 + count], refs[1 + count :]
    column_ref, cos_ref, sin_ref, midcos_ref, midsin_ref, refs = *refs[:5], refs[5:]
    valid_ref, gain_ref, newcos_ref, newsin_ref, refs = *refs[:4], refs[4:]
    out_refs, keys_ref = refs[-5:-1], refs[-1]
    step = pl.program_id(0)
    request = step + requests[0]

    @pl.when(rank[0] == 3)
    def _():
        for k in range(count):

            @pl.when(step == k)
            def _(k=k):
                for i, (cosine, sine) in enumerate(
                    ((cos_ref, sin_ref), (midcos_ref, midsin_ref))
                ):
                    for u in range(UNITS):
                        comp = own_ref[u, i] + decode(got_refs[k][i, u])
                        rows = key_rows(comp, column_ref[...], cosine[u], sine[u])
                        start = (1 - i) * SHARE + u * UNIT
                        keys_ref[:, start : start + UNIT] = rows.astype(BF)

        scale = (DN + DR) ** (-0.5)
        local_rows = out_refs[0].shape[1]
        new = 2 * RP
        comp = 0.0
        for ref in draft_refs:
            terms = ref[...].astype(F32)
            comp = comp + (terms[0:new] + terms[new : 2 * new] + terms[2 * new : 3 * new])
        lat = comp[:, :KVL]
        norm = lax.rsqrt(jnp.mean(lat * lat, axis=-1, keepdims=True) + 1e-06)
        first = comp[:, KVL : KVL + HALF]
        second = comp[:, KVL + HALF :]
        cosine, sine = newcos_ref[...], newsin_ref[...]
        drafts = jnp.concatenate(
            [
                lat * norm * gain_ref[...],
                first * cosine - second * sine,
                first * sine + second * cosine,
            ],
            1,
        )
        drafts = jnp.concatenate([drafts, jnp.zeros((UNIT - new, WIDTH), F32)], 0).astype(BF)
        query = jnp.concatenate([ref[...] for ref in q_refs], 0)
        scores = jnp.dot(query, keys_ref[...], preferred_element_type=F32) * scale
        scores = jnp.where(valid_ref[0] > 0.0, scores, -1e30)
        fresh = lax.dot_general(query, drafts, NT, preferred_element_type=F32) * scale
        row = lax.broadcasted_iota(jnp.int32, fresh.shape, 0)
        late = (row % local_rows) // (local_rows // 2)
        offset = lax.broadcasted_iota(jnp.int32, fresh.shape, 1) - 2 * request
        fresh = jnp.where((offset >= 0) & (offset <= late), fresh, -1e30)
        top = jnp.maximum(
            jnp.max(scores, axis=1, keepdims=True), jnp.max(fresh, axis=1, keepdims=True)
        )
        weights = jnp.exp(scores - top)
        fresh = jnp.exp(fresh - top)
        total = jnp.sum(weights, axis=1, keepdims=True) + jnp.sum(fresh, axis=1, keepdims=True)
        numer = lax.dot_general(
            weights.astype(BF), keys_ref[0:KVL, :], NT, preferred_element_type=F32
        )
        numer = numer + jnp.dot(fresh.astype(BF), drafts[:, :KVL], preferred_element_type=F32)
        result = (numer / total).astype(BF)
        for t, ref in enumerate(out_refs):
            ref[0] = result[t * local_rows : (t + 1) * local_rows]


def attend(requests, rank, messages, own, got, column, tables, valid, gain, cosine, sine, after):
    new = 2 * RP
    local_rows = (messages[0].shape[0] - 4 * new) // RP
    last = RP * local_rows // (4 * new)
    start, count = requests[0], len(requests)
    got = got[start : start + count]
    out = jax.ShapeDtypeStruct((count, local_rows, KVL), BF)
    whole = lambda i, rank: (0, 0)
    whole3 = lambda i, rank: (0, 0, 0)
    return pl.pallas_call(
        functools.partial(attend_kernel, requests),
        grid_spec=pltpu.PrefetchScalarGridSpec(
            num_scalar_prefetch=1,
            grid=(count,),
            in_specs=[
                *([pl.BlockSpec((local_rows, WIDTH), lambda i, rank: (i + start, 0))] * 4),
                *([pl.BlockSpec((4 * new, WIDTH), lambda i, rank: (last, 0))] * 4),
                pl.BlockSpec(
                    (UNITS, 2, None, WIDTH, UNIT), lambda i, rank: (0, 0, i + start, 0, 0)
                ),
                *([pl.BlockSpec((2, UNITS, CODED, UNIT), lambda i, rank: (0, 0, 0, 0))] * count),
                pl.BlockSpec((KVL, UNIT), whole),
                *([pl.BlockSpec((UNITS, HALF, UNIT), whole3)] * 4),
                pl.BlockSpec((1, 1, valid.shape[2]), lambda i, rank: (i + start, 0, 0)),
                pl.BlockSpec((1, KVL), whole),
                pl.BlockSpec(cosine.shape, whole),
                pl.BlockSpec(sine.shape, whole),
                *([ANY] * len(after)),
            ],
            out_specs=[pl.BlockSpec((1, local_rows, KVL), lambda i, rank: (i, 0, 0))] * 4,
            scratch_shapes=[pltpu.VMEM((WIDTH, 2 * SHARE), BF)],
        ),
        out_shape=[out] * 4,
        compiler_params=ROOM,
        cost_estimate=COST,
        name="attend",
    )(rank, *messages, *messages, own, *got, column, *tables, valid, gain, cosine, sine, *after)


def heads_kernel(step, o_ref, keep_ref, *refs):
    out_ref = refs[-1]
    for h, value_ref in enumerate(refs[:step]):
        row = jnp.dot(o_ref[h].astype(BF), value_ref[...], preferred_element_type=F32)
        out_ref[:, h * DV : (h + 1) * DV] = row * keep_ref[...]


def heads_out(attended, keep, kv_up, after):
    heads, rows, _ = attended.shape
    step = 8
    value_spec = [
        pl.BlockSpec((KVL, DV), lambda i, h=h: (0, 2 * (step * i + h) + 1)) for h in range(step)
    ]
    return pl.pallas_call(
        functools.partial(heads_kernel, step),
        grid=(heads // step,),
        in_specs=[
            pl.BlockSpec((step, rows, KVL), lambda i: (i, 0, 0)),
            pl.BlockSpec((rows, DV), lambda i: (0, 0)),
            *value_spec,
            *([ANY] * len(after)),
        ],
        out_specs=pl.BlockSpec((rows, step * DV), lambda i: (0, i)),
        out_shape=jax.ShapeDtypeStruct((rows, heads * DV), F32),
        compiler_params=ROOM,
        cost_estimate=COST,
        name="heads_out",
    )(attended, keep, *([kv_up] * step), *after)


def route_kernel(slot, answer_ref, *refs):
    out_ref = refs[-1]
    out_ref[...] = jnp.zeros_like(out_ref)
    for r in range(RP):
        out_ref[slot[r]] = answer_ref[2 * r : 2 * r + 2, :]


def route(slot, answer, count, after):
    width = answer.shape[1]
    return pl.pallas_call(
        route_kernel,
        in_specs=[SMEM, VMEM, *([ANY] * len(after))],
        out_specs=VMEM,
        out_shape=jax.ShapeDtypeStruct((count, 2, width), F32),
        compiler_params=SOME,
        cost_estimate=COST,
        name="route",
    )(slot, answer, *after)


def rope_tables(position):
    freq = jnp.exp(-jnp.log(10000.0) * jnp.arange(HALF, dtype=F32) / HALF)
    angle = position.astype(F32)[..., None] * freq
    return jnp.cos(angle), jnp.sin(angle)


def local_line(
    prefill_hidden,
    draft_hidden,
    kv_down,
    kv_gain,
    query_latent,
    q_up,
    kv_up,
    owners,
    segment_ids,
    accepted,
):
    pd_count = lax.axis_size("pd")
    z = lax.axis_index("tp")
    p = lax.axis_index("pd")
    first_req = p * RP

    rank = z.astype(jnp.int32).reshape(1)
    hidden = prefill_hidden.reshape(RP, PRE_TOK, prefill_hidden.shape[1])
    down_t = kv_down.T
    inward, across, outward = [(0, 1), (3, 2)], [(1, 2), (2, 1)], [(2, 3), (1, 0)]

    far_sums, inner, crossed, sent, outer = [], [], [], [], []

    def send_far(r, after):
        total, codes = project_far(rank, hidden, down_t, r, after)
        far_sums.append(total)
        inner.append(lax.ppermute(codes, "tp", inward))

    def first_hop(r, after):
        block = add_on(rank, far_sums[r], inner[r], after=after)
        crossed.append(lax.ppermute(block, "tp", across))
        return block

    def second_hop(r, after):
        block = add_on(rank, near_sums, crossed[r], r, after)
        sent.append(block)
        outer.append(lax.ppermute(block, "tp", outward))
        return block

    send_far(0, [])
    send_far(1, far_sums[:1])

    latents = lax.dynamic_slice_in_dim(query_latent, first_req, RP, 0).reshape(RP * 2, QL)
    new_pos = jnp.tile(PRE_TOK + jnp.arange(2, dtype=jnp.int32), RP)
    new_cos, new_sin = rope_tables(new_pos)
    query, terms = queries(
        latents, q_up, kv_up, draft_hidden, down_t, new_cos, new_sin, far_sums[1]
    )
    heads = query.shape[0]
    query = query.reshape(heads, RP, 2, WIDTH).transpose(1, 2, 0, 3)
    message = jnp.concatenate(
        [query.reshape(RP * 2 * heads, WIDTH), terms.reshape(8 * RP, WIDTH)], 0
    ).astype(BF)
    messages = [lax.ppermute(message, "tp", [(t, 3)]) for t in range(3)] + [message]

    block = first_hop(0, [message])
    send_far(2, [block])
    near_sums, *side = project_near(rank, hidden, down_t, far_sums[2:])
    block = first_hop(1, [near_sums, *messages[:3]])
    block = second_hop(0, [block])
    send_far(3, [block])
    block = first_hop(2, far_sums[3:])
    block = second_hop(1, [block, outer[0]])

    my_segments = lax.dynamic_slice_in_dim(segment_ids, first_req, RP, 0)
    valid = (my_segments == my_segments[:, -1:])[:, PRE_TOK // 2 :].astype(F32)
    valid = valid.reshape(RP, 1, PRE_TOK // 2)
    column = jnp.broadcast_to(kv_gain[:, None], (KVL, UNIT))
    steps = jnp.arange(SHARE, dtype=jnp.int32).reshape(UNITS, UNIT)
    tables = [
        jnp.swapaxes(t, 1, 2)
        for t in (*rope_tables(z * SHARE + steps), *rope_tables(2 * SHARE + steps))
    ]

    block = first_hop(3, [block, column, valid, *tables])
    side = [lax.ppermute(codes, "tp", inward) for codes in side]
    second_hop(2, [block, outer[1]])
    block = second_hop(3, [side[0], outer[2]])

    def attend_to(requests, after):
        result = attend(
            requests,
            rank,
            messages,
            near_sums,
            outer,
            column,
            tables,
            valid,
            kv_gain.reshape(1, KVL),
            new_cos,
            new_sin,
            after,
        )
        return result, [lax.ppermute(result[t], "tp", [(3, t)]) for t in range(3)]

    my_owners = lax.dynamic_slice_in_dim(owners, first_req, RP, 0)
    early, late = tuple(range(RP - 1)), (RP - 1,)

    def pages_to(requests, halves, base, after):
        return pages_of(
            requests,
            halves,
            rank,
            my_owners,
            near_sums,
            outer,
            sent,
            side,
            column,
            tables[0],
            tables[1],
            base,
            pd_count,
            after,
        )

    results, backs = [None] * 2, [None] * 2
    results[0], backs[0] = attend_to(early, [block])
    base = [jnp.zeros((pd_count, PART, SHARE), BF)] * 2 if pd_count > RP else []
    pages = pages_to(early, (0, 1), base, results[0][:1])
    results[1], backs[1] = attend_to(late, pages[:1])
    first = pages_to(late, (0,), pages[:1], [*results[1][:1], *backs[0]])
    second = pages_to(late, (1,), pages[1:], [*first, *backs[1]])
    pages = [*first, *second]
    cache = [lax.all_to_all(page, "pd", split_axis=0, concat_axis=0, tiled=True) for page in pages]

    attended = [
        jnp.where(z == 3, result[3], back[0] + back[1] + back[2])
        for result, back in zip(results, backs)
    ]
    attended = jnp.concatenate(attended, 0).reshape(RP, 2, heads, KVL).transpose(2, 0, 1, 3)
    attended = attended.reshape(heads, RP * 2, KVL).astype(F32)
    my_accepted = lax.dynamic_slice_in_dim(accepted, first_req, RP, 0)
    keep = (jnp.arange(2)[None, :] <= my_accepted[:, None]).astype(F32).reshape(RP * 2, 1)
    answer = heads_out(attended, jnp.broadcast_to(keep, (RP * 2, DV)), kv_up, pages[1:])
    placed = route(my_owners, answer, pd_count, cache[:1]).astype(BF)
    placed = lax.all_to_all(placed, "pd", split_axis=0, concat_axis=0, tiled=True)
    cache = jnp.swapaxes(jnp.concatenate(cache, 1), 1, 2)
    return (placed.reshape(pd_count * 2, heads * DV), cache)


def solution(mesh):
    placed = (
        P(("groups", "pd"), "tp"),
        P(("groups", "pd"), "tp"),
        P("tp", None),
        P(),
        P("groups", None, None),
        P(None, "tp"),
        P(None, "tp"),
        P("groups"),
        P("groups", None),
        P("groups"),
    )
    return jax.shard_map(
        local_line if mesh.shape["tp"] == 4 else local_general,
        mesh=mesh,
        in_specs=placed,
        out_specs=(P(("groups", "pd"), "tp"), P(("groups", "pd"), "tp", None)),
        check_vma=False,
    )
```

```python
import functools

import jax
import jax.numpy as jnp
from jax import lax
from jax.experimental import pallas as pl
from jax.experimental.pallas import tpu as pltpu
from jax.sharding import PartitionSpec as P

DN = 128
DR = 64
DV = 128
KVL = 512
QL = 1536
PRE_TOK = 1536
RP = 4
WIDTH = KVL + DR
HALF = DR // 2
CODED = WIDTH + 16
SHARE = PRE_TOK // 4
UNIT = 128
UNITS = SHARE // UNIT
LANES = RP * UNIT
STEPS = 256.0
TOP = 32767.0
BF = jnp.bfloat16
F32 = jnp.float32
I16 = jnp.int16
NT = (((1,), (1,)), ((), ()))
ROOM = pltpu.CompilerParams(vmem_limit_bytes=60 << 20)
ANY = pl.BlockSpec(memory_space=pl.ANY)
VMEM = pl.BlockSpec(memory_space=pltpu.VMEM)
SMEM = pl.BlockSpec(memory_space=pltpu.SMEM)


COST = pl.CostEstimate(flops=1024, bytes_accessed=1024, transcendentals=0)


def rms_latent(comp, gain):
    lat = comp[:, :KVL]
    scale = lax.rsqrt(jnp.mean(lat * lat, axis=-1, keepdims=True) + 1e-06)
    return (lat * scale * gain).astype(jnp.bfloat16)


def rotate(values, position):
    half = values.shape[-1] // 2
    freq = jnp.exp(-jnp.log(10000.0) * jnp.arange(half, dtype=jnp.float32) / half)
    angle = position.astype(jnp.float32)[..., None] * freq
    cosine = jnp.cos(angle)
    sine = jnp.sin(angle)
    first = values[..., :half]
    second = values[..., half:]
    return jnp.concatenate([first * cosine - second * sine, first * sine + second * cosine], -1)


def block_stats(keys, q_lat, q_pos, valid):
    scale = (DN + DR) ** (-0.5)
    scores = jnp.einsum("jhk,tk->jht", q_lat, keys[:, :KVL], preferred_element_type=jnp.float32)
    scores = (
        scores + jnp.einsum("jhk,tk->jht", q_pos, keys[:, KVL:], preferred_element_type=jnp.float32)
    ) * scale
    scores = jnp.where(valid, scores, -1e30)
    top = jnp.max(scores, axis=-1)
    weights = jnp.where(valid, jnp.exp(scores - top[..., None]), 0.0)
    total = jnp.sum(weights, axis=-1)
    numer = jnp.einsum(
        "jht,tk->jhk",
        weights.astype(jnp.bfloat16),
        keys[:, :KVL],
        preferred_element_type=jnp.float32,
    )
    return (top, total, numer)


def combine(left, right):
    top = jnp.maximum(left[0], right[0])
    left_scale = jnp.exp(left[0] - top)
    right_scale = jnp.exp(right[0] - top)
    total = left[1] * left_scale + right[1] * right_scale
    numer = left[2] * left_scale[..., None] + right[2] * right_scale[..., None]
    return (top, total, numer)


def local_general(
    prefill_hidden,
    draft_hidden,
    kv_down,
    kv_gain,
    query_latent,
    q_up,
    kv_up,
    owners,
    segment_ids,
    accepted,
):
    tp_count = lax.axis_size("tp")
    pd_count = lax.axis_size("pd")
    tp_rank = lax.axis_index("tp")
    mine_rank = lax.axis_index("pd")
    requests = owners.shape[0]
    share = PRE_TOK // tp_count
    width = KVL + DR
    local_hidden = prefill_hidden.reshape(RP, PRE_TOK, prefill_hidden.shape[1])
    summed = lax.psum_scatter(
        jnp.einsum(
            "rtd,dw->trw", local_hidden, kv_down, preferred_element_type=jnp.float32
        ).reshape(lax.axis_size("tp") * share, RP * width),
        "tp",
        scatter_dimension=0,
        tiled=True,
    ).reshape(share * RP, width)
    draft_sum = lax.psum(jnp.dot(draft_hidden, kv_down, preferred_element_type=jnp.float32), "tp")
    first_req = mine_rank * RP
    row_pos = jnp.broadcast_to(
        tp_rank * share + jnp.arange(share, dtype=jnp.int32)[:, None], (share, RP)
    )
    page_rows = jnp.concatenate(
        [
            rms_latent(summed, kv_gain),
            rotate(summed[:, KVL:], row_pos.reshape(-1)).astype(jnp.bfloat16),
        ],
        1,
    )
    page_rows = page_rows.reshape(share, RP, width)
    draft_pos = jnp.tile(PRE_TOK + jnp.arange(2, dtype=jnp.int32), RP)
    draft_rows = jnp.concatenate(
        [
            rms_latent(draft_sum, kv_gain),
            rotate(draft_sum[:, KVL:], draft_pos).astype(jnp.bfloat16),
        ],
        1,
    )
    draft_rows = draft_rows.reshape(RP, 2, width)
    my_owners = lax.dynamic_slice_in_dim(owners, first_req, RP, 0)
    routing = (my_owners[None, :] == jnp.arange(pd_count, dtype=jnp.int32)[:, None]).astype(
        jnp.bfloat16
    )
    send_pages = jnp.einsum(
        "dk,tkw->dtw", routing, page_rows, preferred_element_type=jnp.float32
    ).astype(jnp.bfloat16)
    send_drafts = jnp.einsum(
        "dk,kjw->djw", routing, draft_rows, preferred_element_type=jnp.float32
    ).astype(jnp.bfloat16)
    pages, drafts = (
        lax.all_to_all(send_pages, "pd", split_axis=0, concat_axis=0, tiled=True),
        lax.all_to_all(send_drafts, "pd", split_axis=0, concat_axis=0, tiled=True),
    )
    heads_local = q_up.shape[1] // (DN + DR)
    query_full = jnp.dot(
        query_latent.reshape(requests * 2, QL), q_up, preferred_element_type=jnp.float32
    )
    query_full = query_full.reshape(requests, 2, heads_local, DN + DR)
    new_pos = jnp.broadcast_to(PRE_TOK + jnp.arange(2, dtype=jnp.int32)[None, :], (requests, 2))
    q_nope = query_full[..., :DN].astype(jnp.bfloat16)
    q_rot = rotate(query_full[..., DN:], new_pos[:, :, None]).astype(jnp.bfloat16)
    up_heads = kv_up.reshape(KVL, heads_local, DN + DV)
    w_value = up_heads[:, :, DN:]
    q_abs = jnp.einsum(
        "rjhd,khd->rjhk", q_nope, up_heads[:, :, :DN], preferred_element_type=jnp.float32
    ).astype(jnp.bfloat16)
    owner_table = owners.reshape(pd_count, RP) == mine_rank
    holding = jnp.sum(owner_table.astype(jnp.int32), axis=1)
    slot_of = jnp.sum(
        owner_table.astype(jnp.int32) * jnp.arange(RP, dtype=jnp.int32)[None, :], axis=1
    )
    owned_count = jnp.sum(holding)
    order = jnp.argsort((1 - holding) * pd_count + jnp.arange(pd_count, dtype=jnp.int32))
    draft_valid = (jnp.arange(2)[None, :] <= jnp.arange(2)[:, None])[:, None, :]
    empty = jnp.zeros((pd_count, 2, heads_local * DV), jnp.bfloat16)

    def finish(stats, source, request, q_lat, q_pos, result):
        stats = combine(stats, block_stats(drafts[source], q_lat, q_pos, draft_valid))
        attended = (stats[2] / stats[1][..., None]).astype(jnp.bfloat16)
        head_out = jnp.einsum("jhk,khd->jhd", attended, w_value, preferred_element_type=jnp.float32)
        keep = (jnp.arange(2) <= accepted[request]).astype(jnp.float32)[:, None, None]
        answer = (head_out * keep).astype(jnp.bfloat16).reshape(1, 2, heads_local * DV)
        return lax.dynamic_update_slice(result, answer, (source, 0, 0))

    def attend(turn, result):
        source = order[turn]
        request = source * RP + slot_of[source]
        q_lat = q_abs[request]
        q_pos = q_rot[request]
        seg_row = segment_ids[request]
        current = seg_row[PRE_TOK - 1]
        init = (
            jnp.full((2, heads_local), -1e30, jnp.float32),
            jnp.zeros((2, heads_local), jnp.float32),
            jnp.zeros((2, heads_local, KVL), jnp.float32),
        )
        valid = (seg_row == current)[None, None, :]
        stats = combine(
            init,
            block_stats(
                lax.all_gather(pages[source], "tp", axis=0, tiled=True), q_lat, q_pos, valid
            ),
        )
        return finish(stats, source, request, q_lat, q_pos, result)

    result = lax.fori_loop(0, owned_count, attend, empty)
    return (result.reshape(pd_count * 2, heads_local * DV), pages)


def encode(values):
    levels = []
    parts = []
    for first, last in ((0, KVL), (KVL, WIDTH)):
        block = values[first:last]
        top = jnp.maximum(jnp.max(jnp.abs(block), axis=0, keepdims=True), 1e-30)
        level = jnp.ceil(jnp.log2(top) * STEPS)
        codes = jnp.round(block * (jnp.exp2(level * (-1.0 / STEPS)) * TOP))
        parts.append(jnp.clip(codes, -TOP, TOP).astype(jnp.int32).astype(I16))
        levels.append(level.astype(jnp.int32))
    row = lax.broadcasted_iota(jnp.int32, (16, values.shape[1]), 0)
    extra = jnp.where(row == 0, levels[0], jnp.where(row == 1, levels[1], 0))
    return jnp.concatenate([*parts, extra.astype(I16)], 0)


def decode(codes):
    level = codes[WIDTH:CODED].astype(jnp.int32).astype(F32)
    step = jnp.exp2(level * (1.0 / STEPS)) * (1.0 / TOP)
    lat = codes[0:KVL].astype(jnp.int32).astype(F32) * step[0:1]
    rot = codes[KVL:WIDTH].astype(jnp.int32).astype(F32) * step[1:2]
    return jnp.concatenate([lat, rot], 0)


def key_rows(comp, gain, cosine, sine):
    lat = comp[:KVL]
    scale = lax.rsqrt(jnp.mean(lat * lat, axis=0, keepdims=True) + 1e-06)
    first = comp[KVL : KVL + HALF]
    second = comp[KVL + HALF :]
    return jnp.concatenate(
        [
            lat * scale * gain,
            first * cosine - second * sine,
            first * sine + second * cosine,
        ],
        0,
    )


def far(z, i):
    return jnp.where(z < 2, 3 - i, i)


def near(z, i):
    return jnp.where(z < 2, i, 3 - i)


def outer_rank(z):
    return (z == 0) | (z == 3)


def project_far_kernel(rank, hid_ref, down_ref, *refs):
    sum_ref, code_ref = refs[-2:]
    total = lax.dot_general(down_ref[...], hid_ref[0], NT, preferred_element_type=F32)
    for u in range(UNITS):
        sum_ref[0, u] = total[:, u * UNIT : (u + 1) * UNIT]

    @pl.when(outer_rank(rank[0]))
    def _():
        for u in range(UNITS):
            code_ref[0, u] = encode(total[:, u * UNIT : (u + 1) * UNIT])


def project_far(rank, hidden, down_t, request, after):
    depth = hidden.shape[-1]
    return pl.pallas_call(
        project_far_kernel,
        grid_spec=pltpu.PrefetchScalarGridSpec(
            num_scalar_prefetch=1,
            grid=(2,),
            in_specs=[
                pl.BlockSpec((1, SHARE, depth), lambda i, rank: (request, far(rank[0], i), 0)),
                VMEM,
                *([ANY] * len(after)),
            ],
            out_specs=[
                pl.BlockSpec((1, UNITS, WIDTH, UNIT), lambda i, rank: (i, 0, 0, 0)),
                pl.BlockSpec((1, UNITS, CODED, UNIT), lambda i, rank: (i, 0, 0, 0)),
            ],
        ),
        out_shape=[
            jax.ShapeDtypeStruct((2, UNITS, WIDTH, UNIT), F32),
            jax.ShapeDtypeStruct((2, UNITS, CODED, UNIT), I16),
        ],
        compiler_params=ROOM,
        cost_estimate=COST,
        name="project_far",
    )(rank, hidden, down_t, *after)


def project_near_kernel(rank, hid_ref, down_ref, *refs):
    sum_ref, *code_refs = refs[-3:]
    unit = pl.program_id(0)
    rows = hid_ref[...].reshape(LANES, hid_ref.shape[-1])
    total = lax.dot_general(down_ref[...], rows, NT, preferred_element_type=F32)
    for r in range(RP):
        sum_ref[0, 0, r] = total[:, r * UNIT : (r + 1) * UNIT]
    coded = outer_rank(rank[0]) & (pl.program_id(1) == 1)
    for mine, ref in zip((unit == 0, unit > 0), code_refs):

        @pl.when(coded & mine)
        def _(ref=ref):
            for r in range(RP):
                ref[0, r] = encode(total[:, r * UNIT : (r + 1) * UNIT])


def project_near(rank, hidden, down_t, after):
    depth = hidden.shape[-1]
    return pl.pallas_call(
        project_near_kernel,
        grid_spec=pltpu.PrefetchScalarGridSpec(
            num_scalar_prefetch=1,
            grid=(UNITS, 2),
            in_specs=[
                pl.BlockSpec(
                    (RP, UNIT, depth), lambda u, i, rank: (0, near(rank[0], i) * UNITS + u, 0)
                ),
                VMEM,
                *([ANY] * len(after)),
            ],
            out_specs=[
                pl.BlockSpec((1, 1, RP, WIDTH, UNIT), lambda u, i, rank: (u, i, 0, 0, 0)),
                pl.BlockSpec((1, RP, CODED, UNIT), lambda u, i, rank: (0, 0, 0, 0)),
                pl.BlockSpec(
                    (1, RP, CODED, UNIT), lambda u, i, rank: (jnp.maximum(u, 1) - 1, 0, 0, 0)
                ),
            ],
        ),
        out_shape=[
            jax.ShapeDtypeStruct((UNITS, 2, RP, WIDTH, UNIT), F32),
            jax.ShapeDtypeStruct((1, RP, CODED, UNIT), I16),
            jax.ShapeDtypeStruct((UNITS - 1, RP, CODED, UNIT), I16),
        ],
        compiler_params=ROOM,
        cost_estimate=COST,
        name="project_near",
    )(rank, hidden, down_t, *after)


def add_kernel(out_at, rank, own_ref, got_ref, *refs):
    @pl.when(~outer_rank(rank[0]))
    def _():
        for u in range(UNITS):
            refs[out_at][0, u] = encode(own_ref[u] + decode(got_ref[0, u]))


def add_on(rank, own, got, request=None, after=(), carried=()):
    chunk = lambda i, rank: (i, 0, 0, 0)
    if request is None:
        own_spec = pl.BlockSpec((None, UNITS, WIDTH, UNIT), chunk)
    else:
        own_spec = pl.BlockSpec(
            (UNITS, None, None, WIDTH, UNIT), lambda i, rank: (0, i, request, 0, 0)
        )
    return pl.pallas_call(
        functools.partial(add_kernel, -1 - len(carried)),
        grid_spec=pltpu.PrefetchScalarGridSpec(
            num_scalar_prefetch=1,
            grid=(2,),
            in_specs=[
                own_spec,
                pl.BlockSpec((1, UNITS, CODED, UNIT), chunk),
                *([ANY] * (len(after) + len(carried))),
            ],
            out_specs=[
                pl.BlockSpec((1, UNITS, CODED, UNIT), chunk),
                *([ANY] * len(carried)),
            ],
        ),
        out_shape=[
            jax.ShapeDtypeStruct((2, UNITS, CODED, UNIT), I16),
            *[jax.ShapeDtypeStruct(c.shape, c.dtype) for c in carried],
        ],
        input_output_aliases={3 + len(after) + n: 1 + n for n in range(len(carried))},
        compiler_params=ROOM,
        cost_estimate=COST,
        name="add_on",
    )(rank, own, got, *after, *carried)


def gain_column(gain_ref):
    return jnp.broadcast_to(gain_ref[...], (UNIT, KVL)).T


def page_kernel(requests, rank, slot, own_ref, *refs):
    count = len(requests)
    got_refs, sent_refs, refs = refs[:count], refs[count : 2 * count], refs[2 * count :]
    side_refs, (gain_ref, cos_ref, sin_ref) = refs[:2], refs[2:5]
    out_ref = refs[-1]
    step = pl.program_id(0)
    column = gain_column(gain_ref)

    def write(u, comp):
        rows = key_rows(comp, column, cos_ref[u], sin_ref[u]).astype(BF)
        out_ref[0, :, u * UNIT : (u + 1) * UNIT] = rows

    for k in range(count):

        @pl.when((step == k) & outer_rank(rank[0]))
        def _(k=k):
            for u in range(UNITS):
                write(u, own_ref[u] + decode(got_refs[k][u]))

        @pl.when((step == k) & ~outer_rank(rank[0]))
        def _(k=k):
            for u in range(UNITS):
                side = side_refs[u > 0][max(u - 1, 0)]
                write(u, decode(sent_refs[k][u]) + decode(side))


def pages_of(requests, rank, slot, own, got, sent, side, gain, cosine, sine, base, count, after):
    first = pl.BlockSpec((None, UNITS, CODED, UNIT), lambda i, *_: (0, 0, 0, 0))
    second = pl.BlockSpec((None, UNITS, CODED, UNIT), lambda i, *_: (1, 0, 0, 0))
    table = pl.BlockSpec((UNITS, HALF, UNIT), lambda i, *_: (0, 0, 0))
    start, total = requests[0], len(requests)
    got, sent = got[start : start + total], sent[start : start + total]
    return pl.pallas_call(
        functools.partial(page_kernel, requests),
        grid_spec=pltpu.PrefetchScalarGridSpec(
            num_scalar_prefetch=2,
            grid=(total,),
            in_specs=[
                pl.BlockSpec(
                    (UNITS, None, None, WIDTH, UNIT), lambda i, *_: (0, 0, i + start, 0, 0)
                ),
                *([first] * total),
                *([second] * total),
                pl.BlockSpec((1, None, CODED, UNIT), lambda i, *_: (0, i + start, 0, 0)),
                pl.BlockSpec((UNITS - 1, None, CODED, UNIT), lambda i, *_: (0, i + start, 0, 0)),
                pl.BlockSpec((1, KVL), lambda i, *_: (0, 0)),
                table,
                table,
                *([ANY] * (len(base) + len(after))),
            ],
            out_specs=pl.BlockSpec(
                (1, WIDTH, SHARE), lambda i, rank, slot: (slot[i + start], 0, 0)
            ),
        ),
        out_shape=jax.ShapeDtypeStruct((count, WIDTH, SHARE), BF),
        input_output_aliases={8 + 2 * total + n: n for n in range(len(base))},
        compiler_params=ROOM,
        cost_estimate=COST,
        name="pages",
    )(rank, slot, own, *got, *sent, *side, gain, cosine, sine, *base, *after)


def query_kernel(lat_ref, up_ref, draft_ref, down_ref, *refs):
    *key_refs, cos_ref, sin_ref, out_ref, split_ref = refs

    @pl.when(pl.program_id(0) == 0)
    def _():
        rest = lax.dot_general(draft_ref[...], down_ref[...], NT, preferred_element_type=F32)
        for n in range(3):
            term = rest.astype(BF).astype(F32)
            split_ref[n] = term
            rest = rest - term
        split_ref[3] = jnp.zeros_like(rest)

    full = jnp.dot(lat_ref[...], up_ref[...], preferred_element_type=F32)
    for h, key_ref in enumerate(key_refs):
        base = h * (DN + DR)
        nope = full[:, base : base + DN].astype(BF)
        first = full[:, base + DN : base + DN + HALF]
        second = full[:, base + DN + HALF : base + DN + DR]
        absorbed = lax.dot_general(nope, key_ref[...], NT, preferred_element_type=F32)
        cosine, sine = cos_ref[...], sin_ref[...]
        out_ref[h] = jnp.concatenate(
            [absorbed, first * cosine - second * sine, first * sine + second * cosine], 1
        )


def queries(latents, q_up, kv_up, draft, down_t, cosine, sine, after):
    rows = latents.shape[0]
    heads = q_up.shape[1] // (DN + DR)
    step = 4
    key_spec = [
        pl.BlockSpec((KVL, DN), lambda i, h=h: (0, 2 * (step * i + h))) for h in range(step)
    ]
    whole = lambda i: (0, 0)
    table = pl.BlockSpec((rows, HALF), whole)
    body = lambda *refs: query_kernel(*refs[:-3], *refs[-2:])
    return pl.pallas_call(
        body,
        grid=(heads // step,),
        in_specs=[
            pl.BlockSpec((rows, QL), whole),
            pl.BlockSpec((QL, step * (DN + DR)), lambda i: (0, i)),
            pl.BlockSpec(draft.shape, whole),
            pl.BlockSpec(down_t.shape, whole),
            *key_spec,
            table,
            table,
            ANY,
        ],
        out_specs=[
            pl.BlockSpec((step, rows, WIDTH), lambda i: (i, 0, 0)),
            pl.BlockSpec((4, rows, WIDTH), lambda i: (0, 0, 0)),
        ],
        out_shape=[
            jax.ShapeDtypeStruct((heads, rows, WIDTH), F32),
            jax.ShapeDtypeStruct((4, rows, WIDTH), F32),
        ],
        compiler_params=ROOM,
        cost_estimate=COST,
        name="queries",
    )(latents, q_up, draft, down_t, *([kv_up] * step), cosine, sine, after)


def attend_kernel(requests, rank, *refs):
    count = len(requests)
    q_refs, draft_refs, refs = refs[:4], refs[4:8], refs[8:]
    own_ref, got_refs, refs = refs[0], refs[1 : 1 + count], refs[1 + count :]
    cos_ref, sin_ref, midcos_ref, midsin_ref, refs = *refs[:4], refs[4:]
    segment_ref, gain_ref, newcos_ref, newsin_ref, refs = *refs[:4], refs[4:]
    out_refs, keys_ref = refs[-5:-1], refs[-1]
    step = pl.program_id(0)
    request = step + requests[0]

    @pl.when(rank[0] == 3)
    def _():
        column = gain_column(gain_ref)
        for k in range(count):

            @pl.when(step == k)
            def _(k=k):
                for i, (cosine, sine) in enumerate(
                    ((cos_ref, sin_ref), (midcos_ref, midsin_ref))
                ):
                    for u in range(UNITS):
                        comp = own_ref[u, i] + decode(got_refs[k][i, u])
                        rows = key_rows(comp, column, cosine[u], sine[u])
                        start = (1 - i) * SHARE + u * UNIT
                        keys_ref[:, start : start + UNIT] = rows.astype(BF)

        scale = (DN + DR) ** (-0.5)
        local_rows = out_refs[0].shape[1]
        new = 2 * RP
        comp = 0.0
        for ref in draft_refs:
            terms = ref[...].astype(F32)
            comp = comp + (terms[0:new] + terms[new : 2 * new] + terms[2 * new : 3 * new])
        lat = comp[:, :KVL]
        norm = lax.rsqrt(jnp.mean(lat * lat, axis=-1, keepdims=True) + 1e-06)
        first = comp[:, KVL : KVL + HALF]
        second = comp[:, KVL + HALF :]
        cosine, sine = newcos_ref[...], newsin_ref[...]
        drafts = jnp.concatenate(
            [
                lat * norm * gain_ref[...],
                first * cosine - second * sine,
                first * sine + second * cosine,
            ],
            1,
        )
        drafts = jnp.concatenate([drafts, jnp.zeros((UNIT - new, WIDTH), F32)], 0).astype(BF)
        query = jnp.concatenate([ref[...] for ref in q_refs], 0)
        scores = jnp.dot(query, keys_ref[...], preferred_element_type=F32) * scale
        segments = segment_ref[pl.ds(rank[1] * RP + request, 1), :]
        valid = segments[:, PRE_TOK // 2 :] == segments[:, PRE_TOK - 1 :]
        scores = jnp.where(valid, scores, -1e30)
        fresh = lax.dot_general(query, drafts, NT, preferred_element_type=F32) * scale
        row = lax.broadcasted_iota(jnp.int32, fresh.shape, 0)
        late = (row % local_rows) // (local_rows // 2)
        offset = lax.broadcasted_iota(jnp.int32, fresh.shape, 1) - 2 * request
        fresh = jnp.where((offset >= 0) & (offset <= late), fresh, -1e30)
        top = jnp.maximum(
            jnp.max(scores, axis=1, keepdims=True), jnp.max(fresh, axis=1, keepdims=True)
        )
        weights = jnp.exp(scores - top)
        fresh = jnp.exp(fresh - top)
        total = jnp.sum(weights, axis=1, keepdims=True) + jnp.sum(fresh, axis=1, keepdims=True)
        numer = lax.dot_general(
            weights.astype(BF), keys_ref[0:KVL, :], NT, preferred_element_type=F32
        )
        numer = numer + jnp.dot(fresh.astype(BF), drafts[:, :KVL], preferred_element_type=F32)
        result = (numer / total).astype(BF)
        for t, ref in enumerate(out_refs):
            ref[0] = result[t * local_rows : (t + 1) * local_rows]


def attend(requests, rank, messages, own, got, tables, segments, gain, cosine, sine, after):
    new = 2 * RP
    local_rows = (messages[0].shape[0] - 4 * new) // RP
    last = RP * local_rows // (4 * new)
    start, count = requests[0], len(requests)
    got = got[start : start + count]
    out = jax.ShapeDtypeStruct((count, local_rows, KVL), BF)
    whole = lambda i, rank: (0, 0)
    whole3 = lambda i, rank: (0, 0, 0)
    return pl.pallas_call(
        functools.partial(attend_kernel, requests),
        grid_spec=pltpu.PrefetchScalarGridSpec(
            num_scalar_prefetch=1,
            grid=(count,),
            in_specs=[
                *([pl.BlockSpec((local_rows, WIDTH), lambda i, rank: (i + start, 0))] * 4),
                *([pl.BlockSpec((4 * new, WIDTH), lambda i, rank: (last, 0))] * 4),
                pl.BlockSpec(
                    (UNITS, 2, None, WIDTH, UNIT), lambda i, rank: (0, 0, i + start, 0, 0)
                ),
                *([pl.BlockSpec((2, UNITS, CODED, UNIT), lambda i, rank: (0, 0, 0, 0))] * count),
                *([pl.BlockSpec((UNITS, HALF, UNIT), whole3)] * 4),
                pl.BlockSpec(segments.shape, whole),
                pl.BlockSpec((1, KVL), whole),
                pl.BlockSpec(cosine.shape, whole),
                pl.BlockSpec(sine.shape, whole),
                *([ANY] * len(after)),
            ],
            out_specs=[pl.BlockSpec((1, local_rows, KVL), lambda i, rank: (i, 0, 0))] * 4,
            scratch_shapes=[pltpu.VMEM((WIDTH, 2 * SHARE), BF)],
        ),
        out_shape=[out] * 4,
        compiler_params=ROOM,
        cost_estimate=COST,
        name="attend",
    )(rank, *messages, *messages, own, *got, *tables, segments, gain, cosine, sine, *after)


def heads_kernel(step, o_ref, keep_ref, *refs):
    out_ref = refs[-1]
    for h, value_ref in enumerate(refs[:step]):
        row = jnp.dot(o_ref[h].astype(BF), value_ref[...], preferred_element_type=F32)
        out_ref[:, h * DV : (h + 1) * DV] = row * keep_ref[...]


def heads_out(attended, keep, kv_up, after):
    heads, rows, _ = attended.shape
    step = 8
    value_spec = [
        pl.BlockSpec((KVL, DV), lambda i, h=h: (0, 2 * (step * i + h) + 1)) for h in range(step)
    ]
    return pl.pallas_call(
        functools.partial(heads_kernel, step),
        grid=(heads // step,),
        in_specs=[
            pl.BlockSpec((step, rows, KVL), lambda i: (i, 0, 0)),
            pl.BlockSpec((rows, DV), lambda i: (0, 0)),
            *value_spec,
            *([ANY] * len(after)),
        ],
        out_specs=pl.BlockSpec((rows, step * DV), lambda i: (0, i)),
        out_shape=jax.ShapeDtypeStruct((rows, heads * DV), F32),
        compiler_params=ROOM,
        cost_estimate=COST,
        name="heads_out",
    )(attended, keep, *([kv_up] * step), *after)


def route_kernel(slot, answer_ref, *refs):
    out_ref = refs[-1]
    out_ref[...] = jnp.zeros_like(out_ref)
    for r in range(RP):
        out_ref[slot[r]] = answer_ref[2 * r : 2 * r + 2, :]


def route(slot, answer, count, after):
    width = answer.shape[1]
    return pl.pallas_call(
        route_kernel,
        in_specs=[SMEM, VMEM, *([ANY] * len(after))],
        out_specs=VMEM,
        out_shape=jax.ShapeDtypeStruct((count, 2, width), F32),
        compiler_params=ROOM,
        cost_estimate=COST,
        name="route",
    )(slot, answer, *after)


def rope_tables(position):
    freq = jnp.exp(-jnp.log(10000.0) * jnp.arange(HALF, dtype=F32) / HALF)
    angle = position.astype(F32)[..., None] * freq
    return jnp.cos(angle), jnp.sin(angle)


def local_line(
    prefill_hidden,
    draft_hidden,
    kv_down,
    kv_gain,
    query_latent,
    q_up,
    kv_up,
    owners,
    segment_ids,
    accepted,
):
    pd_count = lax.axis_size("pd")
    z = lax.axis_index("tp")
    p = lax.axis_index("pd")
    first_req = p * RP

    gain = kv_gain.reshape(1, KVL)
    rank = jnp.stack([z, p]).astype(jnp.int32)
    hidden = prefill_hidden.reshape(RP, PRE_TOK, prefill_hidden.shape[1])
    down_t = kv_down.T
    inward, across, outward = [(0, 1), (3, 2)], [(1, 2), (2, 1)], [(2, 3), (1, 0)]

    far_sums, inner, crossed, sent, outer = [], [], [], [], []

    def send_far(r, after):
        total, codes = project_far(rank, hidden, down_t, r, after)
        far_sums.append(total)
        inner.append(lax.ppermute(codes, "tp", inward))

    def first_hop(r, after, carried=()):
        block, *carried = add_on(rank, far_sums[r], inner[r], after=after, carried=carried)
        crossed.append(lax.ppermute(block, "tp", across))
        return [block, *carried]

    def second_hop(r, after):
        (block,) = add_on(rank, near_sums, crossed[r], r, after)
        sent.append(block)
        outer.append(lax.ppermute(block, "tp", outward))
        return [block]

    send_far(0, [])
    send_far(1, far_sums[:1])

    latents = lax.dynamic_slice_in_dim(query_latent, first_req, RP, 0).reshape(RP * 2, QL)
    new_pos = jnp.tile(PRE_TOK + jnp.arange(2, dtype=jnp.int32), RP)
    new_cos, new_sin = rope_tables(new_pos)
    query, terms = queries(
        latents, q_up, kv_up, draft_hidden, down_t, new_cos, new_sin, far_sums[1]
    )
    heads = query.shape[0]
    query = query.reshape(heads, RP, 2, WIDTH).transpose(1, 2, 0, 3)
    message = jnp.concatenate(
        [query.reshape(RP * 2 * heads, WIDTH), terms.reshape(8 * RP, WIDTH)], 0
    ).astype(BF)
    messages = [lax.ppermute(message, "tp", [(t, 3)]) for t in range(3)] + [message]

    done = first_hop(0, [message])
    send_far(2, done)
    near_sums, *side = project_near(rank, hidden, down_t, far_sums[2:])
    done = first_hop(1, [near_sums])
    done = second_hop(0, [*done, *messages[:3]])
    send_far(3, done)
    steps = jnp.arange(SHARE, dtype=jnp.int32).reshape(UNITS, UNIT)
    tables = [
        jnp.swapaxes(t, 1, 2)
        for t in (*rope_tables(z * SHARE + steps), *rope_tables(2 * SHARE + steps))
    ]
    block, side[0] = first_hop(2, far_sums[3:], side[:1])
    side = [lax.ppermute(codes, "tp", inward) for codes in side]
    done = second_hop(1, [block, outer[0]])
    done = first_hop(3, done)
    done = second_hop(2, [*done, outer[1], side[0], *tables])
    done = second_hop(3, [*done, outer[2]])

    def attend_to(requests, after):
        result = attend(
            requests,
            rank,
            messages,
            near_sums,
            outer,
            tables,
            segment_ids,
            gain,
            new_cos,
            new_sin,
            after,
        )
        return result, [lax.ppermute(result[t], "tp", [(3, t)]) for t in range(3)]

    my_owners = lax.dynamic_slice_in_dim(owners, first_req, RP, 0)
    early, late = tuple(range(RP - 1)), (RP - 1,)

    def pages_to(requests, base, after):
        return pages_of(
            requests,
            rank,
            my_owners,
            near_sums,
            outer,
            sent,
            side,
            gain,
            tables[0],
            tables[1],
            base,
            pd_count,
            after,
        )

    results, backs = [None] * 2, [None] * 2
    results[0], backs[0] = attend_to(early, done)
    base = [jnp.zeros((pd_count, WIDTH, SHARE), BF)] if pd_count > RP else []
    pages = pages_to(early, base, results[0][:1])
    results[1], backs[1] = attend_to(late, [pages])
    pages = pages_to(late, [pages], [*results[1][:1], *backs[0], backs[1][2]])
    cache = lax.all_to_all(pages, "pd", split_axis=0, concat_axis=0, tiled=True)

    attended = [
        jnp.where(z == 3, result[3], back[0] + back[1] + back[2])
        for result, back in zip(results, backs)
    ]
    attended = jnp.concatenate(attended, 0).reshape(RP, 2, heads, KVL).transpose(2, 0, 1, 3)
    attended = attended.reshape(heads, RP * 2, KVL).astype(F32)
    my_accepted = lax.dynamic_slice_in_dim(accepted, first_req, RP, 0)
    keep = (jnp.arange(2)[None, :] <= my_accepted[:, None]).astype(F32).reshape(RP * 2, 1)
    answer = heads_out(attended, jnp.broadcast_to(keep, (RP * 2, DV)), kv_up, [pages])
    placed = route(my_owners, answer, pd_count, [cache]).astype(BF)
    placed = lax.all_to_all(placed, "pd", split_axis=0, concat_axis=0, tiled=True)
    cache = jnp.swapaxes(cache, 1, 2)
    return (placed.reshape(pd_count * 2, heads * DV), cache)


def solution(mesh):
    placed = (
        P(("groups", "pd"), "tp"),
        P(("groups", "pd"), "tp"),
        P("tp", None),
        P(),
        P("groups", None, None),
        P(None, "tp"),
        P(None, "tp"),
        P("groups"),
        P("groups", None),
        P("groups"),
    )
    return jax.shard_map(
        local_line if mesh.shape["tp"] == 4 else local_general,
        mesh=mesh,
        in_specs=placed,
        out_specs=(P(("groups", "pd"), "tp"), P(("groups", "pd"), "tp", None)),
        check_vma=False,
    )
```

```python
import functools

import jax
import jax.numpy as jnp
from jax import lax
from jax.experimental import pallas as pl
from jax.experimental.pallas import tpu as pltpu
from jax.sharding import PartitionSpec as P

DN = 128
DR = 64
DV = 128
KVL = 512
QL = 1536
PRE_TOK = 1536
RP = 4
WIDTH = KVL + DR
HALF = DR // 2
CODED = WIDTH + 16
SHARE = PRE_TOK // 4
UNIT = 128
UNITS = SHARE // UNIT
LANES = RP * UNIT
STEPS = 256.0
TOP = 32767.0
BF = jnp.bfloat16
F32 = jnp.float32
I16 = jnp.int16
NT = (((1,), (1,)), ((), ()))
ROOM = pltpu.CompilerParams(vmem_limit_bytes=60 << 20)
SOME = pltpu.CompilerParams(vmem_limit_bytes=52 << 20)
ANY = pl.BlockSpec(memory_space=pl.ANY)
VMEM = pl.BlockSpec(memory_space=pltpu.VMEM)
SMEM = pl.BlockSpec(memory_space=pltpu.SMEM)


COST = pl.CostEstimate(flops=1024, bytes_accessed=1024, transcendentals=0)


def rms_latent(comp, gain):
    lat = comp[:, :KVL]
    scale = lax.rsqrt(jnp.mean(lat * lat, axis=-1, keepdims=True) + 1e-06)
    return (lat * scale * gain).astype(jnp.bfloat16)


def rotate(values, position):
    half = values.shape[-1] // 2
    freq = jnp.exp(-jnp.log(10000.0) * jnp.arange(half, dtype=jnp.float32) / half)
    angle = position.astype(jnp.float32)[..., None] * freq
    cosine = jnp.cos(angle)
    sine = jnp.sin(angle)
    first = values[..., :half]
    second = values[..., half:]
    return jnp.concatenate([first * cosine - second * sine, first * sine + second * cosine], -1)


def block_stats(keys, q_lat, q_pos, valid):
    scale = (DN + DR) ** (-0.5)
    scores = jnp.einsum("jhk,tk->jht", q_lat, keys[:, :KVL], preferred_element_type=jnp.float32)
    scores = (
        scores + jnp.einsum("jhk,tk->jht", q_pos, keys[:, KVL:], preferred_element_type=jnp.float32)
    ) * scale
    scores = jnp.where(valid, scores, -1e30)
    top = jnp.max(scores, axis=-1)
    weights = jnp.where(valid, jnp.exp(scores - top[..., None]), 0.0)
    total = jnp.sum(weights, axis=-1)
    numer = jnp.einsum(
        "jht,tk->jhk",
        weights.astype(jnp.bfloat16),
        keys[:, :KVL],
        preferred_element_type=jnp.float32,
    )
    return (top, total, numer)


def combine(left, right):
    top = jnp.maximum(left[0], right[0])
    left_scale = jnp.exp(left[0] - top)
    right_scale = jnp.exp(right[0] - top)
    total = left[1] * left_scale + right[1] * right_scale
    numer = left[2] * left_scale[..., None] + right[2] * right_scale[..., None]
    return (top, total, numer)


def local_general(
    prefill_hidden,
    draft_hidden,
    kv_down,
    kv_gain,
    query_latent,
    q_up,
    kv_up,
    owners,
    segment_ids,
    accepted,
):
    tp_count = lax.axis_size("tp")
    pd_count = lax.axis_size("pd")
    tp_rank = lax.axis_index("tp")
    mine_rank = lax.axis_index("pd")
    requests = owners.shape[0]
    share = PRE_TOK // tp_count
    width = KVL + DR
    local_hidden = prefill_hidden.reshape(RP, PRE_TOK, prefill_hidden.shape[1])
    summed = lax.psum_scatter(
        jnp.einsum(
            "rtd,dw->trw", local_hidden, kv_down, preferred_element_type=jnp.float32
        ).reshape(lax.axis_size("tp") * share, RP * width),
        "tp",
        scatter_dimension=0,
        tiled=True,
    ).reshape(share * RP, width)
    draft_sum = lax.psum(jnp.dot(draft_hidden, kv_down, preferred_element_type=jnp.float32), "tp")
    first_req = mine_rank * RP
    row_pos = jnp.broadcast_to(
        tp_rank * share + jnp.arange(share, dtype=jnp.int32)[:, None], (share, RP)
    )
    page_rows = jnp.concatenate(
        [
            rms_latent(summed, kv_gain),
            rotate(summed[:, KVL:], row_pos.reshape(-1)).astype(jnp.bfloat16),
        ],
        1,
    )
    page_rows = page_rows.reshape(share, RP, width)
    draft_pos = jnp.tile(PRE_TOK + jnp.arange(2, dtype=jnp.int32), RP)
    draft_rows = jnp.concatenate(
        [
            rms_latent(draft_sum, kv_gain),
            rotate(draft_sum[:, KVL:], draft_pos).astype(jnp.bfloat16),
        ],
        1,
    )
    draft_rows = draft_rows.reshape(RP, 2, width)
    my_owners = lax.dynamic_slice_in_dim(owners, first_req, RP, 0)
    routing = (my_owners[None, :] == jnp.arange(pd_count, dtype=jnp.int32)[:, None]).astype(
        jnp.bfloat16
    )
    send_pages = jnp.einsum(
        "dk,tkw->dtw", routing, page_rows, preferred_element_type=jnp.float32
    ).astype(jnp.bfloat16)
    send_drafts = jnp.einsum(
        "dk,kjw->djw", routing, draft_rows, preferred_element_type=jnp.float32
    ).astype(jnp.bfloat16)
    pages, drafts = (
        lax.all_to_all(send_pages, "pd", split_axis=0, concat_axis=0, tiled=True),
        lax.all_to_all(send_drafts, "pd", split_axis=0, concat_axis=0, tiled=True),
    )
    heads_local = q_up.shape[1] // (DN + DR)
    query_full = jnp.dot(
        query_latent.reshape(requests * 2, QL), q_up, preferred_element_type=jnp.float32
    )
    query_full = query_full.reshape(requests, 2, heads_local, DN + DR)
    new_pos = jnp.broadcast_to(PRE_TOK + jnp.arange(2, dtype=jnp.int32)[None, :], (requests, 2))
    q_nope = query_full[..., :DN].astype(jnp.bfloat16)
    q_rot = rotate(query_full[..., DN:], new_pos[:, :, None]).astype(jnp.bfloat16)
    up_heads = kv_up.reshape(KVL, heads_local, DN + DV)
    w_value = up_heads[:, :, DN:]
    q_abs = jnp.einsum(
        "rjhd,khd->rjhk", q_nope, up_heads[:, :, :DN], preferred_element_type=jnp.float32
    ).astype(jnp.bfloat16)
    owner_table = owners.reshape(pd_count, RP) == mine_rank
    holding = jnp.sum(owner_table.astype(jnp.int32), axis=1)
    slot_of = jnp.sum(
        owner_table.astype(jnp.int32) * jnp.arange(RP, dtype=jnp.int32)[None, :], axis=1
    )
    owned_count = jnp.sum(holding)
    order = jnp.argsort((1 - holding) * pd_count + jnp.arange(pd_count, dtype=jnp.int32))
    draft_valid = (jnp.arange(2)[None, :] <= jnp.arange(2)[:, None])[:, None, :]
    empty = jnp.zeros((pd_count, 2, heads_local * DV), jnp.bfloat16)

    def finish(stats, source, request, q_lat, q_pos, result):
        stats = combine(stats, block_stats(drafts[source], q_lat, q_pos, draft_valid))
        attended = (stats[2] / stats[1][..., None]).astype(jnp.bfloat16)
        head_out = jnp.einsum("jhk,khd->jhd", attended, w_value, preferred_element_type=jnp.float32)
        keep = (jnp.arange(2) <= accepted[request]).astype(jnp.float32)[:, None, None]
        answer = (head_out * keep).astype(jnp.bfloat16).reshape(1, 2, heads_local * DV)
        return lax.dynamic_update_slice(result, answer, (source, 0, 0))

    def attend(turn, result):
        source = order[turn]
        request = source * RP + slot_of[source]
        q_lat = q_abs[request]
        q_pos = q_rot[request]
        seg_row = segment_ids[request]
        current = seg_row[PRE_TOK - 1]
        init = (
            jnp.full((2, heads_local), -1e30, jnp.float32),
            jnp.zeros((2, heads_local), jnp.float32),
            jnp.zeros((2, heads_local, KVL), jnp.float32),
        )
        valid = (seg_row == current)[None, None, :]
        stats = combine(
            init,
            block_stats(
                lax.all_gather(pages[source], "tp", axis=0, tiled=True), q_lat, q_pos, valid
            ),
        )
        return finish(stats, source, request, q_lat, q_pos, result)

    result = lax.fori_loop(0, owned_count, attend, empty)
    return (result.reshape(pd_count * 2, heads_local * DV), pages)


def encode(values):
    levels = []
    parts = []
    for first, last in ((0, KVL), (KVL, WIDTH)):
        block = values[first:last]
        top = jnp.maximum(jnp.max(jnp.abs(block), axis=0, keepdims=True), 1e-30)
        level = jnp.ceil(jnp.log2(top) * STEPS)
        codes = jnp.round(block * (jnp.exp2(level * (-1.0 / STEPS)) * TOP))
        parts.append(jnp.clip(codes, -TOP, TOP).astype(jnp.int32).astype(I16))
        levels.append(level.astype(jnp.int32))
    row = lax.broadcasted_iota(jnp.int32, (16, values.shape[1]), 0)
    extra = jnp.where(row == 0, levels[0], jnp.where(row == 1, levels[1], 0))
    return jnp.concatenate([*parts, extra.astype(I16)], 0)


def decode(codes):
    level = codes[WIDTH:CODED].astype(jnp.int32).astype(F32)
    step = jnp.exp2(level * (1.0 / STEPS)) * (1.0 / TOP)
    lat = codes[0:KVL].astype(jnp.int32).astype(F32) * step[0:1]
    rot = codes[KVL:WIDTH].astype(jnp.int32).astype(F32) * step[1:2]
    return jnp.concatenate([lat, rot], 0)


def key_rows(comp, gain, cosine, sine):
    lat = comp[:KVL]
    scale = lax.rsqrt(jnp.mean(lat * lat, axis=0, keepdims=True) + 1e-06)
    first = comp[KVL : KVL + HALF]
    second = comp[KVL + HALF :]
    return jnp.concatenate(
        [
            lat * scale * gain,
            first * cosine - second * sine,
            first * sine + second * cosine,
        ],
        0,
    )


def far(z, i):
    return jnp.where(z < 2, 3 - i, i)


def near(z, i):
    return jnp.where(z < 2, i, 3 - i)


def outer_rank(z):
    return (z == 0) | (z == 3)


def project_far_kernel(rank, hid_ref, down_ref, *refs):
    sum_ref, code_ref = refs[-2:]
    total = lax.dot_general(down_ref[...], hid_ref[0], NT, preferred_element_type=F32)
    for u in range(UNITS):
        sum_ref[0, u] = total[:, u * UNIT : (u + 1) * UNIT]

    @pl.when(outer_rank(rank[0]))
    def _():
        for u in range(UNITS):
            code_ref[0, u] = encode(total[:, u * UNIT : (u + 1) * UNIT])


def project_far(rank, hidden, down_t, request, after):
    depth = hidden.shape[-1]
    return pl.pallas_call(
        project_far_kernel,
        grid_spec=pltpu.PrefetchScalarGridSpec(
            num_scalar_prefetch=1,
            grid=(2,),
            in_specs=[
                pl.BlockSpec((1, SHARE, depth), lambda i, rank: (request, far(rank[0], i), 0)),
                VMEM,
                *([ANY] * len(after)),
            ],
            out_specs=[
                pl.BlockSpec((1, UNITS, WIDTH, UNIT), lambda i, rank: (i, 0, 0, 0)),
                pl.BlockSpec((1, UNITS, CODED, UNIT), lambda i, rank: (i, 0, 0, 0)),
            ],
        ),
        out_shape=[
            jax.ShapeDtypeStruct((2, UNITS, WIDTH, UNIT), F32),
            jax.ShapeDtypeStruct((2, UNITS, CODED, UNIT), I16),
        ],
        compiler_params=ROOM,
        cost_estimate=COST,
        name="project_far",
    )(rank, hidden, down_t, *after)


def project_near_kernel(rank, hid_ref, down_ref, *refs):
    sum_ref, *code_refs = refs[-3:]
    unit = pl.program_id(0)
    rows = hid_ref[...].reshape(LANES, hid_ref.shape[-1])
    total = lax.dot_general(down_ref[...], rows, NT, preferred_element_type=F32)
    for r in range(RP):
        sum_ref[0, 0, r] = total[:, r * UNIT : (r + 1) * UNIT]
    coded = outer_rank(rank[0]) & (pl.program_id(1) == 1)
    for mine, ref in zip((unit == 0, unit > 0), code_refs):

        @pl.when(coded & mine)
        def _(ref=ref):
            for r in range(RP):
                ref[0, r] = encode(total[:, r * UNIT : (r + 1) * UNIT])


def project_near(rank, hidden, down_t, after):
    depth = hidden.shape[-1]
    return pl.pallas_call(
        project_near_kernel,
        grid_spec=pltpu.PrefetchScalarGridSpec(
            num_scalar_prefetch=1,
            grid=(UNITS, 2),
            in_specs=[
                pl.BlockSpec(
                    (RP, UNIT, depth), lambda u, i, rank: (0, near(rank[0], i) * UNITS + u, 0)
                ),
                VMEM,
                *([ANY] * len(after)),
            ],
            out_specs=[
                pl.BlockSpec((1, 1, RP, WIDTH, UNIT), lambda u, i, rank: (u, i, 0, 0, 0)),
                pl.BlockSpec((1, RP, CODED, UNIT), lambda u, i, rank: (0, 0, 0, 0)),
                pl.BlockSpec(
                    (1, RP, CODED, UNIT), lambda u, i, rank: (jnp.maximum(u, 1) - 1, 0, 0, 0)
                ),
            ],
        ),
        out_shape=[
            jax.ShapeDtypeStruct((UNITS, 2, RP, WIDTH, UNIT), F32),
            jax.ShapeDtypeStruct((1, RP, CODED, UNIT), I16),
            jax.ShapeDtypeStruct((UNITS - 1, RP, CODED, UNIT), I16),
        ],
        compiler_params=ROOM,
        cost_estimate=COST,
        name="project_near",
    )(rank, hidden, down_t, *after)


def add_kernel(out_at, rank, own_ref, got_ref, *refs):
    @pl.when(~outer_rank(rank[0]))
    def _():
        for u in range(UNITS):
            refs[out_at][0, u] = encode(own_ref[u] + decode(got_ref[0, u]))


def add_on(rank, own, got, request=None, after=(), carried=()):
    chunk = lambda i, rank: (i, 0, 0, 0)
    if request is None:
        own_spec = pl.BlockSpec((None, UNITS, WIDTH, UNIT), chunk)
    else:
        own_spec = pl.BlockSpec(
            (UNITS, None, None, WIDTH, UNIT), lambda i, rank: (0, i, request, 0, 0)
        )
    return pl.pallas_call(
        functools.partial(add_kernel, -1 - len(carried)),
        grid_spec=pltpu.PrefetchScalarGridSpec(
            num_scalar_prefetch=1,
            grid=(2,),
            in_specs=[
                own_spec,
                pl.BlockSpec((1, UNITS, CODED, UNIT), chunk),
                *([ANY] * (len(after) + len(carried))),
            ],
            out_specs=[
                pl.BlockSpec((1, UNITS, CODED, UNIT), chunk),
                *([ANY] * len(carried)),
            ],
        ),
        out_shape=[
            jax.ShapeDtypeStruct((2, UNITS, CODED, UNIT), I16),
            *[jax.ShapeDtypeStruct(c.shape, c.dtype) for c in carried],
        ],
        input_output_aliases={3 + len(after) + n: 1 + n for n in range(len(carried))},
        compiler_params=SOME,
        cost_estimate=COST,
        name="add_on",
    )(rank, own, got, *after, *carried)


def gain_column(gain_ref):
    return jnp.broadcast_to(gain_ref[...], (UNIT, KVL)).T


def page_kernel(requests, rank, slot, own_ref, *refs):
    count = len(requests)
    got_refs, sent_refs, refs = refs[:count], refs[count : 2 * count], refs[2 * count :]
    side_refs, (gain_ref, cos_ref, sin_ref) = refs[:2], refs[2:5]
    out_ref = refs[-1]
    step = pl.program_id(0)
    column = gain_column(gain_ref)

    def write(u, comp):
        rows = key_rows(comp, column, cos_ref[u], sin_ref[u]).astype(BF)
        out_ref[0, :, u * UNIT : (u + 1) * UNIT] = rows

    for k in range(count):

        @pl.when((step == k) & outer_rank(rank[0]))
        def _(k=k):
            for u in range(UNITS):
                write(u, own_ref[u] + decode(got_refs[k][u]))

        @pl.when((step == k) & ~outer_rank(rank[0]))
        def _(k=k):
            for u in range(UNITS):
                side = side_refs[u > 0][max(u - 1, 0)]
                write(u, decode(sent_refs[k][u]) + decode(side))


def pages_of(requests, rank, slot, own, got, sent, side, gain, cosine, sine, base, count, after):
    first = pl.BlockSpec((None, UNITS, CODED, UNIT), lambda i, *_: (0, 0, 0, 0))
    second = pl.BlockSpec((None, UNITS, CODED, UNIT), lambda i, *_: (1, 0, 0, 0))
    table = pl.BlockSpec((UNITS, HALF, UNIT), lambda i, *_: (0, 0, 0))
    start, total = requests[0], len(requests)
    got, sent = got[start : start + total], sent[start : start + total]
    return pl.pallas_call(
        functools.partial(page_kernel, requests),
        grid_spec=pltpu.PrefetchScalarGridSpec(
            num_scalar_prefetch=2,
            grid=(total,),
            in_specs=[
                pl.BlockSpec(
                    (UNITS, None, None, WIDTH, UNIT), lambda i, *_: (0, 0, i + start, 0, 0)
                ),
                *([first] * total),
                *([second] * total),
                pl.BlockSpec((1, None, CODED, UNIT), lambda i, *_: (0, i + start, 0, 0)),
                pl.BlockSpec((UNITS - 1, None, CODED, UNIT), lambda i, *_: (0, i + start, 0, 0)),
                pl.BlockSpec((1, KVL), lambda i, *_: (0, 0)),
                table,
                table,
                *([ANY] * (len(base) + len(after))),
            ],
            out_specs=pl.BlockSpec(
                (1, WIDTH, SHARE), lambda i, rank, slot: (slot[i + start], 0, 0)
            ),
        ),
        out_shape=jax.ShapeDtypeStruct((count, WIDTH, SHARE), BF),
        input_output_aliases={8 + 2 * total + n: n for n in range(len(base))},
        compiler_params=SOME,
        cost_estimate=COST,
        name="pages",
    )(rank, slot, own, *got, *sent, *side, gain, cosine, sine, *base, *after)


def query_kernel(lat_ref, up_ref, draft_ref, down_ref, *refs):
    *key_refs, cos_ref, sin_ref, out_ref, split_ref = refs

    @pl.when(pl.program_id(0) == 0)
    def _():
        rest = lax.dot_general(draft_ref[...], down_ref[...], NT, preferred_element_type=F32)
        for n in range(3):
            term = rest.astype(BF).astype(F32)
            split_ref[n] = term
            rest = rest - term
        split_ref[3] = jnp.zeros_like(rest)

    full = jnp.dot(lat_ref[...], up_ref[...], preferred_element_type=F32)
    for h, key_ref in enumerate(key_refs):
        base = h * (DN + DR)
        nope = full[:, base : base + DN].astype(BF)
        first = full[:, base + DN : base + DN + HALF]
        second = full[:, base + DN + HALF : base + DN + DR]
        absorbed = lax.dot_general(nope, key_ref[...], NT, preferred_element_type=F32)
        cosine, sine = cos_ref[...], sin_ref[...]
        out_ref[h] = jnp.concatenate(
            [absorbed, first * cosine - second * sine, first * sine + second * cosine], 1
        )


def queries(latents, q_up, kv_up, draft, down_t, cosine, sine, after):
    rows = latents.shape[0]
    heads = q_up.shape[1] // (DN + DR)
    step = 4
    key_spec = [
        pl.BlockSpec((KVL, DN), lambda i, h=h: (0, 2 * (step * i + h))) for h in range(step)
    ]
    whole = lambda i: (0, 0)
    table = pl.BlockSpec((rows, HALF), whole)
    body = lambda *refs: query_kernel(*refs[:-3], *refs[-2:])
    return pl.pallas_call(
        body,
        grid=(heads // step,),
        in_specs=[
            pl.BlockSpec((rows, QL), whole),
            pl.BlockSpec((QL, step * (DN + DR)), lambda i: (0, i)),
            pl.BlockSpec(draft.shape, whole),
            pl.BlockSpec(down_t.shape, whole),
            *key_spec,
            table,
            table,
            ANY,
        ],
        out_specs=[
            pl.BlockSpec((step, rows, WIDTH), lambda i: (i, 0, 0)),
            pl.BlockSpec((4, rows, WIDTH), lambda i: (0, 0, 0)),
        ],
        out_shape=[
            jax.ShapeDtypeStruct((heads, rows, WIDTH), F32),
            jax.ShapeDtypeStruct((4, rows, WIDTH), F32),
        ],
        compiler_params=ROOM,
        cost_estimate=COST,
        name="queries",
    )(latents, q_up, draft, down_t, *([kv_up] * step), cosine, sine, after)


def attend_kernel(requests, rank, first_ref, *refs):
    count = len(requests)
    q_refs, draft_refs, refs = refs[:4], refs[4:8], refs[8:]
    own_ref, got_refs, refs = refs[0], refs[1 : 1 + count], refs[1 + count :]
    cos_ref, sin_ref, midcos_ref, midsin_ref, refs = *refs[:4], refs[4:]
    segment_ref, gain_ref, newcos_ref, newsin_ref, refs = *refs[:4], refs[4:]
    out_refs, keys_ref = refs[-5:-1], refs[-1]
    step = pl.program_id(0)
    request = step + requests[0]

    @pl.when(rank[0] == 3)
    def _():
        column = gain_column(gain_ref)
        for k in range(count):

            @pl.when(step == k)
            def _(k=k):
                for i, (cosine, sine) in enumerate(
                    ((cos_ref, sin_ref), (midcos_ref, midsin_ref))
                ):
                    for u in range(UNITS):
                        comp = own_ref[u, i] + decode(got_refs[k][i, u])
                        rows = key_rows(comp, column, cosine[u], sine[u])
                        start = (1 - i) * SHARE + u * UNIT
                        keys_ref[:, start : start + UNIT] = rows.astype(BF)

        scale = (DN + DR) ** (-0.5)
        local_rows = out_refs[0].shape[1]
        new = 2 * RP
        comp = 0.0
        for ref in draft_refs:
            terms = ref[...].astype(F32)
            comp = comp + (terms[0:new] + terms[new : 2 * new] + terms[2 * new : 3 * new])
        lat = comp[:, :KVL]
        norm = lax.rsqrt(jnp.mean(lat * lat, axis=-1, keepdims=True) + 1e-06)
        first = comp[:, KVL : KVL + HALF]
        second = comp[:, KVL + HALF :]
        cosine, sine = newcos_ref[...], newsin_ref[...]
        drafts = jnp.concatenate(
            [
                lat * norm * gain_ref[...],
                first * cosine - second * sine,
                first * sine + second * cosine,
            ],
            1,
        )
        drafts = jnp.concatenate([drafts, jnp.zeros((UNIT - new, WIDTH), F32)], 0).astype(BF)
        query = jnp.concatenate([ref[...] for ref in q_refs], 0)
        scores = jnp.dot(query, keys_ref[...], preferred_element_type=F32) * scale
        segments = segment_ref[pl.ds(first_ref[0] + request, 1), :]
        valid = segments[:, PRE_TOK // 2 :] == segments[:, PRE_TOK - 1 :]
        scores = jnp.where(valid, scores, -1e30)
        fresh = lax.dot_general(query, drafts, NT, preferred_element_type=F32) * scale
        row = lax.broadcasted_iota(jnp.int32, fresh.shape, 0)
        late = (row % local_rows) // (local_rows // 2)
        offset = lax.broadcasted_iota(jnp.int32, fresh.shape, 1) - 2 * request
        fresh = jnp.where((offset >= 0) & (offset <= late), fresh, -1e30)
        top = jnp.maximum(
            jnp.max(scores, axis=1, keepdims=True), jnp.max(fresh, axis=1, keepdims=True)
        )
        weights = jnp.exp(scores - top)
        fresh = jnp.exp(fresh - top)
        total = jnp.sum(weights, axis=1, keepdims=True) + jnp.sum(fresh, axis=1, keepdims=True)
        numer = lax.dot_general(
            weights.astype(BF), keys_ref[0:KVL, :], NT, preferred_element_type=F32
        )
        numer = numer + jnp.dot(fresh.astype(BF), drafts[:, :KVL], preferred_element_type=F32)
        result = (numer / total).astype(BF)
        for t, ref in enumerate(out_refs):
            ref[0] = result[t * local_rows : (t + 1) * local_rows]


def attend(requests, rank, first, messages, own, got, tables, segments, gain, cosine, sine, after):
    new = 2 * RP
    local_rows = (messages[0].shape[0] - 4 * new) // RP
    last = RP * local_rows // (4 * new)
    start, count = requests[0], len(requests)
    got = got[start : start + count]
    out = jax.ShapeDtypeStruct((count, local_rows, KVL), BF)
    whole = lambda i, *_: (0, 0)
    whole3 = lambda i, *_: (0, 0, 0)
    return pl.pallas_call(
        functools.partial(attend_kernel, requests),
        grid_spec=pltpu.PrefetchScalarGridSpec(
            num_scalar_prefetch=2,
            grid=(count,),
            in_specs=[
                *([pl.BlockSpec((local_rows, WIDTH), lambda i, *_: (i + start, 0))] * 4),
                *([pl.BlockSpec((4 * new, WIDTH), lambda i, *_: (last, 0))] * 4),
                pl.BlockSpec(
                    (UNITS, 2, None, WIDTH, UNIT), lambda i, *_: (0, 0, i + start, 0, 0)
                ),
                *([pl.BlockSpec((2, UNITS, CODED, UNIT), lambda i, *_: (0, 0, 0, 0))] * count),
                *([pl.BlockSpec((UNITS, HALF, UNIT), whole3)] * 4),
                pl.BlockSpec(segments.shape, whole),
                pl.BlockSpec((1, KVL), whole),
                pl.BlockSpec(cosine.shape, whole),
                pl.BlockSpec(sine.shape, whole),
                *([ANY] * len(after)),
            ],
            out_specs=[pl.BlockSpec((1, local_rows, KVL), lambda i, *_: (i, 0, 0))] * 4,
            scratch_shapes=[pltpu.VMEM((WIDTH, 2 * SHARE), BF)],
        ),
        out_shape=[out] * 4,
        compiler_params=SOME,
        cost_estimate=COST,
        name="attend",
    )(rank, first, *messages, *messages, own, *got, *tables, segments, gain, cosine, sine, *after)


def heads_kernel(step, o_ref, keep_ref, *refs):
    out_ref = refs[-1]
    for h, value_ref in enumerate(refs[:step]):
        row = jnp.dot(o_ref[h].astype(BF), value_ref[...], preferred_element_type=F32)
        out_ref[:, h * DV : (h + 1) * DV] = row * keep_ref[...]


def heads_out(attended, keep, kv_up, after):
    heads, rows, _ = attended.shape
    step = 8
    value_spec = [
        pl.BlockSpec((KVL, DV), lambda i, h=h: (0, 2 * (step * i + h) + 1)) for h in range(step)
    ]
    return pl.pallas_call(
        functools.partial(heads_kernel, step),
        grid=(heads // step,),
        in_specs=[
            pl.BlockSpec((step, rows, KVL), lambda i: (i, 0, 0)),
            pl.BlockSpec((rows, DV), lambda i: (0, 0)),
            *value_spec,
            *([ANY] * len(after)),
        ],
        out_specs=pl.BlockSpec((rows, step * DV), lambda i: (0, i)),
        out_shape=jax.ShapeDtypeStruct((rows, heads * DV), F32),
        compiler_params=ROOM,
        cost_estimate=COST,
        name="heads_out",
    )(attended, keep, *([kv_up] * step), *after)


def route_kernel(slot, answer_ref, *refs):
    out_ref = refs[-1]
    out_ref[...] = jnp.zeros_like(out_ref)
    for r in range(RP):
        out_ref[slot[r]] = answer_ref[2 * r : 2 * r + 2, :].astype(BF)


def route(slot, answer, count, after):
    width = answer.shape[1]
    return pl.pallas_call(
        route_kernel,
        in_specs=[SMEM, VMEM, *([ANY] * len(after))],
        out_specs=VMEM,
        out_shape=jax.ShapeDtypeStruct((count, 2, width), BF),
        compiler_params=SOME,
        cost_estimate=COST,
        name="route",
    )(slot, answer, *after)


def rope_tables(position):
    freq = jnp.exp(-jnp.log(10000.0) * jnp.arange(HALF, dtype=F32) / HALF)
    angle = position.astype(F32)[..., None] * freq
    return jnp.cos(angle), jnp.sin(angle)


def local_line(
    prefill_hidden,
    draft_hidden,
    kv_down,
    kv_gain,
    query_latent,
    q_up,
    kv_up,
    owners,
    segment_ids,
    accepted,
):
    pd_count = lax.axis_size("pd")
    z = lax.axis_index("tp")
    p = lax.axis_index("pd")
    first_req = p * RP

    gain = kv_gain.reshape(1, KVL)
    rank = z.astype(jnp.int32).reshape(1)
    hidden = prefill_hidden.reshape(RP, PRE_TOK, prefill_hidden.shape[1])
    down_t = kv_down.T
    inward, across, outward = [(0, 1), (3, 2)], [(1, 2), (2, 1)], [(2, 3), (1, 0)]

    far_sums, inner, crossed, sent, outer = [], [], [], [], []

    def send_far(r, after):
        total, codes = project_far(rank, hidden, down_t, r, after)
        far_sums.append(total)
        inner.append(lax.ppermute(codes, "tp", inward))

    def first_hop(r, after, carried=()):
        block, *carried = add_on(rank, far_sums[r], inner[r], after=after, carried=carried)
        crossed.append(lax.ppermute(block, "tp", across))
        return [block, *carried]

    def second_hop(r, after):
        (block,) = add_on(rank, near_sums, crossed[r], r, after)
        sent.append(block)
        outer.append(lax.ppermute(block, "tp", outward))
        return [block]

    send_far(0, [])
    send_far(1, far_sums[:1])

    latents = lax.dynamic_slice_in_dim(query_latent, first_req, RP, 0).reshape(RP * 2, QL)
    new_pos = jnp.tile(PRE_TOK + jnp.arange(2, dtype=jnp.int32), RP)
    new_cos, new_sin = rope_tables(new_pos)
    query, terms = queries(
        latents, q_up, kv_up, draft_hidden, down_t, new_cos, new_sin, far_sums[1]
    )
    heads = query.shape[0]
    query = query.reshape(heads, RP, 2, WIDTH).transpose(1, 2, 0, 3)
    message = jnp.concatenate(
        [query.reshape(RP * 2 * heads, WIDTH), terms.reshape(8 * RP, WIDTH)], 0
    ).astype(BF)
    messages = [lax.ppermute(message, "tp", [(t, 3)]) for t in range(3)] + [message]

    done = first_hop(0, [message])
    send_far(2, done)
    near_sums, *side = project_near(rank, hidden, down_t, far_sums[2:])
    done = first_hop(1, [near_sums])
    done = second_hop(0, [*done, *messages[:3]])
    send_far(3, done)
    steps = jnp.arange(SHARE, dtype=jnp.int32).reshape(UNITS, UNIT)
    tables = [
        jnp.swapaxes(t, 1, 2)
        for t in (*rope_tables(z * SHARE + steps), *rope_tables(2 * SHARE + steps))
    ]
    block, side[0] = first_hop(2, far_sums[3:], side[:1])
    side = [lax.ppermute(codes, "tp", inward) for codes in side]
    done = second_hop(1, [block, outer[0]])
    done = first_hop(3, done)
    done = second_hop(2, [*done, outer[1], side[0], *tables])
    done = second_hop(3, [*done, outer[2]])

    def attend_to(requests, after):
        result = attend(
            requests,
            rank,
            first_req.astype(jnp.int32).reshape(1),
            messages,
            near_sums,
            outer,
            tables,
            segment_ids,
            gain,
            new_cos,
            new_sin,
            after,
        )
        return result, [lax.ppermute(result[t], "tp", [(3, t)]) for t in range(3)]

    my_owners = lax.dynamic_slice_in_dim(owners, first_req, RP, 0)
    early, late = tuple(range(RP - 1)), (RP - 1,)

    def pages_to(requests, base, after):
        return pages_of(
            requests,
            rank,
            my_owners,
            near_sums,
            outer,
            sent,
            side,
            gain,
            tables[0],
            tables[1],
            base,
            pd_count,
            after,
        )

    results, backs = [None] * 2, [None] * 2
    results[0], backs[0] = attend_to(early, done)
    base = [jnp.zeros((pd_count, WIDTH, SHARE), BF)] if pd_count > RP else []
    pages = pages_to(early, base, results[0][:1])
    results[1], backs[1] = attend_to(late, [pages])
    pages = pages_to(late, [pages], [*results[1][:1], *backs[0]])
    cache = lax.all_to_all(pages, "pd", split_axis=0, concat_axis=0, tiled=True)

    attended = [
        jnp.where(z == 3, result[3], back[0] + back[1] + back[2])
        for result, back in zip(results, backs)
    ]
    attended = jnp.concatenate(attended, 0).reshape(RP, 2, heads, KVL).transpose(2, 0, 1, 3)
    attended = attended.reshape(heads, RP * 2, KVL).astype(F32)
    my_accepted = lax.dynamic_slice_in_dim(accepted, first_req, RP, 0)
    keep = (jnp.arange(2)[None, :] <= my_accepted[:, None]).astype(F32).reshape(RP * 2, 1)
    answer = heads_out(attended, jnp.broadcast_to(keep, (RP * 2, DV)), kv_up, [pages])
    placed = route(my_owners, answer, pd_count, [lax.slice(cache, (0, 0, 0), (1, 16, UNIT))])
    placed = lax.all_to_all(placed, "pd", split_axis=0, concat_axis=0, tiled=True)
    cache = jnp.swapaxes(cache, 1, 2)
    return (placed.reshape(pd_count * 2, heads * DV), cache)


def solution(mesh):
    placed = (
        P(("groups", "pd"), "tp"),
        P(("groups", "pd"), "tp"),
        P("tp", None),
        P(),
        P("groups", None, None),
        P(None, "tp"),
        P(None, "tp"),
        P("groups"),
        P("groups", None),
        P("groups"),
    )
    return jax.shard_map(
        local_line if mesh.shape["tp"] == 4 else local_general,
        mesh=mesh,
        in_specs=placed,
        out_specs=(P(("groups", "pd"), "tp"), P(("groups", "pd"), "tp", None)),
        check_vma=False,
    )
```

```python
import functools

import jax
import jax.numpy as jnp
from jax import lax
from jax.experimental import pallas as pl
from jax.experimental.pallas import tpu as pltpu
from jax.sharding import PartitionSpec as P

DN = 128
DR = 64
DV = 128
KVL = 512
QL = 1536
PRE_TOK = 1536
RP = 4
WIDTH = KVL + DR
HALF = DR // 2
CODED = WIDTH + 16
SHARE = PRE_TOK // 4
UNIT = 128
UNITS = SHARE // UNIT
LANES = RP * UNIT
STEPS = 256.0
TOP = 32767.0
BF = jnp.bfloat16
F32 = jnp.float32
I16 = jnp.int16
NT = (((1,), (1,)), ((), ()))
ROOM = pltpu.CompilerParams(vmem_limit_bytes=60 << 20)
SOME = pltpu.CompilerParams(vmem_limit_bytes=52 << 20)
ANY = pl.BlockSpec(memory_space=pl.ANY)
VMEM = pl.BlockSpec(memory_space=pltpu.VMEM)
SMEM = pl.BlockSpec(memory_space=pltpu.SMEM)


COST = pl.CostEstimate(flops=1024, bytes_accessed=1024, transcendentals=0)


def rms_latent(comp, gain):
    lat = comp[:, :KVL]
    scale = lax.rsqrt(jnp.mean(lat * lat, axis=-1, keepdims=True) + 1e-06)
    return (lat * scale * gain).astype(jnp.bfloat16)


def rotate(values, position):
    half = values.shape[-1] // 2
    freq = jnp.exp(-jnp.log(10000.0) * jnp.arange(half, dtype=jnp.float32) / half)
    angle = position.astype(jnp.float32)[..., None] * freq
    cosine = jnp.cos(angle)
    sine = jnp.sin(angle)
    first = values[..., :half]
    second = values[..., half:]
    return jnp.concatenate([first * cosine - second * sine, first * sine + second * cosine], -1)


def block_stats(keys, q_lat, q_pos, valid):
    scale = (DN + DR) ** (-0.5)
    scores = jnp.einsum("jhk,tk->jht", q_lat, keys[:, :KVL], preferred_element_type=jnp.float32)
    scores = (
        scores + jnp.einsum("jhk,tk->jht", q_pos, keys[:, KVL:], preferred_element_type=jnp.float32)
    ) * scale
    scores = jnp.where(valid, scores, -1e30)
    top = jnp.max(scores, axis=-1)
    weights = jnp.where(valid, jnp.exp(scores - top[..., None]), 0.0)
    total = jnp.sum(weights, axis=-1)
    numer = jnp.einsum(
        "jht,tk->jhk",
        weights.astype(jnp.bfloat16),
        keys[:, :KVL],
        preferred_element_type=jnp.float32,
    )
    return (top, total, numer)


def combine(left, right):
    top = jnp.maximum(left[0], right[0])
    left_scale = jnp.exp(left[0] - top)
    right_scale = jnp.exp(right[0] - top)
    total = left[1] * left_scale + right[1] * right_scale
    numer = left[2] * left_scale[..., None] + right[2] * right_scale[..., None]
    return (top, total, numer)


def local_general(
    prefill_hidden,
    draft_hidden,
    kv_down,
    kv_gain,
    query_latent,
    q_up,
    kv_up,
    owners,
    segment_ids,
    accepted,
):
    tp_count = lax.axis_size("tp")
    pd_count = lax.axis_size("pd")
    tp_rank = lax.axis_index("tp")
    mine_rank = lax.axis_index("pd")
    requests = owners.shape[0]
    share = PRE_TOK // tp_count
    width = KVL + DR
    local_hidden = prefill_hidden.reshape(RP, PRE_TOK, prefill_hidden.shape[1])
    summed = lax.psum_scatter(
        jnp.einsum(
            "rtd,dw->trw", local_hidden, kv_down, preferred_element_type=jnp.float32
        ).reshape(lax.axis_size("tp") * share, RP * width),
        "tp",
        scatter_dimension=0,
        tiled=True,
    ).reshape(share * RP, width)
    draft_sum = lax.psum(jnp.dot(draft_hidden, kv_down, preferred_element_type=jnp.float32), "tp")
    first_req = mine_rank * RP
    row_pos = jnp.broadcast_to(
        tp_rank * share + jnp.arange(share, dtype=jnp.int32)[:, None], (share, RP)
    )
    page_rows = jnp.concatenate(
        [
            rms_latent(summed, kv_gain),
            rotate(summed[:, KVL:], row_pos.reshape(-1)).astype(jnp.bfloat16),
        ],
        1,
    )
    page_rows = page_rows.reshape(share, RP, width)
    draft_pos = jnp.tile(PRE_TOK + jnp.arange(2, dtype=jnp.int32), RP)
    draft_rows = jnp.concatenate(
        [
            rms_latent(draft_sum, kv_gain),
            rotate(draft_sum[:, KVL:], draft_pos).astype(jnp.bfloat16),
        ],
        1,
    )
    draft_rows = draft_rows.reshape(RP, 2, width)
    my_owners = lax.dynamic_slice_in_dim(owners, first_req, RP, 0)
    routing = (my_owners[None, :] == jnp.arange(pd_count, dtype=jnp.int32)[:, None]).astype(
        jnp.bfloat16
    )
    send_pages = jnp.einsum(
        "dk,tkw->dtw", routing, page_rows, preferred_element_type=jnp.float32
    ).astype(jnp.bfloat16)
    send_drafts = jnp.einsum(
        "dk,kjw->djw", routing, draft_rows, preferred_element_type=jnp.float32
    ).astype(jnp.bfloat16)
    pages, drafts = (
        lax.all_to_all(send_pages, "pd", split_axis=0, concat_axis=0, tiled=True),
        lax.all_to_all(send_drafts, "pd", split_axis=0, concat_axis=0, tiled=True),
    )
    heads_local = q_up.shape[1] // (DN + DR)
    query_full = jnp.dot(
        query_latent.reshape(requests * 2, QL), q_up, preferred_element_type=jnp.float32
    )
    query_full = query_full.reshape(requests, 2, heads_local, DN + DR)
    new_pos = jnp.broadcast_to(PRE_TOK + jnp.arange(2, dtype=jnp.int32)[None, :], (requests, 2))
    q_nope = query_full[..., :DN].astype(jnp.bfloat16)
    q_rot = rotate(query_full[..., DN:], new_pos[:, :, None]).astype(jnp.bfloat16)
    up_heads = kv_up.reshape(KVL, heads_local, DN + DV)
    w_value = up_heads[:, :, DN:]
    q_abs = jnp.einsum(
        "rjhd,khd->rjhk", q_nope, up_heads[:, :, :DN], preferred_element_type=jnp.float32
    ).astype(jnp.bfloat16)
    owner_table = owners.reshape(pd_count, RP) == mine_rank
    holding = jnp.sum(owner_table.astype(jnp.int32), axis=1)
    slot_of = jnp.sum(
        owner_table.astype(jnp.int32) * jnp.arange(RP, dtype=jnp.int32)[None, :], axis=1
    )
    owned_count = jnp.sum(holding)
    order = jnp.argsort((1 - holding) * pd_count + jnp.arange(pd_count, dtype=jnp.int32))
    draft_valid = (jnp.arange(2)[None, :] <= jnp.arange(2)[:, None])[:, None, :]
    empty = jnp.zeros((pd_count, 2, heads_local * DV), jnp.bfloat16)

    def finish(stats, source, request, q_lat, q_pos, result):
        stats = combine(stats, block_stats(drafts[source], q_lat, q_pos, draft_valid))
        attended = (stats[2] / stats[1][..., None]).astype(jnp.bfloat16)
        head_out = jnp.einsum("jhk,khd->jhd", attended, w_value, preferred_element_type=jnp.float32)
        keep = (jnp.arange(2) <= accepted[request]).astype(jnp.float32)[:, None, None]
        answer = (head_out * keep).astype(jnp.bfloat16).reshape(1, 2, heads_local * DV)
        return lax.dynamic_update_slice(result, answer, (source, 0, 0))

    def attend(turn, result):
        source = order[turn]
        request = source * RP + slot_of[source]
        q_lat = q_abs[request]
        q_pos = q_rot[request]
        seg_row = segment_ids[request]
        current = seg_row[PRE_TOK - 1]
        init = (
            jnp.full((2, heads_local), -1e30, jnp.float32),
            jnp.zeros((2, heads_local), jnp.float32),
            jnp.zeros((2, heads_local, KVL), jnp.float32),
        )
        valid = (seg_row == current)[None, None, :]
        stats = combine(
            init,
            block_stats(
                lax.all_gather(pages[source], "tp", axis=0, tiled=True), q_lat, q_pos, valid
            ),
        )
        return finish(stats, source, request, q_lat, q_pos, result)

    result = lax.fori_loop(0, owned_count, attend, empty)
    return (result.reshape(pd_count * 2, heads_local * DV), pages)


def encode(values):
    levels = []
    parts = []
    for first, last in ((0, KVL), (KVL, WIDTH)):
        block = values[first:last]
        top = jnp.maximum(jnp.max(jnp.abs(block), axis=0, keepdims=True), 1e-30)
        level = jnp.ceil(jnp.log2(top) * STEPS)
        codes = jnp.round(block * (jnp.exp2(level * (-1.0 / STEPS)) * TOP))
        parts.append(jnp.clip(codes, -TOP, TOP).astype(jnp.int32).astype(I16))
        levels.append(level.astype(jnp.int32))
    row = lax.broadcasted_iota(jnp.int32, (16, values.shape[1]), 0)
    extra = jnp.where(row == 0, levels[0], jnp.where(row == 1, levels[1], 0))
    return jnp.concatenate([*parts, extra.astype(I16)], 0)


def decode(codes):
    level = codes[WIDTH:CODED].astype(jnp.int32).astype(F32)
    step = jnp.exp2(level * (1.0 / STEPS)) * (1.0 / TOP)
    lat = codes[0:KVL].astype(jnp.int32).astype(F32) * step[0:1]
    rot = codes[KVL:WIDTH].astype(jnp.int32).astype(F32) * step[1:2]
    return jnp.concatenate([lat, rot], 0)


def key_rows(comp, gain, cosine, sine):
    lat = comp[:KVL]
    scale = lax.rsqrt(jnp.mean(lat * lat, axis=0, keepdims=True) + 1e-06)
    first = comp[KVL : KVL + HALF]
    second = comp[KVL + HALF :]
    return jnp.concatenate(
        [
            lat * scale * gain,
            first * cosine - second * sine,
            first * sine + second * cosine,
        ],
        0,
    )


def far(z, i):
    return jnp.where(z < 2, 3 - i, i)


def near(z, i):
    return jnp.where(z < 2, i, 3 - i)


def outer_rank(z):
    return (z == 0) | (z == 3)


def project_far_kernel(rank, hid_ref, down_ref, *refs):
    sum_ref, code_ref = refs[-2:]
    total = lax.dot_general(down_ref[...], hid_ref[0], NT, preferred_element_type=F32)
    for u in range(UNITS):
        sum_ref[0, u] = total[:, u * UNIT : (u + 1) * UNIT]

    @pl.when(outer_rank(rank[0]))
    def _():
        for u in range(UNITS):
            code_ref[0, u] = encode(total[:, u * UNIT : (u + 1) * UNIT])


def project_far(rank, hidden, down_t, request, after):
    depth = hidden.shape[-1]
    return pl.pallas_call(
        project_far_kernel,
        grid_spec=pltpu.PrefetchScalarGridSpec(
            num_scalar_prefetch=1,
            grid=(2,),
            in_specs=[
                pl.BlockSpec((1, SHARE, depth), lambda i, rank: (request, far(rank[0], i), 0)),
                VMEM,
                *([ANY] * len(after)),
            ],
            out_specs=[
                pl.BlockSpec((1, UNITS, WIDTH, UNIT), lambda i, rank: (i, 0, 0, 0)),
                pl.BlockSpec((1, UNITS, CODED, UNIT), lambda i, rank: (i, 0, 0, 0)),
            ],
        ),
        out_shape=[
            jax.ShapeDtypeStruct((2, UNITS, WIDTH, UNIT), F32),
            jax.ShapeDtypeStruct((2, UNITS, CODED, UNIT), I16),
        ],
        compiler_params=ROOM,
        cost_estimate=COST,
        name="project_far",
    )(rank, hidden, down_t, *after)


def project_near_kernel(rank, hid_ref, down_ref, *refs):
    sum_ref, *code_refs = refs[-3:]
    unit = pl.program_id(0)
    rows = hid_ref[...].reshape(LANES, hid_ref.shape[-1])
    total = lax.dot_general(down_ref[...], rows, NT, preferred_element_type=F32)
    for r in range(RP):
        sum_ref[0, 0, r] = total[:, r * UNIT : (r + 1) * UNIT]
    coded = outer_rank(rank[0]) & (pl.program_id(1) == 1)
    for mine, ref in zip((unit == 0, unit > 0), code_refs):

        @pl.when(coded & mine)
        def _(ref=ref):
            for r in range(RP):
                ref[0, r] = encode(total[:, r * UNIT : (r + 1) * UNIT])


def project_near(rank, hidden, down_t, after):
    depth = hidden.shape[-1]
    return pl.pallas_call(
        project_near_kernel,
        grid_spec=pltpu.PrefetchScalarGridSpec(
            num_scalar_prefetch=1,
            grid=(UNITS, 2),
            in_specs=[
                pl.BlockSpec(
                    (RP, UNIT, depth), lambda u, i, rank: (0, near(rank[0], i) * UNITS + u, 0)
                ),
                VMEM,
                *([ANY] * len(after)),
            ],
            out_specs=[
                pl.BlockSpec((1, 1, RP, WIDTH, UNIT), lambda u, i, rank: (u, i, 0, 0, 0)),
                pl.BlockSpec((1, RP, CODED, UNIT), lambda u, i, rank: (0, 0, 0, 0)),
                pl.BlockSpec(
                    (1, RP, CODED, UNIT), lambda u, i, rank: (jnp.maximum(u, 1) - 1, 0, 0, 0)
                ),
            ],
        ),
        out_shape=[
            jax.ShapeDtypeStruct((UNITS, 2, RP, WIDTH, UNIT), F32),
            jax.ShapeDtypeStruct((1, RP, CODED, UNIT), I16),
            jax.ShapeDtypeStruct((UNITS - 1, RP, CODED, UNIT), I16),
        ],
        compiler_params=ROOM,
        cost_estimate=COST,
        name="project_near",
    )(rank, hidden, down_t, *after)


def add_kernel(out_at, rank, own_ref, got_ref, *refs):
    @pl.when(~outer_rank(rank[0]))
    def _():
        for u in range(UNITS):
            refs[out_at][0, u] = encode(own_ref[u] + decode(got_ref[0, u]))


def add_on(rank, own, got, request=None, after=(), carried=()):
    chunk = lambda i, rank: (i, 0, 0, 0)
    if request is None:
        own_spec = pl.BlockSpec((None, UNITS, WIDTH, UNIT), chunk)
    else:
        own_spec = pl.BlockSpec(
            (UNITS, None, None, WIDTH, UNIT), lambda i, rank: (0, i, request, 0, 0)
        )
    return pl.pallas_call(
        functools.partial(add_kernel, -1 - len(carried)),
        grid_spec=pltpu.PrefetchScalarGridSpec(
            num_scalar_prefetch=1,
            grid=(2,),
            in_specs=[
                own_spec,
                pl.BlockSpec((1, UNITS, CODED, UNIT), chunk),
                *([ANY] * (len(after) + len(carried))),
            ],
            out_specs=[
                pl.BlockSpec((1, UNITS, CODED, UNIT), chunk),
                *([ANY] * len(carried)),
            ],
        ),
        out_shape=[
            jax.ShapeDtypeStruct((2, UNITS, CODED, UNIT), I16),
            *[jax.ShapeDtypeStruct(c.shape, c.dtype) for c in carried],
        ],
        input_output_aliases={3 + len(after) + n: 1 + n for n in range(len(carried))},
        compiler_params=SOME,
        cost_estimate=COST,
        name="add_on",
    )(rank, own, got, *after, *carried)


def gain_column(gain_ref):
    return jnp.broadcast_to(gain_ref[...], (UNIT, KVL)).T


def page_kernel(requests, rank, slot, own_ref, *refs):
    count = len(requests)
    got_refs, sent_refs, refs = refs[:count], refs[count : 2 * count], refs[2 * count :]
    side_refs, (gain_ref, cos_ref, sin_ref) = refs[:2], refs[2:5]
    out_ref = refs[-1]
    step = pl.program_id(0)
    column = gain_column(gain_ref)

    def write(u, comp):
        rows = key_rows(comp, column, cos_ref[u], sin_ref[u]).astype(BF)
        out_ref[0, :, u * UNIT : (u + 1) * UNIT] = rows

    for k in range(count):

        @pl.when((step == k) & outer_rank(rank[0]))
        def _(k=k):
            for u in range(UNITS):
                write(u, own_ref[u] + decode(got_refs[k][u]))

        @pl.when((step == k) & ~outer_rank(rank[0]))
        def _(k=k):
            for u in range(UNITS):
                side = side_refs[u > 0][max(u - 1, 0)]
                write(u, decode(sent_refs[k][u]) + decode(side))


def pages_of(requests, rank, slot, own, got, sent, side, gain, cosine, sine, base, count, after):
    first = pl.BlockSpec((None, UNITS, CODED, UNIT), lambda i, *_: (0, 0, 0, 0))
    second = pl.BlockSpec((None, UNITS, CODED, UNIT), lambda i, *_: (1, 0, 0, 0))
    table = pl.BlockSpec((UNITS, HALF, UNIT), lambda i, *_: (0, 0, 0))
    start, total = requests[0], len(requests)
    got, sent = got[start : start + total], sent[start : start + total]
    return pl.pallas_call(
        functools.partial(page_kernel, requests),
        grid_spec=pltpu.PrefetchScalarGridSpec(
            num_scalar_prefetch=2,
            grid=(total,),
            in_specs=[
                pl.BlockSpec(
                    (UNITS, None, None, WIDTH, UNIT), lambda i, *_: (0, 0, i + start, 0, 0)
                ),
                *([first] * total),
                *([second] * total),
                pl.BlockSpec((1, None, CODED, UNIT), lambda i, *_: (0, i + start, 0, 0)),
                pl.BlockSpec((UNITS - 1, None, CODED, UNIT), lambda i, *_: (0, i + start, 0, 0)),
                pl.BlockSpec((1, KVL), lambda i, *_: (0, 0)),
                table,
                table,
                *([ANY] * (len(base) + len(after))),
            ],
            out_specs=pl.BlockSpec(
                (1, WIDTH, SHARE), lambda i, rank, slot: (slot[i + start], 0, 0)
            ),
        ),
        out_shape=jax.ShapeDtypeStruct((count, WIDTH, SHARE), BF),
        input_output_aliases={8 + 2 * total + n: n for n in range(len(base))},
        compiler_params=SOME,
        cost_estimate=COST,
        name="pages",
    )(rank, slot, own, *got, *sent, *side, gain, cosine, sine, *base, *after)


def query_kernel(lat_ref, up_ref, draft_ref, down_ref, *refs):
    *key_refs, cos_ref, sin_ref, out_ref, split_ref = refs

    @pl.when(pl.program_id(0) == 0)
    def _():
        rest = lax.dot_general(draft_ref[...], down_ref[...], NT, preferred_element_type=F32)
        for n in range(3):
            term = rest.astype(BF).astype(F32)
            split_ref[n] = term
            rest = rest - term
        split_ref[3] = jnp.zeros_like(rest)

    full = jnp.dot(lat_ref[...], up_ref[...], preferred_element_type=F32)
    for h, key_ref in enumerate(key_refs):
        base = h * (DN + DR)
        nope = full[:, base : base + DN].astype(BF)
        first = full[:, base + DN : base + DN + HALF]
        second = full[:, base + DN + HALF : base + DN + DR]
        absorbed = lax.dot_general(nope, key_ref[...], NT, preferred_element_type=F32)
        cosine, sine = cos_ref[...], sin_ref[...]
        out_ref[h] = jnp.concatenate(
            [absorbed, first * cosine - second * sine, first * sine + second * cosine], 1
        )


def queries(latents, q_up, kv_up, draft, down_t, cosine, sine, after):
    rows = latents.shape[0]
    heads = q_up.shape[1] // (DN + DR)
    step = 4
    key_spec = [
        pl.BlockSpec((KVL, DN), lambda i, h=h: (0, 2 * (step * i + h))) for h in range(step)
    ]
    whole = lambda i: (0, 0)
    table = pl.BlockSpec((rows, HALF), whole)
    body = lambda *refs: query_kernel(*refs[:-3], *refs[-2:])
    return pl.pallas_call(
        body,
        grid=(heads // step,),
        in_specs=[
            pl.BlockSpec((rows, QL), whole),
            pl.BlockSpec((QL, step * (DN + DR)), lambda i: (0, i)),
            pl.BlockSpec(draft.shape, whole),
            pl.BlockSpec(down_t.shape, whole),
            *key_spec,
            table,
            table,
            ANY,
        ],
        out_specs=[
            pl.BlockSpec((step, rows, WIDTH), lambda i: (i, 0, 0)),
            pl.BlockSpec((4, rows, WIDTH), lambda i: (0, 0, 0)),
        ],
        out_shape=[
            jax.ShapeDtypeStruct((heads, rows, WIDTH), F32),
            jax.ShapeDtypeStruct((4, rows, WIDTH), F32),
        ],
        compiler_params=ROOM,
        cost_estimate=COST,
        name="queries",
    )(latents, q_up, draft, down_t, *([kv_up] * step), cosine, sine, after)


def attend_kernel(requests, rank, first_ref, *refs):
    count = len(requests)
    q_refs, draft_refs, refs = refs[:4], refs[4:8], refs[8:]
    own_ref, got_refs, refs = refs[0], refs[1 : 1 + count], refs[1 + count :]
    cos_ref, sin_ref, midcos_ref, midsin_ref, refs = *refs[:4], refs[4:]
    segment_ref, gain_ref, newcos_ref, newsin_ref, refs = *refs[:4], refs[4:]
    out_refs, keys_ref = refs[-5:-1], refs[-1]
    step = pl.program_id(0)
    request = step + requests[0]

    @pl.when(rank[0] == 3)
    def _():
        column = gain_column(gain_ref)
        for k in range(count):

            @pl.when(step == k)
            def _(k=k):
                for i, (cosine, sine) in enumerate(
                    ((cos_ref, sin_ref), (midcos_ref, midsin_ref))
                ):
                    for u in range(UNITS):
                        comp = own_ref[u, i] + decode(got_refs[k][i, u])
                        rows = key_rows(comp, column, cosine[u], sine[u])
                        start = (1 - i) * SHARE + u * UNIT
                        keys_ref[:, start : start + UNIT] = rows.astype(BF)

        scale = (DN + DR) ** (-0.5)
        local_rows = out_refs[0].shape[1]
        new = 2 * RP
        comp = 0.0
        for ref in draft_refs:
            terms = ref[...].astype(F32)
            comp = comp + (terms[0:new] + terms[new : 2 * new] + terms[2 * new : 3 * new])
        lat = comp[:, :KVL]
        norm = lax.rsqrt(jnp.mean(lat * lat, axis=-1, keepdims=True) + 1e-06)
        first = comp[:, KVL : KVL + HALF]
        second = comp[:, KVL + HALF :]
        cosine, sine = newcos_ref[...], newsin_ref[...]
        drafts = jnp.concatenate(
            [
                lat * norm * gain_ref[...],
                first * cosine - second * sine,
                first * sine + second * cosine,
            ],
            1,
        )
        drafts = jnp.concatenate([drafts, jnp.zeros((UNIT - new, WIDTH), F32)], 0).astype(BF)
        query = jnp.concatenate([ref[...] for ref in q_refs], 0)
        scores = jnp.dot(query, keys_ref[...], preferred_element_type=F32) * scale
        segments = segment_ref[pl.ds(first_ref[0] + request, 1), :]
        valid = segments[:, PRE_TOK // 2 :] == segments[:, PRE_TOK - 1 :]
        scores = jnp.where(valid, scores, -1e30)
        fresh = lax.dot_general(query, drafts, NT, preferred_element_type=F32) * scale
        row = lax.broadcasted_iota(jnp.int32, fresh.shape, 0)
        late = (row % local_rows) // (local_rows // 2)
        offset = lax.broadcasted_iota(jnp.int32, fresh.shape, 1) - 2 * request
        fresh = jnp.where((offset >= 0) & (offset <= late), fresh, -1e30)
        top = jnp.maximum(
            jnp.max(scores, axis=1, keepdims=True), jnp.max(fresh, axis=1, keepdims=True)
        )
        weights = jnp.exp(scores - top)
        fresh = jnp.exp(fresh - top)
        total = jnp.sum(weights, axis=1, keepdims=True) + jnp.sum(fresh, axis=1, keepdims=True)
        numer = lax.dot_general(
            weights.astype(BF), keys_ref[0:KVL, :], NT, preferred_element_type=F32
        )
        numer = numer + jnp.dot(fresh.astype(BF), drafts[:, :KVL], preferred_element_type=F32)
        result = (numer / total).astype(BF)
        for t, ref in enumerate(out_refs):
            ref[0] = result[t * local_rows : (t + 1) * local_rows]


def attend(requests, rank, first, messages, own, got, tables, segments, gain, cosine, sine, after):
    new = 2 * RP
    local_rows = (messages[0].shape[0] - 4 * new) // RP
    last = RP * local_rows // (4 * new)
    start, count = requests[0], len(requests)
    got = got[start : start + count]
    out = jax.ShapeDtypeStruct((count, local_rows, KVL), BF)
    whole = lambda i, *_: (0, 0)
    whole3 = lambda i, *_: (0, 0, 0)
    return pl.pallas_call(
        functools.partial(attend_kernel, requests),
        grid_spec=pltpu.PrefetchScalarGridSpec(
            num_scalar_prefetch=2,
            grid=(count,),
            in_specs=[
                *([pl.BlockSpec((local_rows, WIDTH), lambda i, *_: (i + start, 0))] * 4),
                *([pl.BlockSpec((4 * new, WIDTH), lambda i, *_: (last, 0))] * 4),
                pl.BlockSpec(
                    (UNITS, 2, None, WIDTH, UNIT), lambda i, *_: (0, 0, i + start, 0, 0)
                ),
                *([pl.BlockSpec((2, UNITS, CODED, UNIT), lambda i, *_: (0, 0, 0, 0))] * count),
                *([pl.BlockSpec((UNITS, HALF, UNIT), whole3)] * 4),
                pl.BlockSpec(segments.shape, whole),
                pl.BlockSpec((1, KVL), whole),
                pl.BlockSpec(cosine.shape, whole),
                pl.BlockSpec(sine.shape, whole),
                *([ANY] * len(after)),
            ],
            out_specs=[pl.BlockSpec((1, local_rows, KVL), lambda i, *_: (i, 0, 0))] * 4,
            scratch_shapes=[pltpu.VMEM((WIDTH, 2 * SHARE), BF)],
        ),
        out_shape=[out] * 4,
        compiler_params=SOME,
        cost_estimate=COST,
        name="attend",
    )(rank, first, *messages, *messages, own, *got, *tables, segments, gain, cosine, sine, *after)


def heads_kernel(step, slot, o_ref, keep_ref, *refs):
    out_ref = refs[-1]
    out_ref[...] = jnp.zeros_like(out_ref)
    for h, value_ref in enumerate(refs[:step]):
        row = jnp.dot(o_ref[h].astype(BF), value_ref[...], preferred_element_type=F32)
        row = (row * keep_ref[...]).astype(BF)
        for r in range(RP):
            out_ref[slot[r], :, h * DV : (h + 1) * DV] = row[2 * r : 2 * r + 2]


def heads_out(slot, attended, keep, kv_up, count, after):
    heads, rows, _ = attended.shape
    step = 8
    value_spec = [
        pl.BlockSpec((KVL, DV), lambda i, slot, h=h: (0, 2 * (step * i + h) + 1))
        for h in range(step)
    ]
    return pl.pallas_call(
        functools.partial(heads_kernel, step),
        grid_spec=pltpu.PrefetchScalarGridSpec(
            num_scalar_prefetch=1,
            grid=(heads // step,),
            in_specs=[
                pl.BlockSpec((step, rows, KVL), lambda i, slot: (i, 0, 0)),
                pl.BlockSpec((rows, DV), lambda i, slot: (0, 0)),
                *value_spec,
                *([ANY] * len(after)),
            ],
            out_specs=pl.BlockSpec((count, 2, step * DV), lambda i, slot: (0, 0, i)),
        ),
        out_shape=jax.ShapeDtypeStruct((count, 2, heads * DV), BF),
        compiler_params=ROOM,
        cost_estimate=COST,
        name="heads_out",
    )(slot, attended, keep, *([kv_up] * step), *after)


def emit_kernel(pages_ref, placed_ref, out_ref, same_ref, done):
    copies = [
        pltpu.make_async_copy(pages_ref.at[n], out_ref.at[n], done.at[n])
        for n in range(pages_ref.shape[0])
    ]
    for copy in copies:
        copy.start()
    for copy in copies:
        copy.wait()


def emit(pages, placed):
    return pl.pallas_call(
        emit_kernel,
        in_specs=[ANY, ANY],
        out_specs=[ANY, ANY],
        out_shape=[
            jax.ShapeDtypeStruct(pages.shape, pages.dtype),
            jax.ShapeDtypeStruct(placed.shape, placed.dtype),
        ],
        scratch_shapes=[pltpu.SemaphoreType.DMA((pages.shape[0],))],
        input_output_aliases={1: 1},
        compiler_params=SOME,
        cost_estimate=COST,
        name="emit",
    )(pages, placed)


def rope_tables(position):
    freq = jnp.exp(-jnp.log(10000.0) * jnp.arange(HALF, dtype=F32) / HALF)
    angle = position.astype(F32)[..., None] * freq
    return jnp.cos(angle), jnp.sin(angle)


def local_line(
    prefill_hidden,
    draft_hidden,
    kv_down,
    kv_gain,
    query_latent,
    q_up,
    kv_up,
    owners,
    segment_ids,
    accepted,
):
    pd_count = lax.axis_size("pd")
    z = lax.axis_index("tp")
    p = lax.axis_index("pd")
    first_req = p * RP

    gain = kv_gain.reshape(1, KVL)
    rank = z.astype(jnp.int32).reshape(1)
    hidden = prefill_hidden.reshape(RP, PRE_TOK, prefill_hidden.shape[1])
    down_t = kv_down.T
    inward, across, outward = [(0, 1), (3, 2)], [(1, 2), (2, 1)], [(2, 3), (1, 0)]

    far_sums, inner, crossed, sent, outer = [], [], [], [], []

    def send_far(r, after):
        total, codes = project_far(rank, hidden, down_t, r, after)
        far_sums.append(total)
        inner.append(lax.ppermute(codes, "tp", inward))

    def first_hop(r, after, carried=()):
        block, *carried = add_on(rank, far_sums[r], inner[r], after=after, carried=carried)
        crossed.append(lax.ppermute(block, "tp", across))
        return [block, *carried]

    def second_hop(r, after):
        (block,) = add_on(rank, near_sums, crossed[r], r, after)
        sent.append(block)
        outer.append(lax.ppermute(block, "tp", outward))
        return [block]

    send_far(0, [])
    send_far(1, far_sums[:1])

    latents = lax.dynamic_slice_in_dim(query_latent, first_req, RP, 0).reshape(RP * 2, QL)
    new_pos = jnp.tile(PRE_TOK + jnp.arange(2, dtype=jnp.int32), RP)
    new_cos, new_sin = rope_tables(new_pos)
    query, terms = queries(
        latents, q_up, kv_up, draft_hidden, down_t, new_cos, new_sin, far_sums[1]
    )
    heads = query.shape[0]
    query = query.reshape(heads, RP, 2, WIDTH).transpose(1, 2, 0, 3)
    message = jnp.concatenate(
        [query.reshape(RP * 2 * heads, WIDTH), terms.reshape(8 * RP, WIDTH)], 0
    ).astype(BF)
    messages = [lax.ppermute(message, "tp", [(t, 3)]) for t in range(3)] + [message]

    done = first_hop(0, [message])
    send_far(2, done)
    near_sums, *side = project_near(rank, hidden, down_t, far_sums[2:])
    done = first_hop(1, [near_sums])
    done = second_hop(0, [*done, *messages[:3]])
    send_far(3, done)
    steps = jnp.arange(SHARE, dtype=jnp.int32).reshape(UNITS, UNIT)
    tables = [
        jnp.swapaxes(t, 1, 2)
        for t in (*rope_tables(z * SHARE + steps), *rope_tables(2 * SHARE + steps))
    ]
    block, side[0] = first_hop(2, far_sums[3:], side[:1])
    side = [lax.ppermute(codes, "tp", inward) for codes in side]
    done = second_hop(1, [block, outer[0]])
    done = first_hop(3, done)
    done = second_hop(2, [*done, outer[1], side[0], *tables])
    done = second_hop(3, [*done, outer[2]])

    def attend_to(requests, after):
        result = attend(
            requests,
            rank,
            first_req.astype(jnp.int32).reshape(1),
            messages,
            near_sums,
            outer,
            tables,
            segment_ids,
            gain,
            new_cos,
            new_sin,
            after,
        )
        return result, [lax.ppermute(result[t], "tp", [(3, t)]) for t in range(3)]

    my_owners = lax.dynamic_slice_in_dim(owners, first_req, RP, 0)
    early, late = tuple(range(RP - 1)), (RP - 1,)

    def pages_to(requests, base, after):
        return pages_of(
            requests,
            rank,
            my_owners,
            near_sums,
            outer,
            sent,
            side,
            gain,
            tables[0],
            tables[1],
            base,
            pd_count,
            after,
        )

    results, backs = [None] * 2, [None] * 2
    results[0], backs[0] = attend_to(early, done)
    base = [jnp.zeros((pd_count, WIDTH, SHARE), BF)] if pd_count > RP else []
    pages = pages_to(early, base, results[0][:1])
    pages = pages_to(late, [pages], backs[0])
    results[1], backs[1] = attend_to(late, [pages])
    cache = lax.all_to_all(pages, "pd", split_axis=0, concat_axis=0, tiled=True)

    attended = [
        jnp.where(z == 3, result[3], back[0] + back[1] + back[2])
        for result, back in zip(results, backs)
    ]
    attended = jnp.concatenate(attended, 0).reshape(RP, 2, heads, KVL).transpose(2, 0, 1, 3)
    attended = attended.reshape(heads, RP * 2, KVL).astype(F32)
    my_accepted = lax.dynamic_slice_in_dim(accepted, first_req, RP, 0)
    keep = (jnp.arange(2)[None, :] <= my_accepted[:, None]).astype(F32).reshape(RP * 2, 1)
    placed = heads_out(
        my_owners,
        attended,
        jnp.broadcast_to(keep, (RP * 2, DV)),
        kv_up,
        pd_count,
        [pages],
    )
    cache, placed = emit(cache, placed)
    placed = lax.all_to_all(placed, "pd", split_axis=0, concat_axis=0, tiled=True)
    return (placed.reshape(pd_count * 2, heads * DV), jnp.swapaxes(cache, 1, 2))


def solution(mesh):
    placed = (
        P(("groups", "pd"), "tp"),
        P(("groups", "pd"), "tp"),
        P("tp", None),
        P(),
        P("groups", None, None),
        P(None, "tp"),
        P(None, "tp"),
        P("groups"),
        P("groups", None),
        P("groups"),
    )
    return jax.shard_map(
        local_line if mesh.shape["tp"] == 4 else local_general,
        mesh=mesh,
        in_specs=placed,
        out_specs=(P(("groups", "pd"), "tp"), P(("groups", "pd"), "tp", None)),
        check_vma=False,
    )
```

```python
import functools

import jax
import jax.numpy as jnp
from jax import lax
from jax.experimental import pallas as pl
from jax.experimental.pallas import tpu as pltpu
from jax.sharding import PartitionSpec as P

DN = 128
DR = 64
DV = 128
KVL = 512
QL = 1536
PRE_TOK = 1536
RP = 4
WIDTH = KVL + DR
HALF = DR // 2
CODED = WIDTH + 16
SHARE = PRE_TOK // 4
UNIT = 128
UNITS = SHARE // UNIT
LANES = RP * UNIT
STEPS = 256.0
TOP = 32767.0
BF = jnp.bfloat16
F32 = jnp.float32
I16 = jnp.int16
NT = (((1,), (1,)), ((), ()))
ROOM = pltpu.CompilerParams(vmem_limit_bytes=60 << 20)
SOME = pltpu.CompilerParams(vmem_limit_bytes=52 << 20)
ANY = pl.BlockSpec(memory_space=pl.ANY)
VMEM = pl.BlockSpec(memory_space=pltpu.VMEM)
SMEM = pl.BlockSpec(memory_space=pltpu.SMEM)


COST = pl.CostEstimate(flops=1024, bytes_accessed=1024, transcendentals=0)


def rms_latent(comp, gain):
    lat = comp[:, :KVL]
    scale = lax.rsqrt(jnp.mean(lat * lat, axis=-1, keepdims=True) + 1e-06)
    return (lat * scale * gain).astype(jnp.bfloat16)


def rotate(values, position):
    half = values.shape[-1] // 2
    freq = jnp.exp(-jnp.log(10000.0) * jnp.arange(half, dtype=jnp.float32) / half)
    angle = position.astype(jnp.float32)[..., None] * freq
    cosine = jnp.cos(angle)
    sine = jnp.sin(angle)
    first = values[..., :half]
    second = values[..., half:]
    return jnp.concatenate([first * cosine - second * sine, first * sine + second * cosine], -1)


def block_stats(keys, q_lat, q_pos, valid):
    scale = (DN + DR) ** (-0.5)
    scores = jnp.einsum("jhk,tk->jht", q_lat, keys[:, :KVL], preferred_element_type=jnp.float32)
    scores = (
        scores + jnp.einsum("jhk,tk->jht", q_pos, keys[:, KVL:], preferred_element_type=jnp.float32)
    ) * scale
    scores = jnp.where(valid, scores, -1e30)
    top = jnp.max(scores, axis=-1)
    weights = jnp.where(valid, jnp.exp(scores - top[..., None]), 0.0)
    total = jnp.sum(weights, axis=-1)
    numer = jnp.einsum(
        "jht,tk->jhk",
        weights.astype(jnp.bfloat16),
        keys[:, :KVL],
        preferred_element_type=jnp.float32,
    )
    return (top, total, numer)


def combine(left, right):
    top = jnp.maximum(left[0], right[0])
    left_scale = jnp.exp(left[0] - top)
    right_scale = jnp.exp(right[0] - top)
    total = left[1] * left_scale + right[1] * right_scale
    numer = left[2] * left_scale[..., None] + right[2] * right_scale[..., None]
    return (top, total, numer)


def local_general(
    prefill_hidden,
    draft_hidden,
    kv_down,
    kv_gain,
    query_latent,
    q_up,
    kv_up,
    owners,
    segment_ids,
    accepted,
):
    tp_count = lax.axis_size("tp")
    pd_count = lax.axis_size("pd")
    tp_rank = lax.axis_index("tp")
    mine_rank = lax.axis_index("pd")
    requests = owners.shape[0]
    share = PRE_TOK // tp_count
    width = KVL + DR
    local_hidden = prefill_hidden.reshape(RP, PRE_TOK, prefill_hidden.shape[1])
    summed = lax.psum_scatter(
        jnp.einsum(
            "rtd,dw->trw", local_hidden, kv_down, preferred_element_type=jnp.float32
        ).reshape(lax.axis_size("tp") * share, RP * width),
        "tp",
        scatter_dimension=0,
        tiled=True,
    ).reshape(share * RP, width)
    draft_sum = lax.psum(jnp.dot(draft_hidden, kv_down, preferred_element_type=jnp.float32), "tp")
    first_req = mine_rank * RP
    row_pos = jnp.broadcast_to(
        tp_rank * share + jnp.arange(share, dtype=jnp.int32)[:, None], (share, RP)
    )
    page_rows = jnp.concatenate(
        [
            rms_latent(summed, kv_gain),
            rotate(summed[:, KVL:], row_pos.reshape(-1)).astype(jnp.bfloat16),
        ],
        1,
    )
    page_rows = page_rows.reshape(share, RP, width)
    draft_pos = jnp.tile(PRE_TOK + jnp.arange(2, dtype=jnp.int32), RP)
    draft_rows = jnp.concatenate(
        [
            rms_latent(draft_sum, kv_gain),
            rotate(draft_sum[:, KVL:], draft_pos).astype(jnp.bfloat16),
        ],
        1,
    )
    draft_rows = draft_rows.reshape(RP, 2, width)
    my_owners = lax.dynamic_slice_in_dim(owners, first_req, RP, 0)
    routing = (my_owners[None, :] == jnp.arange(pd_count, dtype=jnp.int32)[:, None]).astype(
        jnp.bfloat16
    )
    send_pages = jnp.einsum(
        "dk,tkw->dtw", routing, page_rows, preferred_element_type=jnp.float32
    ).astype(jnp.bfloat16)
    send_drafts = jnp.einsum(
        "dk,kjw->djw", routing, draft_rows, preferred_element_type=jnp.float32
    ).astype(jnp.bfloat16)
    pages, drafts = (
        lax.all_to_all(send_pages, "pd", split_axis=0, concat_axis=0, tiled=True),
        lax.all_to_all(send_drafts, "pd", split_axis=0, concat_axis=0, tiled=True),
    )
    heads_local = q_up.shape[1] // (DN + DR)
    query_full = jnp.dot(
        query_latent.reshape(requests * 2, QL), q_up, preferred_element_type=jnp.float32
    )
    query_full = query_full.reshape(requests, 2, heads_local, DN + DR)
    new_pos = jnp.broadcast_to(PRE_TOK + jnp.arange(2, dtype=jnp.int32)[None, :], (requests, 2))
    q_nope = query_full[..., :DN].astype(jnp.bfloat16)
    q_rot = rotate(query_full[..., DN:], new_pos[:, :, None]).astype(jnp.bfloat16)
    up_heads = kv_up.reshape(KVL, heads_local, DN + DV)
    w_value = up_heads[:, :, DN:]
    q_abs = jnp.einsum(
        "rjhd,khd->rjhk", q_nope, up_heads[:, :, :DN], preferred_element_type=jnp.float32
    ).astype(jnp.bfloat16)
    owner_table = owners.reshape(pd_count, RP) == mine_rank
    holding = jnp.sum(owner_table.astype(jnp.int32), axis=1)
    slot_of = jnp.sum(
        owner_table.astype(jnp.int32) * jnp.arange(RP, dtype=jnp.int32)[None, :], axis=1
    )
    owned_count = jnp.sum(holding)
    order = jnp.argsort((1 - holding) * pd_count + jnp.arange(pd_count, dtype=jnp.int32))
    draft_valid = (jnp.arange(2)[None, :] <= jnp.arange(2)[:, None])[:, None, :]
    empty = jnp.zeros((pd_count, 2, heads_local * DV), jnp.bfloat16)

    def finish(stats, source, request, q_lat, q_pos, result):
        stats = combine(stats, block_stats(drafts[source], q_lat, q_pos, draft_valid))
        attended = (stats[2] / stats[1][..., None]).astype(jnp.bfloat16)
        head_out = jnp.einsum("jhk,khd->jhd", attended, w_value, preferred_element_type=jnp.float32)
        keep = (jnp.arange(2) <= accepted[request]).astype(jnp.float32)[:, None, None]
        answer = (head_out * keep).astype(jnp.bfloat16).reshape(1, 2, heads_local * DV)
        return lax.dynamic_update_slice(result, answer, (source, 0, 0))

    def attend(turn, result):
        source = order[turn]
        request = source * RP + slot_of[source]
        q_lat = q_abs[request]
        q_pos = q_rot[request]
        seg_row = segment_ids[request]
        current = seg_row[PRE_TOK - 1]
        init = (
            jnp.full((2, heads_local), -1e30, jnp.float32),
            jnp.zeros((2, heads_local), jnp.float32),
            jnp.zeros((2, heads_local, KVL), jnp.float32),
        )
        valid = (seg_row == current)[None, None, :]
        stats = combine(
            init,
            block_stats(
                lax.all_gather(pages[source], "tp", axis=0, tiled=True), q_lat, q_pos, valid
            ),
        )
        return finish(stats, source, request, q_lat, q_pos, result)

    result = lax.fori_loop(0, owned_count, attend, empty)
    return (result.reshape(pd_count * 2, heads_local * DV), pages)


def encode(values):
    levels = []
    parts = []
    for first, last in ((0, KVL), (KVL, WIDTH)):
        block = values[first:last]
        top = jnp.maximum(jnp.max(jnp.abs(block), axis=0, keepdims=True), 1e-30)
        level = jnp.ceil(jnp.log2(top) * STEPS)
        codes = jnp.round(block * (jnp.exp2(level * (-1.0 / STEPS)) * TOP))
        parts.append(jnp.clip(codes, -TOP, TOP).astype(jnp.int32).astype(I16))
        levels.append(level.astype(jnp.int32))
    row = lax.broadcasted_iota(jnp.int32, (16, values.shape[1]), 0)
    extra = jnp.where(row == 0, levels[0], jnp.where(row == 1, levels[1], 0))
    return jnp.concatenate([*parts, extra.astype(I16)], 0)


def decode(codes):
    level = codes[WIDTH:CODED].astype(jnp.int32).astype(F32)
    step = jnp.exp2(level * (1.0 / STEPS)) * (1.0 / TOP)
    lat = codes[0:KVL].astype(jnp.int32).astype(F32) * step[0:1]
    rot = codes[KVL:WIDTH].astype(jnp.int32).astype(F32) * step[1:2]
    return jnp.concatenate([lat, rot], 0)


def key_rows(comp, gain, cosine, sine):
    lat = comp[:KVL]
    scale = lax.rsqrt(jnp.mean(lat * lat, axis=0, keepdims=True) + 1e-06)
    first = comp[KVL : KVL + HALF]
    second = comp[KVL + HALF :]
    return jnp.concatenate(
        [
            lat * scale * gain,
            first * cosine - second * sine,
            first * sine + second * cosine,
        ],
        0,
    )


def far(z, i):
    return jnp.where(z < 2, 3 - i, i)


def near(z, i):
    return jnp.where(z < 2, i, 3 - i)


def outer_rank(z):
    return (z == 0) | (z == 3)


def project_far_kernel(rank, hid_ref, down_ref, *refs):
    sum_ref, code_ref = refs[-2:]
    total = lax.dot_general(down_ref[...], hid_ref[0], NT, preferred_element_type=F32)
    for u in range(UNITS):
        sum_ref[0, u] = total[:, u * UNIT : (u + 1) * UNIT]

    @pl.when(outer_rank(rank[0]))
    def _():
        for u in range(UNITS):
            code_ref[0, u] = encode(total[:, u * UNIT : (u + 1) * UNIT])


def project_far(rank, hidden, down_t, request, after):
    depth = hidden.shape[-1]
    return pl.pallas_call(
        project_far_kernel,
        grid_spec=pltpu.PrefetchScalarGridSpec(
            num_scalar_prefetch=1,
            grid=(2,),
            in_specs=[
                pl.BlockSpec((1, SHARE, depth), lambda i, rank: (request, far(rank[0], i), 0)),
                VMEM,
                *([ANY] * len(after)),
            ],
            out_specs=[
                pl.BlockSpec((1, UNITS, WIDTH, UNIT), lambda i, rank: (i, 0, 0, 0)),
                pl.BlockSpec((1, UNITS, CODED, UNIT), lambda i, rank: (i, 0, 0, 0)),
            ],
        ),
        out_shape=[
            jax.ShapeDtypeStruct((2, UNITS, WIDTH, UNIT), F32),
            jax.ShapeDtypeStruct((2, UNITS, CODED, UNIT), I16),
        ],
        compiler_params=ROOM,
        cost_estimate=COST,
        name="project_far",
    )(rank, hidden, down_t, *after)


def project_near_kernel(rank, hid_ref, down_ref, *refs):
    sum_ref, *code_refs = refs[-3:]
    unit = pl.program_id(0)
    rows = hid_ref[...].reshape(LANES, hid_ref.shape[-1])
    total = lax.dot_general(down_ref[...], rows, NT, preferred_element_type=F32)
    for r in range(RP):
        sum_ref[0, 0, r] = total[:, r * UNIT : (r + 1) * UNIT]
    coded = outer_rank(rank[0]) & (pl.program_id(1) == 1)
    for mine, ref in zip((unit == 0, unit > 0), code_refs):

        @pl.when(coded & mine)
        def _(ref=ref):
            for r in range(RP):
                ref[0, r] = encode(total[:, r * UNIT : (r + 1) * UNIT])


def project_near(rank, hidden, down_t, after):
    depth = hidden.shape[-1]
    return pl.pallas_call(
        project_near_kernel,
        grid_spec=pltpu.PrefetchScalarGridSpec(
            num_scalar_prefetch=1,
            grid=(UNITS, 2),
            in_specs=[
                pl.BlockSpec(
                    (RP, UNIT, depth), lambda u, i, rank: (0, near(rank[0], i) * UNITS + u, 0)
                ),
                VMEM,
                *([ANY] * len(after)),
            ],
            out_specs=[
                pl.BlockSpec((1, 1, RP, WIDTH, UNIT), lambda u, i, rank: (u, i, 0, 0, 0)),
                pl.BlockSpec((1, RP, CODED, UNIT), lambda u, i, rank: (0, 0, 0, 0)),
                pl.BlockSpec(
                    (1, RP, CODED, UNIT), lambda u, i, rank: (jnp.maximum(u, 1) - 1, 0, 0, 0)
                ),
            ],
        ),
        out_shape=[
            jax.ShapeDtypeStruct((UNITS, 2, RP, WIDTH, UNIT), F32),
            jax.ShapeDtypeStruct((1, RP, CODED, UNIT), I16),
            jax.ShapeDtypeStruct((UNITS - 1, RP, CODED, UNIT), I16),
        ],
        compiler_params=ROOM,
        cost_estimate=COST,
        name="project_near",
    )(rank, hidden, down_t, *after)


def add_kernel(out_at, rank, own_ref, got_ref, *refs):
    @pl.when(~outer_rank(rank[0]))
    def _():
        for u in range(UNITS):
            refs[out_at][0, u] = encode(own_ref[u] + decode(got_ref[0, u]))


def add_on(rank, own, got, request=None, after=(), carried=()):
    chunk = lambda i, rank: (i, 0, 0, 0)
    if request is None:
        own_spec = pl.BlockSpec((None, UNITS, WIDTH, UNIT), chunk)
    else:
        own_spec = pl.BlockSpec(
            (UNITS, None, None, WIDTH, UNIT), lambda i, rank: (0, i, request, 0, 0)
        )
    return pl.pallas_call(
        functools.partial(add_kernel, -1 - len(carried)),
        grid_spec=pltpu.PrefetchScalarGridSpec(
            num_scalar_prefetch=1,
            grid=(2,),
            in_specs=[
                own_spec,
                pl.BlockSpec((1, UNITS, CODED, UNIT), chunk),
                *([ANY] * (len(after) + len(carried))),
            ],
            out_specs=[
                pl.BlockSpec((1, UNITS, CODED, UNIT), chunk),
                *([ANY] * len(carried)),
            ],
        ),
        out_shape=[
            jax.ShapeDtypeStruct((2, UNITS, CODED, UNIT), I16),
            *[jax.ShapeDtypeStruct(c.shape, c.dtype) for c in carried],
        ],
        input_output_aliases={3 + len(after) + n: 1 + n for n in range(len(carried))},
        compiler_params=SOME,
        cost_estimate=COST,
        name="add_on",
    )(rank, own, got, *after, *carried)


def hold_kernel(*refs):
    pass


def hold(block, after):
    return pl.pallas_call(
        hold_kernel,
        in_specs=[ANY] * (1 + len(after)),
        out_specs=ANY,
        out_shape=jax.ShapeDtypeStruct(block.shape, block.dtype),
        input_output_aliases={0: 0},
        compiler_params=SOME,
        cost_estimate=COST,
        name="hold",
    )(block, *after)


def gain_column(gain_ref):
    return jnp.broadcast_to(gain_ref[...], (UNIT, KVL)).T


def page_kernel(requests, rank, slot, own_ref, *refs):
    count = len(requests)
    got_refs, sent_refs, refs = refs[:count], refs[count : 2 * count], refs[2 * count :]
    side_refs, (gain_ref, cos_ref, sin_ref) = refs[:2], refs[2:5]
    out_ref = refs[-1]
    step = pl.program_id(0)
    column = gain_column(gain_ref)

    def write(u, comp):
        rows = key_rows(comp, column, cos_ref[u], sin_ref[u]).astype(BF)
        out_ref[0, :, u * UNIT : (u + 1) * UNIT] = rows

    for k in range(count):

        @pl.when((step == k) & outer_rank(rank[0]))
        def _(k=k):
            for u in range(UNITS):
                write(u, own_ref[u] + decode(got_refs[k][u]))

        @pl.when((step == k) & ~outer_rank(rank[0]))
        def _(k=k):
            for u in range(UNITS):
                side = side_refs[u > 0][max(u - 1, 0)]
                write(u, decode(sent_refs[k][u]) + decode(side))


def pages_of(requests, rank, slot, own, got, sent, side, gain, cosine, sine, base, count, after):
    first = pl.BlockSpec((None, UNITS, CODED, UNIT), lambda i, *_: (0, 0, 0, 0))
    second = pl.BlockSpec((None, UNITS, CODED, UNIT), lambda i, *_: (1, 0, 0, 0))
    table = pl.BlockSpec((UNITS, HALF, UNIT), lambda i, *_: (0, 0, 0))
    start, total = requests[0], len(requests)
    got, sent = got[start : start + total], sent[start : start + total]
    return pl.pallas_call(
        functools.partial(page_kernel, requests),
        grid_spec=pltpu.PrefetchScalarGridSpec(
            num_scalar_prefetch=2,
            grid=(total,),
            in_specs=[
                pl.BlockSpec(
                    (UNITS, None, None, WIDTH, UNIT), lambda i, *_: (0, 0, i + start, 0, 0)
                ),
                *([first] * total),
                *([second] * total),
                pl.BlockSpec((1, None, CODED, UNIT), lambda i, *_: (0, i + start, 0, 0)),
                pl.BlockSpec((UNITS - 1, None, CODED, UNIT), lambda i, *_: (0, i + start, 0, 0)),
                pl.BlockSpec((1, KVL), lambda i, *_: (0, 0)),
                table,
                table,
                *([ANY] * (len(base) + len(after))),
            ],
            out_specs=pl.BlockSpec(
                (1, WIDTH, SHARE), lambda i, rank, slot: (slot[i + start], 0, 0)
            ),
        ),
        out_shape=jax.ShapeDtypeStruct((count, WIDTH, SHARE), BF),
        input_output_aliases={8 + 2 * total + n: n for n in range(len(base))},
        compiler_params=SOME,
        cost_estimate=COST,
        name="pages",
    )(rank, slot, own, *got, *sent, *side, gain, cosine, sine, *base, *after)


def query_kernel(lat_ref, up_ref, draft_ref, down_ref, *refs):
    *key_refs, cos_ref, sin_ref, out_ref, split_ref = refs

    @pl.when(pl.program_id(0) == 0)
    def _():
        rest = lax.dot_general(draft_ref[...], down_ref[...], NT, preferred_element_type=F32)
        for n in range(3):
            term = rest.astype(BF).astype(F32)
            split_ref[n] = term
            rest = rest - term
        split_ref[3] = jnp.zeros_like(rest)

    full = jnp.dot(lat_ref[...], up_ref[...], preferred_element_type=F32)
    for h, key_ref in enumerate(key_refs):
        base = h * (DN + DR)
        nope = full[:, base : base + DN].astype(BF)
        first = full[:, base + DN : base + DN + HALF]
        second = full[:, base + DN + HALF : base + DN + DR]
        absorbed = lax.dot_general(nope, key_ref[...], NT, preferred_element_type=F32)
        cosine, sine = cos_ref[...], sin_ref[...]
        out_ref[h] = jnp.concatenate(
            [absorbed, first * cosine - second * sine, first * sine + second * cosine], 1
        )


def queries(latents, q_up, kv_up, draft, down_t, cosine, sine, after):
    rows = latents.shape[0]
    heads = q_up.shape[1] // (DN + DR)
    step = 4
    key_spec = [
        pl.BlockSpec((KVL, DN), lambda i, h=h: (0, 2 * (step * i + h))) for h in range(step)
    ]
    whole = lambda i: (0, 0)
    table = pl.BlockSpec((rows, HALF), whole)
    body = lambda *refs: query_kernel(*refs[:-3], *refs[-2:])
    return pl.pallas_call(
        body,
        grid=(heads // step,),
        in_specs=[
            pl.BlockSpec((rows, QL), whole),
            pl.BlockSpec((QL, step * (DN + DR)), lambda i: (0, i)),
            pl.BlockSpec(draft.shape, whole),
            pl.BlockSpec(down_t.shape, whole),
            *key_spec,
            table,
            table,
            ANY,
        ],
        out_specs=[
            pl.BlockSpec((step, rows, WIDTH), lambda i: (i, 0, 0)),
            pl.BlockSpec((4, rows, WIDTH), lambda i: (0, 0, 0)),
        ],
        out_shape=[
            jax.ShapeDtypeStruct((heads, rows, WIDTH), F32),
            jax.ShapeDtypeStruct((4, rows, WIDTH), F32),
        ],
        compiler_params=ROOM,
        cost_estimate=COST,
        name="queries",
    )(latents, q_up, draft, down_t, *([kv_up] * step), cosine, sine, after)


def attend_kernel(requests, rank, first_ref, *refs):
    count = len(requests)
    q_refs, draft_refs, refs = refs[:4], refs[4:8], refs[8:]
    own_ref, got_refs, refs = refs[0], refs[1 : 1 + count], refs[1 + count :]
    cos_ref, sin_ref, midcos_ref, midsin_ref, refs = *refs[:4], refs[4:]
    segment_ref, gain_ref, newcos_ref, newsin_ref, refs = *refs[:4], refs[4:]
    out_refs, keys_ref = refs[-5:-1], refs[-1]
    step = pl.program_id(0)
    request = step + requests[0]

    @pl.when(rank[0] == 3)
    def _():
        column = gain_column(gain_ref)
        for k in range(count):

            @pl.when(step == k)
            def _(k=k):
                for i, (cosine, sine) in enumerate(
                    ((cos_ref, sin_ref), (midcos_ref, midsin_ref))
                ):
                    for u in range(UNITS):
                        comp = own_ref[u, i] + decode(got_refs[k][i, u])
                        rows = key_rows(comp, column, cosine[u], sine[u])
                        start = (1 - i) * SHARE + u * UNIT
                        keys_ref[:, start : start + UNIT] = rows.astype(BF)

        scale = (DN + DR) ** (-0.5)
        local_rows = out_refs[0].shape[1]
        new = 2 * RP
        comp = 0.0
        for ref in draft_refs:
            terms = ref[...].astype(F32)
            comp = comp + (terms[0:new] + terms[new : 2 * new] + terms[2 * new : 3 * new])
        lat = comp[:, :KVL]
        norm = lax.rsqrt(jnp.mean(lat * lat, axis=-1, keepdims=True) + 1e-06)
        first = comp[:, KVL : KVL + HALF]
        second = comp[:, KVL + HALF :]
        cosine, sine = newcos_ref[...], newsin_ref[...]
        drafts = jnp.concatenate(
            [
                lat * norm * gain_ref[...],
                first * cosine - second * sine,
                first * sine + second * cosine,
            ],
            1,
        )
        drafts = jnp.concatenate([drafts, jnp.zeros((UNIT - new, WIDTH), F32)], 0).astype(BF)
        query = jnp.concatenate([ref[...] for ref in q_refs], 0)
        scores = jnp.dot(query, keys_ref[...], preferred_element_type=F32) * scale
        segments = segment_ref[pl.ds(first_ref[0] + request, 1), :]
        valid = segments[:, PRE_TOK // 2 :] == segments[:, PRE_TOK - 1 :]
        scores = jnp.where(valid, scores, -1e30)
        fresh = lax.dot_general(query, drafts, NT, preferred_element_type=F32) * scale
        row = lax.broadcasted_iota(jnp.int32, fresh.shape, 0)
        late = (row % local_rows) // (local_rows // 2)
        offset = lax.broadcasted_iota(jnp.int32, fresh.shape, 1) - 2 * request
        fresh = jnp.where((offset >= 0) & (offset <= late), fresh, -1e30)
        top = jnp.maximum(
            jnp.max(scores, axis=1, keepdims=True), jnp.max(fresh, axis=1, keepdims=True)
        )
        weights = jnp.exp(scores - top)
        fresh = jnp.exp(fresh - top)
        total = jnp.sum(weights, axis=1, keepdims=True) + jnp.sum(fresh, axis=1, keepdims=True)
        numer = lax.dot_general(
            weights.astype(BF), keys_ref[0:KVL, :], NT, preferred_element_type=F32
        )
        numer = numer + jnp.dot(fresh.astype(BF), drafts[:, :KVL], preferred_element_type=F32)
        result = (numer / total).astype(BF)
        for t, ref in enumerate(out_refs):
            ref[0] = result[t * local_rows : (t + 1) * local_rows]


def attend(requests, rank, first, messages, own, got, tables, segments, gain, cosine, sine, after):
    new = 2 * RP
    local_rows = (messages[0].shape[0] - 4 * new) // RP
    last = RP * local_rows // (4 * new)
    start, count = requests[0], len(requests)
    got = got[start : start + count]
    out = jax.ShapeDtypeStruct((count, local_rows, KVL), BF)
    whole = lambda i, *_: (0, 0)
    whole3 = lambda i, *_: (0, 0, 0)
    return pl.pallas_call(
        functools.partial(attend_kernel, requests),
        grid_spec=pltpu.PrefetchScalarGridSpec(
            num_scalar_prefetch=2,
            grid=(count,),
            in_specs=[
                *([pl.BlockSpec((local_rows, WIDTH), lambda i, *_: (i + start, 0))] * 4),
                *([pl.BlockSpec((4 * new, WIDTH), lambda i, *_: (last, 0))] * 4),
                pl.BlockSpec(
                    (UNITS, 2, None, WIDTH, UNIT), lambda i, *_: (0, 0, i + start, 0, 0)
                ),
                *([pl.BlockSpec((2, UNITS, CODED, UNIT), lambda i, *_: (0, 0, 0, 0))] * count),
                *([pl.BlockSpec((UNITS, HALF, UNIT), whole3)] * 4),
                pl.BlockSpec(segments.shape, whole),
                pl.BlockSpec((1, KVL), whole),
                pl.BlockSpec(cosine.shape, whole),
                pl.BlockSpec(sine.shape, whole),
                *([ANY] * len(after)),
            ],
            out_specs=[pl.BlockSpec((1, local_rows, KVL), lambda i, *_: (i, 0, 0))] * 4,
            scratch_shapes=[pltpu.VMEM((WIDTH, 2 * SHARE), BF)],
        ),
        out_shape=[out] * 4,
        compiler_params=SOME,
        cost_estimate=COST,
        name="attend",
    )(rank, first, *messages, *messages, own, *got, *tables, segments, gain, cosine, sine, *after)


def heads_kernel(step, slot, o_ref, keep_ref, *refs):
    out_ref = refs[-1]
    out_ref[...] = jnp.zeros_like(out_ref)
    for h, value_ref in enumerate(refs[:step]):
        row = jnp.dot(o_ref[h].astype(BF), value_ref[...], preferred_element_type=F32)
        row = (row * keep_ref[...]).astype(BF)
        for r in range(RP):
            out_ref[slot[r], :, h * DV : (h + 1) * DV] = row[2 * r : 2 * r + 2]


def heads_out(slot, attended, keep, kv_up, count, after):
    heads, rows, _ = attended.shape
    step = 8
    value_spec = [
        pl.BlockSpec((KVL, DV), lambda i, slot, h=h: (0, 2 * (step * i + h) + 1))
        for h in range(step)
    ]
    return pl.pallas_call(
        functools.partial(heads_kernel, step),
        grid_spec=pltpu.PrefetchScalarGridSpec(
            num_scalar_prefetch=1,
            grid=(heads // step,),
            in_specs=[
                pl.BlockSpec((step, rows, KVL), lambda i, slot: (i, 0, 0)),
                pl.BlockSpec((rows, DV), lambda i, slot: (0, 0)),
                *value_spec,
                *([ANY] * len(after)),
            ],
            out_specs=pl.BlockSpec((count, 2, step * DV), lambda i, slot: (0, 0, i)),
        ),
        out_shape=jax.ShapeDtypeStruct((count, 2, heads * DV), BF),
        compiler_params=ROOM,
        cost_estimate=COST,
        name="heads_out",
    )(slot, attended, keep, *([kv_up] * step), *after)


def emit_kernel(pages_ref, placed_ref, out_ref, same_ref, done):
    copies = [
        pltpu.make_async_copy(pages_ref.at[n], out_ref.at[n], done.at[n])
        for n in range(pages_ref.shape[0])
    ]
    for copy in copies:
        copy.start()
    for copy in copies:
        copy.wait()


def emit(pages, placed):
    return pl.pallas_call(
        emit_kernel,
        in_specs=[ANY, ANY],
        out_specs=[ANY, ANY],
        out_shape=[
            jax.ShapeDtypeStruct(pages.shape, pages.dtype),
            jax.ShapeDtypeStruct(placed.shape, placed.dtype),
        ],
        scratch_shapes=[pltpu.SemaphoreType.DMA((pages.shape[0],))],
        input_output_aliases={1: 1},
        compiler_params=SOME,
        cost_estimate=COST,
        name="emit",
    )(pages, placed)


def rope_tables(position):
    freq = jnp.exp(-jnp.log(10000.0) * jnp.arange(HALF, dtype=F32) / HALF)
    angle = position.astype(F32)[..., None] * freq
    return jnp.cos(angle), jnp.sin(angle)


def local_line(
    prefill_hidden,
    draft_hidden,
    kv_down,
    kv_gain,
    query_latent,
    q_up,
    kv_up,
    owners,
    segment_ids,
    accepted,
):
    pd_count = lax.axis_size("pd")
    z = lax.axis_index("tp")
    p = lax.axis_index("pd")
    first_req = p * RP

    gain = kv_gain.reshape(1, KVL)
    rank = z.astype(jnp.int32).reshape(1)
    hidden = prefill_hidden.reshape(RP, PRE_TOK, prefill_hidden.shape[1])
    down_t = kv_down.T
    inward, across, outward = [(0, 1), (3, 2)], [(1, 2), (2, 1)], [(2, 3), (1, 0)]

    far_sums, inner, crossed, sent, outer = [], [], [], [], []

    def send_far(r, after):
        total, codes = project_far(rank, hidden, down_t, r, after)
        far_sums.append(total)
        inner.append(lax.ppermute(codes, "tp", inward))

    def first_hop(r, after, carried=()):
        block, *carried = add_on(rank, far_sums[r], inner[r], after=after, carried=carried)
        crossed.append(lax.ppermute(block, "tp", across))
        return [block, *carried]

    def second_hop(r, after, awaited=()):
        (block,) = add_on(rank, near_sums, crossed[r], r, after)
        if awaited:
            block = hold(block, awaited)
        sent.append(block)
        outer.append(lax.ppermute(block, "tp", outward))
        return [block]

    send_far(0, [])
    send_far(1, far_sums[:1])

    latents = lax.dynamic_slice_in_dim(query_latent, first_req, RP, 0).reshape(RP * 2, QL)
    new_pos = jnp.tile(PRE_TOK + jnp.arange(2, dtype=jnp.int32), RP)
    new_cos, new_sin = rope_tables(new_pos)
    query, terms = queries(
        latents, q_up, kv_up, draft_hidden, down_t, new_cos, new_sin, far_sums[1]
    )
    heads = query.shape[0]
    query = query.reshape(heads, RP, 2, WIDTH).transpose(1, 2, 0, 3)
    message = jnp.concatenate(
        [query.reshape(RP * 2 * heads, WIDTH), terms.reshape(8 * RP, WIDTH)], 0
    ).astype(BF)
    messages = [lax.ppermute(message, "tp", [(t, 3)]) for t in range(3)] + [message]

    done = first_hop(0, [message])
    send_far(2, done)
    near_sums, *side = project_near(rank, hidden, down_t, far_sums[2:])
    done = first_hop(1, [near_sums])
    done = second_hop(0, [*done, *messages[:3]])
    send_far(3, done)
    steps = jnp.arange(SHARE, dtype=jnp.int32).reshape(UNITS, UNIT)
    tables = [
        jnp.swapaxes(t, 1, 2)
        for t in (*rope_tables(z * SHARE + steps), *rope_tables(2 * SHARE + steps))
    ]
    block, side[0] = first_hop(2, far_sums[3:], side[:1])
    side = [lax.ppermute(codes, "tp", inward) for codes in side]
    done = second_hop(1, [block], outer[:1])
    done = first_hop(3, done)
    done = second_hop(2, [*done, *tables], [outer[1], side[0]])
    done = second_hop(3, done, outer[2:])

    def attend_to(requests, after):
        result = attend(
            requests,
            rank,
            first_req.astype(jnp.int32).reshape(1),
            messages,
            near_sums,
            outer,
            tables,
            segment_ids,
            gain,
            new_cos,
            new_sin,
            after,
        )
        return result, [lax.ppermute(result[t], "tp", [(3, t)]) for t in range(3)]

    my_owners = lax.dynamic_slice_in_dim(owners, first_req, RP, 0)
    early, late = tuple(range(RP - 1)), (RP - 1,)

    def pages_to(requests, base, after):
        return pages_of(
            requests,
            rank,
            my_owners,
            near_sums,
            outer,
            sent,
            side,
            gain,
            tables[0],
            tables[1],
            base,
            pd_count,
            after,
        )

    results, backs = [None] * 2, [None] * 2
    results[0], backs[0] = attend_to(early, done)
    base = [jnp.zeros((pd_count, WIDTH, SHARE), BF)] if pd_count > RP else []
    pages = pages_to(early, base, results[0][:1])
    pages = pages_to(late, [pages], [])
    results[1], backs[1] = attend_to(late, [pages, *backs[0]])
    cache = lax.all_to_all(pages, "pd", split_axis=0, concat_axis=0, tiled=True)

    attended = [
        jnp.where(z == 3, result[3], back[0] + back[1] + back[2])
        for result, back in zip(results, backs)
    ]
    attended = jnp.concatenate(attended, 0).reshape(RP, 2, heads, KVL).transpose(2, 0, 1, 3)
    attended = attended.reshape(heads, RP * 2, KVL).astype(F32)
    my_accepted = lax.dynamic_slice_in_dim(accepted, first_req, RP, 0)
    keep = (jnp.arange(2)[None, :] <= my_accepted[:, None]).astype(F32).reshape(RP * 2, 1)
    placed = heads_out(
        my_owners,
        attended,
        jnp.broadcast_to(keep, (RP * 2, DV)),
        kv_up,
        pd_count,
        [pages],
    )
    cache, placed = emit(cache, placed)
    placed = lax.all_to_all(placed, "pd", split_axis=0, concat_axis=0, tiled=True)
    return (placed.reshape(pd_count * 2, heads * DV), jnp.swapaxes(cache, 1, 2))


def solution(mesh):
    placed = (
        P(("groups", "pd"), "tp"),
        P(("groups", "pd"), "tp"),
        P("tp", None),
        P(),
        P("groups", None, None),
        P(None, "tp"),
        P(None, "tp"),
        P("groups"),
        P("groups", None),
        P("groups"),
    )
    return jax.shard_map(
        local_line if mesh.shape["tp"] == 4 else local_general,
        mesh=mesh,
        in_specs=placed,
        out_specs=(P(("groups", "pd"), "tp"), P(("groups", "pd"), "tp", None)),
        check_vma=False,
    )
```

```python
import functools

import jax
import jax.numpy as jnp
from jax import lax
from jax.experimental import pallas as pl
from jax.experimental.pallas import tpu as pltpu
from jax.sharding import PartitionSpec as P

DN = 128
DR = 64
DV = 128
KVL = 512
QL = 1536
PRE_TOK = 1536
RP = 4
WIDTH = KVL + DR
HALF = DR // 2
CODED = WIDTH + 16
SHARE = PRE_TOK // 4
UNIT = 128
UNITS = SHARE // UNIT
LANES = RP * UNIT
STEPS = 256.0
TOP = 32767.0
BF = jnp.bfloat16
F32 = jnp.float32
I16 = jnp.int16
NT = (((1,), (1,)), ((), ()))
ROOM = pltpu.CompilerParams(vmem_limit_bytes=60 << 20)
SOME = pltpu.CompilerParams(vmem_limit_bytes=52 << 20)
ANY = pl.BlockSpec(memory_space=pl.ANY)
VMEM = pl.BlockSpec(memory_space=pltpu.VMEM)
SMEM = pl.BlockSpec(memory_space=pltpu.SMEM)


COST = pl.CostEstimate(flops=1024, bytes_accessed=1024, transcendentals=0)


def rms_latent(comp, gain):
    lat = comp[:, :KVL]
    scale = lax.rsqrt(jnp.mean(lat * lat, axis=-1, keepdims=True) + 1e-06)
    return (lat * scale * gain).astype(jnp.bfloat16)


def rotate(values, position):
    half = values.shape[-1] // 2
    freq = jnp.exp(-jnp.log(10000.0) * jnp.arange(half, dtype=jnp.float32) / half)
    angle = position.astype(jnp.float32)[..., None] * freq
    cosine = jnp.cos(angle)
    sine = jnp.sin(angle)
    first = values[..., :half]
    second = values[..., half:]
    return jnp.concatenate([first * cosine - second * sine, first * sine + second * cosine], -1)


def block_stats(keys, q_lat, q_pos, valid):
    scale = (DN + DR) ** (-0.5)
    scores = jnp.einsum("jhk,tk->jht", q_lat, keys[:, :KVL], preferred_element_type=jnp.float32)
    scores = (
        scores + jnp.einsum("jhk,tk->jht", q_pos, keys[:, KVL:], preferred_element_type=jnp.float32)
    ) * scale
    scores = jnp.where(valid, scores, -1e30)
    top = jnp.max(scores, axis=-1)
    weights = jnp.where(valid, jnp.exp(scores - top[..., None]), 0.0)
    total = jnp.sum(weights, axis=-1)
    numer = jnp.einsum(
        "jht,tk->jhk",
        weights.astype(jnp.bfloat16),
        keys[:, :KVL],
        preferred_element_type=jnp.float32,
    )
    return (top, total, numer)


def combine(left, right):
    top = jnp.maximum(left[0], right[0])
    left_scale = jnp.exp(left[0] - top)
    right_scale = jnp.exp(right[0] - top)
    total = left[1] * left_scale + right[1] * right_scale
    numer = left[2] * left_scale[..., None] + right[2] * right_scale[..., None]
    return (top, total, numer)


def local_general(
    prefill_hidden,
    draft_hidden,
    kv_down,
    kv_gain,
    query_latent,
    q_up,
    kv_up,
    owners,
    segment_ids,
    accepted,
):
    tp_count = lax.axis_size("tp")
    pd_count = lax.axis_size("pd")
    tp_rank = lax.axis_index("tp")
    mine_rank = lax.axis_index("pd")
    requests = owners.shape[0]
    share = PRE_TOK // tp_count
    width = KVL + DR
    local_hidden = prefill_hidden.reshape(RP, PRE_TOK, prefill_hidden.shape[1])
    summed = lax.psum_scatter(
        jnp.einsum(
            "rtd,dw->trw", local_hidden, kv_down, preferred_element_type=jnp.float32
        ).reshape(lax.axis_size("tp") * share, RP * width),
        "tp",
        scatter_dimension=0,
        tiled=True,
    ).reshape(share * RP, width)
    draft_sum = lax.psum(jnp.dot(draft_hidden, kv_down, preferred_element_type=jnp.float32), "tp")
    first_req = mine_rank * RP
    row_pos = jnp.broadcast_to(
        tp_rank * share + jnp.arange(share, dtype=jnp.int32)[:, None], (share, RP)
    )
    page_rows = jnp.concatenate(
        [
            rms_latent(summed, kv_gain),
            rotate(summed[:, KVL:], row_pos.reshape(-1)).astype(jnp.bfloat16),
        ],
        1,
    )
    page_rows = page_rows.reshape(share, RP, width)
    draft_pos = jnp.tile(PRE_TOK + jnp.arange(2, dtype=jnp.int32), RP)
    draft_rows = jnp.concatenate(
        [
            rms_latent(draft_sum, kv_gain),
            rotate(draft_sum[:, KVL:], draft_pos).astype(jnp.bfloat16),
        ],
        1,
    )
    draft_rows = draft_rows.reshape(RP, 2, width)
    my_owners = lax.dynamic_slice_in_dim(owners, first_req, RP, 0)
    routing = (my_owners[None, :] == jnp.arange(pd_count, dtype=jnp.int32)[:, None]).astype(
        jnp.bfloat16
    )
    send_pages = jnp.einsum(
        "dk,tkw->dtw", routing, page_rows, preferred_element_type=jnp.float32
    ).astype(jnp.bfloat16)
    send_drafts = jnp.einsum(
        "dk,kjw->djw", routing, draft_rows, preferred_element_type=jnp.float32
    ).astype(jnp.bfloat16)
    pages, drafts = (
        lax.all_to_all(send_pages, "pd", split_axis=0, concat_axis=0, tiled=True),
        lax.all_to_all(send_drafts, "pd", split_axis=0, concat_axis=0, tiled=True),
    )
    heads_local = q_up.shape[1] // (DN + DR)
    query_full = jnp.dot(
        query_latent.reshape(requests * 2, QL), q_up, preferred_element_type=jnp.float32
    )
    query_full = query_full.reshape(requests, 2, heads_local, DN + DR)
    new_pos = jnp.broadcast_to(PRE_TOK + jnp.arange(2, dtype=jnp.int32)[None, :], (requests, 2))
    q_nope = query_full[..., :DN].astype(jnp.bfloat16)
    q_rot = rotate(query_full[..., DN:], new_pos[:, :, None]).astype(jnp.bfloat16)
    up_heads = kv_up.reshape(KVL, heads_local, DN + DV)
    w_value = up_heads[:, :, DN:]
    q_abs = jnp.einsum(
        "rjhd,khd->rjhk", q_nope, up_heads[:, :, :DN], preferred_element_type=jnp.float32
    ).astype(jnp.bfloat16)
    owner_table = owners.reshape(pd_count, RP) == mine_rank
    holding = jnp.sum(owner_table.astype(jnp.int32), axis=1)
    slot_of = jnp.sum(
        owner_table.astype(jnp.int32) * jnp.arange(RP, dtype=jnp.int32)[None, :], axis=1
    )
    owned_count = jnp.sum(holding)
    order = jnp.argsort((1 - holding) * pd_count + jnp.arange(pd_count, dtype=jnp.int32))
    draft_valid = (jnp.arange(2)[None, :] <= jnp.arange(2)[:, None])[:, None, :]
    empty = jnp.zeros((pd_count, 2, heads_local * DV), jnp.bfloat16)

    def finish(stats, source, request, q_lat, q_pos, result):
        stats = combine(stats, block_stats(drafts[source], q_lat, q_pos, draft_valid))
        attended = (stats[2] / stats[1][..., None]).astype(jnp.bfloat16)
        head_out = jnp.einsum("jhk,khd->jhd", attended, w_value, preferred_element_type=jnp.float32)
        keep = (jnp.arange(2) <= accepted[request]).astype(jnp.float32)[:, None, None]
        answer = (head_out * keep).astype(jnp.bfloat16).reshape(1, 2, heads_local * DV)
        return lax.dynamic_update_slice(result, answer, (source, 0, 0))

    def attend(turn, result):
        source = order[turn]
        request = source * RP + slot_of[source]
        q_lat = q_abs[request]
        q_pos = q_rot[request]
        seg_row = segment_ids[request]
        current = seg_row[PRE_TOK - 1]
        init = (
            jnp.full((2, heads_local), -1e30, jnp.float32),
            jnp.zeros((2, heads_local), jnp.float32),
            jnp.zeros((2, heads_local, KVL), jnp.float32),
        )
        valid = (seg_row == current)[None, None, :]
        stats = combine(
            init,
            block_stats(
                lax.all_gather(pages[source], "tp", axis=0, tiled=True), q_lat, q_pos, valid
            ),
        )
        return finish(stats, source, request, q_lat, q_pos, result)

    result = lax.fori_loop(0, owned_count, attend, empty)
    return (result.reshape(pd_count * 2, heads_local * DV), pages)


def encode(values):
    levels = []
    parts = []
    for first, last in ((0, KVL), (KVL, WIDTH)):
        block = values[first:last]
        top = jnp.maximum(jnp.max(jnp.abs(block), axis=0, keepdims=True), 1e-30)
        level = jnp.ceil(jnp.log2(top) * STEPS)
        codes = jnp.round(block * (jnp.exp2(level * (-1.0 / STEPS)) * TOP))
        parts.append(jnp.clip(codes, -TOP, TOP).astype(jnp.int32).astype(I16))
        levels.append(level.astype(jnp.int32))
    row = lax.broadcasted_iota(jnp.int32, (16, values.shape[1]), 0)
    extra = jnp.where(row == 0, levels[0], jnp.where(row == 1, levels[1], 0))
    return jnp.concatenate([*parts, extra.astype(I16)], 0)


def decode(codes):
    level = codes[WIDTH:CODED].astype(jnp.int32).astype(F32)
    step = jnp.exp2(level * (1.0 / STEPS)) * (1.0 / TOP)
    lat = codes[0:KVL].astype(jnp.int32).astype(F32) * step[0:1]
    rot = codes[KVL:WIDTH].astype(jnp.int32).astype(F32) * step[1:2]
    return jnp.concatenate([lat, rot], 0)


def key_rows(comp, gain, cosine, sine):
    lat = comp[:KVL]
    scale = lax.rsqrt(jnp.mean(lat * lat, axis=0, keepdims=True) + 1e-06)
    first = comp[KVL : KVL + HALF]
    second = comp[KVL + HALF :]
    return jnp.concatenate(
        [
            lat * scale * gain,
            first * cosine - second * sine,
            first * sine + second * cosine,
        ],
        0,
    )


def far(z, i):
    return jnp.where(z < 2, 3 - i, i)


def near(z, i):
    return jnp.where(z < 2, i, 3 - i)


def outer_rank(z):
    return (z == 0) | (z == 3)


def project_far_kernel(rank, hid_ref, down_ref, *refs):
    sum_ref, code_ref = refs[-2:]
    total = lax.dot_general(down_ref[...], hid_ref[0], NT, preferred_element_type=F32)
    for u in range(UNITS):
        sum_ref[0, u] = total[:, u * UNIT : (u + 1) * UNIT]

    @pl.when(outer_rank(rank[0]))
    def _():
        for u in range(UNITS):
            code_ref[0, u] = encode(total[:, u * UNIT : (u + 1) * UNIT])


def project_far(rank, hidden, down_t, request, after):
    depth = hidden.shape[-1]
    return pl.pallas_call(
        project_far_kernel,
        grid_spec=pltpu.PrefetchScalarGridSpec(
            num_scalar_prefetch=1,
            grid=(2,),
            in_specs=[
                pl.BlockSpec((1, SHARE, depth), lambda i, rank: (request, far(rank[0], i), 0)),
                VMEM,
                *([ANY] * len(after)),
            ],
            out_specs=[
                pl.BlockSpec((1, UNITS, WIDTH, UNIT), lambda i, rank: (i, 0, 0, 0)),
                pl.BlockSpec((1, UNITS, CODED, UNIT), lambda i, rank: (i, 0, 0, 0)),
            ],
        ),
        out_shape=[
            jax.ShapeDtypeStruct((2, UNITS, WIDTH, UNIT), F32),
            jax.ShapeDtypeStruct((2, UNITS, CODED, UNIT), I16),
        ],
        compiler_params=ROOM,
        cost_estimate=COST,
        name="project_far",
    )(rank, hidden, down_t, *after)


def project_near_kernel(rank, hid_ref, down_ref, *refs):
    sum_ref, *code_refs = refs[-3:]
    unit = pl.program_id(0)
    rows = hid_ref[...].reshape(LANES, hid_ref.shape[-1])
    total = lax.dot_general(down_ref[...], rows, NT, preferred_element_type=F32)
    for r in range(RP):
        sum_ref[0, 0, r] = total[:, r * UNIT : (r + 1) * UNIT]
    coded = outer_rank(rank[0]) & (pl.program_id(1) == 1)
    for mine, ref in zip((unit == 0, unit > 0), code_refs):

        @pl.when(coded & mine)
        def _(ref=ref):
            for r in range(RP):
                ref[0, r] = encode(total[:, r * UNIT : (r + 1) * UNIT])


def project_near(rank, hidden, down_t, after):
    depth = hidden.shape[-1]
    return pl.pallas_call(
        project_near_kernel,
        grid_spec=pltpu.PrefetchScalarGridSpec(
            num_scalar_prefetch=1,
            grid=(UNITS, 2),
            in_specs=[
                pl.BlockSpec(
                    (RP, UNIT, depth), lambda u, i, rank: (0, near(rank[0], i) * UNITS + u, 0)
                ),
                VMEM,
                *([ANY] * len(after)),
            ],
            out_specs=[
                pl.BlockSpec((1, 1, RP, WIDTH, UNIT), lambda u, i, rank: (u, i, 0, 0, 0)),
                pl.BlockSpec((1, RP, CODED, UNIT), lambda u, i, rank: (0, 0, 0, 0)),
                pl.BlockSpec(
                    (1, RP, CODED, UNIT), lambda u, i, rank: (jnp.maximum(u, 1) - 1, 0, 0, 0)
                ),
            ],
        ),
        out_shape=[
            jax.ShapeDtypeStruct((UNITS, 2, RP, WIDTH, UNIT), F32),
            jax.ShapeDtypeStruct((1, RP, CODED, UNIT), I16),
            jax.ShapeDtypeStruct((UNITS - 1, RP, CODED, UNIT), I16),
        ],
        compiler_params=ROOM,
        cost_estimate=COST,
        name="project_near",
    )(rank, hidden, down_t, *after)


def add_kernel(out_at, rank, own_ref, got_ref, *refs):
    @pl.when(~outer_rank(rank[0]))
    def _():
        for u in range(UNITS):
            refs[out_at][0, u] = encode(own_ref[u] + decode(got_ref[0, u]))


def add_on(rank, own, got, request=None, after=(), carried=()):
    chunk = lambda i, rank: (i, 0, 0, 0)
    if request is None:
        own_spec = pl.BlockSpec((None, UNITS, WIDTH, UNIT), chunk)
    else:
        own_spec = pl.BlockSpec(
            (UNITS, None, None, WIDTH, UNIT), lambda i, rank: (0, i, request, 0, 0)
        )
    return pl.pallas_call(
        functools.partial(add_kernel, -1 - len(carried)),
        grid_spec=pltpu.PrefetchScalarGridSpec(
            num_scalar_prefetch=1,
            grid=(2,),
            in_specs=[
                own_spec,
                pl.BlockSpec((1, UNITS, CODED, UNIT), chunk),
                *([ANY] * (len(after) + len(carried))),
            ],
            out_specs=[
                pl.BlockSpec((1, UNITS, CODED, UNIT), chunk),
                *([ANY] * len(carried)),
            ],
        ),
        out_shape=[
            jax.ShapeDtypeStruct((2, UNITS, CODED, UNIT), I16),
            *[jax.ShapeDtypeStruct(c.shape, c.dtype) for c in carried],
        ],
        input_output_aliases={3 + len(after) + n: 1 + n for n in range(len(carried))},
        compiler_params=SOME,
        cost_estimate=COST,
        name="add_on",
    )(rank, own, got, *after, *carried)


def hold_kernel(*refs):
    pass


def hold(block, after):
    return pl.pallas_call(
        hold_kernel,
        in_specs=[ANY] * (1 + len(after)),
        out_specs=ANY,
        out_shape=jax.ShapeDtypeStruct(block.shape, block.dtype),
        input_output_aliases={0: 0},
        compiler_params=SOME,
        cost_estimate=COST,
        name="hold",
    )(block, *after)


def gain_column(gain_ref):
    return jnp.broadcast_to(gain_ref[...], (UNIT, KVL)).T


def page_kernel(requests, rank, slot, own_ref, *refs):
    count = len(requests)
    got_refs, sent_refs, refs = refs[:count], refs[count : 2 * count], refs[2 * count :]
    side_refs, (gain_ref, cos_ref, sin_ref) = refs[:2], refs[2:5]
    out_ref = refs[-1]
    step = pl.program_id(0)
    column = gain_column(gain_ref)

    def write(u, comp):
        rows = key_rows(comp, column, cos_ref[u], sin_ref[u]).astype(BF)
        out_ref[0, :, u * UNIT : (u + 1) * UNIT] = rows

    for k in range(count):

        @pl.when((step == k) & outer_rank(rank[0]))
        def _(k=k):
            for u in range(UNITS):
                write(u, own_ref[u] + decode(got_refs[k][u]))

        @pl.when((step == k) & ~outer_rank(rank[0]))
        def _(k=k):
            for u in range(UNITS):
                side = side_refs[u > 0][max(u - 1, 0)]
                write(u, decode(sent_refs[k][u]) + decode(side))


def pages_of(requests, rank, slot, own, got, sent, side, gain, cosine, sine, base, count, after):
    first = pl.BlockSpec((None, UNITS, CODED, UNIT), lambda i, *_: (0, 0, 0, 0))
    second = pl.BlockSpec((None, UNITS, CODED, UNIT), lambda i, *_: (1, 0, 0, 0))
    table = pl.BlockSpec((UNITS, HALF, UNIT), lambda i, *_: (0, 0, 0))
    start, total = requests[0], len(requests)
    got, sent = got[start : start + total], sent[start : start + total]
    return pl.pallas_call(
        functools.partial(page_kernel, requests),
        grid_spec=pltpu.PrefetchScalarGridSpec(
            num_scalar_prefetch=2,
            grid=(total,),
            in_specs=[
                pl.BlockSpec(
                    (UNITS, None, None, WIDTH, UNIT), lambda i, *_: (0, 0, i + start, 0, 0)
                ),
                *([first] * total),
                *([second] * total),
                pl.BlockSpec((1, None, CODED, UNIT), lambda i, *_: (0, i + start, 0, 0)),
                pl.BlockSpec((UNITS - 1, None, CODED, UNIT), lambda i, *_: (0, i + start, 0, 0)),
                pl.BlockSpec((1, KVL), lambda i, *_: (0, 0)),
                table,
                table,
                *([ANY] * (len(base) + len(after))),
            ],
            out_specs=pl.BlockSpec(
                (1, WIDTH, SHARE), lambda i, rank, slot: (slot[i + start], 0, 0)
            ),
        ),
        out_shape=jax.ShapeDtypeStruct((count, WIDTH, SHARE), BF),
        input_output_aliases={8 + 2 * total + n: n for n in range(len(base))},
        compiler_params=SOME,
        cost_estimate=COST,
        name="pages",
    )(rank, slot, own, *got, *sent, *side, gain, cosine, sine, *base, *after)


def query_kernel(lat_ref, up_ref, draft_ref, down_ref, *refs):
    *key_refs, cos_ref, sin_ref, out_ref, split_ref = refs

    @pl.when(pl.program_id(0) == 0)
    def _():
        rest = lax.dot_general(draft_ref[...], down_ref[...], NT, preferred_element_type=F32)
        for n in range(3):
            term = rest.astype(BF).astype(F32)
            split_ref[n] = term
            rest = rest - term
        split_ref[3] = jnp.zeros_like(rest)

    full = jnp.dot(lat_ref[...], up_ref[...], preferred_element_type=F32)
    for h, key_ref in enumerate(key_refs):
        base = h * (DN + DR)
        nope = full[:, base : base + DN].astype(BF)
        first = full[:, base + DN : base + DN + HALF]
        second = full[:, base + DN + HALF : base + DN + DR]
        absorbed = lax.dot_general(nope, key_ref[...], NT, preferred_element_type=F32)
        cosine, sine = cos_ref[...], sin_ref[...]
        out_ref[h] = jnp.concatenate(
            [absorbed, first * cosine - second * sine, first * sine + second * cosine], 1
        )


def queries(latents, q_up, kv_up, draft, down_t, cosine, sine, after):
    rows = latents.shape[0]
    heads = q_up.shape[1] // (DN + DR)
    step = 4
    key_spec = [
        pl.BlockSpec((KVL, DN), lambda i, h=h: (0, 2 * (step * i + h))) for h in range(step)
    ]
    whole = lambda i: (0, 0)
    table = pl.BlockSpec((rows, HALF), whole)
    body = lambda *refs: query_kernel(*refs[:-3], *refs[-2:])
    return pl.pallas_call(
        body,
        grid=(heads // step,),
        in_specs=[
            pl.BlockSpec((rows, QL), whole),
            pl.BlockSpec((QL, step * (DN + DR)), lambda i: (0, i)),
            pl.BlockSpec(draft.shape, whole),
            pl.BlockSpec(down_t.shape, whole),
            *key_spec,
            table,
            table,
            ANY,
        ],
        out_specs=[
            pl.BlockSpec((step, rows, WIDTH), lambda i: (i, 0, 0)),
            pl.BlockSpec((4, rows, WIDTH), lambda i: (0, 0, 0)),
        ],
        out_shape=[
            jax.ShapeDtypeStruct((heads, rows, WIDTH), F32),
            jax.ShapeDtypeStruct((4, rows, WIDTH), F32),
        ],
        compiler_params=ROOM,
        cost_estimate=COST,
        name="queries",
    )(latents, q_up, draft, down_t, *([kv_up] * step), cosine, sine, after)


def attend_kernel(requests, rank, first_ref, *refs):
    count = len(requests)
    q_refs, draft_refs, refs = refs[:4], refs[4:8], refs[8:]
    own_ref, got_refs, refs = refs[0], refs[1 : 1 + count], refs[1 + count :]
    cos_ref, sin_ref, midcos_ref, midsin_ref, refs = *refs[:4], refs[4:]
    segment_ref, gain_ref, newcos_ref, newsin_ref, refs = *refs[:4], refs[4:]
    out_refs, keys_ref = refs[-5:-1], refs[-1]
    step = pl.program_id(0)
    request = step + requests[0]

    @pl.when(rank[0] == 3)
    def _():
        column = gain_column(gain_ref)
        for k in range(count):

            @pl.when(step == k)
            def _(k=k):
                for i, (cosine, sine) in enumerate(
                    ((cos_ref, sin_ref), (midcos_ref, midsin_ref))
                ):
                    for u in range(UNITS):
                        comp = own_ref[u, i] + decode(got_refs[k][i, u])
                        rows = key_rows(comp, column, cosine[u], sine[u])
                        start = (1 - i) * SHARE + u * UNIT
                        keys_ref[:, start : start + UNIT] = rows.astype(BF)

        scale = (DN + DR) ** (-0.5)
        local_rows = out_refs[0].shape[1]
        new = 2 * RP
        comp = 0.0
        for ref in draft_refs:
            terms = ref[...].astype(F32)
            comp = comp + (terms[0:new] + terms[new : 2 * new] + terms[2 * new : 3 * new])
        lat = comp[:, :KVL]
        norm = lax.rsqrt(jnp.mean(lat * lat, axis=-1, keepdims=True) + 1e-06)
        first = comp[:, KVL : KVL + HALF]
        second = comp[:, KVL + HALF :]
        cosine, sine = newcos_ref[...], newsin_ref[...]
        drafts = jnp.concatenate(
            [
                lat * norm * gain_ref[...],
                first * cosine - second * sine,
                first * sine + second * cosine,
            ],
            1,
        )
        drafts = jnp.concatenate([drafts, jnp.zeros((UNIT - new, WIDTH), F32)], 0).astype(BF)
        query = jnp.concatenate([ref[...] for ref in q_refs], 0)
        scores = jnp.dot(query, keys_ref[...], preferred_element_type=F32) * scale
        segments = segment_ref[pl.ds(first_ref[0] + request, 1), :]
        valid = segments[:, PRE_TOK // 2 :] == segments[:, PRE_TOK - 1 :]
        scores = jnp.where(valid, scores, -1e30)
        fresh = lax.dot_general(query, drafts, NT, preferred_element_type=F32) * scale
        row = lax.broadcasted_iota(jnp.int32, fresh.shape, 0)
        late = (row % local_rows) // (local_rows // 2)
        offset = lax.broadcasted_iota(jnp.int32, fresh.shape, 1) - 2 * request
        fresh = jnp.where((offset >= 0) & (offset <= late), fresh, -1e30)
        top = jnp.maximum(
            jnp.max(scores, axis=1, keepdims=True), jnp.max(fresh, axis=1, keepdims=True)
        )
        weights = jnp.exp(scores - top)
        fresh = jnp.exp(fresh - top)
        total = jnp.sum(weights, axis=1, keepdims=True) + jnp.sum(fresh, axis=1, keepdims=True)
        numer = lax.dot_general(
            weights.astype(BF), keys_ref[0:KVL, :], NT, preferred_element_type=F32
        )
        numer = numer + jnp.dot(fresh.astype(BF), drafts[:, :KVL], preferred_element_type=F32)
        result = (numer / total).astype(BF)
        for t, ref in enumerate(out_refs):
            ref[0] = result[t * local_rows : (t + 1) * local_rows]


def attend(requests, rank, first, messages, own, got, tables, segments, gain, cosine, sine, after):
    new = 2 * RP
    local_rows = (messages[0].shape[0] - 4 * new) // RP
    last = RP * local_rows // (4 * new)
    start, count = requests[0], len(requests)
    got = got[start : start + count]
    out = jax.ShapeDtypeStruct((count, local_rows, KVL), BF)
    whole = lambda i, *_: (0, 0)
    whole3 = lambda i, *_: (0, 0, 0)
    return pl.pallas_call(
        functools.partial(attend_kernel, requests),
        grid_spec=pltpu.PrefetchScalarGridSpec(
            num_scalar_prefetch=2,
            grid=(count,),
            in_specs=[
                *([pl.BlockSpec((local_rows, WIDTH), lambda i, *_: (i + start, 0))] * 4),
                *([pl.BlockSpec((4 * new, WIDTH), lambda i, *_: (last, 0))] * 4),
                pl.BlockSpec(
                    (UNITS, 2, None, WIDTH, UNIT), lambda i, *_: (0, 0, i + start, 0, 0)
                ),
                *([pl.BlockSpec((2, UNITS, CODED, UNIT), lambda i, *_: (0, 0, 0, 0))] * count),
                *([pl.BlockSpec((UNITS, HALF, UNIT), whole3)] * 4),
                pl.BlockSpec(segments.shape, whole),
                pl.BlockSpec((1, KVL), whole),
                pl.BlockSpec(cosine.shape, whole),
                pl.BlockSpec(sine.shape, whole),
                *([ANY] * len(after)),
            ],
            out_specs=[pl.BlockSpec((1, local_rows, KVL), lambda i, *_: (i, 0, 0))] * 4,
            scratch_shapes=[pltpu.VMEM((WIDTH, 2 * SHARE), BF)],
        ),
        out_shape=[out] * 4,
        compiler_params=SOME,
        cost_estimate=COST,
        name="attend",
    )(rank, first, *messages, *messages, own, *got, *tables, segments, gain, cosine, sine, *after)


def heads_kernel(step, slot, o_ref, keep_ref, *refs):
    out_ref = refs[-1]
    out_ref[...] = jnp.zeros_like(out_ref)
    for h, value_ref in enumerate(refs[:step]):
        row = jnp.dot(o_ref[h].astype(BF), value_ref[...], preferred_element_type=F32)
        row = (row * keep_ref[...]).astype(BF)
        for r in range(RP):
            out_ref[slot[r], :, h * DV : (h + 1) * DV] = row[2 * r : 2 * r + 2]


def heads_out(slot, attended, keep, kv_up, count, after):
    heads, rows, _ = attended.shape
    step = 8
    value_spec = [
        pl.BlockSpec((KVL, DV), lambda i, slot, h=h: (0, 2 * (step * i + h) + 1))
        for h in range(step)
    ]
    return pl.pallas_call(
        functools.partial(heads_kernel, step),
        grid_spec=pltpu.PrefetchScalarGridSpec(
            num_scalar_prefetch=1,
            grid=(heads // step,),
            in_specs=[
                pl.BlockSpec((step, rows, KVL), lambda i, slot: (i, 0, 0)),
                pl.BlockSpec((rows, DV), lambda i, slot: (0, 0)),
                *value_spec,
                *([ANY] * len(after)),
            ],
            out_specs=pl.BlockSpec((count, 2, step * DV), lambda i, slot: (0, 0, i)),
        ),
        out_shape=jax.ShapeDtypeStruct((count, 2, heads * DV), BF),
        compiler_params=ROOM,
        cost_estimate=COST,
        name="heads_out",
    )(slot, attended, keep, *([kv_up] * step), *after)


def emit_kernel(pages_ref, placed_ref, out_ref, same_ref):
    out_ref[...] = pages_ref[...]


def emit(pages, placed):
    page = pl.BlockSpec((1, *pages.shape[1:]), lambda i: (i, 0, 0))
    return pl.pallas_call(
        emit_kernel,
        grid=(pages.shape[0],),
        in_specs=[page, ANY],
        out_specs=[page, ANY],
        out_shape=[
            jax.ShapeDtypeStruct(pages.shape, pages.dtype),
            jax.ShapeDtypeStruct(placed.shape, placed.dtype),
        ],
        input_output_aliases={1: 1},
        compiler_params=SOME,
        cost_estimate=COST,
        name="emit",
    )(pages, placed)


def rope_tables(position):
    freq = jnp.exp(-jnp.log(10000.0) * jnp.arange(HALF, dtype=F32) / HALF)
    angle = position.astype(F32)[..., None] * freq
    return jnp.cos(angle), jnp.sin(angle)


def local_line(
    prefill_hidden,
    draft_hidden,
    kv_down,
    kv_gain,
    query_latent,
    q_up,
    kv_up,
    owners,
    segment_ids,
    accepted,
):
    pd_count = lax.axis_size("pd")
    z = lax.axis_index("tp")
    p = lax.axis_index("pd")
    first_req = p * RP

    gain = kv_gain.reshape(1, KVL)
    rank = z.astype(jnp.int32).reshape(1)
    hidden = prefill_hidden.reshape(RP, PRE_TOK, prefill_hidden.shape[1])
    down_t = kv_down.T
    inward, across, outward = [(0, 1), (3, 2)], [(1, 2), (2, 1)], [(2, 3), (1, 0)]

    far_sums, inner, crossed, sent, outer = [], [], [], [], []

    def send_far(r, after):
        total, codes = project_far(rank, hidden, down_t, r, after)
        far_sums.append(total)
        inner.append(lax.ppermute(codes, "tp", inward))

    def first_hop(r, after, carried=()):
        block, *carried = add_on(rank, far_sums[r], inner[r], after=after, carried=carried)
        crossed.append(lax.ppermute(block, "tp", across))
        return [block, *carried]

    def second_hop(r, after, awaited=()):
        (block,) = add_on(rank, near_sums, crossed[r], r, after)
        if awaited:
            block = hold(block, awaited)
        sent.append(block)
        outer.append(lax.ppermute(block, "tp", outward))
        return [block]

    send_far(0, [])
    send_far(1, far_sums[:1])

    latents = lax.dynamic_slice_in_dim(query_latent, first_req, RP, 0).reshape(RP * 2, QL)
    new_pos = jnp.tile(PRE_TOK + jnp.arange(2, dtype=jnp.int32), RP)
    new_cos, new_sin = rope_tables(new_pos)
    query, terms = queries(
        latents, q_up, kv_up, draft_hidden, down_t, new_cos, new_sin, far_sums[1]
    )
    heads = query.shape[0]
    query = query.reshape(heads, RP, 2, WIDTH).transpose(1, 2, 0, 3)
    message = jnp.concatenate(
        [query.reshape(RP * 2 * heads, WIDTH), terms.reshape(8 * RP, WIDTH)], 0
    ).astype(BF)
    messages = [lax.ppermute(message, "tp", [(t, 3)]) for t in range(3)] + [message]

    done = first_hop(0, [message])
    send_far(2, done)
    near_sums, *side = project_near(rank, hidden, down_t, far_sums[2:])
    done = first_hop(1, [near_sums])
    done = second_hop(0, [*done, *messages[:3]])
    send_far(3, done)
    steps = jnp.arange(SHARE, dtype=jnp.int32).reshape(UNITS, UNIT)
    tables = [
        jnp.swapaxes(t, 1, 2)
        for t in (*rope_tables(z * SHARE + steps), *rope_tables(2 * SHARE + steps))
    ]
    block, side[0] = first_hop(2, far_sums[3:], side[:1])
    side = [lax.ppermute(codes, "tp", inward) for codes in side]
    done = second_hop(1, [block], outer[:1])
    done = first_hop(3, done)
    done = second_hop(2, [*done, *tables], [outer[1], side[0]])
    done = second_hop(3, done, outer[2:])

    def attend_to(requests, after):
        result = attend(
            requests,
            rank,
            first_req.astype(jnp.int32).reshape(1),
            messages,
            near_sums,
            outer,
            tables,
            segment_ids,
            gain,
            new_cos,
            new_sin,
            after,
        )
        return result, [lax.ppermute(result[t], "tp", [(3, t)]) for t in range(3)]

    my_owners = lax.dynamic_slice_in_dim(owners, first_req, RP, 0)
    early, late = tuple(range(RP - 1)), (RP - 1,)

    def pages_to(requests, base, after):
        return pages_of(
            requests,
            rank,
            my_owners,
            near_sums,
            outer,
            sent,
            side,
            gain,
            tables[0],
            tables[1],
            base,
            pd_count,
            after,
        )

    results, backs = [None] * 2, [None] * 2
    results[0], backs[0] = attend_to(early, done)
    base = [jnp.zeros((pd_count, WIDTH, SHARE), BF)] if pd_count > RP else []
    pages = pages_to(early, base, results[0][:1])
    pages = pages_to(late, [pages], backs[0])
    results[1], backs[1] = attend_to(late, [pages])
    cache = lax.all_to_all(pages, "pd", split_axis=0, concat_axis=0, tiled=True)

    attended = [
        jnp.where(z == 3, result[3], back[0] + back[1] + back[2])
        for result, back in zip(results, backs)
    ]
    attended = jnp.concatenate(attended, 0).reshape(RP, 2, heads, KVL).transpose(2, 0, 1, 3)
    attended = attended.reshape(heads, RP * 2, KVL).astype(F32)
    my_accepted = lax.dynamic_slice_in_dim(accepted, first_req, RP, 0)
    keep = (jnp.arange(2)[None, :] <= my_accepted[:, None]).astype(F32).reshape(RP * 2, 1)
    placed = heads_out(
        my_owners,
        attended,
        jnp.broadcast_to(keep, (RP * 2, DV)),
        kv_up,
        pd_count,
        [pages],
    )
    cache, placed = emit(cache, placed)
    placed = lax.all_to_all(placed, "pd", split_axis=0, concat_axis=0, tiled=True)
    return (placed.reshape(pd_count * 2, heads * DV), jnp.swapaxes(cache, 1, 2))


def solution(mesh):
    placed = (
        P(("groups", "pd"), "tp"),
        P(("groups", "pd"), "tp"),
        P("tp", None),
        P(),
        P("groups", None, None),
        P(None, "tp"),
        P(None, "tp"),
        P("groups"),
        P("groups", None),
        P("groups"),
    )
    return jax.shard_map(
        local_line if mesh.shape["tp"] == 4 else local_general,
        mesh=mesh,
        in_specs=placed,
        out_specs=(P(("groups", "pd"), "tp"), P(("groups", "pd"), "tp", None)),
        check_vma=False,
    )
```

```python
import functools

import jax
import jax.numpy as jnp
from jax import lax
from jax.experimental import pallas as pl
from jax.experimental.pallas import tpu as pltpu
from jax.sharding import PartitionSpec as P

DN = 128
DR = 64
DV = 128
KVL = 512
QL = 1536
PRE_TOK = 1536
RP = 4
WIDTH = KVL + DR
HALF = DR // 2
CODED = WIDTH + 16
SHARE = PRE_TOK // 4
UNIT = 128
UNITS = SHARE // UNIT
LANES = RP * UNIT
STEPS = 256.0
TOP = 32767.0
BF = jnp.bfloat16
F32 = jnp.float32
I16 = jnp.int16
NT = (((1,), (1,)), ((), ()))
ROOM = pltpu.CompilerParams(vmem_limit_bytes=60 << 20)
SOME = pltpu.CompilerParams(vmem_limit_bytes=52 << 20)
ANY = pl.BlockSpec(memory_space=pl.ANY)
VMEM = pl.BlockSpec(memory_space=pltpu.VMEM)
SMEM = pl.BlockSpec(memory_space=pltpu.SMEM)


COST = pl.CostEstimate(flops=1024, bytes_accessed=1024, transcendentals=0)


def rms_latent(comp, gain):
    lat = comp[:, :KVL]
    scale = lax.rsqrt(jnp.mean(lat * lat, axis=-1, keepdims=True) + 1e-06)
    return (lat * scale * gain).astype(jnp.bfloat16)


def rotate(values, position):
    half = values.shape[-1] // 2
    freq = jnp.exp(-jnp.log(10000.0) * jnp.arange(half, dtype=jnp.float32) / half)
    angle = position.astype(jnp.float32)[..., None] * freq
    cosine = jnp.cos(angle)
    sine = jnp.sin(angle)
    first = values[..., :half]
    second = values[..., half:]
    return jnp.concatenate([first * cosine - second * sine, first * sine + second * cosine], -1)


def block_stats(keys, q_lat, q_pos, valid):
    scale = (DN + DR) ** (-0.5)
    scores = jnp.einsum("jhk,tk->jht", q_lat, keys[:, :KVL], preferred_element_type=jnp.float32)
    scores = (
        scores + jnp.einsum("jhk,tk->jht", q_pos, keys[:, KVL:], preferred_element_type=jnp.float32)
    ) * scale
    scores = jnp.where(valid, scores, -1e30)
    top = jnp.max(scores, axis=-1)
    weights = jnp.where(valid, jnp.exp(scores - top[..., None]), 0.0)
    total = jnp.sum(weights, axis=-1)
    numer = jnp.einsum(
        "jht,tk->jhk",
        weights.astype(jnp.bfloat16),
        keys[:, :KVL],
        preferred_element_type=jnp.float32,
    )
    return (top, total, numer)


def combine(left, right):
    top = jnp.maximum(left[0], right[0])
    left_scale = jnp.exp(left[0] - top)
    right_scale = jnp.exp(right[0] - top)
    total = left[1] * left_scale + right[1] * right_scale
    numer = left[2] * left_scale[..., None] + right[2] * right_scale[..., None]
    return (top, total, numer)


def local_general(
    prefill_hidden,
    draft_hidden,
    kv_down,
    kv_gain,
    query_latent,
    q_up,
    kv_up,
    owners,
    segment_ids,
    accepted,
):
    tp_count = lax.axis_size("tp")
    pd_count = lax.axis_size("pd")
    tp_rank = lax.axis_index("tp")
    mine_rank = lax.axis_index("pd")
    requests = owners.shape[0]
    share = PRE_TOK // tp_count
    width = KVL + DR
    local_hidden = prefill_hidden.reshape(RP, PRE_TOK, prefill_hidden.shape[1])
    summed = lax.psum_scatter(
        jnp.einsum(
            "rtd,dw->trw", local_hidden, kv_down, preferred_element_type=jnp.float32
        ).reshape(lax.axis_size("tp") * share, RP * width),
        "tp",
        scatter_dimension=0,
        tiled=True,
    ).reshape(share * RP, width)
    draft_sum = lax.psum(jnp.dot(draft_hidden, kv_down, preferred_element_type=jnp.float32), "tp")
    first_req = mine_rank * RP
    row_pos = jnp.broadcast_to(
        tp_rank * share + jnp.arange(share, dtype=jnp.int32)[:, None], (share, RP)
    )
    page_rows = jnp.concatenate(
        [
            rms_latent(summed, kv_gain),
            rotate(summed[:, KVL:], row_pos.reshape(-1)).astype(jnp.bfloat16),
        ],
        1,
    )
    page_rows = page_rows.reshape(share, RP, width)
    draft_pos = jnp.tile(PRE_TOK + jnp.arange(2, dtype=jnp.int32), RP)
    draft_rows = jnp.concatenate(
        [
            rms_latent(draft_sum, kv_gain),
            rotate(draft_sum[:, KVL:], draft_pos).astype(jnp.bfloat16),
        ],
        1,
    )
    draft_rows = draft_rows.reshape(RP, 2, width)
    my_owners = lax.dynamic_slice_in_dim(owners, first_req, RP, 0)
    routing = (my_owners[None, :] == jnp.arange(pd_count, dtype=jnp.int32)[:, None]).astype(
        jnp.bfloat16
    )
    send_pages = jnp.einsum(
        "dk,tkw->dtw", routing, page_rows, preferred_element_type=jnp.float32
    ).astype(jnp.bfloat16)
    send_drafts = jnp.einsum(
        "dk,kjw->djw", routing, draft_rows, preferred_element_type=jnp.float32
    ).astype(jnp.bfloat16)
    pages, drafts = (
        lax.all_to_all(send_pages, "pd", split_axis=0, concat_axis=0, tiled=True),
        lax.all_to_all(send_drafts, "pd", split_axis=0, concat_axis=0, tiled=True),
    )
    heads_local = q_up.shape[1] // (DN + DR)
    query_full = jnp.dot(
        query_latent.reshape(requests * 2, QL), q_up, preferred_element_type=jnp.float32
    )
    query_full = query_full.reshape(requests, 2, heads_local, DN + DR)
    new_pos = jnp.broadcast_to(PRE_TOK + jnp.arange(2, dtype=jnp.int32)[None, :], (requests, 2))
    q_nope = query_full[..., :DN].astype(jnp.bfloat16)
    q_rot = rotate(query_full[..., DN:], new_pos[:, :, None]).astype(jnp.bfloat16)
    up_heads = kv_up.reshape(KVL, heads_local, DN + DV)
    w_value = up_heads[:, :, DN:]
    q_abs = jnp.einsum(
        "rjhd,khd->rjhk", q_nope, up_heads[:, :, :DN], preferred_element_type=jnp.float32
    ).astype(jnp.bfloat16)
    owner_table = owners.reshape(pd_count, RP) == mine_rank
    holding = jnp.sum(owner_table.astype(jnp.int32), axis=1)
    slot_of = jnp.sum(
        owner_table.astype(jnp.int32) * jnp.arange(RP, dtype=jnp.int32)[None, :], axis=1
    )
    owned_count = jnp.sum(holding)
    order = jnp.argsort((1 - holding) * pd_count + jnp.arange(pd_count, dtype=jnp.int32))
    draft_valid = (jnp.arange(2)[None, :] <= jnp.arange(2)[:, None])[:, None, :]
    empty = jnp.zeros((pd_count, 2, heads_local * DV), jnp.bfloat16)

    def finish(stats, source, request, q_lat, q_pos, result):
        stats = combine(stats, block_stats(drafts[source], q_lat, q_pos, draft_valid))
        attended = (stats[2] / stats[1][..., None]).astype(jnp.bfloat16)
        head_out = jnp.einsum("jhk,khd->jhd", attended, w_value, preferred_element_type=jnp.float32)
        keep = (jnp.arange(2) <= accepted[request]).astype(jnp.float32)[:, None, None]
        answer = (head_out * keep).astype(jnp.bfloat16).reshape(1, 2, heads_local * DV)
        return lax.dynamic_update_slice(result, answer, (source, 0, 0))

    def attend(turn, result):
        source = order[turn]
        request = source * RP + slot_of[source]
        q_lat = q_abs[request]
        q_pos = q_rot[request]
        seg_row = segment_ids[request]
        current = seg_row[PRE_TOK - 1]
        init = (
            jnp.full((2, heads_local), -1e30, jnp.float32),
            jnp.zeros((2, heads_local), jnp.float32),
            jnp.zeros((2, heads_local, KVL), jnp.float32),
        )
        valid = (seg_row == current)[None, None, :]
        stats = combine(
            init,
            block_stats(
                lax.all_gather(pages[source], "tp", axis=0, tiled=True), q_lat, q_pos, valid
            ),
        )
        return finish(stats, source, request, q_lat, q_pos, result)

    result = lax.fori_loop(0, owned_count, attend, empty)
    return (result.reshape(pd_count * 2, heads_local * DV), pages)


def encode(values):
    levels = []
    parts = []
    for first, last in ((0, KVL), (KVL, WIDTH)):
        block = values[first:last]
        top = jnp.maximum(jnp.max(jnp.abs(block), axis=0, keepdims=True), 1e-30)
        level = jnp.ceil(jnp.log2(top) * STEPS)
        codes = jnp.round(block * (jnp.exp2(level * (-1.0 / STEPS)) * TOP))
        parts.append(jnp.clip(codes, -TOP, TOP).astype(jnp.int32).astype(I16))
        levels.append(level.astype(jnp.int32))
    row = lax.broadcasted_iota(jnp.int32, (16, values.shape[1]), 0)
    extra = jnp.where(row == 0, levels[0], jnp.where(row == 1, levels[1], 0))
    return jnp.concatenate([*parts, extra.astype(I16)], 0)


def decode(codes):
    level = codes[WIDTH:CODED].astype(jnp.int32).astype(F32)
    step = jnp.exp2(level * (1.0 / STEPS)) * (1.0 / TOP)
    lat = codes[0:KVL].astype(jnp.int32).astype(F32) * step[0:1]
    rot = codes[KVL:WIDTH].astype(jnp.int32).astype(F32) * step[1:2]
    return jnp.concatenate([lat, rot], 0)


def key_rows(comp, gain, cosine, sine):
    lat = comp[:KVL]
    scale = lax.rsqrt(jnp.mean(lat * lat, axis=0, keepdims=True) + 1e-06)
    first = comp[KVL : KVL + HALF]
    second = comp[KVL + HALF :]
    return jnp.concatenate(
        [
            lat * scale * gain,
            first * cosine - second * sine,
            first * sine + second * cosine,
        ],
        0,
    )


def far(z, i):
    return jnp.where(z < 2, 3 - i, i)


def near(z, i):
    return jnp.where(z < 2, i, 3 - i)


def outer_rank(z):
    return (z == 0) | (z == 3)


def project_far_kernel(rank, hid_ref, down_ref, *refs):
    sum_ref, code_ref = refs[-2:]
    total = lax.dot_general(down_ref[...], hid_ref[0], NT, preferred_element_type=F32)
    for u in range(UNITS):
        sum_ref[0, u] = total[:, u * UNIT : (u + 1) * UNIT]

    @pl.when(outer_rank(rank[0]))
    def _():
        for u in range(UNITS):
            code_ref[0, u] = encode(total[:, u * UNIT : (u + 1) * UNIT])


def project_far(rank, hidden, down_t, request, after):
    depth = hidden.shape[-1]
    return pl.pallas_call(
        project_far_kernel,
        grid_spec=pltpu.PrefetchScalarGridSpec(
            num_scalar_prefetch=1,
            grid=(2,),
            in_specs=[
                pl.BlockSpec((1, SHARE, depth), lambda i, rank: (request, far(rank[0], i), 0)),
                VMEM,
                *([ANY] * len(after)),
            ],
            out_specs=[
                pl.BlockSpec((1, UNITS, WIDTH, UNIT), lambda i, rank: (i, 0, 0, 0)),
                pl.BlockSpec((1, UNITS, CODED, UNIT), lambda i, rank: (i, 0, 0, 0)),
            ],
        ),
        out_shape=[
            jax.ShapeDtypeStruct((2, UNITS, WIDTH, UNIT), F32),
            jax.ShapeDtypeStruct((2, UNITS, CODED, UNIT), I16),
        ],
        compiler_params=ROOM,
        cost_estimate=COST,
        name="project_far",
    )(rank, hidden, down_t, *after)


def project_near_kernel(rank, hid_ref, down_ref, *refs):
    sum_ref, *code_refs = refs[-3:]
    unit = pl.program_id(0)
    rows = hid_ref[...].reshape(LANES, hid_ref.shape[-1])
    total = lax.dot_general(down_ref[...], rows, NT, preferred_element_type=F32)
    for r in range(RP):
        sum_ref[0, 0, r] = total[:, r * UNIT : (r + 1) * UNIT]
    coded = outer_rank(rank[0]) & (pl.program_id(1) == 1)
    for mine, ref in zip((unit == 0, unit > 0), code_refs):

        @pl.when(coded & mine)
        def _(ref=ref):
            for r in range(RP):
                ref[0, r] = encode(total[:, r * UNIT : (r + 1) * UNIT])


def project_near(rank, hidden, down_t, after):
    depth = hidden.shape[-1]
    return pl.pallas_call(
        project_near_kernel,
        grid_spec=pltpu.PrefetchScalarGridSpec(
            num_scalar_prefetch=1,
            grid=(UNITS, 2),
            in_specs=[
                pl.BlockSpec(
                    (RP, UNIT, depth), lambda u, i, rank: (0, near(rank[0], i) * UNITS + u, 0)
                ),
                VMEM,
                *([ANY] * len(after)),
            ],
            out_specs=[
                pl.BlockSpec((1, 1, RP, WIDTH, UNIT), lambda u, i, rank: (u, i, 0, 0, 0)),
                pl.BlockSpec((1, RP, CODED, UNIT), lambda u, i, rank: (0, 0, 0, 0)),
                pl.BlockSpec(
                    (1, RP, CODED, UNIT), lambda u, i, rank: (jnp.maximum(u, 1) - 1, 0, 0, 0)
                ),
            ],
        ),
        out_shape=[
            jax.ShapeDtypeStruct((UNITS, 2, RP, WIDTH, UNIT), F32),
            jax.ShapeDtypeStruct((1, RP, CODED, UNIT), I16),
            jax.ShapeDtypeStruct((UNITS - 1, RP, CODED, UNIT), I16),
        ],
        compiler_params=ROOM,
        cost_estimate=COST,
        name="project_near",
    )(rank, hidden, down_t, *after)


def add_kernel(out_at, rank, own_ref, got_ref, *refs):
    @pl.when(~outer_rank(rank[0]))
    def _():
        for u in range(UNITS):
            refs[out_at][0, u] = encode(own_ref[u] + decode(got_ref[0, u]))


def add_on(rank, own, got, request=None, after=(), carried=()):
    chunk = lambda i, rank: (i, 0, 0, 0)
    if request is None:
        own_spec = pl.BlockSpec((None, UNITS, WIDTH, UNIT), chunk)
    else:
        own_spec = pl.BlockSpec(
            (UNITS, None, None, WIDTH, UNIT), lambda i, rank: (0, i, request, 0, 0)
        )
    return pl.pallas_call(
        functools.partial(add_kernel, -1 - len(carried)),
        grid_spec=pltpu.PrefetchScalarGridSpec(
            num_scalar_prefetch=1,
            grid=(2,),
            in_specs=[
                own_spec,
                pl.BlockSpec((1, UNITS, CODED, UNIT), chunk),
                *([ANY] * (len(after) + len(carried))),
            ],
            out_specs=[
                pl.BlockSpec((1, UNITS, CODED, UNIT), chunk),
                *([ANY] * len(carried)),
            ],
        ),
        out_shape=[
            jax.ShapeDtypeStruct((2, UNITS, CODED, UNIT), I16),
            *[jax.ShapeDtypeStruct(c.shape, c.dtype) for c in carried],
        ],
        input_output_aliases={3 + len(after) + n: 1 + n for n in range(len(carried))},
        compiler_params=SOME,
        cost_estimate=COST,
        name="add_on",
    )(rank, own, got, *after, *carried)


def hold_kernel(*refs):
    pass


def hold(block, after):
    return pl.pallas_call(
        hold_kernel,
        in_specs=[ANY] * (1 + len(after)),
        out_specs=ANY,
        out_shape=jax.ShapeDtypeStruct(block.shape, block.dtype),
        input_output_aliases={0: 0},
        compiler_params=SOME,
        cost_estimate=COST,
        name="hold",
    )(block, *after)


def gain_column(gain_ref):
    return jnp.broadcast_to(gain_ref[...], (UNIT, KVL)).T


def page_kernel(requests, rank, slot, own_ref, *refs):
    count = len(requests)
    got_refs, sent_refs, refs = refs[:count], refs[count : 2 * count], refs[2 * count :]
    side_refs, (gain_ref, cos_ref, sin_ref) = refs[:2], refs[2:5]
    out_ref = refs[-1]
    step = pl.program_id(0)
    column = gain_column(gain_ref)

    def write(u, comp):
        rows = key_rows(comp, column, cos_ref[u], sin_ref[u]).astype(BF)
        out_ref[0, :, u * UNIT : (u + 1) * UNIT] = rows

    for k in range(count):

        @pl.when((step == k) & outer_rank(rank[0]))
        def _(k=k):
            for u in range(UNITS):
                write(u, own_ref[u] + decode(got_refs[k][u]))

        @pl.when((step == k) & ~outer_rank(rank[0]))
        def _(k=k):
            for u in range(UNITS):
                side = side_refs[u > 0][max(u - 1, 0)]
                write(u, decode(sent_refs[k][u]) + decode(side))


def pages_of(requests, rank, slot, own, got, sent, side, gain, cosine, sine, base, count, after):
    first = pl.BlockSpec((None, UNITS, CODED, UNIT), lambda i, *_: (0, 0, 0, 0))
    second = pl.BlockSpec((None, UNITS, CODED, UNIT), lambda i, *_: (1, 0, 0, 0))
    table = pl.BlockSpec((UNITS, HALF, UNIT), lambda i, *_: (0, 0, 0))
    start, total = requests[0], len(requests)
    got, sent = got[start : start + total], sent[start : start + total]
    return pl.pallas_call(
        functools.partial(page_kernel, requests),
        grid_spec=pltpu.PrefetchScalarGridSpec(
            num_scalar_prefetch=2,
            grid=(total,),
            in_specs=[
                pl.BlockSpec(
                    (UNITS, None, None, WIDTH, UNIT), lambda i, *_: (0, 0, i + start, 0, 0)
                ),
                *([first] * total),
                *([second] * total),
                pl.BlockSpec((1, None, CODED, UNIT), lambda i, *_: (0, i + start, 0, 0)),
                pl.BlockSpec((UNITS - 1, None, CODED, UNIT), lambda i, *_: (0, i + start, 0, 0)),
                pl.BlockSpec((1, KVL), lambda i, *_: (0, 0)),
                table,
                table,
                *([ANY] * (len(base) + len(after))),
            ],
            out_specs=pl.BlockSpec(
                (1, WIDTH, SHARE), lambda i, rank, slot: (slot[i + start], 0, 0)
            ),
        ),
        out_shape=jax.ShapeDtypeStruct((count, WIDTH, SHARE), BF),
        input_output_aliases={8 + 2 * total + n: n for n in range(len(base))},
        compiler_params=SOME,
        cost_estimate=COST,
        name="pages",
    )(rank, slot, own, *got, *sent, *side, gain, cosine, sine, *base, *after)


def query_kernel(lat_ref, up_ref, draft_ref, down_ref, *refs):
    *key_refs, cos_ref, sin_ref, out_ref, split_ref = refs

    @pl.when(pl.program_id(0) == 0)
    def _():
        rest = lax.dot_general(draft_ref[...], down_ref[...], NT, preferred_element_type=F32)
        for n in range(3):
            term = rest.astype(BF).astype(F32)
            split_ref[n] = term
            rest = rest - term
        split_ref[3] = jnp.zeros_like(rest)

    full = jnp.dot(lat_ref[...], up_ref[...], preferred_element_type=F32)
    for h, key_ref in enumerate(key_refs):
        base = h * (DN + DR)
        nope = full[:, base : base + DN].astype(BF)
        first = full[:, base + DN : base + DN + HALF]
        second = full[:, base + DN + HALF : base + DN + DR]
        absorbed = lax.dot_general(nope, key_ref[...], NT, preferred_element_type=F32)
        cosine, sine = cos_ref[...], sin_ref[...]
        out_ref[h] = jnp.concatenate(
            [absorbed, first * cosine - second * sine, first * sine + second * cosine], 1
        )


def queries(latents, q_up, kv_up, draft, down_t, cosine, sine, after):
    rows = latents.shape[0]
    heads = q_up.shape[1] // (DN + DR)
    step = 4
    key_spec = [
        pl.BlockSpec((KVL, DN), lambda i, h=h: (0, 2 * (step * i + h))) for h in range(step)
    ]
    whole = lambda i: (0, 0)
    table = pl.BlockSpec((rows, HALF), whole)
    body = lambda *refs: query_kernel(*refs[:-3], *refs[-2:])
    return pl.pallas_call(
        body,
        grid=(heads // step,),
        in_specs=[
            pl.BlockSpec((rows, QL), whole),
            pl.BlockSpec((QL, step * (DN + DR)), lambda i: (0, i)),
            pl.BlockSpec(draft.shape, whole),
            pl.BlockSpec(down_t.shape, whole),
            *key_spec,
            table,
            table,
            ANY,
        ],
        out_specs=[
            pl.BlockSpec((step, rows, WIDTH), lambda i: (i, 0, 0)),
            pl.BlockSpec((4, rows, WIDTH), lambda i: (0, 0, 0)),
        ],
        out_shape=[
            jax.ShapeDtypeStruct((heads, rows, WIDTH), F32),
            jax.ShapeDtypeStruct((4, rows, WIDTH), F32),
        ],
        compiler_params=ROOM,
        cost_estimate=COST,
        name="queries",
    )(latents, q_up, draft, down_t, *([kv_up] * step), cosine, sine, after)


def attend_kernel(requests, rank, first_ref, *refs):
    count = len(requests)
    q_refs, draft_refs, refs = refs[:4], refs[4:8], refs[8:]
    own_ref, got_refs, refs = refs[0], refs[1 : 1 + count], refs[1 + count :]
    cos_ref, sin_ref, midcos_ref, midsin_ref, refs = *refs[:4], refs[4:]
    segment_ref, gain_ref, newcos_ref, newsin_ref, refs = *refs[:4], refs[4:]
    out_refs, keys_ref = refs[-5:-1], refs[-1]
    step = pl.program_id(0)
    request = step + requests[0]

    @pl.when(rank[0] == 3)
    def _():
        column = gain_column(gain_ref)
        for k in range(count):

            @pl.when(step == k)
            def _(k=k):
                for i, (cosine, sine) in enumerate(
                    ((cos_ref, sin_ref), (midcos_ref, midsin_ref))
                ):
                    for u in range(UNITS):
                        comp = own_ref[u, i] + decode(got_refs[k][i, u])
                        rows = key_rows(comp, column, cosine[u], sine[u])
                        start = (1 - i) * SHARE + u * UNIT
                        keys_ref[:, start : start + UNIT] = rows.astype(BF)

        scale = (DN + DR) ** (-0.5)
        local_rows = out_refs[0].shape[1]
        new = 2 * RP
        comp = 0.0
        for ref in draft_refs:
            terms = ref[...].astype(F32)
            comp = comp + (terms[0:new] + terms[new : 2 * new] + terms[2 * new : 3 * new])
        lat = comp[:, :KVL]
        norm = lax.rsqrt(jnp.mean(lat * lat, axis=-1, keepdims=True) + 1e-06)
        first = comp[:, KVL : KVL + HALF]
        second = comp[:, KVL + HALF :]
        cosine, sine = newcos_ref[...], newsin_ref[...]
        drafts = jnp.concatenate(
            [
                lat * norm * gain_ref[...],
                first * cosine - second * sine,
                first * sine + second * cosine,
            ],
            1,
        )
        drafts = jnp.concatenate([drafts, jnp.zeros((UNIT - new, WIDTH), F32)], 0).astype(BF)
        query = jnp.concatenate([ref[...] for ref in q_refs], 0)
        scores = jnp.dot(query, keys_ref[...], preferred_element_type=F32) * scale
        segments = segment_ref[pl.ds(first_ref[0] + request, 1), :]
        valid = segments[:, PRE_TOK // 2 :] == segments[:, PRE_TOK - 1 :]
        scores = jnp.where(valid, scores, -1e30)
        fresh = lax.dot_general(query, drafts, NT, preferred_element_type=F32) * scale
        row = lax.broadcasted_iota(jnp.int32, fresh.shape, 0)
        late = (row % local_rows) // (local_rows // 2)
        offset = lax.broadcasted_iota(jnp.int32, fresh.shape, 1) - 2 * request
        fresh = jnp.where((offset >= 0) & (offset <= late), fresh, -1e30)
        top = jnp.maximum(
            jnp.max(scores, axis=1, keepdims=True), jnp.max(fresh, axis=1, keepdims=True)
        )
        weights = jnp.exp(scores - top)
        fresh = jnp.exp(fresh - top)
        total = jnp.sum(weights, axis=1, keepdims=True) + jnp.sum(fresh, axis=1, keepdims=True)
        numer = lax.dot_general(
            weights.astype(BF), keys_ref[0:KVL, :], NT, preferred_element_type=F32
        )
        numer = numer + jnp.dot(fresh.astype(BF), drafts[:, :KVL], preferred_element_type=F32)
        result = (numer / total).astype(BF)
        for t, ref in enumerate(out_refs):
            ref[0] = result[t * local_rows : (t + 1) * local_rows]


def attend(requests, rank, first, messages, own, got, tables, segments, gain, cosine, sine, after):
    new = 2 * RP
    local_rows = (messages[0].shape[0] - 4 * new) // RP
    last = RP * local_rows // (4 * new)
    start, count = requests[0], len(requests)
    got = got[start : start + count]
    out = jax.ShapeDtypeStruct((count, local_rows, KVL), BF)
    whole = lambda i, *_: (0, 0)
    whole3 = lambda i, *_: (0, 0, 0)
    return pl.pallas_call(
        functools.partial(attend_kernel, requests),
        grid_spec=pltpu.PrefetchScalarGridSpec(
            num_scalar_prefetch=2,
            grid=(count,),
            in_specs=[
                *([pl.BlockSpec((local_rows, WIDTH), lambda i, *_: (i + start, 0))] * 4),
                *([pl.BlockSpec((4 * new, WIDTH), lambda i, *_: (last, 0))] * 4),
                pl.BlockSpec(
                    (UNITS, 2, None, WIDTH, UNIT), lambda i, *_: (0, 0, i + start, 0, 0)
                ),
                *([pl.BlockSpec((2, UNITS, CODED, UNIT), lambda i, *_: (0, 0, 0, 0))] * count),
                *([pl.BlockSpec((UNITS, HALF, UNIT), whole3)] * 4),
                pl.BlockSpec(segments.shape, whole),
                pl.BlockSpec((1, KVL), whole),
                pl.BlockSpec(cosine.shape, whole),
                pl.BlockSpec(sine.shape, whole),
                *([ANY] * len(after)),
            ],
            out_specs=[pl.BlockSpec((1, local_rows, KVL), lambda i, *_: (i, 0, 0))] * 4,
            scratch_shapes=[pltpu.VMEM((WIDTH, 2 * SHARE), BF)],
        ),
        out_shape=[out] * 4,
        compiler_params=SOME,
        cost_estimate=COST,
        name="attend",
    )(rank, first, *messages, *messages, own, *got, *tables, segments, gain, cosine, sine, *after)


def heads_kernel(step, slot, o_ref, keep_ref, *refs):
    out_ref = refs[-1]
    out_ref[...] = jnp.zeros_like(out_ref)
    for h, value_ref in enumerate(refs[:step]):
        row = jnp.dot(o_ref[h].astype(BF), value_ref[...], preferred_element_type=F32)
        row = (row * keep_ref[...]).astype(BF)
        for r in range(RP):
            out_ref[slot[r], :, h * DV : (h + 1) * DV] = row[2 * r : 2 * r + 2]


def heads_out(slot, attended, keep, kv_up, count, after):
    heads, rows, _ = attended.shape
    step = 8
    value_spec = [
        pl.BlockSpec((KVL, DV), lambda i, slot, h=h: (0, 2 * (step * i + h) + 1))
        for h in range(step)
    ]
    return pl.pallas_call(
        functools.partial(heads_kernel, step),
        grid_spec=pltpu.PrefetchScalarGridSpec(
            num_scalar_prefetch=1,
            grid=(heads // step,),
            in_specs=[
                pl.BlockSpec((step, rows, KVL), lambda i, slot: (i, 0, 0)),
                pl.BlockSpec((rows, DV), lambda i, slot: (0, 0)),
                *value_spec,
                *([ANY] * len(after)),
            ],
            out_specs=pl.BlockSpec((count, 2, step * DV), lambda i, slot: (0, 0, i)),
        ),
        out_shape=jax.ShapeDtypeStruct((count, 2, heads * DV), BF),
        compiler_params=ROOM,
        cost_estimate=COST,
        name="heads_out",
    )(slot, attended, keep, *([kv_up] * step), *after)


def emit_kernel(pages_ref, placed_ref, out_ref, same_ref, done):
    copy = pltpu.make_async_copy(pages_ref, out_ref, done)
    copy.start()
    copy.wait()


def emit(pages, placed):
    return pl.pallas_call(
        emit_kernel,
        in_specs=[VMEM, ANY],
        out_specs=[ANY, ANY],
        out_shape=[
            jax.ShapeDtypeStruct(pages.shape, pages.dtype),
            jax.ShapeDtypeStruct(placed.shape, placed.dtype),
        ],
        scratch_shapes=[pltpu.SemaphoreType.DMA],
        input_output_aliases={1: 1},
        compiler_params=SOME,
        cost_estimate=COST,
        name="emit",
    )(pages, placed)


def rope_tables(position):
    freq = jnp.exp(-jnp.log(10000.0) * jnp.arange(HALF, dtype=F32) / HALF)
    angle = position.astype(F32)[..., None] * freq
    return jnp.cos(angle), jnp.sin(angle)


def local_line(
    prefill_hidden,
    draft_hidden,
    kv_down,
    kv_gain,
    query_latent,
    q_up,
    kv_up,
    owners,
    segment_ids,
    accepted,
):
    pd_count = lax.axis_size("pd")
    z = lax.axis_index("tp")
    p = lax.axis_index("pd")
    first_req = p * RP

    gain = kv_gain.reshape(1, KVL)
    rank = z.astype(jnp.int32).reshape(1)
    hidden = prefill_hidden.reshape(RP, PRE_TOK, prefill_hidden.shape[1])
    down_t = kv_down.T
    inward, across, outward = [(0, 1), (3, 2)], [(1, 2), (2, 1)], [(2, 3), (1, 0)]

    far_sums, inner, crossed, sent, outer = [], [], [], [], []

    def send_far(r, after):
        total, codes = project_far(rank, hidden, down_t, r, after)
        far_sums.append(total)
        inner.append(lax.ppermute(codes, "tp", inward))

    def first_hop(r, after, carried=()):
        block, *carried = add_on(rank, far_sums[r], inner[r], after=after, carried=carried)
        crossed.append(lax.ppermute(block, "tp", across))
        return [block, *carried]

    def second_hop(r, after, awaited=()):
        (block,) = add_on(rank, near_sums, crossed[r], r, after)
        if awaited:
            block = hold(block, awaited)
        sent.append(block)
        outer.append(lax.ppermute(block, "tp", outward))
        return [block]

    send_far(0, [])
    send_far(1, far_sums[:1])

    latents = lax.dynamic_slice_in_dim(query_latent, first_req, RP, 0).reshape(RP * 2, QL)
    new_pos = jnp.tile(PRE_TOK + jnp.arange(2, dtype=jnp.int32), RP)
    new_cos, new_sin = rope_tables(new_pos)
    query, terms = queries(
        latents, q_up, kv_up, draft_hidden, down_t, new_cos, new_sin, far_sums[1]
    )
    heads = query.shape[0]
    query = query.reshape(heads, RP, 2, WIDTH).transpose(1, 2, 0, 3)
    message = jnp.concatenate(
        [query.reshape(RP * 2 * heads, WIDTH), terms.reshape(8 * RP, WIDTH)], 0
    ).astype(BF)
    messages = [lax.ppermute(message, "tp", [(t, 3)]) for t in range(3)] + [message]

    done = first_hop(0, [message])
    send_far(2, done)
    near_sums, *side = project_near(rank, hidden, down_t, far_sums[2:])
    done = first_hop(1, [near_sums])
    done = second_hop(0, done, messages[:3])
    send_far(3, done)
    steps = jnp.arange(SHARE, dtype=jnp.int32).reshape(UNITS, UNIT)
    tables = [
        jnp.swapaxes(t, 1, 2)
        for t in (*rope_tables(z * SHARE + steps), *rope_tables(2 * SHARE + steps))
    ]
    block, side[0] = first_hop(2, far_sums[3:], side[:1])
    side = [lax.ppermute(codes, "tp", inward) for codes in side]
    done = second_hop(1, [block], outer[:1])
    done = first_hop(3, done)
    done = second_hop(2, [*done, *tables], [outer[1], side[0]])
    done = second_hop(3, done, outer[2:])

    def attend_to(requests, after):
        result = attend(
            requests,
            rank,
            first_req.astype(jnp.int32).reshape(1),
            messages,
            near_sums,
            outer,
            tables,
            segment_ids,
            gain,
            new_cos,
            new_sin,
            after,
        )
        return result, [lax.ppermute(result[t], "tp", [(3, t)]) for t in range(3)]

    my_owners = lax.dynamic_slice_in_dim(owners, first_req, RP, 0)
    early, late = tuple(range(RP - 1)), (RP - 1,)

    def pages_to(requests, base, after):
        return pages_of(
            requests,
            rank,
            my_owners,
            near_sums,
            outer,
            sent,
            side,
            gain,
            tables[0],
            tables[1],
            base,
            pd_count,
            after,
        )

    results, backs = [None] * 2, [None] * 2
    results[0], backs[0] = attend_to(early, done)
    base = [jnp.zeros((pd_count, WIDTH, SHARE), BF)] if pd_count > RP else []
    pages = pages_to(early, base, results[0][:1])
    pages = pages_to(late, [pages], backs[0])
    results[1], backs[1] = attend_to(late, [pages])
    cache = lax.all_to_all(pages, "pd", split_axis=0, concat_axis=0, tiled=True)

    attended = [
        jnp.where(z == 3, result[3], back[0] + back[1] + back[2])
        for result, back in zip(results, backs)
    ]
    attended = jnp.concatenate(attended, 0).reshape(RP, 2, heads, KVL).transpose(2, 0, 1, 3)
    attended = attended.reshape(heads, RP * 2, KVL).astype(F32)
    my_accepted = lax.dynamic_slice_in_dim(accepted, first_req, RP, 0)
    keep = (jnp.arange(2)[None, :] <= my_accepted[:, None]).astype(F32).reshape(RP * 2, 1)
    placed = heads_out(
        my_owners,
        attended,
        jnp.broadcast_to(keep, (RP * 2, DV)),
        kv_up,
        pd_count,
        [pages],
    )
    cache, placed = emit(cache, placed)
    placed = lax.all_to_all(placed, "pd", split_axis=0, concat_axis=0, tiled=True)
    return (placed.reshape(pd_count * 2, heads * DV), jnp.swapaxes(cache, 1, 2))


def solution(mesh):
    placed = (
        P(("groups", "pd"), "tp"),
        P(("groups", "pd"), "tp"),
        P("tp", None),
        P(),
        P("groups", None, None),
        P(None, "tp"),
        P(None, "tp"),
        P("groups"),
        P("groups", None),
        P("groups"),
    )
    return jax.shard_map(
        local_line if mesh.shape["tp"] == 4 else local_general,
        mesh=mesh,
        in_specs=placed,
        out_specs=(P(("groups", "pd"), "tp"), P(("groups", "pd"), "tp", None)),
        check_vma=False,
    )
```

```python
import functools

import jax
import jax.numpy as jnp
from jax import lax
from jax.experimental import pallas as pl
from jax.experimental.pallas import tpu as pltpu
from jax.sharding import PartitionSpec as P

DN = 128
DR = 64
DV = 128
KVL = 512
QL = 1536
PRE_TOK = 1536
RP = 4
WIDTH = KVL + DR
HALF = DR // 2
CODED = WIDTH + 16
SHARE = PRE_TOK // 4
UNIT = 128
UNITS = SHARE // UNIT
LANES = RP * UNIT
STEPS = 256.0
TOP = 32767.0
BF = jnp.bfloat16
F32 = jnp.float32
I16 = jnp.int16
NT = (((1,), (1,)), ((), ()))
ROOM = pltpu.CompilerParams(vmem_limit_bytes=60 << 20)
SOME = pltpu.CompilerParams(vmem_limit_bytes=52 << 20)
ANY = pl.BlockSpec(memory_space=pl.ANY)
VMEM = pl.BlockSpec(memory_space=pltpu.VMEM)
SMEM = pl.BlockSpec(memory_space=pltpu.SMEM)


COST = pl.CostEstimate(flops=1024, bytes_accessed=1024, transcendentals=0)


def rms_latent(comp, gain):
    lat = comp[:, :KVL]
    scale = lax.rsqrt(jnp.mean(lat * lat, axis=-1, keepdims=True) + 1e-06)
    return (lat * scale * gain).astype(jnp.bfloat16)


def rotate(values, position):
    half = values.shape[-1] // 2
    freq = jnp.exp(-jnp.log(10000.0) * jnp.arange(half, dtype=jnp.float32) / half)
    angle = position.astype(jnp.float32)[..., None] * freq
    cosine = jnp.cos(angle)
    sine = jnp.sin(angle)
    first = values[..., :half]
    second = values[..., half:]
    return jnp.concatenate([first * cosine - second * sine, first * sine + second * cosine], -1)


def block_stats(keys, q_lat, q_pos, valid):
    scale = (DN + DR) ** (-0.5)
    scores = jnp.einsum("jhk,tk->jht", q_lat, keys[:, :KVL], preferred_element_type=jnp.float32)
    scores = (
        scores + jnp.einsum("jhk,tk->jht", q_pos, keys[:, KVL:], preferred_element_type=jnp.float32)
    ) * scale
    scores = jnp.where(valid, scores, -1e30)
    top = jnp.max(scores, axis=-1)
    weights = jnp.where(valid, jnp.exp(scores - top[..., None]), 0.0)
    total = jnp.sum(weights, axis=-1)
    numer = jnp.einsum(
        "jht,tk->jhk",
        weights.astype(jnp.bfloat16),
        keys[:, :KVL],
        preferred_element_type=jnp.float32,
    )
    return (top, total, numer)


def combine(left, right):
    top = jnp.maximum(left[0], right[0])
    left_scale = jnp.exp(left[0] - top)
    right_scale = jnp.exp(right[0] - top)
    total = left[1] * left_scale + right[1] * right_scale
    numer = left[2] * left_scale[..., None] + right[2] * right_scale[..., None]
    return (top, total, numer)


def local_general(
    prefill_hidden,
    draft_hidden,
    kv_down,
    kv_gain,
    query_latent,
    q_up,
    kv_up,
    owners,
    segment_ids,
    accepted,
):
    tp_count = lax.axis_size("tp")
    pd_count = lax.axis_size("pd")
    tp_rank = lax.axis_index("tp")
    mine_rank = lax.axis_index("pd")
    requests = owners.shape[0]
    share = PRE_TOK // tp_count
    width = KVL + DR
    local_hidden = prefill_hidden.reshape(RP, PRE_TOK, prefill_hidden.shape[1])
    summed = lax.psum_scatter(
        jnp.einsum(
            "rtd,dw->trw", local_hidden, kv_down, preferred_element_type=jnp.float32
        ).reshape(lax.axis_size("tp") * share, RP * width),
        "tp",
        scatter_dimension=0,
        tiled=True,
    ).reshape(share * RP, width)
    draft_sum = lax.psum(jnp.dot(draft_hidden, kv_down, preferred_element_type=jnp.float32), "tp")
    first_req = mine_rank * RP
    row_pos = jnp.broadcast_to(
        tp_rank * share + jnp.arange(share, dtype=jnp.int32)[:, None], (share, RP)
    )
    page_rows = jnp.concatenate(
        [
            rms_latent(summed, kv_gain),
            rotate(summed[:, KVL:], row_pos.reshape(-1)).astype(jnp.bfloat16),
        ],
        1,
    )
    page_rows = page_rows.reshape(share, RP, width)
    draft_pos = jnp.tile(PRE_TOK + jnp.arange(2, dtype=jnp.int32), RP)
    draft_rows = jnp.concatenate(
        [
            rms_latent(draft_sum, kv_gain),
            rotate(draft_sum[:, KVL:], draft_pos).astype(jnp.bfloat16),
        ],
        1,
    )
    draft_rows = draft_rows.reshape(RP, 2, width)
    my_owners = lax.dynamic_slice_in_dim(owners, first_req, RP, 0)
    routing = (my_owners[None, :] == jnp.arange(pd_count, dtype=jnp.int32)[:, None]).astype(
        jnp.bfloat16
    )
    send_pages = jnp.einsum(
        "dk,tkw->dtw", routing, page_rows, preferred_element_type=jnp.float32
    ).astype(jnp.bfloat16)
    send_drafts = jnp.einsum(
        "dk,kjw->djw", routing, draft_rows, preferred_element_type=jnp.float32
    ).astype(jnp.bfloat16)
    pages, drafts = (
        lax.all_to_all(send_pages, "pd", split_axis=0, concat_axis=0, tiled=True),
        lax.all_to_all(send_drafts, "pd", split_axis=0, concat_axis=0, tiled=True),
    )
    heads_local = q_up.shape[1] // (DN + DR)
    query_full = jnp.dot(
        query_latent.reshape(requests * 2, QL), q_up, preferred_element_type=jnp.float32
    )
    query_full = query_full.reshape(requests, 2, heads_local, DN + DR)
    new_pos = jnp.broadcast_to(PRE_TOK + jnp.arange(2, dtype=jnp.int32)[None, :], (requests, 2))
    q_nope = query_full[..., :DN].astype(jnp.bfloat16)
    q_rot = rotate(query_full[..., DN:], new_pos[:, :, None]).astype(jnp.bfloat16)
    up_heads = kv_up.reshape(KVL, heads_local, DN + DV)
    w_value = up_heads[:, :, DN:]
    q_abs = jnp.einsum(
        "rjhd,khd->rjhk", q_nope, up_heads[:, :, :DN], preferred_element_type=jnp.float32
    ).astype(jnp.bfloat16)
    owner_table = owners.reshape(pd_count, RP) == mine_rank
    holding = jnp.sum(owner_table.astype(jnp.int32), axis=1)
    slot_of = jnp.sum(
        owner_table.astype(jnp.int32) * jnp.arange(RP, dtype=jnp.int32)[None, :], axis=1
    )
    owned_count = jnp.sum(holding)
    order = jnp.argsort((1 - holding) * pd_count + jnp.arange(pd_count, dtype=jnp.int32))
    draft_valid = (jnp.arange(2)[None, :] <= jnp.arange(2)[:, None])[:, None, :]
    empty = jnp.zeros((pd_count, 2, heads_local * DV), jnp.bfloat16)

    def finish(stats, source, request, q_lat, q_pos, result):
        stats = combine(stats, block_stats(drafts[source], q_lat, q_pos, draft_valid))
        attended = (stats[2] / stats[1][..., None]).astype(jnp.bfloat16)
        head_out = jnp.einsum("jhk,khd->jhd", attended, w_value, preferred_element_type=jnp.float32)
        keep = (jnp.arange(2) <= accepted[request]).astype(jnp.float32)[:, None, None]
        answer = (head_out * keep).astype(jnp.bfloat16).reshape(1, 2, heads_local * DV)
        return lax.dynamic_update_slice(result, answer, (source, 0, 0))

    def attend(turn, result):
        source = order[turn]
        request = source * RP + slot_of[source]
        q_lat = q_abs[request]
        q_pos = q_rot[request]
        seg_row = segment_ids[request]
        current = seg_row[PRE_TOK - 1]
        init = (
            jnp.full((2, heads_local), -1e30, jnp.float32),
            jnp.zeros((2, heads_local), jnp.float32),
            jnp.zeros((2, heads_local, KVL), jnp.float32),
        )
        valid = (seg_row == current)[None, None, :]
        stats = combine(
            init,
            block_stats(
                lax.all_gather(pages[source], "tp", axis=0, tiled=True), q_lat, q_pos, valid
            ),
        )
        return finish(stats, source, request, q_lat, q_pos, result)

    result = lax.fori_loop(0, owned_count, attend, empty)
    return (result.reshape(pd_count * 2, heads_local * DV), pages)


def encode(values):
    levels = []
    parts = []
    for first, last in ((0, KVL), (KVL, WIDTH)):
        block = values[first:last]
        top = jnp.maximum(jnp.max(jnp.abs(block), axis=0, keepdims=True), 1e-30)
        level = jnp.ceil(jnp.log2(top) * STEPS)
        codes = jnp.round(block * (jnp.exp2(level * (-1.0 / STEPS)) * TOP))
        parts.append(jnp.clip(codes, -TOP, TOP).astype(jnp.int32).astype(I16))
        levels.append(level.astype(jnp.int32))
    row = lax.broadcasted_iota(jnp.int32, (16, values.shape[1]), 0)
    extra = jnp.where(row == 0, levels[0], jnp.where(row == 1, levels[1], 0))
    return jnp.concatenate([*parts, extra.astype(I16)], 0)


def decode(codes):
    level = codes[WIDTH:CODED].astype(jnp.int32).astype(F32)
    step = jnp.exp2(level * (1.0 / STEPS)) * (1.0 / TOP)
    lat = codes[0:KVL].astype(jnp.int32).astype(F32) * step[0:1]
    rot = codes[KVL:WIDTH].astype(jnp.int32).astype(F32) * step[1:2]
    return jnp.concatenate([lat, rot], 0)


def key_rows(comp, gain, cosine, sine):
    lat = comp[:KVL]
    scale = lax.rsqrt(jnp.mean(lat * lat, axis=0, keepdims=True) + 1e-06)
    first = comp[KVL : KVL + HALF]
    second = comp[KVL + HALF :]
    return jnp.concatenate(
        [
            lat * scale * gain,
            first * cosine - second * sine,
            first * sine + second * cosine,
        ],
        0,
    )


def far(z, i):
    return jnp.where(z < 2, 3 - i, i)


def near(z, i):
    return jnp.where(z < 2, i, 3 - i)


def outer_rank(z):
    return (z == 0) | (z == 3)


def project_far_kernel(rank, hid_ref, down_ref, *refs):
    sum_ref, code_ref = refs[-2:]
    total = lax.dot_general(down_ref[...], hid_ref[0], NT, preferred_element_type=F32)
    for u in range(UNITS):
        sum_ref[0, u] = total[:, u * UNIT : (u + 1) * UNIT]

    @pl.when(outer_rank(rank[0]))
    def _():
        for u in range(UNITS):
            code_ref[0, u] = encode(total[:, u * UNIT : (u + 1) * UNIT])


def project_far(rank, hidden, down_t, request, after):
    depth = hidden.shape[-1]
    return pl.pallas_call(
        project_far_kernel,
        grid_spec=pltpu.PrefetchScalarGridSpec(
            num_scalar_prefetch=1,
            grid=(2,),
            in_specs=[
                pl.BlockSpec((1, SHARE, depth), lambda i, rank: (request, far(rank[0], i), 0)),
                VMEM,
                *([ANY] * len(after)),
            ],
            out_specs=[
                pl.BlockSpec((1, UNITS, WIDTH, UNIT), lambda i, rank: (i, 0, 0, 0)),
                pl.BlockSpec((1, UNITS, CODED, UNIT), lambda i, rank: (i, 0, 0, 0)),
            ],
        ),
        out_shape=[
            jax.ShapeDtypeStruct((2, UNITS, WIDTH, UNIT), F32),
            jax.ShapeDtypeStruct((2, UNITS, CODED, UNIT), I16),
        ],
        compiler_params=ROOM,
        cost_estimate=COST,
        name="project_far",
    )(rank, hidden, down_t, *after)


def project_near_kernel(rank, hid_ref, down_ref, *refs):
    sum_ref, *code_refs = refs[-3:]
    unit = pl.program_id(0)
    rows = hid_ref[...].reshape(LANES, hid_ref.shape[-1])
    total = lax.dot_general(down_ref[...], rows, NT, preferred_element_type=F32)
    for r in range(RP):
        sum_ref[0, 0, r] = total[:, r * UNIT : (r + 1) * UNIT]
    coded = outer_rank(rank[0]) & (pl.program_id(1) == 1)
    for mine, ref in zip((unit == 0, unit > 0), code_refs):

        @pl.when(coded & mine)
        def _(ref=ref):
            for r in range(RP):
                ref[0, r] = encode(total[:, r * UNIT : (r + 1) * UNIT])


def project_near(rank, hidden, down_t, after):
    depth = hidden.shape[-1]
    return pl.pallas_call(
        project_near_kernel,
        grid_spec=pltpu.PrefetchScalarGridSpec(
            num_scalar_prefetch=1,
            grid=(UNITS, 2),
            in_specs=[
                pl.BlockSpec(
                    (RP, UNIT, depth), lambda u, i, rank: (0, near(rank[0], i) * UNITS + u, 0)
                ),
                VMEM,
                *([ANY] * len(after)),
            ],
            out_specs=[
                pl.BlockSpec((1, 1, RP, WIDTH, UNIT), lambda u, i, rank: (u, i, 0, 0, 0)),
                pl.BlockSpec((1, RP, CODED, UNIT), lambda u, i, rank: (0, 0, 0, 0)),
                pl.BlockSpec(
                    (1, RP, CODED, UNIT), lambda u, i, rank: (jnp.maximum(u, 1) - 1, 0, 0, 0)
                ),
            ],
        ),
        out_shape=[
            jax.ShapeDtypeStruct((UNITS, 2, RP, WIDTH, UNIT), F32),
            jax.ShapeDtypeStruct((1, RP, CODED, UNIT), I16),
            jax.ShapeDtypeStruct((UNITS - 1, RP, CODED, UNIT), I16),
        ],
        compiler_params=ROOM,
        cost_estimate=COST,
        name="project_near",
    )(rank, hidden, down_t, *after)


def add_kernel(out_at, rank, own_ref, got_ref, *refs):
    @pl.when(~outer_rank(rank[0]))
    def _():
        for u in range(UNITS):
            refs[out_at][0, u] = encode(own_ref[u] + decode(got_ref[0, u]))


def add_on(rank, own, got, request=None, after=(), carried=()):
    chunk = lambda i, rank: (i, 0, 0, 0)
    if request is None:
        own_spec = pl.BlockSpec((None, UNITS, WIDTH, UNIT), chunk)
    else:
        own_spec = pl.BlockSpec(
            (UNITS, None, None, WIDTH, UNIT), lambda i, rank: (0, i, request, 0, 0)
        )
    return pl.pallas_call(
        functools.partial(add_kernel, -1 - len(carried)),
        grid_spec=pltpu.PrefetchScalarGridSpec(
            num_scalar_prefetch=1,
            grid=(2,),
            in_specs=[
                own_spec,
                pl.BlockSpec((1, UNITS, CODED, UNIT), chunk),
                *([ANY] * (len(after) + len(carried))),
            ],
            out_specs=[
                pl.BlockSpec((1, UNITS, CODED, UNIT), chunk),
                *([ANY] * len(carried)),
            ],
        ),
        out_shape=[
            jax.ShapeDtypeStruct((2, UNITS, CODED, UNIT), I16),
            *[jax.ShapeDtypeStruct(c.shape, c.dtype) for c in carried],
        ],
        input_output_aliases={3 + len(after) + n: 1 + n for n in range(len(carried))},
        compiler_params=SOME,
        cost_estimate=COST,
        name="add_on",
    )(rank, own, got, *after, *carried)


def hold_kernel(*refs):
    pass


def hold(block, after):
    return pl.pallas_call(
        hold_kernel,
        in_specs=[ANY] * (1 + len(after)),
        out_specs=ANY,
        out_shape=jax.ShapeDtypeStruct(block.shape, block.dtype),
        input_output_aliases={0: 0},
        compiler_params=SOME,
        cost_estimate=COST,
        name="hold",
    )(block, *after)


def gain_column(gain_ref):
    return jnp.broadcast_to(gain_ref[...], (UNIT, KVL)).T


def page_kernel(requests, rank, slot, own_ref, *refs):
    count = len(requests)
    got_refs, sent_refs, refs = refs[:count], refs[count : 2 * count], refs[2 * count :]
    side_refs, (gain_ref, cos_ref, sin_ref) = refs[:2], refs[2:5]
    out_ref = refs[-1]
    step = pl.program_id(0)
    column = gain_column(gain_ref)

    def write(u, comp):
        rows = key_rows(comp, column, cos_ref[u], sin_ref[u]).astype(BF)
        out_ref[0, :, u * UNIT : (u + 1) * UNIT] = rows

    for k in range(count):

        @pl.when((step == k) & outer_rank(rank[0]))
        def _(k=k):
            for u in range(UNITS):
                write(u, own_ref[u] + decode(got_refs[k][u]))

        @pl.when((step == k) & ~outer_rank(rank[0]))
        def _(k=k):
            for u in range(UNITS):
                side = side_refs[u > 0][max(u - 1, 0)]
                write(u, decode(sent_refs[k][u]) + decode(side))


def pages_of(requests, rank, slot, own, got, sent, side, gain, cosine, sine, base, count, after):
    first = pl.BlockSpec((None, UNITS, CODED, UNIT), lambda i, *_: (0, 0, 0, 0))
    second = pl.BlockSpec((None, UNITS, CODED, UNIT), lambda i, *_: (1, 0, 0, 0))
    table = pl.BlockSpec((UNITS, HALF, UNIT), lambda i, *_: (0, 0, 0))
    start, total = requests[0], len(requests)
    got, sent = got[start : start + total], sent[start : start + total]
    return pl.pallas_call(
        functools.partial(page_kernel, requests),
        grid_spec=pltpu.PrefetchScalarGridSpec(
            num_scalar_prefetch=2,
            grid=(total,),
            in_specs=[
                pl.BlockSpec(
                    (UNITS, None, None, WIDTH, UNIT), lambda i, *_: (0, 0, i + start, 0, 0)
                ),
                *([first] * total),
                *([second] * total),
                pl.BlockSpec((1, None, CODED, UNIT), lambda i, *_: (0, i + start, 0, 0)),
                pl.BlockSpec((UNITS - 1, None, CODED, UNIT), lambda i, *_: (0, i + start, 0, 0)),
                pl.BlockSpec((1, KVL), lambda i, *_: (0, 0)),
                table,
                table,
                *([ANY] * (len(base) + len(after))),
            ],
            out_specs=pl.BlockSpec(
                (1, WIDTH, SHARE), lambda i, rank, slot: (slot[i + start], 0, 0)
            ),
        ),
        out_shape=jax.ShapeDtypeStruct((count, WIDTH, SHARE), BF),
        input_output_aliases={8 + 2 * total + n: n for n in range(len(base))},
        compiler_params=SOME,
        cost_estimate=COST,
        name="pages",
    )(rank, slot, own, *got, *sent, *side, gain, cosine, sine, *base, *after)


def query_kernel(lat_ref, up_ref, draft_ref, down_ref, *refs):
    *key_refs, cos_ref, sin_ref, out_ref, split_ref = refs

    @pl.when(pl.program_id(0) == 0)
    def _():
        rest = lax.dot_general(draft_ref[...], down_ref[...], NT, preferred_element_type=F32)
        for n in range(3):
            term = rest.astype(BF).astype(F32)
            split_ref[n] = term
            rest = rest - term
        split_ref[3] = jnp.zeros_like(rest)

    full = jnp.dot(lat_ref[...], up_ref[...], preferred_element_type=F32)
    for h, key_ref in enumerate(key_refs):
        base = h * (DN + DR)
        nope = full[:, base : base + DN].astype(BF)
        first = full[:, base + DN : base + DN + HALF]
        second = full[:, base + DN + HALF : base + DN + DR]
        absorbed = lax.dot_general(nope, key_ref[...], NT, preferred_element_type=F32)
        cosine, sine = cos_ref[...], sin_ref[...]
        out_ref[h] = jnp.concatenate(
            [absorbed, first * cosine - second * sine, first * sine + second * cosine], 1
        )


def queries(latents, q_up, kv_up, draft, down_t, cosine, sine, after):
    rows = latents.shape[0]
    heads = q_up.shape[1] // (DN + DR)
    step = 4
    key_spec = [
        pl.BlockSpec((KVL, DN), lambda i, h=h: (0, 2 * (step * i + h))) for h in range(step)
    ]
    whole = lambda i: (0, 0)
    table = pl.BlockSpec((rows, HALF), whole)
    body = lambda *refs: query_kernel(*refs[:-3], *refs[-2:])
    return pl.pallas_call(
        body,
        grid=(heads // step,),
        in_specs=[
            pl.BlockSpec((rows, QL), whole),
            pl.BlockSpec((QL, step * (DN + DR)), lambda i: (0, i)),
            pl.BlockSpec(draft.shape, whole),
            pl.BlockSpec(down_t.shape, whole),
            *key_spec,
            table,
            table,
            ANY,
        ],
        out_specs=[
            pl.BlockSpec((step, rows, WIDTH), lambda i: (i, 0, 0)),
            pl.BlockSpec((4, rows, WIDTH), lambda i: (0, 0, 0)),
        ],
        out_shape=[
            jax.ShapeDtypeStruct((heads, rows, WIDTH), F32),
            jax.ShapeDtypeStruct((4, rows, WIDTH), F32),
        ],
        compiler_params=ROOM,
        cost_estimate=COST,
        name="queries",
    )(latents, q_up, draft, down_t, *([kv_up] * step), cosine, sine, after)


def attend_kernel(requests, rank, first_ref, *refs):
    count = len(requests)
    q_refs, draft_refs, refs = refs[:4], refs[4:8], refs[8:]
    own_ref, got_refs, refs = refs[0], refs[1 : 1 + count], refs[1 + count :]
    cos_ref, sin_ref, midcos_ref, midsin_ref, refs = *refs[:4], refs[4:]
    segment_ref, gain_ref, newcos_ref, newsin_ref, refs = *refs[:4], refs[4:]
    out_refs, keys_ref = refs[-5:-1], refs[-1]
    step = pl.program_id(0)
    request = step + requests[0]

    @pl.when(rank[0] == 3)
    def _():
        column = gain_column(gain_ref)
        for k in range(count):

            @pl.when(step == k)
            def _(k=k):
                for i, (cosine, sine) in enumerate(
                    ((cos_ref, sin_ref), (midcos_ref, midsin_ref))
                ):
                    for u in range(UNITS):
                        comp = own_ref[u, i] + decode(got_refs[k][i, u])
                        rows = key_rows(comp, column, cosine[u], sine[u])
                        start = (1 - i) * SHARE + u * UNIT
                        keys_ref[:, start : start + UNIT] = rows.astype(BF)

        scale = (DN + DR) ** (-0.5)
        local_rows = out_refs[0].shape[1]
        new = 2 * RP
        comp = 0.0
        for ref in draft_refs:
            terms = ref[...].astype(F32)
            comp = comp + (terms[0:new] + terms[new : 2 * new] + terms[2 * new : 3 * new])
        lat = comp[:, :KVL]
        norm = lax.rsqrt(jnp.mean(lat * lat, axis=-1, keepdims=True) + 1e-06)
        first = comp[:, KVL : KVL + HALF]
        second = comp[:, KVL + HALF :]
        cosine, sine = newcos_ref[...], newsin_ref[...]
        drafts = jnp.concatenate(
            [
                lat * norm * gain_ref[...],
                first * cosine - second * sine,
                first * sine + second * cosine,
            ],
            1,
        )
        drafts = jnp.concatenate([drafts, jnp.zeros((UNIT - new, WIDTH), F32)], 0).astype(BF)
        query = jnp.concatenate([ref[...] for ref in q_refs], 0)
        scores = jnp.dot(query, keys_ref[...], preferred_element_type=F32) * scale
        segments = segment_ref[pl.ds(first_ref[0] + request, 1), :]
        valid = segments[:, PRE_TOK // 2 :] == segments[:, PRE_TOK - 1 :]
        scores = jnp.where(valid, scores, -1e30)
        fresh = lax.dot_general(query, drafts, NT, preferred_element_type=F32) * scale
        row = lax.broadcasted_iota(jnp.int32, fresh.shape, 0)
        late = (row % local_rows) // (local_rows // 2)
        offset = lax.broadcasted_iota(jnp.int32, fresh.shape, 1) - 2 * request
        fresh = jnp.where((offset >= 0) & (offset <= late), fresh, -1e30)
        top = jnp.maximum(
            jnp.max(scores, axis=1, keepdims=True), jnp.max(fresh, axis=1, keepdims=True)
        )
        weights = jnp.exp(scores - top)
        fresh = jnp.exp(fresh - top)
        total = jnp.sum(weights, axis=1, keepdims=True) + jnp.sum(fresh, axis=1, keepdims=True)
        numer = lax.dot_general(
            weights.astype(BF), keys_ref[0:KVL, :], NT, preferred_element_type=F32
        )
        numer = numer + jnp.dot(fresh.astype(BF), drafts[:, :KVL], preferred_element_type=F32)
        result = (numer / total).astype(BF)
        for t, ref in enumerate(out_refs):
            ref[0] = result[t * local_rows : (t + 1) * local_rows]


def attend(requests, rank, first, messages, own, got, tables, segments, gain, cosine, sine, after):
    new = 2 * RP
    local_rows = (messages[0].shape[0] - 4 * new) // RP
    last = RP * local_rows // (4 * new)
    start, count = requests[0], len(requests)
    got = got[start : start + count]
    out = jax.ShapeDtypeStruct((count, local_rows, KVL), BF)
    whole = lambda i, *_: (0, 0)
    whole3 = lambda i, *_: (0, 0, 0)
    return pl.pallas_call(
        functools.partial(attend_kernel, requests),
        grid_spec=pltpu.PrefetchScalarGridSpec(
            num_scalar_prefetch=2,
            grid=(count,),
            in_specs=[
                *([pl.BlockSpec((local_rows, WIDTH), lambda i, *_: (i + start, 0))] * 4),
                *([pl.BlockSpec((4 * new, WIDTH), lambda i, *_: (last, 0))] * 4),
                pl.BlockSpec(
                    (UNITS, 2, None, WIDTH, UNIT), lambda i, *_: (0, 0, i + start, 0, 0)
                ),
                *([pl.BlockSpec((2, UNITS, CODED, UNIT), lambda i, *_: (0, 0, 0, 0))] * count),
                *([pl.BlockSpec((UNITS, HALF, UNIT), whole3)] * 4),
                pl.BlockSpec(segments.shape, whole),
                pl.BlockSpec((1, KVL), whole),
                pl.BlockSpec(cosine.shape, whole),
                pl.BlockSpec(sine.shape, whole),
                *([ANY] * len(after)),
            ],
            out_specs=[pl.BlockSpec((1, local_rows, KVL), lambda i, *_: (i, 0, 0))] * 4,
            scratch_shapes=[pltpu.VMEM((WIDTH, 2 * SHARE), BF)],
        ),
        out_shape=[out] * 4,
        compiler_params=SOME,
        cost_estimate=COST,
        name="attend",
    )(rank, first, *messages, *messages, own, *got, *tables, segments, gain, cosine, sine, *after)


def heads_kernel(step, slot, o_ref, keep_ref, *refs):
    out_ref = refs[-1]
    out_ref[...] = jnp.zeros_like(out_ref)
    for h, value_ref in enumerate(refs[:step]):
        row = jnp.dot(o_ref[h].astype(BF), value_ref[...], preferred_element_type=F32)
        row = (row * keep_ref[...]).astype(BF)
        for r in range(RP):
            out_ref[slot[r], :, h * DV : (h + 1) * DV] = row[2 * r : 2 * r + 2]


def heads_out(slot, attended, keep, kv_up, count, after):
    heads, rows, _ = attended.shape
    step = 8
    value_spec = [
        pl.BlockSpec((KVL, DV), lambda i, slot, h=h: (0, 2 * (step * i + h) + 1))
        for h in range(step)
    ]
    return pl.pallas_call(
        functools.partial(heads_kernel, step),
        grid_spec=pltpu.PrefetchScalarGridSpec(
            num_scalar_prefetch=1,
            grid=(heads // step,),
            in_specs=[
                pl.BlockSpec((step, rows, KVL), lambda i, slot: (i, 0, 0)),
                pl.BlockSpec((rows, DV), lambda i, slot: (0, 0)),
                *value_spec,
                *([ANY] * len(after)),
            ],
            out_specs=pl.BlockSpec((count, 2, step * DV), lambda i, slot: (0, 0, i)),
        ),
        out_shape=jax.ShapeDtypeStruct((count, 2, heads * DV), BF),
        compiler_params=ROOM,
        cost_estimate=COST,
        name="heads_out",
    )(slot, attended, keep, *([kv_up] * step), *after)


def emit_kernel(pages_ref, placed_ref, out_ref, same_ref, done):
    copy = pltpu.make_async_copy(pages_ref, out_ref, done)
    copy.start()
    copy.wait()


def emit(pages, placed):
    return pl.pallas_call(
        emit_kernel,
        in_specs=[VMEM, ANY],
        out_specs=[ANY, ANY],
        out_shape=[
            jax.ShapeDtypeStruct(pages.shape, pages.dtype),
            jax.ShapeDtypeStruct(placed.shape, placed.dtype),
        ],
        scratch_shapes=[pltpu.SemaphoreType.DMA],
        input_output_aliases={1: 1},
        compiler_params=SOME,
        cost_estimate=COST,
        name="emit",
    )(pages, placed)


def rope_tables(position):
    freq = jnp.exp(-jnp.log(10000.0) * jnp.arange(HALF, dtype=F32) / HALF)
    angle = position.astype(F32)[..., None] * freq
    return jnp.cos(angle), jnp.sin(angle)


def local_line(
    prefill_hidden,
    draft_hidden,
    kv_down,
    kv_gain,
    query_latent,
    q_up,
    kv_up,
    owners,
    segment_ids,
    accepted,
):
    pd_count = lax.axis_size("pd")
    z = lax.axis_index("tp")
    p = lax.axis_index("pd")
    first_req = p * RP

    gain = kv_gain.reshape(1, KVL)
    rank = z.astype(jnp.int32).reshape(1)
    hidden = prefill_hidden.reshape(RP, PRE_TOK, prefill_hidden.shape[1])
    down_t = kv_down.T
    inward, across, outward = [(0, 1), (3, 2)], [(1, 2), (2, 1)], [(2, 3), (1, 0)]

    far_sums, inner, crossed, sent, outer = [], [], [], [], []

    def send_far(r, after):
        total, codes = project_far(rank, hidden, down_t, r, after)
        far_sums.append(total)
        inner.append(lax.ppermute(codes, "tp", inward))

    def first_hop(r, after, carried=()):
        block, *carried = add_on(rank, far_sums[r], inner[r], after=after, carried=carried)
        crossed.append(lax.ppermute(block, "tp", across))
        return [block, *carried]

    def second_hop(r, after, awaited=()):
        (block,) = add_on(rank, near_sums, crossed[r], r, after)
        if awaited:
            block = hold(block, awaited)
        sent.append(block)
        outer.append(lax.ppermute(block, "tp", outward))
        return [block]

    send_far(0, [])
    send_far(1, far_sums[:1])

    latents = lax.dynamic_slice_in_dim(query_latent, first_req, RP, 0).reshape(RP * 2, QL)
    new_pos = jnp.tile(PRE_TOK + jnp.arange(2, dtype=jnp.int32), RP)
    new_cos, new_sin = rope_tables(new_pos)
    query, terms = queries(
        latents, q_up, kv_up, draft_hidden, down_t, new_cos, new_sin, far_sums[1]
    )
    heads = query.shape[0]
    query = query.reshape(heads, RP, 2, WIDTH).transpose(1, 2, 0, 3)
    message = jnp.concatenate(
        [query.reshape(RP * 2 * heads, WIDTH), terms.reshape(8 * RP, WIDTH)], 0
    ).astype(BF)
    messages = [lax.ppermute(message, "tp", [(t, 3)]) for t in range(3)] + [message]

    done = first_hop(0, [terms])
    send_far(2, done)
    near_sums, *side = project_near(rank, hidden, down_t, far_sums[2:])
    done = first_hop(1, [near_sums])
    done = second_hop(0, done, messages[:3])
    send_far(3, done)
    steps = jnp.arange(SHARE, dtype=jnp.int32).reshape(UNITS, UNIT)
    tables = [
        jnp.swapaxes(t, 1, 2)
        for t in (*rope_tables(z * SHARE + steps), *rope_tables(2 * SHARE + steps))
    ]
    block, side[0] = first_hop(2, far_sums[3:], side[:1])
    side = [lax.ppermute(codes, "tp", inward) for codes in side]
    done = second_hop(1, [block], outer[:1])
    done = first_hop(3, done)
    done = second_hop(2, [*done, *tables], [outer[1], side[0]])
    done = second_hop(3, done, outer[2:])

    def attend_to(requests, after):
        result = attend(
            requests,
            rank,
            first_req.astype(jnp.int32).reshape(1),
            messages,
            near_sums,
            outer,
            tables,
            segment_ids,
            gain,
            new_cos,
            new_sin,
            after,
        )
        return result, [lax.ppermute(result[t], "tp", [(3, t)]) for t in range(3)]

    my_owners = lax.dynamic_slice_in_dim(owners, first_req, RP, 0)
    early, late = tuple(range(RP - 1)), (RP - 1,)

    def pages_to(requests, base, after):
        return pages_of(
            requests,
            rank,
            my_owners,
            near_sums,
            outer,
            sent,
            side,
            gain,
            tables[0],
            tables[1],
            base,
            pd_count,
            after,
        )

    results, backs = [None] * 2, [None] * 2
    results[0], backs[0] = attend_to(early, done)
    base = [jnp.zeros((pd_count, WIDTH, SHARE), BF)] if pd_count > RP else []
    pages = pages_to(early, base, results[0][:1])
    pages = pages_to(late, [pages], backs[0])
    results[1], backs[1] = attend_to(late, [pages])
    cache = lax.all_to_all(pages, "pd", split_axis=0, concat_axis=0, tiled=True)

    attended = [
        jnp.where(z == 3, result[3], back[0] + back[1] + back[2])
        for result, back in zip(results, backs)
    ]
    attended = jnp.concatenate(attended, 0).reshape(RP, 2, heads, KVL).transpose(2, 0, 1, 3)
    attended = attended.reshape(heads, RP * 2, KVL).astype(F32)
    my_accepted = lax.dynamic_slice_in_dim(accepted, first_req, RP, 0)
    keep = (jnp.arange(2)[None, :] <= my_accepted[:, None]).astype(F32).reshape(RP * 2, 1)
    placed = heads_out(
        my_owners,
        attended,
        jnp.broadcast_to(keep, (RP * 2, DV)),
        kv_up,
        pd_count,
        [pages],
    )
    cache, placed = emit(cache, placed)
    placed = lax.all_to_all(placed, "pd", split_axis=0, concat_axis=0, tiled=True)
    return (placed.reshape(pd_count * 2, heads * DV), jnp.swapaxes(cache, 1, 2))


def solution(mesh):
    placed = (
        P(("groups", "pd"), "tp"),
        P(("groups", "pd"), "tp"),
        P("tp", None),
        P(),
        P("groups", None, None),
        P(None, "tp"),
        P(None, "tp"),
        P("groups"),
        P("groups", None),
        P("groups"),
    )
    return jax.shard_map(
        local_line if mesh.shape["tp"] == 4 else local_general,
        mesh=mesh,
        in_specs=placed,
        out_specs=(P(("groups", "pd"), "tp"), P(("groups", "pd"), "tp", None)),
        check_vma=False,
    )
```

```python
import functools

import jax
import jax.numpy as jnp
from jax import lax
from jax.experimental import pallas as pl
from jax.experimental.pallas import tpu as pltpu
from jax.sharding import PartitionSpec as P

DN = 128
DR = 64
DV = 128
KVL = 512
QL = 1536
PRE_TOK = 1536
RP = 4
WIDTH = KVL + DR
HALF = DR // 2
CODED = WIDTH + 16
SHARE = PRE_TOK // 4
UNIT = 128
UNITS = SHARE // UNIT
LANES = RP * UNIT
STEPS = 256.0
TOP = 32767.0
BF = jnp.bfloat16
F32 = jnp.float32
I16 = jnp.int16
NT = (((1,), (1,)), ((), ()))
ROOM = pltpu.CompilerParams(vmem_limit_bytes=60 << 20)
SOME = pltpu.CompilerParams(vmem_limit_bytes=52 << 20)
ANY = pl.BlockSpec(memory_space=pl.ANY)
VMEM = pl.BlockSpec(memory_space=pltpu.VMEM)
SMEM = pl.BlockSpec(memory_space=pltpu.SMEM)


COST = pl.CostEstimate(flops=1024, bytes_accessed=1024, transcendentals=0)


def rms_latent(comp, gain):
    lat = comp[:, :KVL]
    scale = lax.rsqrt(jnp.mean(lat * lat, axis=-1, keepdims=True) + 1e-06)
    return (lat * scale * gain).astype(jnp.bfloat16)


def rotate(values, position):
    half = values.shape[-1] // 2
    freq = jnp.exp(-jnp.log(10000.0) * jnp.arange(half, dtype=jnp.float32) / half)
    angle = position.astype(jnp.float32)[..., None] * freq
    cosine = jnp.cos(angle)
    sine = jnp.sin(angle)
    first = values[..., :half]
    second = values[..., half:]
    return jnp.concatenate([first * cosine - second * sine, first * sine + second * cosine], -1)


def block_stats(keys, q_lat, q_pos, valid):
    scale = (DN + DR) ** (-0.5)
    scores = jnp.einsum("jhk,tk->jht", q_lat, keys[:, :KVL], preferred_element_type=jnp.float32)
    scores = (
        scores + jnp.einsum("jhk,tk->jht", q_pos, keys[:, KVL:], preferred_element_type=jnp.float32)
    ) * scale
    scores = jnp.where(valid, scores, -1e30)
    top = jnp.max(scores, axis=-1)
    weights = jnp.where(valid, jnp.exp(scores - top[..., None]), 0.0)
    total = jnp.sum(weights, axis=-1)
    numer = jnp.einsum(
        "jht,tk->jhk",
        weights.astype(jnp.bfloat16),
        keys[:, :KVL],
        preferred_element_type=jnp.float32,
    )
    return (top, total, numer)


def combine(left, right):
    top = jnp.maximum(left[0], right[0])
    left_scale = jnp.exp(left[0] - top)
    right_scale = jnp.exp(right[0] - top)
    total = left[1] * left_scale + right[1] * right_scale
    numer = left[2] * left_scale[..., None] + right[2] * right_scale[..., None]
    return (top, total, numer)


def local_general(
    prefill_hidden,
    draft_hidden,
    kv_down,
    kv_gain,
    query_latent,
    q_up,
    kv_up,
    owners,
    segment_ids,
    accepted,
):
    tp_count = lax.axis_size("tp")
    pd_count = lax.axis_size("pd")
    tp_rank = lax.axis_index("tp")
    mine_rank = lax.axis_index("pd")
    requests = owners.shape[0]
    share = PRE_TOK // tp_count
    width = KVL + DR
    local_hidden = prefill_hidden.reshape(RP, PRE_TOK, prefill_hidden.shape[1])
    summed = lax.psum_scatter(
        jnp.einsum(
            "rtd,dw->trw", local_hidden, kv_down, preferred_element_type=jnp.float32
        ).reshape(lax.axis_size("tp") * share, RP * width),
        "tp",
        scatter_dimension=0,
        tiled=True,
    ).reshape(share * RP, width)
    draft_sum = lax.psum(jnp.dot(draft_hidden, kv_down, preferred_element_type=jnp.float32), "tp")
    first_req = mine_rank * RP
    row_pos = jnp.broadcast_to(
        tp_rank * share + jnp.arange(share, dtype=jnp.int32)[:, None], (share, RP)
    )
    page_rows = jnp.concatenate(
        [
            rms_latent(summed, kv_gain),
            rotate(summed[:, KVL:], row_pos.reshape(-1)).astype(jnp.bfloat16),
        ],
        1,
    )
    page_rows = page_rows.reshape(share, RP, width)
    draft_pos = jnp.tile(PRE_TOK + jnp.arange(2, dtype=jnp.int32), RP)
    draft_rows = jnp.concatenate(
        [
            rms_latent(draft_sum, kv_gain),
            rotate(draft_sum[:, KVL:], draft_pos).astype(jnp.bfloat16),
        ],
        1,
    )
    draft_rows = draft_rows.reshape(RP, 2, width)
    my_owners = lax.dynamic_slice_in_dim(owners, first_req, RP, 0)
    routing = (my_owners[None, :] == jnp.arange(pd_count, dtype=jnp.int32)[:, None]).astype(
        jnp.bfloat16
    )
    send_pages = jnp.einsum(
        "dk,tkw->dtw", routing, page_rows, preferred_element_type=jnp.float32
    ).astype(jnp.bfloat16)
    send_drafts = jnp.einsum(
        "dk,kjw->djw", routing, draft_rows, preferred_element_type=jnp.float32
    ).astype(jnp.bfloat16)
    pages, drafts = (
        lax.all_to_all(send_pages, "pd", split_axis=0, concat_axis=0, tiled=True),
        lax.all_to_all(send_drafts, "pd", split_axis=0, concat_axis=0, tiled=True),
    )
    heads_local = q_up.shape[1] // (DN + DR)
    query_full = jnp.dot(
        query_latent.reshape(requests * 2, QL), q_up, preferred_element_type=jnp.float32
    )
    query_full = query_full.reshape(requests, 2, heads_local, DN + DR)
    new_pos = jnp.broadcast_to(PRE_TOK + jnp.arange(2, dtype=jnp.int32)[None, :], (requests, 2))
    q_nope = query_full[..., :DN].astype(jnp.bfloat16)
    q_rot = rotate(query_full[..., DN:], new_pos[:, :, None]).astype(jnp.bfloat16)
    up_heads = kv_up.reshape(KVL, heads_local, DN + DV)
    w_value = up_heads[:, :, DN:]
    q_abs = jnp.einsum(
        "rjhd,khd->rjhk", q_nope, up_heads[:, :, :DN], preferred_element_type=jnp.float32
    ).astype(jnp.bfloat16)
    owner_table = owners.reshape(pd_count, RP) == mine_rank
    holding = jnp.sum(owner_table.astype(jnp.int32), axis=1)
    slot_of = jnp.sum(
        owner_table.astype(jnp.int32) * jnp.arange(RP, dtype=jnp.int32)[None, :], axis=1
    )
    owned_count = jnp.sum(holding)
    order = jnp.argsort((1 - holding) * pd_count + jnp.arange(pd_count, dtype=jnp.int32))
    draft_valid = (jnp.arange(2)[None, :] <= jnp.arange(2)[:, None])[:, None, :]
    empty = jnp.zeros((pd_count, 2, heads_local * DV), jnp.bfloat16)

    def finish(stats, source, request, q_lat, q_pos, result):
        stats = combine(stats, block_stats(drafts[source], q_lat, q_pos, draft_valid))
        attended = (stats[2] / stats[1][..., None]).astype(jnp.bfloat16)
        head_out = jnp.einsum("jhk,khd->jhd", attended, w_value, preferred_element_type=jnp.float32)
        keep = (jnp.arange(2) <= accepted[request]).astype(jnp.float32)[:, None, None]
        answer = (head_out * keep).astype(jnp.bfloat16).reshape(1, 2, heads_local * DV)
        return lax.dynamic_update_slice(result, answer, (source, 0, 0))

    def attend(turn, result):
        source = order[turn]
        request = source * RP + slot_of[source]
        q_lat = q_abs[request]
        q_pos = q_rot[request]
        seg_row = segment_ids[request]
        current = seg_row[PRE_TOK - 1]
        init = (
            jnp.full((2, heads_local), -1e30, jnp.float32),
            jnp.zeros((2, heads_local), jnp.float32),
            jnp.zeros((2, heads_local, KVL), jnp.float32),
        )
        valid = (seg_row == current)[None, None, :]
        stats = combine(
            init,
            block_stats(
                lax.all_gather(pages[source], "tp", axis=0, tiled=True), q_lat, q_pos, valid
            ),
        )
        return finish(stats, source, request, q_lat, q_pos, result)

    result = lax.fori_loop(0, owned_count, attend, empty)
    return (result.reshape(pd_count * 2, heads_local * DV), pages)


def encode(values):
    levels = []
    parts = []
    for first, last in ((0, KVL), (KVL, WIDTH)):
        block = values[first:last]
        top = jnp.maximum(jnp.max(jnp.abs(block), axis=0, keepdims=True), 1e-30)
        level = jnp.ceil(jnp.log2(top) * STEPS)
        codes = jnp.round(block * (jnp.exp2(level * (-1.0 / STEPS)) * TOP))
        parts.append(jnp.clip(codes, -TOP, TOP).astype(jnp.int32).astype(I16))
        levels.append(level.astype(jnp.int32))
    row = lax.broadcasted_iota(jnp.int32, (16, values.shape[1]), 0)
    extra = jnp.where(row == 0, levels[0], jnp.where(row == 1, levels[1], 0))
    return jnp.concatenate([*parts, extra.astype(I16)], 0)


def decode(codes):
    level = codes[WIDTH:CODED].astype(jnp.int32).astype(F32)
    step = jnp.exp2(level * (1.0 / STEPS)) * (1.0 / TOP)
    lat = codes[0:KVL].astype(jnp.int32).astype(F32) * step[0:1]
    rot = codes[KVL:WIDTH].astype(jnp.int32).astype(F32) * step[1:2]
    return jnp.concatenate([lat, rot], 0)


def key_rows(comp, gain, cosine, sine):
    lat = comp[:KVL]
    scale = lax.rsqrt(jnp.mean(lat * lat, axis=0, keepdims=True) + 1e-06)
    first = comp[KVL : KVL + HALF]
    second = comp[KVL + HALF :]
    return jnp.concatenate(
        [
            lat * scale * gain,
            first * cosine - second * sine,
            first * sine + second * cosine,
        ],
        0,
    )


def far(z, i):
    return jnp.where(z < 2, 3 - i, i)


def near(z, i):
    return jnp.where(z < 2, i, 3 - i)


def outer_rank(z):
    return (z == 0) | (z == 3)


def project_far_kernel(new, rank, hid_ref, down_ref, *refs):
    sum_ref, code_ref = refs[-2 - new :][:2]
    if new:
        @pl.when(pl.program_id(0) == 0)
        def _():
            split_ref = refs[-1]
            rest = lax.dot_general(
                refs[0][...], down_ref[...], NT, preferred_element_type=F32
            )
            for n in range(3):
                term = rest.astype(BF).astype(F32)
                split_ref[n] = term
                rest = rest - term
            split_ref[3] = jnp.zeros_like(rest)

    total = lax.dot_general(down_ref[...], hid_ref[0], NT, preferred_element_type=F32)
    for u in range(UNITS):
        sum_ref[0, u] = total[:, u * UNIT : (u + 1) * UNIT]

    @pl.when(outer_rank(rank[0]))
    def _():
        for u in range(UNITS):
            code_ref[0, u] = encode(total[:, u * UNIT : (u + 1) * UNIT])


def project_far(rank, hidden, down_t, request, after, draft=()):
    depth = hidden.shape[-1]
    return pl.pallas_call(
        functools.partial(project_far_kernel, len(draft)),
        grid_spec=pltpu.PrefetchScalarGridSpec(
            num_scalar_prefetch=1,
            grid=(2,),
            in_specs=[
                pl.BlockSpec((1, SHARE, depth), lambda i, rank: (request, far(rank[0], i), 0)),
                VMEM,
                *([VMEM] * len(draft)),
                *([ANY] * len(after)),
            ],
            out_specs=[
                pl.BlockSpec((1, UNITS, WIDTH, UNIT), lambda i, rank: (i, 0, 0, 0)),
                pl.BlockSpec((1, UNITS, CODED, UNIT), lambda i, rank: (i, 0, 0, 0)),
                *[
                    pl.BlockSpec((4, d.shape[0], WIDTH), lambda i, rank: (0, 0, 0)) for d in draft
                ],
            ],
        ),
        out_shape=[
            jax.ShapeDtypeStruct((2, UNITS, WIDTH, UNIT), F32),
            jax.ShapeDtypeStruct((2, UNITS, CODED, UNIT), I16),
            *[jax.ShapeDtypeStruct((4, d.shape[0], WIDTH), F32) for d in draft],
        ],
        compiler_params=ROOM,
        cost_estimate=COST,
        name="project_far",
    )(rank, hidden, down_t, *draft, *after)


def project_near_kernel(rank, hid_ref, down_ref, *refs):
    sum_ref, *code_refs = refs[-3:]
    unit = pl.program_id(0)
    rows = hid_ref[...].reshape(LANES, hid_ref.shape[-1])
    total = lax.dot_general(down_ref[...], rows, NT, preferred_element_type=F32)
    for r in range(RP):
        sum_ref[0, 0, r] = total[:, r * UNIT : (r + 1) * UNIT]
    coded = outer_rank(rank[0]) & (pl.program_id(1) == 1)
    for mine, ref in zip((unit == 0, unit > 0), code_refs):

        @pl.when(coded & mine)
        def _(ref=ref):
            for r in range(RP):
                ref[0, r] = encode(total[:, r * UNIT : (r + 1) * UNIT])


def project_near(rank, hidden, down_t, after):
    depth = hidden.shape[-1]
    return pl.pallas_call(
        project_near_kernel,
        grid_spec=pltpu.PrefetchScalarGridSpec(
            num_scalar_prefetch=1,
            grid=(UNITS, 2),
            in_specs=[
                pl.BlockSpec(
                    (RP, UNIT, depth), lambda u, i, rank: (0, near(rank[0], i) * UNITS + u, 0)
                ),
                VMEM,
                *([ANY] * len(after)),
            ],
            out_specs=[
                pl.BlockSpec((1, 1, RP, WIDTH, UNIT), lambda u, i, rank: (u, i, 0, 0, 0)),
                pl.BlockSpec((1, RP, CODED, UNIT), lambda u, i, rank: (0, 0, 0, 0)),
                pl.BlockSpec(
                    (1, RP, CODED, UNIT), lambda u, i, rank: (jnp.maximum(u, 1) - 1, 0, 0, 0)
                ),
            ],
        ),
        out_shape=[
            jax.ShapeDtypeStruct((UNITS, 2, RP, WIDTH, UNIT), F32),
            jax.ShapeDtypeStruct((1, RP, CODED, UNIT), I16),
            jax.ShapeDtypeStruct((UNITS - 1, RP, CODED, UNIT), I16),
        ],
        compiler_params=ROOM,
        cost_estimate=COST,
        name="project_near",
    )(rank, hidden, down_t, *after)


def add_kernel(out_at, rank, own_ref, got_ref, *refs):
    @pl.when(~outer_rank(rank[0]))
    def _():
        for u in range(UNITS):
            refs[out_at][0, u] = encode(own_ref[u] + decode(got_ref[0, u]))


def add_on(rank, own, got, request=None, after=(), carried=()):
    chunk = lambda i, rank: (i, 0, 0, 0)
    if request is None:
        own_spec = pl.BlockSpec((None, UNITS, WIDTH, UNIT), chunk)
    else:
        own_spec = pl.BlockSpec(
            (UNITS, None, None, WIDTH, UNIT), lambda i, rank: (0, i, request, 0, 0)
        )
    return pl.pallas_call(
        functools.partial(add_kernel, -1 - len(carried)),
        grid_spec=pltpu.PrefetchScalarGridSpec(
            num_scalar_prefetch=1,
            grid=(2,),
            in_specs=[
                own_spec,
                pl.BlockSpec((1, UNITS, CODED, UNIT), chunk),
                *([ANY] * (len(after) + len(carried))),
            ],
            out_specs=[
                pl.BlockSpec((1, UNITS, CODED, UNIT), chunk),
                *([ANY] * len(carried)),
            ],
        ),
        out_shape=[
            jax.ShapeDtypeStruct((2, UNITS, CODED, UNIT), I16),
            *[jax.ShapeDtypeStruct(c.shape, c.dtype) for c in carried],
        ],
        input_output_aliases={3 + len(after) + n: 1 + n for n in range(len(carried))},
        compiler_params=SOME,
        cost_estimate=COST,
        name="add_on",
    )(rank, own, got, *after, *carried)


def hold_kernel(*refs):
    pass


def hold(block, after):
    return pl.pallas_call(
        hold_kernel,
        in_specs=[ANY] * (1 + len(after)),
        out_specs=ANY,
        out_shape=jax.ShapeDtypeStruct(block.shape, block.dtype),
        input_output_aliases={0: 0},
        compiler_params=SOME,
        cost_estimate=COST,
        name="hold",
    )(block, *after)


def gain_column(gain_ref):
    return jnp.broadcast_to(gain_ref[...], (UNIT, KVL)).T


def page_kernel(requests, rank, slot, own_ref, *refs):
    count = len(requests)
    got_refs, sent_refs, refs = refs[:count], refs[count : 2 * count], refs[2 * count :]
    side_refs, (gain_ref, cos_ref, sin_ref) = refs[:2], refs[2:5]
    out_ref = refs[-1]
    step = pl.program_id(0)
    column = gain_column(gain_ref)

    def write(u, comp):
        rows = key_rows(comp, column, cos_ref[u], sin_ref[u]).astype(BF)
        out_ref[0, :, u * UNIT : (u + 1) * UNIT] = rows

    for k in range(count):

        @pl.when((step == k) & outer_rank(rank[0]))
        def _(k=k):
            for u in range(UNITS):
                write(u, own_ref[u] + decode(got_refs[k][u]))

        @pl.when((step == k) & ~outer_rank(rank[0]))
        def _(k=k):
            for u in range(UNITS):
                side = side_refs[u > 0][max(u - 1, 0)]
                write(u, decode(sent_refs[k][u]) + decode(side))


def pages_of(requests, rank, slot, own, got, sent, side, gain, cosine, sine, base, count, after):
    first = pl.BlockSpec((None, UNITS, CODED, UNIT), lambda i, *_: (0, 0, 0, 0))
    second = pl.BlockSpec((None, UNITS, CODED, UNIT), lambda i, *_: (1, 0, 0, 0))
    table = pl.BlockSpec((UNITS, HALF, UNIT), lambda i, *_: (0, 0, 0))
    start, total = requests[0], len(requests)
    got, sent = got[start : start + total], sent[start : start + total]
    return pl.pallas_call(
        functools.partial(page_kernel, requests),
        grid_spec=pltpu.PrefetchScalarGridSpec(
            num_scalar_prefetch=2,
            grid=(total,),
            in_specs=[
                pl.BlockSpec(
                    (UNITS, None, None, WIDTH, UNIT), lambda i, *_: (0, 0, i + start, 0, 0)
                ),
                *([first] * total),
                *([second] * total),
                pl.BlockSpec((1, None, CODED, UNIT), lambda i, *_: (0, i + start, 0, 0)),
                pl.BlockSpec((UNITS - 1, None, CODED, UNIT), lambda i, *_: (0, i + start, 0, 0)),
                pl.BlockSpec((1, KVL), lambda i, *_: (0, 0)),
                table,
                table,
                *([ANY] * (len(base) + len(after))),
            ],
            out_specs=pl.BlockSpec(
                (1, WIDTH, SHARE), lambda i, rank, slot: (slot[i + start], 0, 0)
            ),
        ),
        out_shape=jax.ShapeDtypeStruct((count, WIDTH, SHARE), BF),
        input_output_aliases={8 + 2 * total + n: n for n in range(len(base))},
        compiler_params=SOME,
        cost_estimate=COST,
        name="pages",
    )(rank, slot, own, *got, *sent, *side, gain, cosine, sine, *base, *after)


def query_kernel(lat_ref, up_ref, *refs):
    *key_refs, cos_ref, sin_ref, out_ref = refs

    full = jnp.dot(lat_ref[...], up_ref[...], preferred_element_type=F32)
    for h, key_ref in enumerate(key_refs):
        base = h * (DN + DR)
        nope = full[:, base : base + DN].astype(BF)
        first = full[:, base + DN : base + DN + HALF]
        second = full[:, base + DN + HALF : base + DN + DR]
        absorbed = lax.dot_general(nope, key_ref[...], NT, preferred_element_type=F32)
        cosine, sine = cos_ref[...], sin_ref[...]
        out_ref[h] = jnp.concatenate(
            [absorbed, first * cosine - second * sine, first * sine + second * cosine], 1
        )


def queries(latents, q_up, kv_up, cosine, sine, after):
    rows = latents.shape[0]
    heads = q_up.shape[1] // (DN + DR)
    step = 4
    key_spec = [
        pl.BlockSpec((KVL, DN), lambda i, h=h: (0, 2 * (step * i + h))) for h in range(step)
    ]
    whole = lambda i: (0, 0)
    table = pl.BlockSpec((rows, HALF), whole)
    body = lambda *refs: query_kernel(*refs[:-2], refs[-1])
    return pl.pallas_call(
        body,
        grid=(heads // step,),
        in_specs=[
            pl.BlockSpec((rows, QL), whole),
            pl.BlockSpec((QL, step * (DN + DR)), lambda i: (0, i)),
            *key_spec,
            table,
            table,
            ANY,
        ],
        out_specs=pl.BlockSpec((step, rows, WIDTH), lambda i: (i, 0, 0)),
        out_shape=jax.ShapeDtypeStruct((heads, rows, WIDTH), F32),
        compiler_params=ROOM,
        cost_estimate=COST,
        name="queries",
    )(latents, q_up, *([kv_up] * step), cosine, sine, after)


def attend_kernel(requests, rank, first_ref, *refs):
    count = len(requests)
    q_refs, draft_refs, refs = refs[:4], refs[4:8], refs[8:]
    own_ref, got_refs, refs = refs[0], refs[1 : 1 + count], refs[1 + count :]
    cos_ref, sin_ref, midcos_ref, midsin_ref, refs = *refs[:4], refs[4:]
    segment_ref, gain_ref, newcos_ref, newsin_ref, refs = *refs[:4], refs[4:]
    out_refs, keys_ref = refs[-5:-1], refs[-1]
    step = pl.program_id(0)
    request = step + requests[0]

    @pl.when(rank[0] == 3)
    def _():
        column = gain_column(gain_ref)
        for k in range(count):

            @pl.when(step == k)
            def _(k=k):
                for i, (cosine, sine) in enumerate(
                    ((cos_ref, sin_ref), (midcos_ref, midsin_ref))
                ):
                    for u in range(UNITS):
                        comp = own_ref[u, i] + decode(got_refs[k][i, u])
                        rows = key_rows(comp, column, cosine[u], sine[u])
                        start = (1 - i) * SHARE + u * UNIT
                        keys_ref[:, start : start + UNIT] = rows.astype(BF)

        scale = (DN + DR) ** (-0.5)
        local_rows = out_refs[0].shape[1]
        new = 2 * RP
        comp = 0.0
        for ref in draft_refs:
            terms = ref[...].astype(F32)
            comp = comp + (terms[0:new] + terms[new : 2 * new] + terms[2 * new : 3 * new])
        lat = comp[:, :KVL]
        norm = lax.rsqrt(jnp.mean(lat * lat, axis=-1, keepdims=True) + 1e-06)
        first = comp[:, KVL : KVL + HALF]
        second = comp[:, KVL + HALF :]
        cosine, sine = newcos_ref[...], newsin_ref[...]
        drafts = jnp.concatenate(
            [
                lat * norm * gain_ref[...],
                first * cosine - second * sine,
                first * sine + second * cosine,
            ],
            1,
        )
        drafts = jnp.concatenate([drafts, jnp.zeros((UNIT - new, WIDTH), F32)], 0).astype(BF)
        query = jnp.concatenate([ref[...] for ref in q_refs], 0)
        scores = jnp.dot(query, keys_ref[...], preferred_element_type=F32) * scale
        segments = segment_ref[pl.ds(first_ref[0] + request, 1), :]
        valid = segments[:, PRE_TOK // 2 :] == segments[:, PRE_TOK - 1 :]
        scores = jnp.where(valid, scores, -1e30)
        fresh = lax.dot_general(query, drafts, NT, preferred_element_type=F32) * scale
        row = lax.broadcasted_iota(jnp.int32, fresh.shape, 0)
        late = (row % local_rows) // (local_rows // 2)
        offset = lax.broadcasted_iota(jnp.int32, fresh.shape, 1) - 2 * request
        fresh = jnp.where((offset >= 0) & (offset <= late), fresh, -1e30)
        top = jnp.maximum(
            jnp.max(scores, axis=1, keepdims=True), jnp.max(fresh, axis=1, keepdims=True)
        )
        weights = jnp.exp(scores - top)
        fresh = jnp.exp(fresh - top)
        total = jnp.sum(weights, axis=1, keepdims=True) + jnp.sum(fresh, axis=1, keepdims=True)
        numer = lax.dot_general(
            weights.astype(BF), keys_ref[0:KVL, :], NT, preferred_element_type=F32
        )
        numer = numer + jnp.dot(fresh.astype(BF), drafts[:, :KVL], preferred_element_type=F32)
        result = (numer / total).astype(BF)
        for t, ref in enumerate(out_refs):
            ref[0] = result[t * local_rows : (t + 1) * local_rows]


def attend(requests, rank, first, messages, own, got, tables, segments, gain, cosine, sine, after):
    new = 2 * RP
    local_rows = (messages[0].shape[0] - 4 * new) // RP
    last = RP * local_rows // (4 * new)
    start, count = requests[0], len(requests)
    got = got[start : start + count]
    out = jax.ShapeDtypeStruct((count, local_rows, KVL), BF)
    whole = lambda i, *_: (0, 0)
    whole3 = lambda i, *_: (0, 0, 0)
    return pl.pallas_call(
        functools.partial(attend_kernel, requests),
        grid_spec=pltpu.PrefetchScalarGridSpec(
            num_scalar_prefetch=2,
            grid=(count,),
            in_specs=[
                *([pl.BlockSpec((local_rows, WIDTH), lambda i, *_: (i + start, 0))] * 4),
                *([pl.BlockSpec((4 * new, WIDTH), lambda i, *_: (last, 0))] * 4),
                pl.BlockSpec(
                    (UNITS, 2, None, WIDTH, UNIT), lambda i, *_: (0, 0, i + start, 0, 0)
                ),
                *([pl.BlockSpec((2, UNITS, CODED, UNIT), lambda i, *_: (0, 0, 0, 0))] * count),
                *([pl.BlockSpec((UNITS, HALF, UNIT), whole3)] * 4),
                pl.BlockSpec(segments.shape, whole),
                pl.BlockSpec((1, KVL), whole),
                pl.BlockSpec(cosine.shape, whole),
                pl.BlockSpec(sine.shape, whole),
                *([ANY] * len(after)),
            ],
            out_specs=[pl.BlockSpec((1, local_rows, KVL), lambda i, *_: (i, 0, 0))] * 4,
            scratch_shapes=[pltpu.VMEM((WIDTH, 2 * SHARE), BF)],
        ),
        out_shape=[out] * 4,
        compiler_params=SOME,
        cost_estimate=COST,
        name="attend",
    )(rank, first, *messages, *messages, own, *got, *tables, segments, gain, cosine, sine, *after)


def heads_kernel(step, slot, o_ref, keep_ref, *refs):
    out_ref = refs[-1]
    out_ref[...] = jnp.zeros_like(out_ref)
    for h, value_ref in enumerate(refs[:step]):
        row = jnp.dot(o_ref[h].astype(BF), value_ref[...], preferred_element_type=F32)
        row = (row * keep_ref[...]).astype(BF)
        for r in range(RP):
            out_ref[slot[r], :, h * DV : (h + 1) * DV] = row[2 * r : 2 * r + 2]


def heads_out(slot, attended, keep, kv_up, count, after):
    heads, rows, _ = attended.shape
    step = 8
    value_spec = [
        pl.BlockSpec((KVL, DV), lambda i, slot, h=h: (0, 2 * (step * i + h) + 1))
        for h in range(step)
    ]
    return pl.pallas_call(
        functools.partial(heads_kernel, step),
        grid_spec=pltpu.PrefetchScalarGridSpec(
            num_scalar_prefetch=1,
            grid=(heads // step,),
            in_specs=[
                pl.BlockSpec((step, rows, KVL), lambda i, slot: (i, 0, 0)),
                pl.BlockSpec((rows, DV), lambda i, slot: (0, 0)),
                *value_spec,
                *([ANY] * len(after)),
            ],
            out_specs=pl.BlockSpec((count, 2, step * DV), lambda i, slot: (0, 0, i)),
        ),
        out_shape=jax.ShapeDtypeStruct((count, 2, heads * DV), BF),
        compiler_params=ROOM,
        cost_estimate=COST,
        name="heads_out",
    )(slot, attended, keep, *([kv_up] * step), *after)


def emit_kernel(pages_ref, placed_ref, out_ref, same_ref, done):
    copy = pltpu.make_async_copy(pages_ref, out_ref, done)
    copy.start()
    copy.wait()


def emit(pages, placed):
    return pl.pallas_call(
        emit_kernel,
        in_specs=[VMEM, ANY],
        out_specs=[ANY, ANY],
        out_shape=[
            jax.ShapeDtypeStruct(pages.shape, pages.dtype),
            jax.ShapeDtypeStruct(placed.shape, placed.dtype),
        ],
        scratch_shapes=[pltpu.SemaphoreType.DMA],
        input_output_aliases={1: 1},
        compiler_params=SOME,
        cost_estimate=COST,
        name="emit",
    )(pages, placed)


def rope_tables(position):
    freq = jnp.exp(-jnp.log(10000.0) * jnp.arange(HALF, dtype=F32) / HALF)
    angle = position.astype(F32)[..., None] * freq
    return jnp.cos(angle), jnp.sin(angle)


def local_line(
    prefill_hidden,
    draft_hidden,
    kv_down,
    kv_gain,
    query_latent,
    q_up,
    kv_up,
    owners,
    segment_ids,
    accepted,
):
    pd_count = lax.axis_size("pd")
    z = lax.axis_index("tp")
    p = lax.axis_index("pd")
    first_req = p * RP

    gain = kv_gain.reshape(1, KVL)
    rank = z.astype(jnp.int32).reshape(1)
    hidden = prefill_hidden.reshape(RP, PRE_TOK, prefill_hidden.shape[1])
    down_t = kv_down.T
    inward, across, outward = [(0, 1), (3, 2)], [(1, 2), (2, 1)], [(2, 3), (1, 0)]

    far_sums, inner, crossed, sent, outer = [], [], [], [], []

    def send_far(r, after, draft=()):
        total, codes, *terms = project_far(rank, hidden, down_t, r, after, draft)
        far_sums.append(total)
        inner.append(lax.ppermute(codes, "tp", inward))
        return terms

    def first_hop(r, after, carried=()):
        block, *carried = add_on(rank, far_sums[r], inner[r], after=after, carried=carried)
        crossed.append(lax.ppermute(block, "tp", across))
        return [block, *carried]

    def second_hop(r, after, awaited=()):
        (block,) = add_on(rank, near_sums, crossed[r], r, after)
        if awaited:
            block = hold(block, awaited)
        sent.append(block)
        outer.append(lax.ppermute(block, "tp", outward))
        return [block]

    send_far(0, [])
    (terms,) = send_far(1, far_sums[:1], [draft_hidden])

    latents = lax.dynamic_slice_in_dim(query_latent, first_req, RP, 0).reshape(RP * 2, QL)
    new_pos = jnp.tile(PRE_TOK + jnp.arange(2, dtype=jnp.int32), RP)
    new_cos, new_sin = rope_tables(new_pos)
    query = queries(latents, q_up, kv_up, new_cos, new_sin, far_sums[1])
    heads = query.shape[0]
    query = query.reshape(heads, RP, 2, WIDTH).transpose(1, 2, 0, 3)
    message = jnp.concatenate(
        [query.reshape(RP * 2 * heads, WIDTH), terms.reshape(8 * RP, WIDTH)], 0
    ).astype(BF)
    messages = [lax.ppermute(message, "tp", [(t, 3)]) for t in range(3)] + [message]

    done = first_hop(0, [message])
    send_far(2, done)
    near_sums, *side = project_near(rank, hidden, down_t, far_sums[2:])
    done = first_hop(1, [near_sums])
    done = second_hop(0, done, messages[:3])
    send_far(3, done)
    steps = jnp.arange(SHARE, dtype=jnp.int32).reshape(UNITS, UNIT)
    tables = [
        jnp.swapaxes(t, 1, 2)
        for t in (*rope_tables(z * SHARE + steps), *rope_tables(2 * SHARE + steps))
    ]
    block, side[0] = first_hop(2, far_sums[3:], side[:1])
    side = [lax.ppermute(codes, "tp", inward) for codes in side]
    done = second_hop(1, [block], outer[:1])
    done = first_hop(3, done)
    done = second_hop(2, [*done, *tables], [outer[1], side[0]])
    done = second_hop(3, done, outer[2:])

    def attend_to(requests, after):
        result = attend(
            requests,
            rank,
            first_req.astype(jnp.int32).reshape(1),
            messages,
            near_sums,
            outer,
            tables,
            segment_ids,
            gain,
            new_cos,
            new_sin,
            after,
        )
        return result, [lax.ppermute(result[t], "tp", [(3, t)]) for t in range(3)]

    my_owners = lax.dynamic_slice_in_dim(owners, first_req, RP, 0)
    early, late = tuple(range(RP - 1)), (RP - 1,)

    def pages_to(requests, base, after):
        return pages_of(
            requests,
            rank,
            my_owners,
            near_sums,
            outer,
            sent,
            side,
            gain,
            tables[0],
            tables[1],
            base,
            pd_count,
            after,
        )

    results, backs = [None] * 2, [None] * 2
    results[0], backs[0] = attend_to(early, done)
    base = [jnp.zeros((pd_count, WIDTH, SHARE), BF)] if pd_count > RP else []
    pages = pages_to(early, base, results[0][:1])
    pages = pages_to(late, [pages], backs[0])
    results[1], backs[1] = attend_to(late, [pages])
    cache = lax.all_to_all(pages, "pd", split_axis=0, concat_axis=0, tiled=True)

    attended = [
        jnp.where(z == 3, result[3], back[0] + back[1] + back[2])
        for result, back in zip(results, backs)
    ]
    attended = jnp.concatenate(attended, 0).reshape(RP, 2, heads, KVL).transpose(2, 0, 1, 3)
    attended = attended.reshape(heads, RP * 2, KVL).astype(F32)
    my_accepted = lax.dynamic_slice_in_dim(accepted, first_req, RP, 0)
    keep = (jnp.arange(2)[None, :] <= my_accepted[:, None]).astype(F32).reshape(RP * 2, 1)
    placed = heads_out(
        my_owners,
        attended,
        jnp.broadcast_to(keep, (RP * 2, DV)),
        kv_up,
        pd_count,
        [pages],
    )
    cache, placed = emit(cache, placed)
    placed = lax.all_to_all(placed, "pd", split_axis=0, concat_axis=0, tiled=True)
    return (placed.reshape(pd_count * 2, heads * DV), jnp.swapaxes(cache, 1, 2))


def solution(mesh):
    placed = (
        P(("groups", "pd"), "tp"),
        P(("groups", "pd"), "tp"),
        P("tp", None),
        P(),
        P("groups", None, None),
        P(None, "tp"),
        P(None, "tp"),
        P("groups"),
        P("groups", None),
        P("groups"),
    )
    return jax.shard_map(
        local_line if mesh.shape["tp"] == 4 else local_general,
        mesh=mesh,
        in_specs=placed,
        out_specs=(P(("groups", "pd"), "tp"), P(("groups", "pd"), "tp", None)),
        check_vma=False,
    )
```
